32 devices in a mesh: batch: 16 (over z, y, core), seq: 2 (over x).
Axes of the slice: x: 2, y: 2, z: 4, core: 2. Of those that a mesh axis runs over, the one named last changes fastest.
Arguments:
- inputs: bfloat16 [48, 1024, 768], P('batch', 'seq'), may hold values from -6 to 6
- timesteps: int32 [48], P('batch'), may hold values from 0 to 1999, as said below
- counts: int32 [16], P('batch'), may hold values from 1 to 3, as said below
- slot_token_mask: int32 [48, 1024], P('batch', 'seq'), may hold values from 0 to 1, as said below
- time_first_weight: bfloat16 [128, 512], replicated, may hold values from -0.5 to 0.5
- time_second_weight: bfloat16 [512, 768], replicated, may hold values from -0.5 to 0.5
- attention_norm_gain: float32 [768], replicated, may hold values from 0.1 to 1.9
- query_key_value_weight: bfloat16 [768, 2304], replicated, may hold values from -0.21875 to 0.21875
- attention_output_weight: bfloat16 [768, 768], replicated, may hold values from -3.5 to 3.5
- feedforward_norm_gain: float32 [768], replicated, may hold values from 0.1 to 1.9
- up_projection_weight: bfloat16 [768, 3072], replicated, may hold values from -0.21875 to 0.21875
- down_projection_weight: bfloat16 [3072, 768], replicated, may hold values from -0.109375 to 0.109375
- cotangent: bfloat16 [48, 1024, 768], P('batch', 'seq'), may hold values from -6 to 6
Outputs:
- output: bfloat16 [48, 1024, 768], P('batch', 'seq')
- grad_inputs: float32 [48, 1024, 768], P('batch', 'seq')
- grad_time_inner: float32 [128, 512], P(None, 'batch')
- grad_time_outer: float32 [512, 768], P(None, 'batch')
- grad_attn_gain: float32 [768], P('batch')
- grad_qkv_weight: float32 [768, 1536], P(None, 'batch')
- grad_value_weight: float32 [768, 768], P(None, 'batch')
- grad_out_weight: float32 [768, 768], P(None, 'batch')
- grad_mlp_gain: float32 [768], P('batch')
- grad_up_weight: float32 [768, 3072], P(None, 'batch')
- grad_down_weight: float32 [3072, 768], P(None, 'batch')
The draws below stay inside these ranges and needn't reach their ends.
Inputs may be any that keep to these rules, and one draw needn't show every extreme that they name: Sorted ascending over the whole array, so each group holds a contiguous range of timesteps; small values are far more common than large ones. Group g holds its sequences in its first counts[g] slots; some group holds 3. `slot_token_mask`: each row is ones then zeros; in every group one of its first counts slots is all ones.
All inputs are finite; a program needn't handle non-finite values.
Results may differ from the reference program's by a relative error of at most 0.019.
Values may be sent and summed in bfloat16 or wider, within the bound.
A program may use at most 384 MiB of HBM per device.

```python
import math
from functools import partial
import jax
import jax.numpy as jnp
from jax import lax

D = 768
H = 12
DH = 64
FF = 3072
TCH = 128
TEMB = 512
TSTEPS = 2000
SEQUENCE_TOKENS = 1024
GROUP_SLOTS = 3
SEQS = 48
N_BATCH = 16


def group_counts(key):
    own_key = jax.random.fold_in(key, 11)
    first_key, second_key = jax.random.split(own_key)
    drawn = jax.random.randint(first_key, (N_BATCH,), 1, GROUP_SLOTS + 1)
    fullest = jax.random.randint(second_key, (), 0, N_BATCH)
    return jnp.where(jnp.arange(N_BATCH) == fullest, GROUP_SLOTS, drawn).astype(jnp.int32)


def draw_counts(key, part):
    return group_counts(key)


def draw_slot_token_mask(key, part):
    own_key = jax.random.fold_in(key, 5)
    group_sizes = group_counts(key)
    first_key, second_key = jax.random.split(own_key)
    lengths = jax.random.randint(first_key, (N_BATCH, GROUP_SLOTS), max(SEQUENCE_TOKENS // 2, 1), SEQUENCE_TOKENS + 1)
    chosen = jax.random.randint(second_key, (N_BATCH,), 0, GROUP_SLOTS) % group_sizes
    lengths = jnp.where(jnp.arange(GROUP_SLOTS)[None, :] == chosen[:, None], SEQUENCE_TOKENS, lengths)
    positions = jnp.arange(SEQUENCE_TOKENS)
    return (positions[None, None, :] < lengths[:, :, None]).astype(jnp.int32).reshape(SEQS, SEQUENCE_TOKENS)


def draw_timesteps(key, part):
    own_key = jax.random.fold_in(key, 7)
    subkeys = jax.random.split(own_key, 4)
    first_draw = jax.random.randint(subkeys[0], (SEQS,), 0, TSTEPS)
    second_draw = jax.random.randint(subkeys[1], (SEQS,), 0, TSTEPS)
    third_draw = jax.random.randint(subkeys[2], (SEQS,), 0, TSTEPS)
    skewed = first_draw * second_draw // TSTEPS * third_draw // TSTEPS
    chosen = jax.random.randint(subkeys[3], (), 0, SEQS)
    skewed = jnp.where(jnp.arange(SEQS) == chosen, TSTEPS - 1, skewed)
    return jnp.sort(skewed).astype(jnp.int32)


def with_spikes(array, key, source, target, blocks, factor):
    def block_of(dim):
        return (jnp.arange(array.shape[dim]) // (array.shape[dim] // blocks)).reshape((-1,) + (1,) * (array.ndim - 1 - dim))

    one_side = jax.random.permutation(key, blocks)[block_of(target)]
    second = (block_of(target) + blocks // 2) % blocks
    return jnp.where((block_of(source) == one_side) | (block_of(source) == second), factor * array, array)


def levels(key, dims, pieces, low, high):
    def one(position, blocks):
        heights = jax.random.uniform(jax.random.fold_in(jax.random.fold_in(key, 6), position), (blocks,), jnp.float32, low / len(pieces), high / len(pieces))
        return jnp.repeat(jnp.exp(heights), dims[position] // blocks).reshape((-1,) + (1,) * (len(dims) - position - 1))

    level = one(*pieces[0])
    for cut in pieces[1:]:
        level = level * one(*cut)
    return level


def normal_values(rng, shape, width, bound, cuts=(), dtype=jnp.bfloat16):
    entries = jax.random.normal(rng, shape, jnp.float32) * width
    if len(cuts) > 0:
        entries = levels(rng, shape, cuts, -0.22, 0.18) * entries
    return jnp.clip(entries, min=-bound, max=bound).astype(dtype)


def bell_draw_with(key, dims, spread, bound, shards, heavy, kind=jnp.bfloat16):
    values = spread * jax.random.normal(key, dims, jnp.float32)
    if shards:
        values = values * levels(key, dims, shards, -0.22, 0.18)
    return jnp.clip(with_spikes(values, jax.random.fold_in(key, 3), *heavy), -bound, bound).astype(kind)


def setup_inputs(seed: int = 0) -> dict:
    streams_of = jax.random.split(jax.random.key(seed), 14)
    return {
        "inputs": normal_values(streams_of[0], (SEQS, SEQUENCE_TOKENS, D), 1.0, 6.0, ((0, 16), (1, 2))),
        "timesteps": draw_timesteps(jax.random.fold_in(streams_of[13], 71), 0),
        "counts": draw_counts(jax.random.fold_in(streams_of[13], 71), 0),
        "slot_token_mask": draw_slot_token_mask(jax.random.fold_in(streams_of[13], 71), 0),
        "time_first_weight": normal_values(streams_of[4], (TCH, TEMB), TCH ** -0.5, 0.5),
        "time_second_weight": normal_values(streams_of[5], (TEMB, D), (TEMB // 4) ** -0.5, 0.5),
        "attention_norm_gain": jnp.clip(1.0 + 0.18 * jax.random.normal(streams_of[6], (D,), jnp.float32), 0.1, 1.9),
        "query_key_value_weight": normal_values(streams_of[7], (D, 3 * D), D ** -0.5, 0.21875),
        "attention_output_weight": normal_values(streams_of[8], (D, D), (D * 4 // SEQUENCE_TOKENS) ** -0.5, 3.5),
        "feedforward_norm_gain": jnp.clip(1.0 + 0.18 * jax.random.normal(streams_of[9], (D,), jnp.float32), 0.1, 1.9),
        "up_projection_weight": normal_values(streams_of[10], (D, FF), D ** -0.5, 0.21875),
        "down_projection_weight": normal_values(streams_of[11], (FF, D), FF ** -0.5, 0.109375),
        "cotangent": bell_draw_with(streams_of[12], (SEQS, SEQUENCE_TOKENS, D), 1.0, 6.0, ((0, 16), (1, 2)), (0, 2, 16, 2.0)),
    }


@jax.custom_vjp
def low(v):
    return lax.optimization_barrier(v.astype(jnp.bfloat16)).astype(jnp.float32)

@jax.custom_vjp
def low_back(v):
    return v

def low_keep(v):
    return (low(v), None)

def low_pass(kept, grad):
    return (grad,)

def back_keep(v):
    return (v, None)

def back_low(kept, grad):
    return (low(grad),)
low.defvjp(low_keep, low_pass)
low_back.defvjp(back_keep, back_low)
TOP_PRECISION = lax.Precision.HIGHEST

def sinusoid(steps):
    half_width = TCH // 2
    frequency = jnp.exp(-math.log(10000.0) * jnp.arange(half_width).astype(jnp.float32) / half_width)
    angles = steps.astype(jnp.float32)[:, None] * frequency[None, :]
    return jnp.concatenate([jnp.cos(angles), jnp.sin(angles)], axis=-1)

def layer_norm(hidden, gain):
    centered = hidden - lax.optimization_barrier(jnp.mean(hidden, axis=-1, keepdims=True))
    variance = lax.optimization_barrier(jnp.mean(centered * centered, axis=-1, keepdims=True))
    return centered * lax.rsqrt(variance + 1e-05) * gain

def time_mlp(time_embedding, time_first_weight, time_second_weight):
    pre_act = jnp.dot(time_embedding, time_first_weight, precision=TOP_PRECISION)
    return jnp.dot(jax.nn.silu(pre_act), time_second_weight, precision=TOP_PRECISION)

def project(input_rows, weight_matrix):
    return jnp.einsum('vmz,zg->vmg', input_rows, weight_matrix, precision=TOP_PRECISION)

def layer_block(slot_alive_flags, time_embedding, inputs, time_first_weight, time_second_weight, attention_norm_gain, query_key_value_weight, attention_output_weight, feedforward_norm_gain, up_projection_weight, down_projection_weight):
    seqs_here = inputs.shape[0]
    length = inputs.shape[1]
    residual = inputs + time_mlp(time_embedding, time_first_weight, time_second_weight)[:, None, :]
    normed = low(layer_norm(residual, attention_norm_gain))
    packed = low(low_back(project(normed, query_key_value_weight)))
    queries = packed[..., :D].reshape(seqs_here, length, H, DH)
    key_rows = packed[..., D:2 * D].reshape(seqs_here, length, H, DH)
    value_rows = packed[..., 2 * D:].reshape(seqs_here, length, H, DH)
    attention_scores = jnp.einsum('sqhd,skhd->shqk', queries, key_rows, precision=TOP_PRECISION) * (1.0 / math.sqrt(DH))
    attention_scores = low_back(jnp.where(slot_alive_flags[:, None, None, :] > 0.5, attention_scores, -1000000000.0))
    weights = low(jax.nn.softmax(attention_scores, axis=-1))
    attended = jnp.einsum('shqk,skhd->sqhd', weights, value_rows, precision=TOP_PRECISION).reshape(seqs_here, length, D)
    attended = low(low_back(attended))
    middle = residual + low_back(project(attended, attention_output_weight))
    normed_two = low(layer_norm(middle, feedforward_norm_gain))
    gate_pre = low_back(project(normed_two, up_projection_weight))
    activated = low(jax.nn.gelu(gate_pre, approximate=True))
    completed_groups = middle + low_back(project(activated, down_projection_weight))
    return slot_alive_flags[..., None] * completed_groups

def reference(inputs, timesteps, counts, slot_token_mask, time_first_weight, time_second_weight, attention_norm_gain, query_key_value_weight, attention_output_weight, feedforward_norm_gain, up_projection_weight, down_projection_weight, cotangent):
    params = tuple((matrix.astype(jnp.float32) for matrix in (time_first_weight, time_second_weight, attention_norm_gain, query_key_value_weight, attention_output_weight, feedforward_norm_gain, up_projection_weight, down_projection_weight)))
    grouped_sequences = inputs.astype(jnp.float32).reshape(N_BATCH, GROUP_SLOTS, SEQUENCE_TOKENS, D)
    cotangent_groups = cotangent.astype(jnp.float32).reshape(N_BATCH, GROUP_SLOTS, SEQUENCE_TOKENS, D)
    timestep_groups = timesteps.reshape(N_BATCH, GROUP_SLOTS)
    filled_slots = jnp.arange(GROUP_SLOTS)[None, :] < counts[:, None]
    slot_alive_flags = (filled_slots[:, :, None] & (slot_token_mask.reshape(N_BATCH, GROUP_SLOTS, SEQUENCE_TOKENS) == 1)).astype(jnp.float32)

    def step_forward(running_totals, group_item):
        group_in, group_steps, group_live, group_cot = group_item
        time_embedding = sinusoid(group_steps)
        result, backward = jax.vjp(partial(layer_block, group_live, time_embedding), group_in, *params)
        gradients = backward(group_cot)
        running_totals = tuple((running + addend for running, addend in zip(running_totals, gradients[1:])))
        return (running_totals, (result.astype(jnp.bfloat16), gradients[0]))
    initial_state = tuple((jnp.zeros_like(matrix) for matrix in params))
    running_totals, (layer_outputs, gradient_groups) = lax.scan(step_forward, initial_state, (grouped_sequences, timestep_groups, slot_alive_flags, cotangent_groups))
    qkv_total = running_totals[3]
    return (layer_outputs.reshape(SEQS, SEQUENCE_TOKENS, D), gradient_groups.reshape(SEQS, SEQUENCE_TOKENS, D), running_totals[0], running_totals[1], running_totals[2], qkv_total[:, :2 * D], qkv_total[:, 2 * D:], running_totals[4], running_totals[5], running_totals[6], running_totals[7])
```

```python
from functools import partial
import math

import jax
import jax.numpy as jnp
from jax import lax
from jax.experimental import pallas as pl
from jax.experimental.pallas import tpu as pltpu
from jax.sharding import PartitionSpec as P

H = 12
DH = 64
TCH = 128


TOP_PRECISION = lax.Precision.HIGHEST


def from_behind(array, axis, by):
    count = lax.axis_size(axis)
    return lax.ppermute(array, axis, [(i, (i + by) % count) for i in range(count)])


def shortened(array):

    def short(part):
        return part.astype(jnp.bfloat16) if part.dtype == jnp.float32 else part

    return jax.tree.map(short, array)


def sinusoid(steps):
    half_width = TCH // 2
    frequency = jnp.exp(
        -math.log(10000.0) * jnp.arange(half_width).astype(jnp.float32) / half_width
    )
    angles = steps.astype(jnp.float32)[:, None] * frequency[None, :]
    return jnp.concatenate([jnp.cos(angles), jnp.sin(angles)], axis=-1)


def layer_norm(hidden, gain):
    centered = hidden - jnp.mean(hidden, axis=-1, keepdims=True)
    variance = jnp.mean(centered * centered, axis=-1, keepdims=True)
    return centered * lax.rsqrt(variance + 1e-05) * gain


def time_mlp(time_embedding, time_first_weight, time_second_weight):
    pre_act = jnp.dot(time_embedding, time_first_weight, precision=TOP_PRECISION)
    return jnp.dot(jax.nn.silu(pre_act), time_second_weight, precision=TOP_PRECISION)


def row_product(left, right):
    return lax.dot_general(
        left, right, (((0,), (0,)), ((), ())), preferred_element_type=jnp.float32
    )


def back_product(left, right):
    return lax.dot_general(
        left, right, (((1,), (1,)), ((), ())), preferred_element_type=jnp.float32
    )


def masked_scores(queries, key_block, mask_block, scale_factor):
    attention_scores = (
        jnp.einsum("sqhd,skhd->shqk", queries, key_block, preferred_element_type=jnp.float32)
        * scale_factor
    )
    return jnp.where(mask_block[:, None, None, :] > 0.5, attention_scores, -1000000000.0)


def ring_plan(
    inputs,
    timesteps,
    counts,
    slot_token_mask,
    time_first_weight,
    time_second_weight,
    attention_norm_gain,
    query_key_value_weight,
    attention_output_weight,
    feedforward_norm_gain,
    up_projection_weight,
    down_projection_weight,
    cotangent,
):
    present_slots, local_len, width = inputs.shape
    total_rows = present_slots * local_len
    scale_factor = 1.0 / math.sqrt(DH)
    slot_alive_flags = (
        (jnp.arange(present_slots)[:, None] < counts[0]) & (slot_token_mask == 1)
    ).astype(jnp.float32)
    time_embedding = sinusoid(timesteps)
    time_vec, time_back = jax.vjp(
        partial(time_mlp, time_embedding),
        time_first_weight.astype(jnp.float32),
        time_second_weight.astype(jnp.float32),
    )
    residual = inputs.astype(jnp.float32) + time_vec[:, None, :]
    normed, norm_back = jax.vjp(layer_norm, residual, attention_norm_gain)
    normed_low = normed.astype(jnp.bfloat16).reshape(total_rows, width)
    packed = (
        jnp.dot(normed_low, query_key_value_weight, preferred_element_type=jnp.float32)
        .astype(jnp.bfloat16)
        .reshape(present_slots, local_len, 3 * width)
    )
    queries = packed[:, :, :width].reshape(present_slots, local_len, H, DH)
    key_rows = packed[:, :, width : 2 * width]
    value_rows = packed[:, :, 2 * width :]
    key_valid_mask = slot_alive_flags.astype(jnp.bfloat16)
    initial_state = (
        jnp.full((present_slots, H, local_len), -1e30, jnp.float32),
        jnp.zeros((present_slots, H, local_len), jnp.float32),
        jnp.zeros((present_slots, local_len, H, DH), jnp.float32),
    )
    key_piece = lax.all_gather(key_rows, "seq", axis=1, tiled=True)
    value_piece = lax.all_gather(value_rows, "seq", axis=1, tiled=True)
    mask_piece = lax.all_gather(key_valid_mask, "seq", axis=1, tiled=True)
    piece_len = key_piece.shape[1]
    block_len = min(piece_len, local_len)

    def one_block(position, inner_state):
        run_max, run_sum, running_totals = inner_state
        offset = position * block_len
        key_block = lax.dynamic_slice_in_dim(key_piece, offset, block_len, 1).reshape(
            present_slots, block_len, H, DH
        )
        value_block = lax.dynamic_slice_in_dim(value_piece, offset, block_len, 1).reshape(
            present_slots, block_len, H, DH
        )
        mask_block = lax.dynamic_slice_in_dim(mask_piece, offset, block_len, 1)
        attention_scores = masked_scores(queries, key_block, mask_block, scale_factor)
        new_max = jnp.maximum(run_max, jnp.max(attention_scores, axis=-1))
        exponent = jnp.exp(attention_scores - new_max[..., None])
        fading = jnp.exp(run_max - new_max)
        run_sum = run_sum * fading + jnp.sum(exponent, axis=-1)
        running_totals = running_totals * jnp.transpose(fading, (0, 2, 1))[..., None] + jnp.einsum(
            "shqk,skhd->sqhd",
            exponent.astype(jnp.bfloat16),
            value_block,
            preferred_element_type=jnp.float32,
        )
        return (new_max, run_sum, running_totals)

    run_max, run_sum, running_totals = lax.fori_loop(
        0, piece_len // block_len, one_block, initial_state
    )
    attended = running_totals / jnp.transpose(run_sum, (0, 2, 1))[..., None]
    log_total = run_max + jnp.log(run_sum)
    attended_low = attended.astype(jnp.bfloat16).reshape(total_rows, width)
    middle = residual + jnp.dot(
        attended_low, attention_output_weight, preferred_element_type=jnp.float32
    ).reshape(present_slots, local_len, width)
    normed_two, norm_two_back = jax.vjp(layer_norm, middle, feedforward_norm_gain)
    normed_two_low = normed_two.astype(jnp.bfloat16).reshape(total_rows, width)
    gate_pre = jnp.dot(normed_two_low, up_projection_weight, preferred_element_type=jnp.float32)
    activated, gelu_back = jax.vjp(partial(jax.nn.gelu, approximate=True), gate_pre)
    activated_low = activated.astype(jnp.bfloat16)
    completed_groups = middle + jnp.dot(
        activated_low, down_projection_weight, preferred_element_type=jnp.float32
    ).reshape(present_slots, local_len, width)
    output = (slot_alive_flags[..., None] * completed_groups).astype(jnp.bfloat16)
    final_gradient = slot_alive_flags[..., None] * cotangent.astype(jnp.float32)
    grad_down_low = final_gradient.reshape(total_rows, width).astype(jnp.bfloat16)
    down_grad = row_product(activated_low, grad_down_low)
    grad_gate = gelu_back(back_product(grad_down_low, down_projection_weight))[0].astype(
        jnp.bfloat16
    )
    up_grad = row_product(normed_two_low, grad_gate)
    grad_middle_norm, mlp_gain_grad = norm_two_back(
        back_product(grad_gate, up_projection_weight).reshape(present_slots, local_len, width)
    )
    grad_middle = final_gradient + grad_middle_norm
    grad_branch_low = grad_middle.reshape(total_rows, width).astype(jnp.bfloat16)
    out_grad = row_product(attended_low, grad_branch_low)
    grad_attended = (
        back_product(grad_branch_low, attention_output_weight)
        .astype(jnp.bfloat16)
        .reshape(present_slots, local_len, H, DH)
    )
    row_delta = jnp.transpose(
        jnp.sum(grad_attended.astype(jnp.float32) * attended, axis=-1), (0, 2, 1)
    )

    def key_terms(key_block, value_block, mask_block):
        attention_scores = masked_scores(queries, key_block, mask_block, scale_factor)
        probability = jnp.exp(attention_scores - log_total[..., None])
        grad_probs = jnp.einsum(
            "sqhd,skhd->shqk", grad_attended, value_block, preferred_element_type=jnp.float32
        )
        grad_scores = (probability * (grad_probs - row_delta[..., None])).astype(jnp.bfloat16)
        query_add = (
            jnp.einsum(
                "shqk,skhd->sqhd", grad_scores, key_block, preferred_element_type=jnp.float32
            )
            * scale_factor
        )
        key_add = (
            jnp.einsum("shqk,sqhd->skhd", grad_scores, queries, preferred_element_type=jnp.float32)
            * scale_factor
        )
        value_add = jnp.einsum(
            "shqk,sqhd->skhd",
            probability.astype(jnp.bfloat16),
            grad_attended,
            preferred_element_type=jnp.float32,
        )
        block_len = key_block.shape[1]
        return (
            query_add,
            key_add.reshape(present_slots, block_len, width),
            value_add.reshape(present_slots, block_len, width),
        )

    cycle_len = lax.axis_size("seq")
    query_zeros = jnp.zeros((present_slots, local_len, H, DH), jnp.float32)

    def visit(visit_index, loop_state):
        grad_queries, visiting, carried = loop_state
        query_add, key_add, value_add = key_terms(
            visiting[0].reshape(present_slots, local_len, H, DH),
            visiting[1].reshape(present_slots, local_len, H, DH),
            visiting[2],
        )
        carried = (carried[0] + key_add, carried[1] + value_add)
        visiting = from_behind((visiting[0], visiting[1], visiting[2]), "seq", 1)
        carried = (
            from_behind(carried[0].astype(jnp.bfloat16), "seq", 1).astype(jnp.float32),
            from_behind(carried[1].astype(jnp.bfloat16), "seq", 1).astype(jnp.float32),
        )
        return (grad_queries + query_add, tuple(visiting), tuple(carried))

    zeros_kv = jnp.zeros((present_slots, local_len, width), jnp.float32)
    grad_queries, visiting, carried = lax.fori_loop(
        0,
        cycle_len,
        visit,
        (query_zeros, (key_rows, value_rows, key_valid_mask), (zeros_kv, zeros_kv)),
    )
    grad_keys, grad_values = carried
    grad_packed = (
        jnp.concatenate(
            [grad_queries.reshape(present_slots, local_len, width), grad_keys, grad_values], axis=-1
        )
        .astype(jnp.bfloat16)
        .reshape(total_rows, 3 * width)
    )
    qkv_grad = row_product(normed_low, grad_packed)
    query_key_grad = qkv_grad[:, : 2 * width]
    value_grad = qkv_grad[:, 2 * width :]
    grad_start_norm, attn_gain_grad = norm_back(
        back_product(grad_packed, query_key_value_weight).reshape(present_slots, local_len, width)
    )
    grad_start = grad_middle + grad_start_norm
    inner_grad, outer_grad = time_back(jnp.sum(grad_start, axis=1))
    shares = (
        lax.psum_scatter(
            inner_grad.astype(jnp.bfloat16), "batch", scatter_dimension=1, tiled=True
        ).astype(jnp.float32),
        lax.psum_scatter(
            outer_grad.astype(jnp.bfloat16), "batch", scatter_dimension=1, tiled=True
        ).astype(jnp.float32),
        lax.psum_scatter(
            attn_gain_grad[None, :].astype(jnp.bfloat16), "batch", scatter_dimension=1, tiled=True
        ).astype(jnp.float32),
        lax.psum_scatter(
            query_key_grad.astype(jnp.bfloat16), "batch", scatter_dimension=1, tiled=True
        ).astype(jnp.float32),
        lax.psum_scatter(
            value_grad.astype(jnp.bfloat16), "batch", scatter_dimension=1, tiled=True
        ).astype(jnp.float32),
        lax.psum_scatter(
            out_grad.astype(jnp.bfloat16), "batch", scatter_dimension=1, tiled=True
        ).astype(jnp.float32),
        lax.psum_scatter(
            mlp_gain_grad[None, :].astype(jnp.bfloat16), "batch", scatter_dimension=1, tiled=True
        ).astype(jnp.float32),
        lax.psum_scatter(
            up_grad.astype(jnp.bfloat16), "batch", scatter_dimension=1, tiled=True
        ).astype(jnp.float32),
        lax.psum_scatter(
            down_grad.astype(jnp.bfloat16), "batch", scatter_dimension=1, tiled=True
        ).astype(jnp.float32),
    )
    summed = tuple(
        jax.tree.map(
            lambda part: part.astype(jnp.float32), lax.psum(shortened(tuple(shares)), "seq")
        )
    )
    return (
        output,
        grad_start,
        summed[0],
        summed[1],
        summed[2][0],
        summed[3],
        summed[4],
        summed[5],
        summed[6][0],
        summed[7],
        summed[8],
    )


BF = jnp.bfloat16
F32 = jnp.float32
MASKED = -1e9
GELU_A = 0.7978845608028654
GELU_B = 0.044715
VMEM_LIMIT = 60 * 2**20


def mm(left, right, left_dim, right_dim):
    return lax.dot_general(
        left, right, (((left_dim,), (right_dim,)), ((), ())), preferred_element_type=F32
    )


def attend_kernel(
    steps, q_ref, k_ref, v_ref, bias_ref, o_ref, exact_ref, inv_ref, even_ref, odd_ref,
    keys, query, v_even, v_odd, s_even, s_odd, m_even, m_odd,
):
    step = pl.program_id(0)
    piece, length = q_ref.shape[0], k_ref.shape[0]
    lane = lax.broadcasted_iota(jnp.int32, (1, 128), 1)
    now = jnp.minimum(step, steps - 1)
    before = jnp.maximum(step - 1, 0)

    @pl.when(step % 6 == 0)
    def _():
        keys[:, 128:] = bias_ref[...]
        query[:, 128:] = jnp.where(
            lax.broadcasted_iota(jnp.int32, (piece, 128), 1) == 0, 1.0, 0.0
        ).astype(BF)
        v_even[64:, :] = jnp.ones((16, length), BF)
        v_odd[64:, :] = jnp.ones((16, length), BF)

    keys[:, :128] = k_ref[...]

    def half(head, made, made_max, used, used_max, values, at, out_ref):
        query[:, :128] = jnp.where((lane // 64) == head, q_ref[...], jnp.zeros((), BF))
        top = used_max[0:1, :]
        scores = mm(keys[...], query[...], 1, 1)
        weight = jnp.exp(used[...] - top).astype(BF)
        made[...] = scores
        made_max[...] = jnp.broadcast_to(jnp.max(scores, axis=0, keepdims=True), made_max.shape)
        out_ref[0] = weight
        total = mm(values[...], weight, 1, 0)
        inverse = 1.0 / total[64:65]
        place = pl.ds(pl.multiple_of((at // 6) * piece, piece), piece)
        which = 2 * (at % 6) + 1 - head
        exact = total[:64] * inverse
        o_ref[which, :, place] = exact.astype(BF)
        exact_ref[which, :, place] = exact
        inv_ref[which, :, place] = jnp.broadcast_to(inverse, (8, piece))

    half(0, s_even, m_even, s_odd, m_odd, v_odd, before, odd_ref)
    turned = v_ref[...].T
    v_even[:64, :] = turned[:64]
    v_odd[:64, :] = turned[64:]
    half(1, s_odd, m_odd, s_even, m_even, v_even, now, even_ref)


def attend(q, kv, bias):
    rows, width = q.shape
    length = 2 * rows // 3
    piece = rows // 3
    steps = 18

    def now(t):
        t = jnp.minimum(t, steps - 1)
        return t // 6, t % 6

    def before(t):
        return jnp.maximum(t - 1, 0)

    whole = pl.BlockSpec(memory_space=pltpu.VMEM)
    return pl.pallas_call(
        partial(attend_kernel, steps),
        grid=(steps + 1,),
        in_specs=[
            pl.BlockSpec((piece, 128), now),
            pl.BlockSpec((length, 128), lambda t: (now(t)[0] // 2, now(t)[1])),
            pl.BlockSpec((length, 128), lambda t: (now(t)[0] // 2, 6 + now(t)[1])),
            pl.BlockSpec((length, 128), lambda t: (now(t)[0] // 2, 0)),
        ],
        out_specs=[
            whole,
            whole,
            whole,
            pl.BlockSpec((1, length, piece), lambda t: (jnp.minimum(t, steps - 1), 0, 0)),
            pl.BlockSpec((1, length, piece), lambda t: (before(t), 0, 0)),
        ],
        out_shape=[
            jax.ShapeDtypeStruct((H, DH, rows), BF),
            jax.ShapeDtypeStruct((H, DH, rows), F32),
            jax.ShapeDtypeStruct((H, 8, rows), F32),
            jax.ShapeDtypeStruct((steps, length, piece), BF),
            jax.ShapeDtypeStruct((steps, length, piece), BF),
        ],
        scratch_shapes=[
            pltpu.VMEM((length, 256), BF),
            pltpu.VMEM((piece, 256), BF),
            pltpu.VMEM((80, length), BF),
            pltpu.VMEM((80, length), BF),
            pltpu.VMEM((length, piece), F32),
            pltpu.VMEM((length, piece), F32),
            pltpu.VMEM((8, piece), F32),
            pltpu.VMEM((8, piece), F32),
        ],
        compiler_params=pltpu.CompilerParams(vmem_limit_bytes=VMEM_LIMIT),
        cost_estimate=pl.CostEstimate(flops=20 * 10**9, bytes_accessed=60 * 10**6, transcendentals=19 * 10**6),
    )(q, kv, kv, bias)


def attend_back_kernel(
    q_ref, k_ref, v_ref, do_ref, o_ref, inv_ref, even_ref, odd_ref, dq_ref, dk_ref, dv_ref,
    values, gradient, dk_sum, dv_sum,
):
    pair, part = pl.program_id(0), pl.program_id(1)
    piece, length = q_ref.shape[0], k_ref.shape[0]
    lane = lax.broadcasted_iota(jnp.int32, (1, 128), 1)
    zero = jnp.zeros((), BF)

    @pl.when((pair == 0) & (part == 0))
    def _():
        values[:, 128:] = jnp.where(
            lax.broadcasted_iota(jnp.int32, (length, 128), 1) < 3, 1.0, 0.0
        ).astype(BF)
        gradient[...] = jnp.zeros_like(gradient)

    values[:, :128] = v_ref[...]
    inverse = jnp.concatenate(
        [jnp.broadcast_to(inv_ref[head, 0:1, :], (DH, piece)) for head in range(2)], axis=0
    )
    scaled = do_ref[...].astype(F32) * inverse
    scaled = scaled.astype(BF)
    product = scaled.astype(F32) * o_ref[...]
    for head in range(2):
        mine = slice(DH * head, DH * head + DH)
        place = slice(piece * head, piece * head + piece)
        delta = -jnp.sum(product[mine], axis=0, keepdims=True)
        high = delta.astype(BF).astype(F32)
        rest = delta - high
        middle = rest.astype(BF).astype(F32)
        gradient[mine, place] = scaled[mine]
        gradient[128:136, place] = jnp.concatenate(
            [high, middle, rest - middle, jnp.zeros((5, piece), F32)], axis=0
        ).astype(BF)
    dp = mm(values[...], gradient[...], 1, 0)
    turned_keys = k_ref[...].T
    natural = scaled.T
    weights = [even_ref[0], odd_ref[0]]
    ds = [
        (weights[head].astype(F32) * dp[:, piece * head : piece * head + piece]).astype(BF)
        for head in range(2)
    ]

    def apart(array):
        return jnp.concatenate(
            [jnp.where(lane < 64, array, zero), jnp.where(lane < 64, zero, array)], axis=0
        )

    dv = mm(jnp.concatenate(weights, axis=1), apart(natural), 1, 0)
    dk = mm(jnp.concatenate(ds, axis=1), apart(q_ref[...]), 1, 0)
    for head in range(2):
        mine = slice(DH * head, DH * head + DH)
        dq_ref[mine, :] = (mm(turned_keys[mine], ds[head], 1, 0) * 0.125).astype(BF)

    @pl.when(part % 2 == 0)
    def _():
        dk_sum[...] = dk
        dv_sum[...] = dv

    @pl.when(part == 1)
    def _():
        dk_sum[...] += dk
        dv_sum[...] += dv

    dk_ref[...] = dk_sum[...].astype(BF)
    dv_ref[...] = dv_sum[...].astype(BF)


def attend_back(q, kv, do, o, inv, even, odd):
    rows, width = q.shape
    length = 2 * rows // 3
    piece = rows // 3
    weight_spec = pl.BlockSpec((1, length, piece), lambda p, j: (j * 6 + p, 0, 0))
    return pl.pallas_call(
        attend_back_kernel,
        grid=(6, 3),
        in_specs=[
            pl.BlockSpec((piece, 128), lambda p, j: (j, p)),
            pl.BlockSpec((length, 128), lambda p, j: (j // 2, p)),
            pl.BlockSpec((length, 128), lambda p, j: (j // 2, 6 + p)),
            pl.BlockSpec((128, piece), lambda p, j: (p, j)),
            pl.BlockSpec((128, piece), lambda p, j: (p, j)),
            pl.BlockSpec((2, 8, piece), lambda p, j: (p, 0, j)),
            weight_spec,
            weight_spec,
        ],
        out_specs=[
            pl.BlockSpec((128, piece), lambda p, j: (p, j)),
            pl.BlockSpec((length, 128), lambda p, j: (j // 2, p)),
            pl.BlockSpec((length, 128), lambda p, j: (j // 2, p)),
        ],
        out_shape=[
            jax.ShapeDtypeStruct((width, rows), BF),
            jax.ShapeDtypeStruct((2 * length, width), BF),
            jax.ShapeDtypeStruct((2 * length, width), BF),
        ],
        scratch_shapes=[
            pltpu.VMEM((length, 256), BF),
            pltpu.VMEM((256, 2 * piece), BF),
            pltpu.VMEM((length, 128), F32),
            pltpu.VMEM((length, 128), F32),
        ],
        compiler_params=pltpu.CompilerParams(vmem_limit_bytes=VMEM_LIMIT),
        cost_estimate=pl.CostEstimate(flops=30 * 10**9, bytes_accessed=60 * 10**6, transcendentals=0),
    )(q, kv, kv, do, o, inv, even, odd)


def gelu_and_slope(g):
    square = g * g
    half_plus = 0.5 * jnp.tanh(g * (GELU_A + GELU_A * GELU_B * square)) + 0.5
    act = g * half_plus
    slope = half_plus + act * (2.0 - 2.0 * half_plus) * (GELU_A + 3.0 * GELU_A * GELU_B * square)
    return act, slope


def feedforward_kernel(
    x_ref, o_ref, dm_in_ref, live_ref, temb_ref, gain_ref, wo_ref, wu_ref, wd_ref,
    out_ref, dh1_ref, do_ref, dwu_ref, dwd_ref, dwo_ref, dgain_ref,
    h1, n2, dm, h2, dn2,
):
    chunk, chunks = pl.program_id(0), pl.num_programs(0)
    rows = x_ref.shape[0]
    block = rows // 2
    third = rows // 3
    blocks = [slice(block * i, block * i + block) for i in range(2)]
    thirds = [slice(third * i, third * i + third) for i in range(3)]

    @pl.when(chunk == 0)
    def _():
        for i, part in enumerate(thirds):
            h0 = x_ref[part, :].astype(F32) + temb_ref[i // 2 : i // 2 + 1, :]
            h = h0 + mm(o_ref[:, part], wo_ref[...], 0, 0)
            h1[part, :] = h
            centered = h - jnp.mean(h, axis=1, keepdims=True)
            variance = jnp.mean(centered * centered, axis=1, keepdims=True)
            n2[part, :] = (centered * lax.rsqrt(variance + 1e-5) * gain_ref[...]).astype(BF)
            dm[part, :] = dm_in_ref[part, :]
            h2[part, :] = h
            dn2[part, :] = jnp.zeros_like(h)

    def first(part):
        return mm(n2[part, :], wu_ref[...], 1, 0), mm(dm[part, :], wd_ref[...], 1, 1)

    def second(pair):
        act, slope = gelu_and_slope(pair[0])
        return act.astype(BF), (pair[1] * slope).astype(BF)

    def third_step(part, pair):
        h2[part, :] += mm(pair[0], wd_ref[...], 1, 0)
        dn2[part, :] += mm(pair[1], wu_ref[...], 1, 1)

    a = first(blocks[0])
    b = first(blocks[1])
    a = second(a)
    b = second(b)
    third_step(blocks[0], a)
    third_step(blocks[1], b)
    act = jnp.concatenate([a[0], b[0]], axis=0)
    dg = jnp.concatenate([a[1], b[1]], axis=0)
    dwd_ref[...] = mm(dm[...], act, 0, 0).astype(BF)
    dwu_ref[...] = mm(dg, n2[...], 0, 0).astype(BF)

    @pl.when(chunk == chunks - 1)
    def _():
        dgain = jnp.zeros_like(dgain_ref)
        for part in thirds:
            h = h1[part, :]
            live = live_ref[part, 0:1].astype(F32)
            out_ref[part, :] = (live * h2[part, :]).astype(BF)
            centered = h - jnp.mean(h, axis=1, keepdims=True)
            variance = jnp.mean(centered * centered, axis=1, keepdims=True)
            r2 = lax.rsqrt(variance + 1e-5)
            x2 = centered * r2
            dn = dn2[part, :]
            dgain += jnp.sum(dn * x2, axis=0, keepdims=True)
            e = dn * gain_ref[...]
            dh1 = dm_in_ref[part, :].astype(F32) + r2 * (
                e
                - jnp.mean(e, axis=1, keepdims=True)
                - x2 * jnp.mean(e * x2, axis=1, keepdims=True)
            )
            dh1_ref[part, :] = dh1
            da = dh1.astype(BF)
            dm[part, :] = da
            do_ref[:, part] = mm(wo_ref[...], da, 1, 1).astype(BF)
        dgain_ref[...] = dgain
        dwo_ref[...] = mm(dm[...], o_ref[...], 0, 1).astype(BF)


def feedforward(x, o, dm, live, temb, gain, wo, wu, wd):
    rows, width = x.shape
    hidden = wu.shape[1]
    size = 512
    whole = pl.BlockSpec(memory_space=pltpu.VMEM)
    return pl.pallas_call(
        feedforward_kernel,
        grid=(hidden // size,),
        in_specs=[whole] * 7
        + [
            pl.BlockSpec((width, size), lambda i: (0, i)),
            pl.BlockSpec((size, width), lambda i: (i, 0)),
        ],
        out_specs=[
            whole,
            whole,
            whole,
            pl.BlockSpec((size, width), lambda i: (i, 0)),
            pl.BlockSpec((width, size), lambda i: (0, i)),
            whole,
            whole,
        ],
        out_shape=[
            jax.ShapeDtypeStruct((rows, width), BF),
            jax.ShapeDtypeStruct((rows, width), F32),
            jax.ShapeDtypeStruct((width, rows), BF),
            jax.ShapeDtypeStruct((hidden, width), BF),
            jax.ShapeDtypeStruct((width, hidden), BF),
            jax.ShapeDtypeStruct((width, width), BF),
            jax.ShapeDtypeStruct((1, width), F32),
        ],
        scratch_shapes=[
            pltpu.VMEM((rows, width), F32),
            pltpu.VMEM((rows, width), BF),
            pltpu.VMEM((rows, width), BF),
            pltpu.VMEM((rows, width), F32),
            pltpu.VMEM((rows, width), F32),
        ],
        compiler_params=pltpu.CompilerParams(vmem_limit_bytes=VMEM_LIMIT),
        cost_estimate=pl.CostEstimate(flops=48 * 10**9, bytes_accessed=50 * 10**6, transcendentals=5 * 10**6),
    )(x, o, dm, live, temb, gain, wo, wu, wd)


def halving_sum(array):
    count = lax.axis_size("batch")
    me = lax.axis_index("batch")
    bits = count.bit_length() - 1
    parts = array.reshape((2,) * bits + array.shape[1:])
    order = [0] + list(range(1, bits))
    left = list(range(bits - 1, -1, -1))
    for bit in order:
        axis = left.index(bit)
        left.remove(bit)
        mine = (me >> bit) & 1
        keep = lax.dynamic_index_in_dim(parts, mine, axis, keepdims=False)
        send = lax.dynamic_index_in_dim(parts, 1 - mine, axis, keepdims=False)
        got = lax.ppermute(send, "batch", [(i, i ^ (1 << bit)) for i in range(count)])
        parts = (keep.astype(F32) + got.astype(F32)).astype(BF)
    got = lax.ppermute(parts, "seq", [(0, 1), (1, 0)])
    return parts.astype(F32) + got.astype(F32)


def pair_plan(
    inputs,
    timesteps,
    counts,
    slot_token_mask,
    time_first_weight,
    time_second_weight,
    attention_norm_gain,
    query_key_value_weight,
    attention_output_weight,
    feedforward_norm_gain,
    up_projection_weight,
    down_projection_weight,
    cotangent,
):
    slots, half, width = inputs.shape
    batches = lax.axis_size("batch")
    me = lax.axis_index("seq")
    swap = [(0, 1), (1, 0)]

    def at(array, index):
        return lax.dynamic_index_in_dim(array, index, 0, keepdims=False)

    def across(array):
        return lax.ppermute(array, "seq", swap)

    x_far = across(at(inputs, 1 - me))
    x_far_two = across(inputs[2])
    live_here = (
        (jnp.arange(slots)[:, None] < counts[0]) & (slot_token_mask == 1)
    ).astype(BF)
    live_far = across(live_here)
    dm_here = cotangent * live_here[:, :, None]
    dm_far = across(at(dm_here, 1 - me))

    x = jnp.concatenate([at(inputs, me), x_far, inputs[2], x_far_two], axis=0)
    live = jnp.concatenate([at(live_here, me), at(live_far, me), live_here[2], live_far[2]], axis=0)
    dm = jnp.concatenate([at(dm_here, me), dm_far, dm_here[2]], axis=0)
    bias = jnp.where(
        (jnp.arange(128) == 0)[None, :] & (live == 0)[:, None], MASKED, 0.0
    ).astype(BF)
    live_wide = jnp.broadcast_to(live[: 3 * half, None], (3 * half, 128))

    time_embedding = sinusoid(timesteps)
    first_low = time_first_weight.astype(F32)
    second_low = time_second_weight.astype(F32)
    time_vec = time_mlp(time_embedding, first_low, second_low)
    temb = jnp.stack([at(time_vec, me), time_vec[2]])

    h0 = (x.astype(F32).reshape(2, 2 * half, width) + temb[:, None, :]).reshape(4 * half, width)
    centered = h0 - jnp.mean(h0, axis=-1, keepdims=True)
    r1 = lax.rsqrt(jnp.mean(centered * centered, axis=-1, keepdims=True) + 1e-05)
    x1 = centered * r1
    n1 = (x1 * attention_norm_gain).astype(BF)
    q = (
        jnp.dot(n1[: 3 * half], query_key_value_weight[:, :width], preferred_element_type=F32)
        * 0.125
    ).astype(BF)
    kv = jnp.dot(n1, query_key_value_weight[:, width:], preferred_element_type=F32).astype(BF)

    o, exact, inv, even, odd = attend(q, kv, bias)
    o = o.reshape(width, 3 * half)
    out, dh1, do, dwu, dwd, dwo, dgain2 = feedforward(
        x[: 3 * half],
        o,
        dm,
        live_wide,
        temb,
        feedforward_norm_gain[None, :],
        attention_output_weight,
        up_projection_weight,
        down_projection_weight,
    )
    out_far = across(out[half : 2 * half])
    output = jnp.where(
        me == 0,
        jnp.stack([out[:half], out_far, out[2 * half :]]),
        jnp.stack([out_far, out[:half], out[2 * half :]]),
    )
    up_sum = halving_sum(dwu.reshape(batches, -1, width))
    down_sum = halving_sum(dwd.reshape(batches, width // batches, -1))

    dq, dk, dv = attend_back(q, kv, do, exact.reshape(width, 3 * half), inv, even, odd)

    dwq = mm(dq, n1[: 3 * half], 1, 0).astype(BF)
    dwk = mm(dk, n1, 0, 0).astype(BF)
    dwv = mm(dv, n1, 0, 0).astype(BF)
    dn1_kv = back_product(jnp.concatenate([dk, dv], axis=1), query_key_value_weight[:, width:])
    dn1_far = across(dn1_kv[3 * half :].astype(BF))
    dn1 = dn1_kv[: 3 * half] + mm(dq, query_key_value_weight[:, :width], 0, 1)
    dn1 = jnp.concatenate([dn1[: 2 * half], dn1[2 * half :] + dn1_far.astype(F32)], axis=0)
    x1, r1 = x1[: 3 * half], r1[: 3 * half]
    dgain1 = jnp.sum(dn1 * x1, axis=0)
    e = dn1 * attention_norm_gain
    dh0 = dh1 + r1 * (
        e - jnp.mean(e, axis=-1, keepdims=True) - x1 * jnp.mean(e * x1, axis=-1, keepdims=True)
    )
    dh0_far = across(dh0[half : 2 * half].astype(BF)).astype(F32)
    grad_inputs = jnp.where(
        me == 0,
        jnp.stack([dh0[:half], dh0_far, dh0[2 * half :]]),
        jnp.stack([dh0_far, dh0[:half], dh0[2 * half :]]),
    )

    dtemb_one = jnp.sum(dh0[: 2 * half], axis=0)
    dtemb_two = jnp.sum(dh0[2 * half :], axis=0)
    is_first = (me == 0).astype(F32)
    small = jnp.stack(
        [is_first * dtemb_one, (1.0 - is_first) * dtemb_one, dtemb_two, dgain1, dgain2[0]]
        + [jnp.zeros_like(dgain1)] * 3
    )
    small = lax.all_gather(lax.all_gather(small, "seq"), "batch")
    small = jnp.sum(small, axis=1)
    steps_all = lax.all_gather(timesteps, "batch", tiled=True)
    dtemb = small[:, :3].reshape(batches * 3, width)
    emb_all = sinusoid(steps_all)
    u_all, silu_back = jax.vjp(
        lambda a: jax.nn.silu(a), jnp.dot(emb_all, first_low, precision=TOP_PRECISION)
    )
    mine = lax.axis_index("batch")
    columns = width // batches
    inner_columns = first_low.shape[1] // batches

    def cut(array, size):
        return lax.dynamic_slice_in_dim(array, mine * size, size, array.ndim - 1)

    grad_outer = lax.dot_general(
        u_all, cut(dtemb, columns), (((0,), (0,)), ((), ())), precision=TOP_PRECISION
    )
    dsilu = lax.dot_general(
        dtemb, second_low, (((1,), (1,)), ((), ())), precision=TOP_PRECISION
    )
    grad_inner = lax.dot_general(
        emb_all,
        cut(silu_back(dsilu)[0], inner_columns),
        (((0,), (0,)), ((), ())),
        precision=TOP_PRECISION,
    )
    gains = jnp.sum(small[:, 3:5], axis=0)
    out_sum = halving_sum(dwo.reshape(batches, -1, width))
    qk_sum = halving_sum(jnp.concatenate([dwq, dwk], axis=0).reshape(batches, -1, width))
    v_sum = halving_sum(dwv.reshape(batches, -1, width))
    return (
        output,
        grad_inputs,
        grad_inner,
        grad_outer,
        cut(gains[0], columns),
        qk_sum.T,
        v_sum.T,
        out_sum.T,
        cut(gains[1], columns),
        up_sum.T,
        down_sum.T,
    )


def solution(mesh):
    on_device = pair_plan if mesh.shape["seq"] == 2 else ring_plan
    return jax.shard_map(
        on_device,
        mesh=mesh,
        in_specs=(
            P("batch", "seq", None),
            P("batch"),
            P("batch"),
            P("batch", "seq"),
            P(),
            P(),
            P(),
            P(),
            P(),
            P(),
            P(),
            P(),
            P("batch", "seq", None),
        ),
        out_specs=(
            P("batch", "seq", None),
            P("batch", "seq", None),
            P(None, "batch"),
            P(None, "batch"),
            P("batch"),
            P(None, "batch"),
            P(None, "batch"),
            P(None, "batch"),
            P("batch"),
            P(None, "batch"),
            P(None, "batch"),
        ),
        check_vma=False,
    )
```

```python
from functools import partial
import math

import jax
import jax.numpy as jnp
from jax import lax
from jax.experimental import pallas as pl
from jax.experimental.pallas import tpu as pltpu
from jax.sharding import PartitionSpec as P

H = 12
DH = 64
TCH = 128


TOP_PRECISION = lax.Precision.HIGHEST


def from_behind(array, axis, by):
    count = lax.axis_size(axis)
    return lax.ppermute(array, axis, [(i, (i + by) % count) for i in range(count)])


def shortened(array):

    def short(part):
        return part.astype(jnp.bfloat16) if part.dtype == jnp.float32 else part

    return jax.tree.map(short, array)


def sinusoid(steps):
    half_width = TCH // 2
    frequency = jnp.exp(
        -math.log(10000.0) * jnp.arange(half_width).astype(jnp.float32) / half_width
    )
    angles = steps.astype(jnp.float32)[:, None] * frequency[None, :]
    return jnp.concatenate([jnp.cos(angles), jnp.sin(angles)], axis=-1)


def layer_norm(hidden, gain):
    centered = hidden - jnp.mean(hidden, axis=-1, keepdims=True)
    variance = jnp.mean(centered * centered, axis=-1, keepdims=True)
    return centered * lax.rsqrt(variance + 1e-05) * gain


def time_mlp(time_embedding, time_first_weight, time_second_weight):
    pre_act = jnp.dot(time_embedding, time_first_weight, precision=TOP_PRECISION)
    return jnp.dot(jax.nn.silu(pre_act), time_second_weight, precision=TOP_PRECISION)


def row_product(left, right):
    return lax.dot_general(
        left, right, (((0,), (0,)), ((), ())), preferred_element_type=jnp.float32
    )


def back_product(left, right):
    return lax.dot_general(
        left, right, (((1,), (1,)), ((), ())), preferred_element_type=jnp.float32
    )


def masked_scores(queries, key_block, mask_block, scale_factor):
    attention_scores = (
        jnp.einsum("sqhd,skhd->shqk", queries, key_block, preferred_element_type=jnp.float32)
        * scale_factor
    )
    return jnp.where(mask_block[:, None, None, :] > 0.5, attention_scores, -1000000000.0)


def ring_plan(
    inputs,
    timesteps,
    counts,
    slot_token_mask,
    time_first_weight,
    time_second_weight,
    attention_norm_gain,
    query_key_value_weight,
    attention_output_weight,
    feedforward_norm_gain,
    up_projection_weight,
    down_projection_weight,
    cotangent,
):
    present_slots, local_len, width = inputs.shape
    total_rows = present_slots * local_len
    scale_factor = 1.0 / math.sqrt(DH)
    slot_alive_flags = (
        (jnp.arange(present_slots)[:, None] < counts[0]) & (slot_token_mask == 1)
    ).astype(jnp.float32)
    time_embedding = sinusoid(timesteps)
    time_vec, time_back = jax.vjp(
        partial(time_mlp, time_embedding),
        time_first_weight.astype(jnp.float32),
        time_second_weight.astype(jnp.float32),
    )
    residual = inputs.astype(jnp.float32) + time_vec[:, None, :]
    normed, norm_back = jax.vjp(layer_norm, residual, attention_norm_gain)
    normed_low = normed.astype(jnp.bfloat16).reshape(total_rows, width)
    packed = (
        jnp.dot(normed_low, query_key_value_weight, preferred_element_type=jnp.float32)
        .astype(jnp.bfloat16)
        .reshape(present_slots, local_len, 3 * width)
    )
    queries = packed[:, :, :width].reshape(present_slots, local_len, H, DH)
    key_rows = packed[:, :, width : 2 * width]
    value_rows = packed[:, :, 2 * width :]
    key_valid_mask = slot_alive_flags.astype(jnp.bfloat16)
    initial_state = (
        jnp.full((present_slots, H, local_len), -1e30, jnp.float32),
        jnp.zeros((present_slots, H, local_len), jnp.float32),
        jnp.zeros((present_slots, local_len, H, DH), jnp.float32),
    )
    key_piece = lax.all_gather(key_rows, "seq", axis=1, tiled=True)
    value_piece = lax.all_gather(value_rows, "seq", axis=1, tiled=True)
    mask_piece = lax.all_gather(key_valid_mask, "seq", axis=1, tiled=True)
    piece_len = key_piece.shape[1]
    block_len = min(piece_len, local_len)

    def one_block(position, inner_state):
        run_max, run_sum, running_totals = inner_state
        offset = position * block_len
        key_block = lax.dynamic_slice_in_dim(key_piece, offset, block_len, 1).reshape(
            present_slots, block_len, H, DH
        )
        value_block = lax.dynamic_slice_in_dim(value_piece, offset, block_len, 1).reshape(
            present_slots, block_len, H, DH
        )
        mask_block = lax.dynamic_slice_in_dim(mask_piece, offset, block_len, 1)
        attention_scores = masked_scores(queries, key_block, mask_block, scale_factor)
        new_max = jnp.maximum(run_max, jnp.max(attention_scores, axis=-1))
        exponent = jnp.exp(attention_scores - new_max[..., None])
        fading = jnp.exp(run_max - new_max)
        run_sum = run_sum * fading + jnp.sum(exponent, axis=-1)
        running_totals = running_totals * jnp.transpose(fading, (0, 2, 1))[..., None] + jnp.einsum(
            "shqk,skhd->sqhd",
            exponent.astype(jnp.bfloat16),
            value_block,
            preferred_element_type=jnp.float32,
        )
        return (new_max, run_sum, running_totals)

    run_max, run_sum, running_totals = lax.fori_loop(
        0, piece_len // block_len, one_block, initial_state
    )
    attended = running_totals / jnp.transpose(run_sum, (0, 2, 1))[..., None]
    log_total = run_max + jnp.log(run_sum)
    attended_low = attended.astype(jnp.bfloat16).reshape(total_rows, width)
    middle = residual + jnp.dot(
        attended_low, attention_output_weight, preferred_element_type=jnp.float32
    ).reshape(present_slots, local_len, width)
    normed_two, norm_two_back = jax.vjp(layer_norm, middle, feedforward_norm_gain)
    normed_two_low = normed_two.astype(jnp.bfloat16).reshape(total_rows, width)
    gate_pre = jnp.dot(normed_two_low, up_projection_weight, preferred_element_type=jnp.float32)
    activated, gelu_back = jax.vjp(partial(jax.nn.gelu, approximate=True), gate_pre)
    activated_low = activated.astype(jnp.bfloat16)
    completed_groups = middle + jnp.dot(
        activated_low, down_projection_weight, preferred_element_type=jnp.float32
    ).reshape(present_slots, local_len, width)
    output = (slot_alive_flags[..., None] * completed_groups).astype(jnp.bfloat16)
    final_gradient = slot_alive_flags[..., None] * cotangent.astype(jnp.float32)
    grad_down_low = final_gradient.reshape(total_rows, width).astype(jnp.bfloat16)
    down_grad = row_product(activated_low, grad_down_low)
    grad_gate = gelu_back(back_product(grad_down_low, down_projection_weight))[0].astype(
        jnp.bfloat16
    )
    up_grad = row_product(normed_two_low, grad_gate)
    grad_middle_norm, mlp_gain_grad = norm_two_back(
        back_product(grad_gate, up_projection_weight).reshape(present_slots, local_len, width)
    )
    grad_middle = final_gradient + grad_middle_norm
    grad_branch_low = grad_middle.reshape(total_rows, width).astype(jnp.bfloat16)
    out_grad = row_product(attended_low, grad_branch_low)
    grad_attended = (
        back_product(grad_branch_low, attention_output_weight)
        .astype(jnp.bfloat16)
        .reshape(present_slots, local_len, H, DH)
    )
    row_delta = jnp.transpose(
        jnp.sum(grad_attended.astype(jnp.float32) * attended, axis=-1), (0, 2, 1)
    )

    def key_terms(key_block, value_block, mask_block):
        attention_scores = masked_scores(queries, key_block, mask_block, scale_factor)
        probability = jnp.exp(attention_scores - log_total[..., None])
        grad_probs = jnp.einsum(
            "sqhd,skhd->shqk", grad_attended, value_block, preferred_element_type=jnp.float32
        )
        grad_scores = (probability * (grad_probs - row_delta[..., None])).astype(jnp.bfloat16)
        query_add = (
            jnp.einsum(
                "shqk,skhd->sqhd", grad_scores, key_block, preferred_element_type=jnp.float32
            )
            * scale_factor
        )
        key_add = (
            jnp.einsum("shqk,sqhd->skhd", grad_scores, queries, preferred_element_type=jnp.float32)
            * scale_factor
        )
        value_add = jnp.einsum(
            "shqk,sqhd->skhd",
            probability.astype(jnp.bfloat16),
            grad_attended,
            preferred_element_type=jnp.float32,
        )
        block_len = key_block.shape[1]
        return (
            query_add,
            key_add.reshape(present_slots, block_len, width),
            value_add.reshape(present_slots, block_len, width),
        )

    cycle_len = lax.axis_size("seq")
    query_zeros = jnp.zeros((present_slots, local_len, H, DH), jnp.float32)

    def visit(visit_index, loop_state):
        grad_queries, visiting, carried = loop_state
        query_add, key_add, value_add = key_terms(
            visiting[0].reshape(present_slots, local_len, H, DH),
            visiting[1].reshape(present_slots, local_len, H, DH),
            visiting[2],
        )
        carried = (carried[0] + key_add, carried[1] + value_add)
        visiting = from_behind((visiting[0], visiting[1], visiting[2]), "seq", 1)
        carried = (
            from_behind(carried[0].astype(jnp.bfloat16), "seq", 1).astype(jnp.float32),
            from_behind(carried[1].astype(jnp.bfloat16), "seq", 1).astype(jnp.float32),
        )
        return (grad_queries + query_add, tuple(visiting), tuple(carried))

    zeros_kv = jnp.zeros((present_slots, local_len, width), jnp.float32)
    grad_queries, visiting, carried = lax.fori_loop(
        0,
        cycle_len,
        visit,
        (query_zeros, (key_rows, value_rows, key_valid_mask), (zeros_kv, zeros_kv)),
    )
    grad_keys, grad_values = carried
    grad_packed = (
        jnp.concatenate(
            [grad_queries.reshape(present_slots, local_len, width), grad_keys, grad_values], axis=-1
        )
        .astype(jnp.bfloat16)
        .reshape(total_rows, 3 * width)
    )
    qkv_grad = row_product(normed_low, grad_packed)
    query_key_grad = qkv_grad[:, : 2 * width]
    value_grad = qkv_grad[:, 2 * width :]
    grad_start_norm, attn_gain_grad = norm_back(
        back_product(grad_packed, query_key_value_weight).reshape(present_slots, local_len, width)
    )
    grad_start = grad_middle + grad_start_norm
    inner_grad, outer_grad = time_back(jnp.sum(grad_start, axis=1))
    shares = (
        lax.psum_scatter(
            inner_grad.astype(jnp.bfloat16), "batch", scatter_dimension=1, tiled=True
        ).astype(jnp.float32),
        lax.psum_scatter(
            outer_grad.astype(jnp.bfloat16), "batch", scatter_dimension=1, tiled=True
        ).astype(jnp.float32),
        lax.psum_scatter(
            attn_gain_grad[None, :].astype(jnp.bfloat16), "batch", scatter_dimension=1, tiled=True
        ).astype(jnp.float32),
        lax.psum_scatter(
            query_key_grad.astype(jnp.bfloat16), "batch", scatter_dimension=1, tiled=True
        ).astype(jnp.float32),
        lax.psum_scatter(
            value_grad.astype(jnp.bfloat16), "batch", scatter_dimension=1, tiled=True
        ).astype(jnp.float32),
        lax.psum_scatter(
            out_grad.astype(jnp.bfloat16), "batch", scatter_dimension=1, tiled=True
        ).astype(jnp.float32),
        lax.psum_scatter(
            mlp_gain_grad[None, :].astype(jnp.bfloat16), "batch", scatter_dimension=1, tiled=True
        ).astype(jnp.float32),
        lax.psum_scatter(
            up_grad.astype(jnp.bfloat16), "batch", scatter_dimension=1, tiled=True
        ).astype(jnp.float32),
        lax.psum_scatter(
            down_grad.astype(jnp.bfloat16), "batch", scatter_dimension=1, tiled=True
        ).astype(jnp.float32),
    )
    summed = tuple(
        jax.tree.map(
            lambda part: part.astype(jnp.float32), lax.psum(shortened(tuple(shares)), "seq")
        )
    )
    return (
        output,
        grad_start,
        summed[0],
        summed[1],
        summed[2][0],
        summed[3],
        summed[4],
        summed[5],
        summed[6][0],
        summed[7],
        summed[8],
    )


BF = jnp.bfloat16
F32 = jnp.float32
MASKED = -1e9
GELU_A = 0.7978845608028654
GELU_B = 0.044715
VMEM_LIMIT = 60 * 2**20


def mm(left, right, left_dim, right_dim):
    return lax.dot_general(
        left, right, (((left_dim,), (right_dim,)), ((), ())), preferred_element_type=F32
    )


def attend_kernel(
    steps, q_ref, k_ref, v_ref, bias_ref, o_ref, exact_ref, inv_ref, even_ref, odd_ref,
    keys, query, v_even, v_odd, s_even, s_odd, m_even, m_odd,
):
    step = pl.program_id(0)
    piece, length = q_ref.shape[0], k_ref.shape[0]
    lane = lax.broadcasted_iota(jnp.int32, (1, 128), 1)
    now = jnp.minimum(step, steps - 1)
    before = jnp.maximum(step - 1, 0)

    @pl.when(step % 6 == 0)
    def _():
        keys[:, 128:] = bias_ref[...]
        query[:, 128:] = jnp.where(
            lax.broadcasted_iota(jnp.int32, (piece, 128), 1) == 0, 1.0, 0.0
        ).astype(BF)
        v_even[64:, :] = jnp.ones((16, length), BF)
        v_odd[64:, :] = jnp.ones((16, length), BF)

    keys[:, :128] = k_ref[...]

    def half(head, made, made_max, used, used_max, values, at, out_ref):
        query[:, :128] = jnp.where((lane // 64) == head, q_ref[...], jnp.zeros((), BF))
        top = used_max[0:1, :]
        scores = mm(keys[...], query[...], 1, 1)
        weight = jnp.exp(used[...] - top).astype(BF)
        made[...] = scores
        made_max[...] = jnp.broadcast_to(jnp.max(scores, axis=0, keepdims=True), made_max.shape)
        out_ref[0] = weight
        total = mm(values[...], weight, 1, 0)
        inverse = 1.0 / total[64:65]
        place = pl.ds(pl.multiple_of((at // 6) * piece, piece), piece)
        which = 2 * (at % 6) + 1 - head
        exact = total[:64] * inverse
        o_ref[which, :, place] = exact.astype(BF)
        exact_ref[which, :, place] = exact
        inv_ref[which, :, place] = jnp.broadcast_to(inverse, (8, piece))

    half(0, s_even, m_even, s_odd, m_odd, v_odd, before, odd_ref)
    turned = v_ref[...].T
    v_even[:64, :] = turned[:64]
    v_odd[:64, :] = turned[64:]
    half(1, s_odd, m_odd, s_even, m_even, v_even, now, even_ref)


def attend(q, kv, bias):
    rows, width = q.shape
    length = 2 * rows // 3
    piece = rows // 3
    steps = 18

    def now(t):
        t = jnp.minimum(t, steps - 1)
        return t // 6, t % 6

    def before(t):
        return jnp.maximum(t - 1, 0)

    whole = pl.BlockSpec(memory_space=pltpu.VMEM)
    return pl.pallas_call(
        partial(attend_kernel, steps),
        grid=(steps + 1,),
        in_specs=[
            pl.BlockSpec((piece, 128), now),
            pl.BlockSpec((length, 128), lambda t: (now(t)[0] // 2, now(t)[1])),
            pl.BlockSpec((length, 128), lambda t: (now(t)[0] // 2, 6 + now(t)[1])),
            pl.BlockSpec((length, 128), lambda t: (now(t)[0] // 2, 0)),
        ],
        out_specs=[
            whole,
            whole,
            whole,
            pl.BlockSpec((1, length, piece), lambda t: (jnp.minimum(t, steps - 1), 0, 0)),
            pl.BlockSpec((1, length, piece), lambda t: (before(t), 0, 0)),
        ],
        out_shape=[
            jax.ShapeDtypeStruct((H, DH, rows), BF),
            jax.ShapeDtypeStruct((H, DH, rows), F32),
            jax.ShapeDtypeStruct((H, 8, rows), F32),
            jax.ShapeDtypeStruct((steps, length, piece), BF),
            jax.ShapeDtypeStruct((steps, length, piece), BF),
        ],
        scratch_shapes=[
            pltpu.VMEM((length, 256), BF),
            pltpu.VMEM((piece, 256), BF),
            pltpu.VMEM((80, length), BF),
            pltpu.VMEM((80, length), BF),
            pltpu.VMEM((length, piece), F32),
            pltpu.VMEM((length, piece), F32),
            pltpu.VMEM((8, piece), F32),
            pltpu.VMEM((8, piece), F32),
        ],
        compiler_params=pltpu.CompilerParams(vmem_limit_bytes=VMEM_LIMIT),
        cost_estimate=pl.CostEstimate(flops=20 * 10**9, bytes_accessed=60 * 10**6, transcendentals=19 * 10**6),
    )(q, kv, kv, bias)


class Shares:
    stages = 6

    def __init__(self, source, acc, inbox, final, send, receive):
        self.source, self.acc, self.inbox, self.final = source, acc, inbox, final
        self.send, self.receive = send, receive
        me, far = lax.axis_index("batch"), lax.axis_index("seq")
        self.core, self.y, self.z0, self.z1 = [(me >> bit) & 1 for bit in range(4)]
        self.me, self.far = me, far
        self.half = acc.shape[-1]

    def partner(self, stage):
        if stage == 4:
            return (self.me, 1 - self.far)
        return (self.me ^ (1, 2, 4, 8, 0, 1)[stage], self.far)

    def ends(self, stage):
        acc = self.acc
        if stage == 0:
            away = pl.multiple_of((1 - self.core) * self.half, 128)
            return self.source.at[:, :, pl.ds(away, self.half)], self.inbox[0]
        if stage == 1:
            return acc.at[:, :, 1 - self.y], self.inbox[1]
        if stage == 2:
            return acc.at[:, 1 - self.z0, self.y], self.inbox[2]
        if stage == 3:
            return acc.at[1 - self.z1, self.z0, self.y], self.inbox[3]
        if stage == 4:
            return acc.at[self.z1, self.z0, self.y], self.inbox[4]
        return self.final.at[self.core], self.final.at[self.core]

    def copy(self, stage):
        here, there = self.ends(stage)
        return pltpu.make_async_remote_copy(
            src_ref=here,
            dst_ref=there,
            send_sem=self.send.at[stage],
            recv_sem=self.receive.at[stage],
            device_id=self.partner(stage),
            device_id_type=pl.DeviceIdType.MESH,
        )

    def load(self):
        mine = pl.multiple_of(self.core * self.half, 128)
        return pltpu.make_async_copy(
            self.source.at[:, :, pl.ds(mine, self.half)], self.inbox[5], self.send.at[6]
        )

    def begin(self):
        self.copy(0).start()
        self.load().start()

    def add(self, stage):
        acc = self.acc

        def total(one, other):
            return (one.astype(F32) + other.astype(F32)).astype(BF)

        if stage == 0:
            for k in range(8):
                acc[k // 4, k // 2 % 2, k % 2] = total(self.inbox[5][k], self.inbox[0][k])
        elif stage == 1:
            for k in range(4):
                acc[k // 2, k % 2, self.y] = total(acc[k // 2, k % 2, self.y], self.inbox[1][k // 2, k % 2])
        elif stage == 2:
            for k in range(2):
                acc[k, self.z0, self.y] = total(acc[k, self.z0, self.y], self.inbox[2][k])
        elif stage == 3:
            acc[self.z1, self.z0, self.y] = total(acc[self.z1, self.z0, self.y], self.inbox[3][...])
        else:
            self.final[self.core] = total(acc[self.z1, self.z0, self.y], self.inbox[4][...])

    def go_on(self, stage):
        if stage == 0:
            self.load().wait()
        self.copy(stage).wait()
        if stage < 5:
            self.add(stage)
            self.copy(stage + 1).start()


def share_scratch(rows, columns):
    half = columns // 2
    shapes = [(2, 2, 2, rows, half), (8, rows, half), (2, 2, rows, half), (2, rows, half)]
    shapes += [(rows, half), (rows, half), (8, rows, half), (2, rows, half)]
    return [pltpu.VMEM(shape, BF) for shape in shapes] + [
        pltpu.SemaphoreType.DMA((7,)),
        pltpu.SemaphoreType.DMA((6,)),
    ]


def pieces_of(partials):
    most = max(array.shape[0] for array in partials)
    return [
        (array, index)
        for index in range(most)
        for array in range(len(partials))
        if index < partials[array].shape[0]
    ]


def greet():
    me, far = lax.axis_index("batch"), lax.axis_index("seq")
    barrier = pltpu.get_barrier_semaphore()
    for other in ((me ^ 1, far), (me ^ 2, far), (me ^ 4, far), (me ^ 8, far), (me, 1 - far)):
        pl.semaphore_signal(barrier, inc=1, device_id=other, device_id_type=pl.DeviceIdType.MESH)
    pl.semaphore_wait(barrier, 5)


def timetable(pieces, first, every, lags):
    table = {}
    for i in range(pieces):
        step = first + every * i
        for stage in range(6):
            step += lags[stage]
            table.setdefault(int(step), []).append((i, stage))
    return table


def attend_back_kernel(
    pieces, q_ref, k_ref, v_ref, do_ref, o_ref, inv_ref, even_ref, odd_ref, *rest
):
    count = len(pieces)
    arrays = 1 + max(array for array, _ in pieces)
    sources, rest = rest[:arrays], rest[arrays:]
    (dq_ref, dk_ref, dv_ref), rest = rest[:3], rest[3:]
    finals, rest = rest[:count], rest[count:]
    (values, gradient, dk_sum, dv_sum), rest = rest[:4], rest[4:]
    shares = []
    for i in range(count):
        acc, a, b, c, d, e, own, final, send, receive = rest[10 * i : 10 * i + 10]
        array, index = pieces[i]
        shares.append(Shares(sources[array].at[index], acc, (a, b, c, d, e, own), final, send, receive))
    pair, part = pl.program_id(0), pl.program_id(1)
    step = 3 * pair + part
    table = timetable(count, 1, 3.4, (0, 3.5, 2, 2, 1, 1))

    @pl.when(step == 0)
    def _():
        greet()
        for share in shares:
            share.begin()

    for when in sorted(table):
        if when < 18:

            @pl.when(step == when)
            def _(when=when):
                for i, stage in table[when]:
                    shares[i].go_on(stage)

    piece, length = q_ref.shape[0], k_ref.shape[0]
    lane = lax.broadcasted_iota(jnp.int32, (1, 128), 1)
    zero = jnp.zeros((), BF)

    @pl.when((pair == 0) & (part == 0))
    def _():
        values[:, 128:] = jnp.where(
            lax.broadcasted_iota(jnp.int32, (length, 128), 1) < 3, 1.0, 0.0
        ).astype(BF)
        gradient[...] = jnp.zeros_like(gradient)

    values[:, :128] = v_ref[...]
    inverse = jnp.concatenate(
        [jnp.broadcast_to(inv_ref[head, 0:1, :], (DH, piece)) for head in range(2)], axis=0
    )
    scaled = do_ref[...].astype(F32) * inverse
    scaled = scaled.astype(BF)
    product = scaled.astype(F32) * o_ref[...]
    for head in range(2):
        mine = slice(DH * head, DH * head + DH)
        place = slice(piece * head, piece * head + piece)
        delta = -jnp.sum(product[mine], axis=0, keepdims=True)
        high = delta.astype(BF).astype(F32)
        rest = delta - high
        middle = rest.astype(BF).astype(F32)
        gradient[mine, place] = scaled[mine]
        gradient[128:136, place] = jnp.concatenate(
            [high, middle, rest - middle, jnp.zeros((5, piece), F32)], axis=0
        ).astype(BF)
    dp = mm(values[...], gradient[...], 1, 0)
    turned_keys = k_ref[...].T
    natural = scaled.T
    weights = [even_ref[0], odd_ref[0]]
    ds = [
        (weights[head].astype(F32) * dp[:, piece * head : piece * head + piece]).astype(BF)
        for head in range(2)
    ]

    def apart(array):
        return jnp.concatenate(
            [jnp.where(lane < 64, array, zero), jnp.where(lane < 64, zero, array)], axis=0
        )

    dv = mm(jnp.concatenate(weights, axis=1), apart(natural), 1, 0)
    dk = mm(jnp.concatenate(ds, axis=1), apart(q_ref[...]), 1, 0)
    for head in range(2):
        mine = slice(DH * head, DH * head + DH)
        dq_ref[mine, :] = (mm(turned_keys[mine], ds[head], 1, 0) * 0.125).astype(BF)

    @pl.when(part % 2 == 0)
    def _():
        dk_sum[...] = dk
        dv_sum[...] = dv

    @pl.when(part == 1)
    def _():
        dk_sum[...] += dk
        dv_sum[...] += dv

    dk_ref[...] = dk_sum[...].astype(BF)
    dv_ref[...] = dv_sum[...].astype(BF)

    @pl.when(step == 17)
    def _():
        for when in sorted(table):
            if when >= 18:
                for i, stage in table[when]:
                    shares[i].go_on(stage)
        for i in range(count):
            finals[i][...] = shares[i].final[...]


def attend_back(q, kv, do, o, inv, even, odd, partials):
    rows, width = q.shape
    length = 2 * rows // 3
    piece = rows // 3
    weight_spec = pl.BlockSpec((1, length, piece), lambda p, j: (j * 6 + p, 0, 0))
    pieces = pieces_of(partials)
    scratch, sizes = [], [partials[array].shape[2:] for array, _ in pieces]
    for size in sizes:
        scratch += share_scratch(*size)
    return pl.pallas_call(
        partial(attend_back_kernel, pieces),
        grid=(6, 3),
        in_specs=[
            pl.BlockSpec((piece, 128), lambda p, j: (j, p)),
            pl.BlockSpec((length, 128), lambda p, j: (j // 2, p)),
            pl.BlockSpec((length, 128), lambda p, j: (j // 2, 6 + p)),
            pl.BlockSpec((128, piece), lambda p, j: (p, j)),
            pl.BlockSpec((128, piece), lambda p, j: (p, j)),
            pl.BlockSpec((2, 8, piece), lambda p, j: (p, 0, j)),
            weight_spec,
            weight_spec,
        ]
        + [pl.BlockSpec(memory_space=pl.ANY)] * len(partials),
        out_specs=[
            pl.BlockSpec((128, piece), lambda p, j: (p, j)),
            pl.BlockSpec((length, 128), lambda p, j: (j // 2, p)),
            pl.BlockSpec((length, 128), lambda p, j: (j // 2, p)),
        ]
        + [pl.BlockSpec(memory_space=pltpu.VMEM)] * len(pieces),
        out_shape=[
            jax.ShapeDtypeStruct((width, rows), BF),
            jax.ShapeDtypeStruct((2 * length, width), BF),
            jax.ShapeDtypeStruct((2 * length, width), BF),
        ]
        + [jax.ShapeDtypeStruct((2, a, b // 2), BF) for a, b in sizes],
        scratch_shapes=[
            pltpu.VMEM((length, 256), BF),
            pltpu.VMEM((256, 2 * piece), BF),
            pltpu.VMEM((length, 128), F32),
            pltpu.VMEM((length, 128), F32),
        ]
        + scratch,
        compiler_params=pltpu.CompilerParams(
            vmem_limit_bytes=VMEM_LIMIT, collective_id=1, has_side_effects=True
        ),
        cost_estimate=pl.CostEstimate(flops=30 * 10**9, bytes_accessed=60 * 10**6, transcendentals=0),
    )(q, kv, kv, do, o, inv, even, odd, *partials)


def gelu_and_slope(g):
    square = g * g
    half_plus = 0.5 * jnp.tanh(g * (GELU_A + GELU_A * GELU_B * square)) + 0.5
    act = g * half_plus
    slope = half_plus + act * (2.0 - 2.0 * half_plus) * (GELU_A + 3.0 * GELU_A * GELU_B * square)
    return act, slope


def feedforward_kernel(
    x_ref, o_ref, dm_in_ref, live_ref, temb_ref, gain_ref, wo_ref, *rest
):
    wu_refs, wd_refs, rest = rest[:4], rest[4:8], rest[8:]
    out_ref, dh1_ref, do_ref, dwu_ref, dwd_ref, dwo_ref, dgain_ref, h1, n2, dm, h2, dn2 = rest
    chunk, chunks = 2 * pl.program_id(0) + pl.program_id(1), 6
    wu = jnp.concatenate([ref[...] for ref in wu_refs], axis=1)
    wd = jnp.concatenate([ref[...] for ref in wd_refs], axis=0)
    rows = x_ref.shape[0]
    block = rows // 2
    third = rows // 3
    blocks = [slice(block * i, block * i + block) for i in range(2)]
    thirds = [slice(third * i, third * i + third) for i in range(3)]

    @pl.when(chunk == 0)
    def _():
        for i, part in enumerate(thirds):
            h0 = x_ref[part, :].astype(F32) + temb_ref[i // 2 : i // 2 + 1, :]
            h = h0 + mm(o_ref[:, part], wo_ref[...], 0, 0)
            h1[part, :] = h
            centered = h - jnp.mean(h, axis=1, keepdims=True)
            variance = jnp.mean(centered * centered, axis=1, keepdims=True)
            n2[part, :] = (centered * lax.rsqrt(variance + 1e-5) * gain_ref[...]).astype(BF)
            dm[part, :] = dm_in_ref[part, :]
            h2[part, :] = h
            dn2[part, :] = jnp.zeros_like(h)

    def first(part):
        return mm(n2[part, :], wu, 1, 0), mm(dm[part, :], wd, 1, 1)

    def second(pair):
        act, slope = gelu_and_slope(pair[0])
        return act.astype(BF), (pair[1] * slope).astype(BF)

    def third_step(part, pair):
        h2[part, :] += mm(pair[0], wd, 1, 0)
        dn2[part, :] += mm(pair[1], wu, 1, 1)

    a = first(blocks[0])
    b = first(blocks[1])
    a = second(a)
    b = second(b)
    third_step(blocks[0], a)
    third_step(blocks[1], b)
    act = jnp.concatenate([a[0], b[0]], axis=0)
    dg = jnp.concatenate([a[1], b[1]], axis=0)
    dwd_ref[...] = mm(dm[...], act, 0, 0).astype(BF).reshape(dwd_ref.shape)
    dwu_ref[...] = mm(dg, n2[...], 0, 0).astype(BF).reshape(dwu_ref.shape)

    @pl.when(chunk == chunks - 1)
    def _():
        dgain = jnp.zeros_like(dgain_ref)
        for part in thirds:
            h = h1[part, :]
            live = live_ref[part, 0:1].astype(F32)
            out_ref[part, :] = (live * h2[part, :]).astype(BF)
            centered = h - jnp.mean(h, axis=1, keepdims=True)
            variance = jnp.mean(centered * centered, axis=1, keepdims=True)
            r2 = lax.rsqrt(variance + 1e-5)
            x2 = centered * r2
            dn = dn2[part, :]
            dgain += jnp.sum(dn * x2, axis=0, keepdims=True)
            e = dn * gain_ref[...]
            dh1 = dm_in_ref[part, :].astype(F32) + r2 * (
                e
                - jnp.mean(e, axis=1, keepdims=True)
                - x2 * jnp.mean(e * x2, axis=1, keepdims=True)
            )
            dh1_ref[part, :] = dh1
            da = dh1.astype(BF)
            dm[part, :] = da
            do_ref[:, part] = mm(wo_ref[...], da, 1, 1).astype(BF)
        dgain_ref[...] = dgain
        dwo_ref[...] = mm(dm[...], o_ref[...], 0, 1).astype(BF)


def feedforward(x, o, dm, live, temb, gain, wo, wu, wd):
    rows, width = x.shape
    hidden = wu.shape[1]
    whole = pl.BlockSpec(memory_space=pltpu.VMEM)
    up_specs = [
        pl.BlockSpec((width, 128), lambda c, h, i=i: (0, 3 * (4 * h + i) + c)) for i in range(4)
    ]
    down_specs = [
        pl.BlockSpec((128, width), lambda c, h, i=i: (3 * (4 * h + i) + c, 0)) for i in range(4)
    ]
    return pl.pallas_call(
        feedforward_kernel,
        grid=(3, 2),
        in_specs=[whole] * 7 + up_specs + down_specs,
        out_specs=[
            whole,
            whole,
            whole,
            pl.BlockSpec((1, 4, 128, width), lambda c, h: (c, h, 0, 0)),
            pl.BlockSpec((1, 8, width // 8, 512), lambda c, h: (c, 0, 0, h)),
            whole,
            whole,
        ],
        out_shape=[
            jax.ShapeDtypeStruct((rows, width), BF),
            jax.ShapeDtypeStruct((rows, width), F32),
            jax.ShapeDtypeStruct((width, rows), BF),
            jax.ShapeDtypeStruct((3, 8, 128, width), BF),
            jax.ShapeDtypeStruct((3, 8, width // 8, 1024), BF),
            jax.ShapeDtypeStruct((width, width), BF),
            jax.ShapeDtypeStruct((1, width), F32),
        ],
        scratch_shapes=[
            pltpu.VMEM((rows, width), F32),
            pltpu.VMEM((rows, width), BF),
            pltpu.VMEM((rows, width), BF),
            pltpu.VMEM((rows, width), F32),
            pltpu.VMEM((rows, width), F32),
        ],
        compiler_params=pltpu.CompilerParams(vmem_limit_bytes=VMEM_LIMIT),
        cost_estimate=pl.CostEstimate(flops=48 * 10**9, bytes_accessed=50 * 10**6, transcendentals=5 * 10**6),
    )(x, o, dm, live, temb, gain, wo, *[wu] * 4, *[wd] * 4)


def halving_sum(array):
    count = lax.axis_size("batch")
    me = lax.axis_index("batch")
    bits = count.bit_length() - 1
    parts = array.reshape((2,) * bits + array.shape[1:])
    order = [0] + list(range(1, bits))
    left = list(range(bits - 1, -1, -1))
    for bit in order:
        axis = left.index(bit)
        left.remove(bit)
        mine = (me >> bit) & 1
        keep = lax.dynamic_index_in_dim(parts, mine, axis, keepdims=False)
        send = lax.dynamic_index_in_dim(parts, 1 - mine, axis, keepdims=False)
        got = lax.ppermute(send, "batch", [(i, i ^ (1 << bit)) for i in range(count)])
        parts = (keep.astype(F32) + got.astype(F32)).astype(BF)
    got = lax.ppermute(parts, "seq", [(0, 1), (1, 0)])
    return parts.astype(F32) + got.astype(F32)


def pair_plan(
    inputs,
    timesteps,
    counts,
    slot_token_mask,
    time_first_weight,
    time_second_weight,
    attention_norm_gain,
    query_key_value_weight,
    attention_output_weight,
    feedforward_norm_gain,
    up_projection_weight,
    down_projection_weight,
    cotangent,
):
    slots, half, width = inputs.shape
    batches = lax.axis_size("batch")
    me = lax.axis_index("seq")
    swap = [(0, 1), (1, 0)]

    def at(array, index):
        return lax.dynamic_index_in_dim(array, index, 0, keepdims=False)

    def across(array):
        return lax.ppermute(array, "seq", swap)

    x_far = across(at(inputs, 1 - me))
    x_far_two = across(inputs[2])
    live_here = (
        (jnp.arange(slots)[:, None] < counts[0]) & (slot_token_mask == 1)
    ).astype(BF)
    live_far = across(live_here)
    dm_here = cotangent * live_here[:, :, None]
    dm_far = across(at(dm_here, 1 - me))

    x = jnp.concatenate([at(inputs, me), x_far, inputs[2], x_far_two], axis=0)
    live = jnp.concatenate([at(live_here, me), at(live_far, me), live_here[2], live_far[2]], axis=0)
    dm = jnp.concatenate([at(dm_here, me), dm_far, dm_here[2]], axis=0)
    bias = jnp.where(
        (jnp.arange(128) == 0)[None, :] & (live == 0)[:, None], MASKED, 0.0
    ).astype(BF)
    live_wide = jnp.broadcast_to(live[: 3 * half, None], (3 * half, 128))

    time_embedding = sinusoid(timesteps)
    first_low = time_first_weight.astype(F32)
    second_low = time_second_weight.astype(F32)
    time_vec = time_mlp(time_embedding, first_low, second_low)
    temb = jnp.stack([at(time_vec, me), time_vec[2]])

    h0 = (x.astype(F32).reshape(2, 2 * half, width) + temb[:, None, :]).reshape(4 * half, width)
    centered = h0 - jnp.mean(h0, axis=-1, keepdims=True)
    r1 = lax.rsqrt(jnp.mean(centered * centered, axis=-1, keepdims=True) + 1e-05)
    x1 = centered * r1
    n1 = (x1 * attention_norm_gain).astype(BF)
    q = (
        jnp.dot(n1[: 3 * half], query_key_value_weight[:, :width], preferred_element_type=F32)
        * 0.125
    ).astype(BF)
    kv = jnp.dot(n1, query_key_value_weight[:, width:], preferred_element_type=F32).astype(BF)

    o, exact, inv, even, odd = attend(q, kv, bias)
    o = o.reshape(width, 3 * half)
    out, dh1, do, dwu, dwd, dwo, dgain2 = feedforward(
        x[: 3 * half],
        o,
        dm,
        live_wide,
        temb,
        feedforward_norm_gain[None, :],
        attention_output_weight,
        up_projection_weight,
        down_projection_weight,
    )
    out_far = across(out[half : 2 * half])
    output = jnp.where(
        me == 0,
        jnp.stack([out[:half], out_far, out[2 * half :]]),
        jnp.stack([out_far, out[:half], out[2 * half :]]),
    )
    partials = [dwu, dwd, dwo.reshape(1, 8, width // 8, width)]
    dq, dk, dv, *sums = attend_back(
        q, kv, do, exact.reshape(width, 3 * half), inv, even, odd, partials
    )
    mine = lax.axis_index("batch")

    places = pieces_of(partials)

    def rows_of(array, index):
        part = sums[places.index((array, index))]
        return jnp.concatenate([part[0], part[1]], axis=1)

    def own_half(array):
        size = array.shape[0] // 2
        return lax.dynamic_slice_in_dim(array, (mine & 1) * size, size, 0).astype(F32)

    up_sum = own_half(jnp.concatenate([rows_of(0, i) for i in range(3)], axis=0))
    down_sum = jnp.stack([own_half(rows_of(1, i)) for i in range(3)], axis=1)
    down_sum = down_sum.reshape(-1, 3, 8, 128).transpose(0, 2, 1, 3).reshape(width // batches, -1)
    out_sum = own_half(rows_of(2, 0))

    dwq = mm(dq, n1[: 3 * half], 1, 0).astype(BF)
    dwk = mm(dk, n1, 0, 0).astype(BF)
    dwv = mm(dv, n1, 0, 0).astype(BF)
    dn1_kv = back_product(jnp.concatenate([dk, dv], axis=1), query_key_value_weight[:, width:])
    dn1_far = across(dn1_kv[3 * half :].astype(BF))
    dn1 = dn1_kv[: 3 * half] + mm(dq, query_key_value_weight[:, :width], 0, 1)
    dn1 = jnp.concatenate([dn1[: 2 * half], dn1[2 * half :] + dn1_far.astype(F32)], axis=0)
    x1, r1 = x1[: 3 * half], r1[: 3 * half]
    dgain1 = jnp.sum(dn1 * x1, axis=0)
    e = dn1 * attention_norm_gain
    dh0 = dh1 + r1 * (
        e - jnp.mean(e, axis=-1, keepdims=True) - x1 * jnp.mean(e * x1, axis=-1, keepdims=True)
    )
    dh0_far = across(dh0[half : 2 * half].astype(BF)).astype(F32)
    grad_inputs = jnp.where(
        me == 0,
        jnp.stack([dh0[:half], dh0_far, dh0[2 * half :]]),
        jnp.stack([dh0_far, dh0[:half], dh0[2 * half :]]),
    )

    dtemb_one = jnp.sum(dh0[: 2 * half], axis=0)
    dtemb_two = jnp.sum(dh0[2 * half :], axis=0)
    is_first = (me == 0).astype(F32)
    small = jnp.stack(
        [is_first * dtemb_one, (1.0 - is_first) * dtemb_one, dtemb_two, dgain1, dgain2[0]]
        + [jnp.zeros_like(dgain1)] * 3
    )
    small = lax.all_gather(lax.all_gather(small, "seq"), "batch")
    small = jnp.sum(small, axis=1)
    steps_all = lax.all_gather(timesteps, "batch", tiled=True)
    dtemb = small[:, :3].reshape(batches * 3, width)
    emb_all = sinusoid(steps_all)
    u_all, silu_back = jax.vjp(
        lambda a: jax.nn.silu(a), jnp.dot(emb_all, first_low, precision=TOP_PRECISION)
    )
    columns = width // batches
    inner_columns = first_low.shape[1] // batches

    def cut(array, size):
        return lax.dynamic_slice_in_dim(array, mine * size, size, array.ndim - 1)

    grad_outer = lax.dot_general(
        u_all, cut(dtemb, columns), (((0,), (0,)), ((), ())), precision=TOP_PRECISION
    )
    dsilu = lax.dot_general(
        dtemb, second_low, (((1,), (1,)), ((), ())), precision=TOP_PRECISION
    )
    grad_inner = lax.dot_general(
        emb_all,
        cut(silu_back(dsilu)[0], inner_columns),
        (((0,), (0,)), ((), ())),
        precision=TOP_PRECISION,
    )
    gains = jnp.sum(small[:, 3:5], axis=0)
    qk_sum = halving_sum(jnp.concatenate([dwq, dwk], axis=0).reshape(batches, -1, width))
    v_sum = halving_sum(dwv.reshape(batches, -1, width))
    return (
        output,
        grad_inputs,
        grad_inner,
        grad_outer,
        cut(gains[0], columns),
        qk_sum.T,
        v_sum.T,
        out_sum.T,
        cut(gains[1], columns),
        up_sum.T,
        down_sum.T,
    )


def solution(mesh):
    on_device = pair_plan if mesh.shape["seq"] == 2 else ring_plan
    return jax.shard_map(
        on_device,
        mesh=mesh,
        in_specs=(
            P("batch", "seq", None),
            P("batch"),
            P("batch"),
            P("batch", "seq"),
            P(),
            P(),
            P(),
            P(),
            P(),
            P(),
            P(),
            P(),
            P("batch", "seq", None),
        ),
        out_specs=(
            P("batch", "seq", None),
            P("batch", "seq", None),
            P(None, "batch"),
            P(None, "batch"),
            P("batch"),
            P(None, "batch"),
            P(None, "batch"),
            P(None, "batch"),
            P("batch"),
            P(None, "batch"),
            P(None, "batch"),
        ),
        check_vma=False,
    )
```

```python
from functools import partial
import math

import jax
import jax.numpy as jnp
from jax import lax
from jax.experimental import pallas as pl
from jax.experimental.pallas import tpu as pltpu
from jax.sharding import PartitionSpec as P

H = 12
DH = 64
TCH = 128


TOP_PRECISION = lax.Precision.HIGHEST


def from_behind(array, axis, by):
    count = lax.axis_size(axis)
    return lax.ppermute(array, axis, [(i, (i + by) % count) for i in range(count)])


def shortened(array):

    def short(part):
        return part.astype(jnp.bfloat16) if part.dtype == jnp.float32 else part

    return jax.tree.map(short, array)


def sinusoid(steps):
    half_width = TCH // 2
    frequency = jnp.exp(
        -math.log(10000.0) * jnp.arange(half_width).astype(jnp.float32) / half_width
    )
    angles = steps.astype(jnp.float32)[:, None] * frequency[None, :]
    return jnp.concatenate([jnp.cos(angles), jnp.sin(angles)], axis=-1)


def layer_norm(hidden, gain):
    centered = hidden - jnp.mean(hidden, axis=-1, keepdims=True)
    variance = jnp.mean(centered * centered, axis=-1, keepdims=True)
    return centered * lax.rsqrt(variance + 1e-05) * gain


def time_mlp(time_embedding, time_first_weight, time_second_weight):
    pre_act = jnp.dot(time_embedding, time_first_weight, precision=TOP_PRECISION)
    return jnp.dot(jax.nn.silu(pre_act), time_second_weight, precision=TOP_PRECISION)


def row_product(left, right):
    return lax.dot_general(
        left, right, (((0,), (0,)), ((), ())), preferred_element_type=jnp.float32
    )


def back_product(left, right):
    return lax.dot_general(
        left, right, (((1,), (1,)), ((), ())), preferred_element_type=jnp.float32
    )


def masked_scores(queries, key_block, mask_block, scale_factor):
    attention_scores = (
        jnp.einsum("sqhd,skhd->shqk", queries, key_block, preferred_element_type=jnp.float32)
        * scale_factor
    )
    return jnp.where(mask_block[:, None, None, :] > 0.5, attention_scores, -1000000000.0)


def ring_plan(
    inputs,
    timesteps,
    counts,
    slot_token_mask,
    time_first_weight,
    time_second_weight,
    attention_norm_gain,
    query_key_value_weight,
    attention_output_weight,
    feedforward_norm_gain,
    up_projection_weight,
    down_projection_weight,
    cotangent,
):
    present_slots, local_len, width = inputs.shape
    total_rows = present_slots * local_len
    scale_factor = 1.0 / math.sqrt(DH)
    slot_alive_flags = (
        (jnp.arange(present_slots)[:, None] < counts[0]) & (slot_token_mask == 1)
    ).astype(jnp.float32)
    time_embedding = sinusoid(timesteps)
    time_vec, time_back = jax.vjp(
        partial(time_mlp, time_embedding),
        time_first_weight.astype(jnp.float32),
        time_second_weight.astype(jnp.float32),
    )
    residual = inputs.astype(jnp.float32) + time_vec[:, None, :]
    normed, norm_back = jax.vjp(layer_norm, residual, attention_norm_gain)
    normed_low = normed.astype(jnp.bfloat16).reshape(total_rows, width)
    packed = (
        jnp.dot(normed_low, query_key_value_weight, preferred_element_type=jnp.float32)
        .astype(jnp.bfloat16)
        .reshape(present_slots, local_len, 3 * width)
    )
    queries = packed[:, :, :width].reshape(present_slots, local_len, H, DH)
    key_rows = packed[:, :, width : 2 * width]
    value_rows = packed[:, :, 2 * width :]
    key_valid_mask = slot_alive_flags.astype(jnp.bfloat16)
    initial_state = (
        jnp.full((present_slots, H, local_len), -1e30, jnp.float32),
        jnp.zeros((present_slots, H, local_len), jnp.float32),
        jnp.zeros((present_slots, local_len, H, DH), jnp.float32),
    )
    key_piece = lax.all_gather(key_rows, "seq", axis=1, tiled=True)
    value_piece = lax.all_gather(value_rows, "seq", axis=1, tiled=True)
    mask_piece = lax.all_gather(key_valid_mask, "seq", axis=1, tiled=True)
    piece_len = key_piece.shape[1]
    block_len = min(piece_len, local_len)

    def one_block(position, inner_state):
        run_max, run_sum, running_totals = inner_state
        offset = position * block_len
        key_block = lax.dynamic_slice_in_dim(key_piece, offset, block_len, 1).reshape(
            present_slots, block_len, H, DH
        )
        value_block = lax.dynamic_slice_in_dim(value_piece, offset, block_len, 1).reshape(
            present_slots, block_len, H, DH
        )
        mask_block = lax.dynamic_slice_in_dim(mask_piece, offset, block_len, 1)
        attention_scores = masked_scores(queries, key_block, mask_block, scale_factor)
        new_max = jnp.maximum(run_max, jnp.max(attention_scores, axis=-1))
        exponent = jnp.exp(attention_scores - new_max[..., None])
        fading = jnp.exp(run_max - new_max)
        run_sum = run_sum * fading + jnp.sum(exponent, axis=-1)
        running_totals = running_totals * jnp.transpose(fading, (0, 2, 1))[..., None] + jnp.einsum(
            "shqk,skhd->sqhd",
            exponent.astype(jnp.bfloat16),
            value_block,
            preferred_element_type=jnp.float32,
        )
        return (new_max, run_sum, running_totals)

    run_max, run_sum, running_totals = lax.fori_loop(
        0, piece_len // block_len, one_block, initial_state
    )
    attended = running_totals / jnp.transpose(run_sum, (0, 2, 1))[..., None]
    log_total = run_max + jnp.log(run_sum)
    attended_low = attended.astype(jnp.bfloat16).reshape(total_rows, width)
    middle = residual + jnp.dot(
        attended_low, attention_output_weight, preferred_element_type=jnp.float32
    ).reshape(present_slots, local_len, width)
    normed_two, norm_two_back = jax.vjp(layer_norm, middle, feedforward_norm_gain)
    normed_two_low = normed_two.astype(jnp.bfloat16).reshape(total_rows, width)
    gate_pre = jnp.dot(normed_two_low, up_projection_weight, preferred_element_type=jnp.float32)
    activated, gelu_back = jax.vjp(partial(jax.nn.gelu, approximate=True), gate_pre)
    activated_low = activated.astype(jnp.bfloat16)
    completed_groups = middle + jnp.dot(
        activated_low, down_projection_weight, preferred_element_type=jnp.float32
    ).reshape(present_slots, local_len, width)
    output = (slot_alive_flags[..., None] * completed_groups).astype(jnp.bfloat16)
    final_gradient = slot_alive_flags[..., None] * cotangent.astype(jnp.float32)
    grad_down_low = final_gradient.reshape(total_rows, width).astype(jnp.bfloat16)
    down_grad = row_product(activated_low, grad_down_low)
    grad_gate = gelu_back(back_product(grad_down_low, down_projection_weight))[0].astype(
        jnp.bfloat16
    )
    up_grad = row_product(normed_two_low, grad_gate)
    grad_middle_norm, mlp_gain_grad = norm_two_back(
        back_product(grad_gate, up_projection_weight).reshape(present_slots, local_len, width)
    )
    grad_middle = final_gradient + grad_middle_norm
    grad_branch_low = grad_middle.reshape(total_rows, width).astype(jnp.bfloat16)
    out_grad = row_product(attended_low, grad_branch_low)
    grad_attended = (
        back_product(grad_branch_low, attention_output_weight)
        .astype(jnp.bfloat16)
        .reshape(present_slots, local_len, H, DH)
    )
    row_delta = jnp.transpose(
        jnp.sum(grad_attended.astype(jnp.float32) * attended, axis=-1), (0, 2, 1)
    )

    def key_terms(key_block, value_block, mask_block):
        attention_scores = masked_scores(queries, key_block, mask_block, scale_factor)
        probability = jnp.exp(attention_scores - log_total[..., None])
        grad_probs = jnp.einsum(
            "sqhd,skhd->shqk", grad_attended, value_block, preferred_element_type=jnp.float32
        )
        grad_scores = (probability * (grad_probs - row_delta[..., None])).astype(jnp.bfloat16)
        query_add = (
            jnp.einsum(
                "shqk,skhd->sqhd", grad_scores, key_block, preferred_element_type=jnp.float32
            )
            * scale_factor
        )
        key_add = (
            jnp.einsum("shqk,sqhd->skhd", grad_scores, queries, preferred_element_type=jnp.float32)
            * scale_factor
        )
        value_add = jnp.einsum(
            "shqk,sqhd->skhd",
            probability.astype(jnp.bfloat16),
            grad_attended,
            preferred_element_type=jnp.float32,
        )
        block_len = key_block.shape[1]
        return (
            query_add,
            key_add.reshape(present_slots, block_len, width),
            value_add.reshape(present_slots, block_len, width),
        )

    cycle_len = lax.axis_size("seq")
    query_zeros = jnp.zeros((present_slots, local_len, H, DH), jnp.float32)

    def visit(visit_index, loop_state):
        grad_queries, visiting, carried = loop_state
        query_add, key_add, value_add = key_terms(
            visiting[0].reshape(present_slots, local_len, H, DH),
            visiting[1].reshape(present_slots, local_len, H, DH),
            visiting[2],
        )
        carried = (carried[0] + key_add, carried[1] + value_add)
        visiting = from_behind((visiting[0], visiting[1], visiting[2]), "seq", 1)
        carried = (
            from_behind(carried[0].astype(jnp.bfloat16), "seq", 1).astype(jnp.float32),
            from_behind(carried[1].astype(jnp.bfloat16), "seq", 1).astype(jnp.float32),
        )
        return (grad_queries + query_add, tuple(visiting), tuple(carried))

    zeros_kv = jnp.zeros((present_slots, local_len, width), jnp.float32)
    grad_queries, visiting, carried = lax.fori_loop(
        0,
        cycle_len,
        visit,
        (query_zeros, (key_rows, value_rows, key_valid_mask), (zeros_kv, zeros_kv)),
    )
    grad_keys, grad_values = carried
    grad_packed = (
        jnp.concatenate(
            [grad_queries.reshape(present_slots, local_len, width), grad_keys, grad_values], axis=-1
        )
        .astype(jnp.bfloat16)
        .reshape(total_rows, 3 * width)
    )
    qkv_grad = row_product(normed_low, grad_packed)
    query_key_grad = qkv_grad[:, : 2 * width]
    value_grad = qkv_grad[:, 2 * width :]
    grad_start_norm, attn_gain_grad = norm_back(
        back_product(grad_packed, query_key_value_weight).reshape(present_slots, local_len, width)
    )
    grad_start = grad_middle + grad_start_norm
    inner_grad, outer_grad = time_back(jnp.sum(grad_start, axis=1))
    shares = (
        lax.psum_scatter(
            inner_grad.astype(jnp.bfloat16), "batch", scatter_dimension=1, tiled=True
        ).astype(jnp.float32),
        lax.psum_scatter(
            outer_grad.astype(jnp.bfloat16), "batch", scatter_dimension=1, tiled=True
        ).astype(jnp.float32),
        lax.psum_scatter(
            attn_gain_grad[None, :].astype(jnp.bfloat16), "batch", scatter_dimension=1, tiled=True
        ).astype(jnp.float32),
        lax.psum_scatter(
            query_key_grad.astype(jnp.bfloat16), "batch", scatter_dimension=1, tiled=True
        ).astype(jnp.float32),
        lax.psum_scatter(
            value_grad.astype(jnp.bfloat16), "batch", scatter_dimension=1, tiled=True
        ).astype(jnp.float32),
        lax.psum_scatter(
            out_grad.astype(jnp.bfloat16), "batch", scatter_dimension=1, tiled=True
        ).astype(jnp.float32),
        lax.psum_scatter(
            mlp_gain_grad[None, :].astype(jnp.bfloat16), "batch", scatter_dimension=1, tiled=True
        ).astype(jnp.float32),
        lax.psum_scatter(
            up_grad.astype(jnp.bfloat16), "batch", scatter_dimension=1, tiled=True
        ).astype(jnp.float32),
        lax.psum_scatter(
            down_grad.astype(jnp.bfloat16), "batch", scatter_dimension=1, tiled=True
        ).astype(jnp.float32),
    )
    summed = tuple(
        jax.tree.map(
            lambda part: part.astype(jnp.float32), lax.psum(shortened(tuple(shares)), "seq")
        )
    )
    return (
        output,
        grad_start,
        summed[0],
        summed[1],
        summed[2][0],
        summed[3],
        summed[4],
        summed[5],
        summed[6][0],
        summed[7],
        summed[8],
    )


BF = jnp.bfloat16
F32 = jnp.float32
MASKED = -1e9
GELU_A = 0.7978845608028654
GELU_B = 0.044715
VMEM_LIMIT = 62 * 2**20


def mm(left, right, left_dim, right_dim):
    return lax.dot_general(
        left, right, (((left_dim,), (right_dim,)), ((), ())), preferred_element_type=F32
    )


def attend_kernel(
    counts_ref, steps_ref, x_hbm, mask_hbm, cot_hbm, w1_ref, w2_ref, gain_ref, w_ref,
    o_ref, exact_ref, inv_ref, even_ref, odd_ref, live_ref, temb_ref, emb_ref, u_ref,
    q_hbm, kv_hbm, n1_hbm, xs_hbm, dm_hbm,
    xs, n1, q, kv, dm, mask, mask_far, bias, live, sems, send, receive,
    keys, query, v_even, v_odd, s_even, s_odd, m_even, m_odd,
):
    step = pl.program_id(0)
    last = pl.num_programs(0) - 1
    piece, width = xs.shape[0] // 4, xs.shape[1]
    length = 2 * piece
    lane = lax.broadcasted_iota(jnp.int32, (1, 128), 1)
    now = jnp.minimum(step, last - 1)
    before = jnp.maximum(step - 1, 0)
    me, seq = lax.axis_index("batch"), lax.axis_index("seq")
    blocks = [pl.ds(piece * i, piece) for i in range(4)]

    def to_partner(k, source, target):
        return pltpu.make_async_remote_copy(
            src_ref=source,
            dst_ref=target,
            send_sem=send.at[k],
            recv_sem=receive.at[k],
            device_id=(me, 1 - seq),
            device_id_type=pl.DeviceIdType.MESH,
        )

    x_one = to_partner(0, x_hbm.at[1 - seq], xs.at[blocks[1]])
    x_two = to_partner(1, x_hbm.at[2], xs.at[blocks[3]])
    cot_one = to_partner(2, cot_hbm.at[1 - seq], dm.at[blocks[1]])
    mask_there = to_partner(3, mask_hbm, mask_far)
    own = [
        pltpu.make_async_copy(x_hbm.at[seq], xs.at[blocks[0]], sems.at[0]),
        pltpu.make_async_copy(x_hbm.at[2], xs.at[blocks[2]], sems.at[1]),
        pltpu.make_async_copy(mask_hbm, mask, sems.at[2]),
        pltpu.make_async_copy(cot_hbm.at[seq], dm.at[blocks[0]], sems.at[3]),
        pltpu.make_async_copy(cot_hbm.at[2], dm.at[blocks[2]], sems.at[4]),
    ]
    keep_early = [
        pltpu.make_async_copy(q, q_hbm, sems.at[5]),
    ]
    keep_late = [
        pltpu.make_async_copy(kv, kv_hbm, sems.at[6]),
        pltpu.make_async_copy(n1, n1_hbm, sems.at[7]),
        pltpu.make_async_copy(xs, xs_hbm, sems.at[8]),
    ]
    keep_dm = pltpu.make_async_copy(dm, dm_hbm, sems.at[9])

    def project(i, with_queries):
        part = blocks[i]
        h = xs[part, :].astype(F32) + temb_ref[i // 2 : i // 2 + 1, :]
        centered = h - jnp.mean(h, axis=1, keepdims=True)
        variance = jnp.mean(centered * centered, axis=1, keepdims=True)
        normed = (centered * lax.rsqrt(variance + 1e-5) * gain_ref[...]).astype(BF)
        n1[part, :] = normed
        if with_queries:
            q[part, :] = (mm(normed, w_ref[:, :width], 1, 0) * 0.125).astype(BF)
        kv[part, :] = mm(normed, w_ref[:, width:], 1, 0).astype(BF)

    def lives(ref):
        rows = lax.broadcasted_iota(jnp.int32, (8, piece), 0)
        held = jnp.concatenate([ref[...], jnp.zeros((5, piece), jnp.int32)], axis=0)
        flags = jnp.where((held == 1) & (rows < counts_ref[0]), 1.0, 0.0)
        return flags.T

    def set_live(i, column):
        live[blocks[i], :] = jnp.broadcast_to(column, (piece, 128)).astype(BF)
        masked = jnp.where(lane == 0, MASKED, 0.0)
        bias[blocks[i], :] = jnp.where(column > 0.5, 0.0, masked).astype(BF)

    def mine(columns):
        return jnp.where(seq == 0, columns[:, 0:1], columns[:, 1:2])

    @pl.when(step == 0)
    def _():
        for copy in own:
            copy.start()
        greet_x()
        mask_there.start()
        x_one.start()
        row = lax.broadcasted_iota(jnp.int32, (8, 1), 0)
        times = jnp.where(
            row == 0, steps_ref[0], jnp.where(row == 1, steps_ref[1], steps_ref[2])
        ).astype(F32)
        half_width = TCH // 2
        column = lax.broadcasted_iota(jnp.int32, (1, TCH), 1)
        index = jnp.where(column < half_width, column, column - half_width).astype(F32)
        angles = times * jnp.exp(-math.log(10000.0) * index / half_width)
        emb = jnp.where(column < half_width, jnp.cos(angles), jnp.sin(angles))
        emb = jnp.where(row < 3, emb, 0.0)

        def exact_product(left, right):
            return lax.dot_general(
                left, right.astype(F32), (((1,), (0,)), ((), ())),
                precision=TOP_PRECISION, preferred_element_type=F32,
            )

        u = exact_product(emb, w1_ref[...])
        temb = exact_product(u / (1.0 + jnp.exp(-u)), w2_ref[...])
        emb_ref[...] = emb
        u_ref[...] = u
        temb_ref[0:1, :] = jnp.where(seq == 0, temb[0:1], temb[1:2])
        temb_ref[1:2, :] = temb[2:3]
        temb_ref[2:8, :] = jnp.zeros((6, width), F32)
        for copy in own[:3]:
            copy.wait()
        columns = lives(mask)
        set_live(0, mine(columns))
        set_live(2, columns[:, 2:3])
        project(0, True)
        project(2, True)
        for copy in own[3:]:
            copy.wait()
        dm[blocks[0], :] *= live[blocks[0], 0:1]
        dm[blocks[2], :] *= live[blocks[2], 0:1]
        mask_there.wait()
        columns = lives(mask_far)
        set_live(1, mine(columns))
        set_live(3, columns[:, 2:3])
        live_ref[...] = live[pl.ds(0, 3 * piece), :]
        x_one.wait()
        x_two.start()
        project(1, True)
        for copy in keep_early:
            copy.start()

    @pl.when(step == 8)
    def _():
        x_two.wait()
        cot_one.start()
        project(3, False)
        for copy in keep_late:
            copy.start()

    @pl.when(step == last)
    def _():
        cot_one.wait()
        dm[blocks[1], :] *= live[blocks[1], 0:1]
        keep_dm.start()

    query_rows = pl.ds(pl.multiple_of((now // 6) * piece, piece), piece)
    key_rows = pl.ds(pl.multiple_of((now // 12) * length, length), length)
    pair_lanes = pl.ds(pl.multiple_of((now % 6) * 128, 128), 128)
    value_lanes = pl.ds(pl.multiple_of(width + (now % 6) * 128, 128), 128)

    @pl.when(step % 6 == 0)
    def _():
        keys[:, 128:] = bias[key_rows, :]
        query[:, 128:] = jnp.where(
            lax.broadcasted_iota(jnp.int32, (piece, 128), 1) == 0, 1.0, 0.0
        ).astype(BF)
        v_even[64:, :] = jnp.ones((16, length), BF)
        v_odd[64:, :] = jnp.ones((16, length), BF)

    keys[:, :128] = kv[key_rows, pair_lanes]

    def half(head, made, made_max, used, used_max, values, at, out_ref):
        query[:, :128] = jnp.where((lane // 64) == head, q[query_rows, pair_lanes], jnp.zeros((), BF))
        top = used_max[0:1, :]
        scores = mm(keys[...], query[...], 1, 1)
        weight = jnp.exp(used[...] - top).astype(BF)
        made[...] = scores
        made_max[...] = jnp.broadcast_to(jnp.max(scores, axis=0, keepdims=True), made_max.shape)
        out_ref[0] = weight
        total = mm(values[...], weight, 1, 0)
        inverse = 1.0 / total[64:65]
        place = pl.ds(pl.multiple_of((at // 6) * piece, piece), piece)
        which = 2 * (at % 6) + 1 - head
        exact = total[:64] * inverse
        o_ref[which, :, place] = exact.astype(BF)
        exact_ref[which, :, place] = exact
        inv_ref[which, :, place] = jnp.broadcast_to(inverse, (8, piece))

    half(0, s_even, m_even, s_odd, m_odd, v_odd, before, odd_ref)
    turned = kv[key_rows, value_lanes].T
    v_even[:64, :] = turned[:64]
    v_odd[:64, :] = turned[64:]
    half(1, s_odd, m_odd, s_even, m_even, v_even, now, even_ref)

    @pl.when(step == last)
    def _():
        for copy in keep_early + keep_late + [keep_dm]:
            copy.wait()


def greet_x():
    partner = (lax.axis_index("batch"), 1 - lax.axis_index("seq"))
    barrier = pltpu.get_barrier_semaphore()
    pl.semaphore_signal(barrier, inc=1, device_id=partner, device_id_type=pl.DeviceIdType.MESH)
    pl.semaphore_wait(barrier, 1)


def attend(counts, timesteps, x, mask, cot, w1, w2, gain, w):
    _, piece, width = x.shape
    length = 2 * piece
    rows = 3 * piece
    steps = 18
    hidden = w1.shape[1]
    whole = pl.BlockSpec(memory_space=pltpu.VMEM)
    scalars = pl.BlockSpec(memory_space=pltpu.SMEM)
    anywhere = pl.BlockSpec(memory_space=pl.ANY)
    return pl.pallas_call(
        attend_kernel,
        grid=(steps + 1,),
        in_specs=[scalars] * 2 + [anywhere] * 3 + [whole] * 4,
        out_specs=[
            whole,
            whole,
            whole,
            pl.BlockSpec((1, length, piece), lambda t: (jnp.minimum(t, steps - 1), 0, 0)),
            pl.BlockSpec((1, length, piece), lambda t: (jnp.maximum(t - 1, 0), 0, 0)),
        ]
        + [whole] * 4
        + [anywhere] * 5,
        out_shape=[
            jax.ShapeDtypeStruct((H, DH, rows), BF),
            jax.ShapeDtypeStruct((H, DH, rows), F32),
            jax.ShapeDtypeStruct((H, 8, rows), F32),
            jax.ShapeDtypeStruct((steps, length, piece), BF),
            jax.ShapeDtypeStruct((steps, length, piece), BF),
            jax.ShapeDtypeStruct((rows, 128), BF),
            jax.ShapeDtypeStruct((8, width), F32),
            jax.ShapeDtypeStruct((8, TCH), F32),
            jax.ShapeDtypeStruct((8, hidden), F32),
            jax.ShapeDtypeStruct((rows, width), BF),
            jax.ShapeDtypeStruct((4 * piece, 2 * width), BF),
            jax.ShapeDtypeStruct((4 * piece, width), BF),
            jax.ShapeDtypeStruct((4 * piece, width), BF),
            jax.ShapeDtypeStruct((rows, width), BF),
        ],
        scratch_shapes=[
            pltpu.VMEM((4 * piece, width), BF),
            pltpu.VMEM((4 * piece, width), BF),
            pltpu.VMEM((rows, width), BF),
            pltpu.VMEM((4 * piece, 2 * width), BF),
            pltpu.VMEM((rows, width), BF),
            pltpu.VMEM((3, piece), jnp.int32),
            pltpu.VMEM((3, piece), jnp.int32),
            pltpu.VMEM((4 * piece, 128), BF),
            pltpu.VMEM((4 * piece, 128), BF),
            pltpu.SemaphoreType.DMA((10,)),
            pltpu.SemaphoreType.DMA((4,)),
            pltpu.SemaphoreType.DMA((4,)),
            pltpu.VMEM((length, 256), BF),
            pltpu.VMEM((piece, 256), BF),
            pltpu.VMEM((80, length), BF),
            pltpu.VMEM((80, length), BF),
            pltpu.VMEM((length, piece), F32),
            pltpu.VMEM((length, piece), F32),
            pltpu.VMEM((8, piece), F32),
            pltpu.VMEM((8, piece), F32),
        ],
        compiler_params=pltpu.CompilerParams(
            vmem_limit_bytes=VMEM_LIMIT, collective_id=4, has_side_effects=True
        ),
        cost_estimate=pl.CostEstimate(flops=20 * 10**9, bytes_accessed=60 * 10**6, transcendentals=19 * 10**6),
    )(counts, timesteps, x, mask, cot, w1, w2, gain, w)


def place_of(pair):
    return 4 * (pair & 1) + 2 * (pair >> 1 & 1) + (pair >> 2)


class Shares:
    def __init__(self, source, scratch, x_second):
        self.source = source
        self.x_second = x_second
        self.names = ["core", "rows", "y", "z0", "z1", "join", "out"] if x_second else [
            "core", "y", "z0", "z1", "x", "out"
        ]
        self.acc, self.final, self.send, self.receive = scratch[0], scratch[1], scratch[-2], scratch[-1]
        boxes = [name for name in self.names if name not in ("join", "out")]
        self.inbox = dict(zip(boxes, scratch[2:-2]))
        me, far = lax.axis_index("batch"), lax.axis_index("seq")
        self.core, self.y, self.z0, self.z1 = [(me >> bit) & 1 for bit in range(4)]
        self.me, self.far = me, far
        self.half = self.acc.shape[2]
        rows = self.acc.shape[1]
        self.rows = slice(0, rows)
        if x_second:
            self.rows = pl.ds(pl.multiple_of(far * (rows // 2), 16), rows // 2)
            self.other_rows = pl.ds(pl.multiple_of((1 - far) * (rows // 2), 16), rows // 2)
        self.own = 4 * self.y + 2 * self.z0 + self.z1

    def partner(self, name):
        if name in ("x", "rows", "join"):
            return (self.me, 1 - self.far)
        return (self.me ^ {"core": 1, "y": 2, "z0": 4, "z1": 8, "out": 1}[name], self.far)

    def ends(self, name):
        acc, rows = self.acc, self.rows
        if name == "core":
            away = pl.multiple_of((1 - self.core) * self.half, 128)
            return self.source.at[:, :, pl.ds(away, self.half)], self.inbox[name]
        if name == "rows":
            return acc.at[:, self.other_rows], self.inbox[name]
        if name == "y":
            return acc.at[pl.ds(4 * (1 - self.y), 4), rows], self.inbox[name]
        if name == "z0":
            return acc.at[pl.ds(4 * self.y + 2 * (1 - self.z0), 2), rows], self.inbox[name]
        if name == "z1":
            return acc.at[4 * self.y + 2 * self.z0 + 1 - self.z1, rows], self.inbox[name]
        if name == "x":
            return acc.at[self.own], self.inbox[name]
        if name == "join":
            return self.final.at[self.core, rows], self.final.at[self.core, rows]
        return self.final.at[self.core], self.final.at[self.core]

    def copy(self, stage):
        name = self.names[stage]
        here, there = self.ends(name)
        return pltpu.make_async_remote_copy(
            src_ref=here,
            dst_ref=there,
            send_sem=self.send.at[stage],
            recv_sem=self.receive.at[stage],
            device_id=self.partner(name),
            device_id_type=pl.DeviceIdType.MESH,
        )

    def load(self):
        mine = pl.multiple_of(self.core * self.half, 128)
        return pltpu.make_async_copy(
            self.source.at[:, :, pl.ds(mine, self.half)], self.acc, self.send.at[7]
        )

    def begin(self):
        self.copy(0).start()
        self.load().start()

    def add(self, name):
        acc, rows = self.acc, self.rows

        def total(one, other):
            return (one.astype(F32) + other.astype(F32)).astype(BF)

        if name in ("core", "rows", "y", "z0"):
            first, count = {
                "core": (0, 8),
                "rows": (0, 8),
                "y": (4 * self.y, 4),
                "z0": (4 * self.y + 2 * self.z0, 2),
            }[name]
            if name == "core":
                rows = slice(None)
            for k in range(count):
                acc[first + k, rows] = total(acc[first + k, rows], self.inbox[name][k])
        elif name == "z1" and not self.x_second:
            acc[self.own] = total(acc[self.own], self.inbox[name][...])
        elif name == "z1":
            self.final[self.core, rows] = total(acc[self.own, rows], self.inbox[name][...])
        elif name == "x":
            self.final[self.core] = total(acc[self.own], self.inbox[name][...])

    def go_on(self, stage):
        if stage == 0:
            self.load().wait()
        self.copy(stage).wait()
        self.add(self.names[stage])
        if stage + 1 < len(self.names):
            self.copy(stage + 1).start()


def share_scratch(rows, columns, x_second):
    half = columns // 2
    part = rows // 2 if x_second else rows
    shapes = [(8, rows, half), (2, rows, half), (8, rows, half)]
    shapes += [(8, part, half)] if x_second else []
    shapes += [(4, part, half), (2, part, half), (part, half)]
    shapes += [] if x_second else [(rows, half)]
    return [pltpu.VMEM(shape, BF) for shape in shapes] + [
        pltpu.SemaphoreType.DMA((8,)),
        pltpu.SemaphoreType.DMA((7,)),
    ]


SCRATCH_COUNT = 9


def greet():
    me, far = lax.axis_index("batch"), lax.axis_index("seq")
    barrier = pltpu.get_barrier_semaphore()
    for other in ((me ^ 1, far), (me ^ 2, far), (me ^ 4, far), (me ^ 8, far), (me, 1 - far)):
        pl.semaphore_signal(barrier, inc=1, device_id=other, device_id_type=pl.DeviceIdType.MESH)
    pl.semaphore_wait(barrier, 5)


def attend_back_kernel(
    pieces, plan, table, q_ref, k_ref, v_ref, do_ref, o_ref, inv_ref, even_ref, odd_ref, *rest
):
    count = len(pieces)
    arrays = 1 + max(array for array, _ in pieces)
    w_ref, out_hbm, *rest = rest
    sources, rest = rest[:arrays], rest[arrays:]
    (dq_ref, dk_ref, dv_ref, far_ref, output_hbm), rest = rest[:5], rest[5:]
    finals, rest = rest[:count], rest[count:]
    values, gradient, dk_sum, dv_sum, far_kv, far_send, far_got, out_got, far_sems, *rest = rest
    shares = []
    for i, (array, index) in enumerate(pieces):
        own = rest[SCRATCH_COUNT * i : SCRATCH_COUNT * (i + 1)]
        shares.append(Shares(sources[array].at[index], own, plan[i]))
    step = pl.program_id(0)
    steps = pl.num_programs(0)
    pair, part = back_place(step)
    piece, length = q_ref.shape[0], k_ref.shape[0]
    lane = lax.broadcasted_iota(jnp.int32, (1, 128), 1)
    zero = jnp.zeros((), BF)
    far_copy = pltpu.make_async_remote_copy(
        src_ref=far_send,
        dst_ref=far_got,
        send_sem=far_sems.at[0],
        recv_sem=far_sems.at[1],
        device_id=(lax.axis_index("batch"), 1 - lax.axis_index("seq")),
        device_id_type=pl.DeviceIdType.MESH,
    )

    seq = lax.axis_index("seq")
    out_copy = pltpu.make_async_remote_copy(
        src_ref=out_hbm.at[pl.ds(piece, piece)],
        dst_ref=out_got,
        send_sem=far_sems.at[2],
        recv_sem=far_sems.at[3],
        device_id=(lax.axis_index("batch"), 1 - seq),
        device_id_type=pl.DeviceIdType.MESH,
    )
    kept = [
        pltpu.make_async_copy(out_hbm.at[pl.ds(0, piece)], output_hbm.at[seq], far_sems.at[4]),
        pltpu.make_async_copy(out_hbm.at[pl.ds(2 * piece, piece)], output_hbm.at[2], far_sems.at[5]),
    ]
    returned = pltpu.make_async_copy(out_got, output_hbm.at[1 - seq], far_sems.at[6])

    @pl.when(step == 0)
    def _():
        greet()
        for share in shares:
            share.begin()
        out_copy.start()
        for copy in kept:
            copy.start()
        values[:, 128:] = jnp.where(
            lax.broadcasted_iota(jnp.int32, (length, 128), 1) < 3, 1.0, 0.0
        ).astype(BF)
        gradient[...] = jnp.zeros_like(gradient)

    for when in sorted(table):
        if when < 18:

            @pl.when(step == when)
            def _(when=when):
                for i, stage in table[when]:
                    shares[i].go_on(stage)

    @pl.when(step == 11)
    def _():
        out_copy.wait()
        returned.start()

    @pl.when(step == 6)
    def _():
        far_send[...] = mm(far_kv[...], w_ref[...], 1, 1).astype(BF)
        far_copy.start()

    values[:, :128] = v_ref[...]
    inverse = jnp.concatenate(
        [jnp.broadcast_to(inv_ref[head, 0:1, :], (DH, piece)) for head in range(2)], axis=0
    )
    scaled = (do_ref[...].astype(F32) * inverse).astype(BF)
    product = scaled.astype(F32) * o_ref[...]
    for head in range(2):
        mine = slice(DH * head, DH * head + DH)
        place = slice(piece * head, piece * head + piece)
        delta = -jnp.sum(product[mine], axis=0, keepdims=True)
        high = delta.astype(BF).astype(F32)
        rest_of = delta - high
        middle = rest_of.astype(BF).astype(F32)
        gradient[mine, place] = scaled[mine]
        gradient[128:144, place] = jnp.concatenate(
            [high, middle, rest_of - middle, jnp.zeros((13, piece), F32)], axis=0
        ).astype(BF)
    dp = mm(values[...], gradient[...], 1, 0)
    turned_keys = k_ref[...].T
    natural = scaled.T
    weights = [even_ref[0], odd_ref[0]]
    ds = [
        (weights[head].astype(F32) * dp[:, piece * head : piece * head + piece]).astype(BF)
        for head in range(2)
    ]

    def apart(array):
        return jnp.concatenate(
            [jnp.where(lane < 64, array, zero), jnp.where(lane < 64, zero, array)], axis=0
        )

    dv = mm(jnp.concatenate(weights, axis=1), apart(natural), 1, 0)
    dk = mm(jnp.concatenate(ds, axis=1), apart(q_ref[...]), 1, 0)
    for head in range(2):
        mine = slice(DH * head, DH * head + DH)
        dq_ref[mine, :] = (mm(turned_keys[mine], ds[head], 1, 0) * 0.125).astype(BF)

    @pl.when(part != 1)
    def _():
        dk_sum[...] = dk
        dv_sum[...] = dv

    @pl.when(part == 1)
    def _():
        dk_sum[...] += dk
        dv_sum[...] += dv

    dk_ref[...] = dk_sum[...].astype(BF)
    dv_ref[...] = dv_sum[...].astype(BF)

    @pl.when(step < 6)
    def _():
        at = pl.multiple_of(pair * 128, 128)
        far_kv[:, pl.ds(at, 128)] = dk[piece:].astype(BF)
        far_kv[:, pl.ds(pl.multiple_of(at + w_ref.shape[0], 128), 128)] = dv[piece:].astype(BF)

    @pl.when(step == steps - 1)
    def _():
        for when in sorted(table):
            if when >= 18:
                for i, stage in table[when]:
                    shares[i].go_on(stage)
        for i in range(count):
            finals[i][...] = shares[i].final[...]
        far_copy.wait()
        far_ref[...] = far_got[...]
        for copy in kept:
            copy.wait()
        returned.wait()


def back_place(step):
    late = jnp.maximum(step - 6, 0)
    return jnp.where(step < 6, step, late // 2), jnp.where(step < 6, 2, late % 2)


def attend_back(q, kv, do, o, inv, even, odd, w_kv, out, partials, pieces, plan, table):
    rows, width = q.shape
    length = 2 * rows // 3
    piece = rows // 3

    def spec(shape, index):
        return pl.BlockSpec(shape, lambda t: index(*back_place(t)))

    weight_spec = spec((1, length, piece), lambda p, j: (j * 6 + p, 0, 0))
    scratch, sizes = [], [partials[array].shape[2:] for array, _ in pieces]
    for size, x_second in zip(sizes, plan):
        scratch += share_scratch(*size, x_second)
    whole = pl.BlockSpec(memory_space=pltpu.VMEM)
    return pl.pallas_call(
        partial(attend_back_kernel, pieces, plan, table),
        grid=(18,),
        in_specs=[
            spec((piece, 128), lambda p, j: (j, p)),
            spec((length, 128), lambda p, j: (j // 2, p)),
            spec((length, 128), lambda p, j: (j // 2, 6 + p)),
            spec((128, piece), lambda p, j: (p, j)),
            spec((128, piece), lambda p, j: (p, j)),
            spec((2, 8, piece), lambda p, j: (p, 0, j)),
            weight_spec,
            weight_spec,
            whole,
        ]
        + [pl.BlockSpec(memory_space=pl.ANY)] * (1 + len(partials)),
        out_specs=[
            spec((128, piece), lambda p, j: (p, j)),
            spec((length, 128), lambda p, j: (j // 2, p)),
            spec((length, 128), lambda p, j: (j // 2, p)),
            whole,
            pl.BlockSpec(memory_space=pl.ANY),
        ]
        + [whole] * len(pieces),
        out_shape=[
            jax.ShapeDtypeStruct((width, rows), BF),
            jax.ShapeDtypeStruct((2 * length, width), BF),
            jax.ShapeDtypeStruct((2 * length, width), BF),
            jax.ShapeDtypeStruct((piece, width), BF),
            jax.ShapeDtypeStruct((3, piece, width), BF),
        ]
        + [jax.ShapeDtypeStruct((2, a, b // 2), BF) for a, b in sizes],
        scratch_shapes=[
            pltpu.VMEM((length, 256), BF),
            pltpu.VMEM((256, 2 * piece), BF),
            pltpu.VMEM((length, 128), F32),
            pltpu.VMEM((length, 128), F32),
            pltpu.VMEM((piece, 2 * width), BF),
            pltpu.VMEM((piece, width), BF),
            pltpu.VMEM((piece, width), BF),
            pltpu.VMEM((piece, width), BF),
            pltpu.SemaphoreType.DMA((7,)),
        ]
        + scratch,
        compiler_params=pltpu.CompilerParams(
            vmem_limit_bytes=VMEM_LIMIT, collective_id=1, has_side_effects=True
        ),
        cost_estimate=pl.CostEstimate(flops=30 * 10**9, bytes_accessed=60 * 10**6, transcendentals=0),
    )(q, kv, kv, do, o, inv, even, odd, w_kv, out, *partials)


def finish_kernel(
    dq_hbm, dk_hbm, dv_hbm, n1_hbm, x_hbm, dh_hbm, w_hbm, far_ref, temb_ref, gain_ref, dgain2_ref,
    w2_ref, emb_ref, u_ref, *rest
):
    out_ref, finals, rest = rest[0], rest[1:6], rest[6:]
    dq, dk, dv, n1, x, dh, w, send, got, sems, far_sems = rest[:11]
    sources, rest = rest[11:16], rest[16:]
    shares = []
    for i in range(5):
        own = rest[SCRATCH_COUNT * i : SCRATCH_COUNT * (i + 1)]
        shares.append(Shares(sources[i], own, False))
    half, width = far_ref.shape
    me, seq = lax.axis_index("batch"), lax.axis_index("seq")

    loads = {}

    def fetch(name, source, target):
        loads[name] = pltpu.make_async_copy(source, target, sems.at[len(loads)])
        loads[name].start()

    blocks = [slice(half * i, half * i + half) for i in range(4)]
    fetch("w", w_hbm, w)
    for b in (1, 0, 2):
        fetch(("dq", b), dq_hbm.at[:, blocks[b]], dq.at[:, blocks[b]])
        fetch(("dk", b), dk_hbm.at[blocks[b]], dk.at[blocks[b]])
        fetch(("dv", b), dv_hbm.at[blocks[b]], dv.at[blocks[b]])
        if b == 1:
            fetch("x", x_hbm.at[pl.ds(0, 3 * half)], x)
            fetch(("dh", 1), dh_hbm.at[blocks[1]], dh.at[blocks[1]])
    fetch(("dk", 3), dk_hbm.at[blocks[3]], dk.at[blocks[3]])
    fetch(("dv", 3), dv_hbm.at[blocks[3]], dv.at[blocks[3]])
    fetch("n1", n1_hbm, n1)
    fetch(("dh", 0), dh_hbm.at[blocks[0]], dh.at[blocks[0]])
    fetch(("dh", 2), dh_hbm.at[blocks[2]], dh.at[blocks[2]])
    back_copy = pltpu.make_async_remote_copy(
        src_ref=send,
        dst_ref=got,
        send_sem=far_sems.at[0],
        recv_sem=far_sems.at[1],
        device_id=(me, 1 - seq),
        device_id_type=pl.DeviceIdType.MESH,
    )
    greet()

    def norm_back(b, more):
        loads[("dh", b)].wait()
        part = blocks[b]
        dn = mm(dq[:, part], w[:, :width], 0, 1)
        dn += mm(dk[part, :], w[:, width : 2 * width], 1, 1)
        dn += mm(dv[part, :], w[:, 2 * width :], 1, 1)
        if more is not None:
            dn += more[...].astype(F32)
        h = x[part, :].astype(F32) + temb_ref[b // 2 : b // 2 + 1, :]
        centered = h - jnp.mean(h, axis=1, keepdims=True)
        r1 = lax.rsqrt(jnp.mean(centered * centered, axis=1, keepdims=True) + 1e-5)
        x1 = centered * r1
        e = dn * gain_ref[...]
        dh0 = dh[part, :] + r1 * (
            e - jnp.mean(e, axis=1, keepdims=True) - x1 * jnp.mean(e * x1, axis=1, keepdims=True)
        )
        return dh0, jnp.sum(dh0, axis=0, keepdims=True), jnp.sum(dn * x1, axis=0, keepdims=True)

    def weight_piece(f):
        columns = slice(256 * f, 256 * f + 256)
        q_part = mm(dq[...], n1[: 3 * half, columns], 1, 0).astype(BF)
        k_part = mm(dk[...], n1[:, columns], 0, 0).astype(BF)
        v_part = mm(dv[...], n1[:, columns], 0, 0).astype(BF)
        pair_rows = width // 4
        for k in range(8):
            source = q_part if k < 4 else k_part
            first = pair_rows * (k % 4)
            sources[f][place_of(k), :pair_rows, :] = source[first : first + pair_rows]
            first = width // 8 * k
            sources[f][place_of(k), pair_rows:, :] = v_part[first : first + width // 8]
        shares[f].begin()

    loads["w"].wait()
    for name in ("dq", "dk", "dv"):
        loads[(name, 1)].wait()
    loads["x"].wait()
    dh0, dtemb_a, dgain_a = norm_back(1, None)
    send[...] = dh0.astype(BF)
    back_copy.start()
    for name in ("dq", "dk", "dv"):
        loads[(name, 0)].wait()
        loads[(name, 2)].wait()
    loads[("dk", 3)].wait()
    loads[("dv", 3)].wait()
    loads["n1"].wait()
    weight_piece(0)
    weight_piece(1)
    shares[0].go_on(0)
    weight_piece(2)
    shares[1].go_on(0)
    dh0, dtemb_b, dgain_b = norm_back(0, None)
    out_ref[seq] = dh0
    shares[2].go_on(0)
    shares[0].go_on(1)
    dh0, dtemb_two, dgain_c = norm_back(2, far_ref)
    out_ref[2] = dh0

    dtemb_one = dtemb_a + dtemb_b
    first = (seq == 0).astype(F32)
    dtemb = jnp.concatenate(
        [first * dtemb_one, (1.0 - first) * dtemb_one, dtemb_two, jnp.zeros((5, width), F32)], axis=0
    )
    u = u_ref[...]
    sigmoid = 1.0 / (1.0 + jnp.exp(-u))
    outer = lax.dot_general(
        dtemb, u * sigmoid, (((0,), (0,)), ((), ())), precision=TOP_PRECISION, preferred_element_type=F32
    ).astype(BF)
    dsilu = lax.dot_general(
        dtemb, w2_ref[...].astype(F32), (((1,), (1,)), ((), ())), precision=TOP_PRECISION, preferred_element_type=F32
    )
    dpre = dsilu * (sigmoid * (1.0 + u * (1.0 - sigmoid)))
    inner = lax.dot_general(
        dpre, emb_ref[...], (((0,), (0,)), ((), ())), precision=TOP_PRECISION, preferred_element_type=F32
    ).astype(BF)
    dgain = dgain_a + dgain_b + dgain_c
    size, inner_size = width // 8, inner.shape[0] // 8
    sources[4][...] = jnp.zeros_like(sources[4])
    for k in range(8):
        sources[3][place_of(k)] = outer[size * k : size * k + size]
        sources[4][place_of(k), :, :128] = inner[inner_size * k : inner_size * k + inner_size]
        both = jnp.concatenate(
            [
                jnp.concatenate([g[:, size * k : size * k + size], jnp.zeros((1, 128 - size), F32)], axis=1)
                for g in (dgain, dgain2_ref[...])
            ]
            + [jnp.zeros((14, 128), F32)],
            axis=0,
        )
        sources[4][place_of(k), :16, 128:] = both.astype(BF)
    shares[3].begin()
    shares[4].begin()
    for i, stage in FINISH_ORDER:
        shares[i].go_on(stage)
    for i in range(5):
        finals[i][...] = shares[i].final[...]
    back_copy.wait()
    out_ref[1 - seq] = got[...].astype(F32)


FINISH_ORDER = [
    (3, 0), (4, 0), (0, 2), (1, 1), (0, 3), (1, 2), (2, 1), (0, 4), (1, 3), (2, 2), (3, 1), (4, 1),
    (0, 5), (1, 4), (2, 3), (3, 2), (4, 2), (1, 5), (2, 4), (3, 3), (4, 3), (2, 5), (3, 4), (4, 4),
    (3, 5), (4, 5),
]


def finish(dq, dk, dv, n1, x, dh1, w, far, temb, gain, dgain2, w2, emb, u):
    half, width = far.shape
    rows = 3 * half
    hidden = w2.shape[0]
    whole = pl.BlockSpec(memory_space=pltpu.VMEM)
    sizes = [(3 * width // 8, 256)] * 3 + [(width // 8, hidden), (hidden // 8, 256)]
    scratch = [pltpu.VMEM((8,) + size, BF) for size in sizes]
    for size in sizes:
        scratch += share_scratch(*size, False)
    return pl.pallas_call(
        finish_kernel,
        in_specs=[pl.BlockSpec(memory_space=pl.ANY)] * 7 + [whole] * 7,
        out_specs=[whole] * 6,
        out_shape=[jax.ShapeDtypeStruct((3, half, width), F32)]
        + [jax.ShapeDtypeStruct((2, a, b // 2), BF) for a, b in sizes],
        scratch_shapes=[
            pltpu.VMEM((width, rows), BF),
            pltpu.VMEM((4 * half, width), BF),
            pltpu.VMEM((4 * half, width), BF),
            pltpu.VMEM((4 * half, width), BF),
            pltpu.VMEM((rows, width), BF),
            pltpu.VMEM((rows, width), F32),
            pltpu.VMEM(w.shape, BF),
            pltpu.VMEM((half, width), BF),
            pltpu.VMEM((half, width), BF),
            pltpu.SemaphoreType.DMA((20,)),
            pltpu.SemaphoreType.DMA((2,)),
        ]
        + scratch,
        compiler_params=pltpu.CompilerParams(
            vmem_limit_bytes=VMEM_LIMIT, collective_id=2, has_side_effects=True
        ),
        cost_estimate=pl.CostEstimate(flops=15 * 10**9, bytes_accessed=60 * 10**6, transcendentals=0),
    )(dq, dk, dv, n1, x, dh1, w, far, temb, gain, dgain2, w2, emb, u)


def gelu_and_slope(g):
    square = g * g
    half_plus = 0.5 * jnp.tanh(g * (GELU_A + GELU_A * GELU_B * square)) + 0.5
    act = g * half_plus
    slope = half_plus + act * (2.0 - 2.0 * half_plus) * (GELU_A + 3.0 * GELU_A * GELU_B * square)
    return act, slope


FF_BEGIN = {6: (0, 1), 12: (2, 3)}
FF_PLAN = [False, True, False, True]
FF_TICKS = {
    7: [(0, 0), (1, 0)],
    10: [(0, 1), (1, 1)],
    12: [(0, 2), (1, 2)],
    13: [(2, 0), (3, 0)],
    14: [(0, 3), (1, 3)],
    15: [(0, 4), (1, 4)],
    16: [(0, 5), (1, 5), (2, 1), (3, 1)],
    17: [(1, 6)],
    18: [(2, 2), (3, 2)],
    19: [(2, 3), (3, 3)],
    20: [(2, 4), (3, 4)],
    21: [(2, 5), (3, 5), (3, 6)],
}


def feedforward_kernel(
    x_hbm, o_ref, dm_ref, live_ref, temb_ref, gain_ref, wo_ref, *rest
):
    wu_refs, wd_refs, rest = rest[:4], rest[4:8], rest[8:]
    out_hbm, dh1_hbm, do_ref, dwu_ref, dwd_ref, dwo_ref, dgain_ref, *rest = rest
    finals, rest = rest[:4], rest[4:]
    x, h1, n2, h2, dn2, sems, *rest = rest
    sources, rest = rest[:4], rest[4:]
    shares = []
    for i in range(4):
        own = rest[SCRATCH_COUNT * i : SCRATCH_COUNT * (i + 1)]
        shares.append(Shares(sources[i], own, FF_PLAN[i]))
    turn, side = pl.program_id(0), pl.program_id(1)
    chunk, chunks = 2 * turn + side, 6
    wu = jnp.concatenate([ref[...] for ref in wu_refs], axis=1)
    wd = jnp.concatenate([ref[...] for ref in wd_refs], axis=0)
    rows, width = x.shape
    block = rows // 2
    third = rows // 3
    blocks = [slice(block * i, block * i + block) for i in range(2)]
    thirds = [slice(third * i, third * i + third) for i in range(3)]
    size = width // 8

    def act_on(now):
        for i, stage in FF_TICKS.get(now, []):
            shares[i].go_on(stage)
        for i in FF_BEGIN.get(now, []):
            shares[i].begin()

    def tick(position):
        for now in sorted(set(FF_TICKS) | set(FF_BEGIN)):
            if now < 18 and now % 3 == position:
                pl.when(chunk == now // 3)(partial(act_on, now))

    load = pltpu.make_async_copy(x_hbm.at[pl.ds(0, rows)], x, sems.at[0])

    @pl.when(chunk == 0)
    def _():
        load.start()
        greet()
        load.wait()
        for i, part in enumerate(thirds):
            h0 = x[part, :].astype(F32) + temb_ref[i // 2 : i // 2 + 1, :]
            h = h0 + mm(o_ref[:, part], wo_ref[...], 0, 0)
            h1[part, :] = h
            centered = h - jnp.mean(h, axis=1, keepdims=True)
            variance = jnp.mean(centered * centered, axis=1, keepdims=True)
            n2[part, :] = (centered * lax.rsqrt(variance + 1e-5) * gain_ref[...]).astype(BF)
            h2[part, :] = h
            dn2[part, :] = jnp.zeros_like(h)

    def first(part):
        return mm(n2[part, :], wu, 1, 0), mm(dm_ref[part, :], wd, 1, 1)

    def second(pair):
        act, slope = gelu_and_slope(pair[0])
        return act.astype(BF), (pair[1] * slope).astype(BF)

    def third_step(part, pair):
        h2[part, :] += mm(pair[0], wd, 1, 0)
        dn2[part, :] += mm(pair[1], wu, 1, 1)

    tick(0)
    a = first(blocks[0])
    b = first(blocks[1])
    a = second(a)
    b = second(b)
    tick(1)
    third_step(blocks[0], a)
    third_step(blocks[1], b)
    tick(2)
    act = jnp.concatenate([a[0], b[0]], axis=0)
    dg = jnp.concatenate([a[1], b[1]], axis=0)
    dwd = mm(dm_ref[...], act, 0, 0).astype(BF)
    dwu = mm(dg, n2[...], 0, 0).astype(BF).reshape(4, 128, width)
    for c in range(3):
        up_to, down_to = (sources[2 * c], sources[2 * c + 1]) if c < 2 else (dwu_ref.at[0], dwd_ref.at[0])

        @pl.when(turn == c)
        def _(up_to=up_to, down_to=down_to):
            up_to[pl.ds(4 * side, 4)] = dwu
            for k in range(8):
                columns = pl.ds(pl.multiple_of(512 * side, 128), 512)
                down_to[place_of(k), :, columns] = dwd[size * k : size * k + size]

    @pl.when(chunk == chunks - 1)
    def _():
        act_on(18)
        dgain = jnp.zeros_like(dgain_ref)
        for i, part in enumerate(thirds):
            h = h1[part, :]
            live = live_ref[part, 0:1].astype(F32)
            x[part, :] = (live * h2[part, :]).astype(BF)
            centered = h - jnp.mean(h, axis=1, keepdims=True)
            variance = jnp.mean(centered * centered, axis=1, keepdims=True)
            r2 = lax.rsqrt(variance + 1e-5)
            x2 = centered * r2
            dn = dn2[part, :]
            dgain += jnp.sum(dn * x2, axis=0, keepdims=True)
            e = dn * gain_ref[...]
            dh1 = dm_ref[part, :].astype(F32) + r2 * (
                e
                - jnp.mean(e, axis=1, keepdims=True)
                - x2 * jnp.mean(e * x2, axis=1, keepdims=True)
            )
            h1[part, :] = dh1
            da = dh1.astype(BF)
            n2[part, :] = da
            do_ref[:, part] = mm(wo_ref[...], da, 1, 1).astype(BF)
            act_on(19 + i)
        stores = [
            pltpu.make_async_copy(x, out_hbm, sems.at[1]),
            pltpu.make_async_copy(h1, dh1_hbm, sems.at[2]),
        ]
        for store in stores:
            store.start()
        dgain_ref[...] = dgain
        dwo = mm(n2[...], o_ref[...], 0, 1).astype(BF)
        for k in range(8):
            dwo_ref[0, place_of(k)] = dwo[size * k : size * k + size]
        for i in range(4):
            finals[i][...] = shares[i].final[...]
        for store in stores:
            store.wait()


def feedforward(x, o, dm, live, temb, gain, wo, wu, wd):
    rows, width = dm.shape
    whole = pl.BlockSpec(memory_space=pltpu.VMEM)
    anywhere = pl.BlockSpec(memory_space=pl.ANY)

    def tile(c, h, i):
        return 3 * (4 * (i % 2) + 2 * (i // 2) + h) + c

    up_specs = [pl.BlockSpec((width, 128), lambda c, h, i=i: (0, tile(c, h, i))) for i in range(4)]
    down_specs = [pl.BlockSpec((128, width), lambda c, h, i=i: (tile(c, h, i), 0)) for i in range(4)]
    sizes = [(128, width), (width // 8, 1024)] * 2
    scratch = [pltpu.VMEM((8,) + size, BF) for size in sizes]
    for size, x_second in zip(sizes, FF_PLAN):
        scratch += share_scratch(*size, x_second)
    return pl.pallas_call(
        feedforward_kernel,
        grid=(3, 2),
        in_specs=[anywhere] + [whole] * 6 + up_specs + down_specs,
        out_specs=[anywhere] * 2 + [whole] * 9,
        out_shape=[
            jax.ShapeDtypeStruct((rows, width), BF),
            jax.ShapeDtypeStruct((rows, width), F32),
            jax.ShapeDtypeStruct((width, rows), BF),
            jax.ShapeDtypeStruct((1, 8, 128, width), BF),
            jax.ShapeDtypeStruct((1, 8, width // 8, 1024), BF),
            jax.ShapeDtypeStruct((1, 8, width // 8, width), BF),
            jax.ShapeDtypeStruct((1, width), F32),
        ]
        + [jax.ShapeDtypeStruct((2, a, b // 2), BF) for a, b in sizes],
        scratch_shapes=[
            pltpu.VMEM((rows, width), BF),
            pltpu.VMEM((rows, width), F32),
            pltpu.VMEM((rows, width), BF),
            pltpu.VMEM((rows, width), F32),
            pltpu.VMEM((rows, width), F32),
            pltpu.SemaphoreType.DMA((3,)),
        ]
        + scratch,
        compiler_params=pltpu.CompilerParams(
            vmem_limit_bytes=VMEM_LIMIT, collective_id=3, has_side_effects=True
        ),
        cost_estimate=pl.CostEstimate(flops=48 * 10**9, bytes_accessed=50 * 10**6, transcendentals=5 * 10**6),
    )(x, o, dm, live, temb, gain, wo, *[wu] * 4, *[wd] * 4)


def pair_plan(
    inputs,
    timesteps,
    counts,
    slot_token_mask,
    time_first_weight,
    time_second_weight,
    attention_norm_gain,
    query_key_value_weight,
    attention_output_weight,
    feedforward_norm_gain,
    up_projection_weight,
    down_projection_weight,
    cotangent,
):
    slots, half, width = inputs.shape
    batches = lax.axis_size("batch")
    (o, exact, inv, even, odd, live_wide, temb, emb, u, q, kv, n1, x, dm) = attend(
        counts,
        timesteps,
        inputs,
        slot_token_mask,
        cotangent,
        time_first_weight,
        time_second_weight,
        attention_norm_gain[None, :],
        query_key_value_weight,
    )
    o = o.reshape(width, 3 * half)
    out, dh1, do, dwu, dwd, dwo, dgain2, *early = feedforward(
        x,
        o,
        dm,
        live_wide,
        temb,
        feedforward_norm_gain[None, :],
        attention_output_weight,
        up_projection_weight,
        down_projection_weight,
    )
    partials = [dwu, dwd, dwo]
    pieces = [(0, 0), (1, 0), (2, 0)]
    plan = [False, False, False]
    dq, dk, dv, far, output, *sums = attend_back(
        q,
        kv,
        do,
        exact.reshape(width, 3 * half),
        inv,
        even,
        odd,
        query_key_value_weight[:, width:],
        out,
        partials,
        pieces,
        plan,
        BACK_TABLE,
    )
    grad_inputs, *last = finish(
        dq,
        dk,
        dv,
        n1,
        x,
        dh1,
        query_key_value_weight,
        far,
        temb,
        attention_norm_gain[None, :],
        dgain2,
        time_second_weight,
        emb,
        u,
    )
    mine = lax.axis_index("batch")

    def joined(part):
        return jnp.concatenate([part[0], part[1]], axis=1)

    def own_half(array):
        size = array.shape[0] // 2
        return lax.dynamic_slice_in_dim(array, (mine & 1) * size, size, 0).astype(F32)

    up_parts = [joined(part) for part in (early[0], early[2], sums[0])]
    down_parts = [joined(part) for part in (early[1], early[3], sums[1])]
    up_sum = own_half(jnp.concatenate(up_parts, axis=0))
    down_sum = jnp.stack([own_half(part) for part in down_parts], axis=1)
    down_sum = down_sum.reshape(-1, 3, 2, 2, 2, 128).transpose(0, 4, 3, 2, 1, 5)
    down_sum = down_sum.reshape(width // batches, -1)
    out_sum = own_half(joined(sums[2]))
    qkv_sum = jnp.concatenate([joined(part) for part in last[:3]], axis=1)
    qk_sum = own_half(qkv_sum[: width // 4])
    v_sum = own_half(qkv_sum[width // 4 :])
    outer_sum = own_half(joined(last[3]))
    inner_sum = own_half(last[4][0])
    gains = own_half(last[4][1, :2, : width // 8].T)
    return (
        output,
        grad_inputs,
        inner_sum.T,
        outer_sum.T,
        gains[:, 0],
        qk_sum.T,
        v_sum.T,
        out_sum.T,
        gains[:, 1],
        up_sum.T,
        down_sum.T,
    )


BACK_TABLE = {
    1: [(0, 0), (1, 0), (2, 0)],
    5: [(0, 1)],
    7: [(0, 2)],
    9: [(0, 3), (1, 1)],
    10: [(0, 4)],
    11: [(0, 5), (1, 2)],
    12: [(2, 1)],
    13: [(1, 3)],
    14: [(1, 4), (2, 2)],
    15: [(1, 5), (2, 3)],
    16: [(2, 4)],
    17: [(2, 5)],
}


def solution(mesh):
    on_device = pair_plan if mesh.shape["seq"] == 2 else ring_plan
    return jax.shard_map(
        on_device,
        mesh=mesh,
        in_specs=(
            P("batch", "seq", None),
            P("batch"),
            P("batch"),
            P("batch", "seq"),
            P(),
            P(),
            P(),
            P(),
            P(),
            P(),
            P(),
            P(),
            P("batch", "seq", None),
        ),
        out_specs=(
            P("batch", "seq", None),
            P("batch", "seq", None),
            P(None, "batch"),
            P(None, "batch"),
            P("batch"),
            P(None, "batch"),
            P(None, "batch"),
            P(None, "batch"),
            P("batch"),
            P(None, "batch"),
            P(None, "batch"),
        ),
        check_vma=False,
    )
```

```python
from functools import partial
import math

import jax
import jax.numpy as jnp
from jax import lax
from jax.experimental import pallas as pl
from jax.experimental.pallas import tpu as pltpu
from jax.sharding import PartitionSpec as P

H = 12
DH = 64
TCH = 128


TOP_PRECISION = lax.Precision.HIGHEST


def from_behind(array, axis, by):
    count = lax.axis_size(axis)
    return lax.ppermute(array, axis, [(i, (i + by) % count) for i in range(count)])


def shortened(array):

    def short(part):
        return part.astype(jnp.bfloat16) if part.dtype == jnp.float32 else part

    return jax.tree.map(short, array)


def sinusoid(steps):
    half_width = TCH // 2
    frequency = jnp.exp(
        -math.log(10000.0) * jnp.arange(half_width).astype(jnp.float32) / half_width
    )
    angles = steps.astype(jnp.float32)[:, None] * frequency[None, :]
    return jnp.concatenate([jnp.cos(angles), jnp.sin(angles)], axis=-1)


def layer_norm(hidden, gain):
    centered = hidden - jnp.mean(hidden, axis=-1, keepdims=True)
    variance = jnp.mean(centered * centered, axis=-1, keepdims=True)
    return centered * lax.rsqrt(variance + 1e-05) * gain


def time_mlp(time_embedding, time_first_weight, time_second_weight):
    pre_act = jnp.dot(time_embedding, time_first_weight, precision=TOP_PRECISION)
    return jnp.dot(jax.nn.silu(pre_act), time_second_weight, precision=TOP_PRECISION)


def row_product(left, right):
    return lax.dot_general(
        left, right, (((0,), (0,)), ((), ())), preferred_element_type=jnp.float32
    )


def back_product(left, right):
    return lax.dot_general(
        left, right, (((1,), (1,)), ((), ())), preferred_element_type=jnp.float32
    )


def masked_scores(queries, key_block, mask_block, scale_factor):
    attention_scores = (
        jnp.einsum("sqhd,skhd->shqk", queries, key_block, preferred_element_type=jnp.float32)
        * scale_factor
    )
    return jnp.where(mask_block[:, None, None, :] > 0.5, attention_scores, -1000000000.0)


def ring_plan(
    inputs,
    timesteps,
    counts,
    slot_token_mask,
    time_first_weight,
    time_second_weight,
    attention_norm_gain,
    query_key_value_weight,
    attention_output_weight,
    feedforward_norm_gain,
    up_projection_weight,
    down_projection_weight,
    cotangent,
):
    present_slots, local_len, width = inputs.shape
    total_rows = present_slots * local_len
    scale_factor = 1.0 / math.sqrt(DH)
    slot_alive_flags = (
        (jnp.arange(present_slots)[:, None] < counts[0]) & (slot_token_mask == 1)
    ).astype(jnp.float32)
    time_embedding = sinusoid(timesteps)
    time_vec, time_back = jax.vjp(
        partial(time_mlp, time_embedding),
        time_first_weight.astype(jnp.float32),
        time_second_weight.astype(jnp.float32),
    )
    residual = inputs.astype(jnp.float32) + time_vec[:, None, :]
    normed, norm_back = jax.vjp(layer_norm, residual, attention_norm_gain)
    normed_low = normed.astype(jnp.bfloat16).reshape(total_rows, width)
    packed = (
        jnp.dot(normed_low, query_key_value_weight, preferred_element_type=jnp.float32)
        .astype(jnp.bfloat16)
        .reshape(present_slots, local_len, 3 * width)
    )
    queries = packed[:, :, :width].reshape(present_slots, local_len, H, DH)
    key_rows = packed[:, :, width : 2 * width]
    value_rows = packed[:, :, 2 * width :]
    key_valid_mask = slot_alive_flags.astype(jnp.bfloat16)
    initial_state = (
        jnp.full((present_slots, H, local_len), -1e30, jnp.float32),
        jnp.zeros((present_slots, H, local_len), jnp.float32),
        jnp.zeros((present_slots, local_len, H, DH), jnp.float32),
    )
    key_piece = lax.all_gather(key_rows, "seq", axis=1, tiled=True)
    value_piece = lax.all_gather(value_rows, "seq", axis=1, tiled=True)
    mask_piece = lax.all_gather(key_valid_mask, "seq", axis=1, tiled=True)
    piece_len = key_piece.shape[1]
    block_len = min(piece_len, local_len)

    def one_block(position, inner_state):
        run_max, run_sum, running_totals = inner_state
        offset = position * block_len
        key_block = lax.dynamic_slice_in_dim(key_piece, offset, block_len, 1).reshape(
            present_slots, block_len, H, DH
        )
        value_block = lax.dynamic_slice_in_dim(value_piece, offset, block_len, 1).reshape(
            present_slots, block_len, H, DH
        )
        mask_block = lax.dynamic_slice_in_dim(mask_piece, offset, block_len, 1)
        attention_scores = masked_scores(queries, key_block, mask_block, scale_factor)
        new_max = jnp.maximum(run_max, jnp.max(attention_scores, axis=-1))
        exponent = jnp.exp(attention_scores - new_max[..., None])
        fading = jnp.exp(run_max - new_max)
        run_sum = run_sum * fading + jnp.sum(exponent, axis=-1)
        running_totals = running_totals * jnp.transpose(fading, (0, 2, 1))[..., None] + jnp.einsum(
            "shqk,skhd->sqhd",
            exponent.astype(jnp.bfloat16),
            value_block,
            preferred_element_type=jnp.float32,
        )
        return (new_max, run_sum, running_totals)

    run_max, run_sum, running_totals = lax.fori_loop(
        0, piece_len // block_len, one_block, initial_state
    )
    attended = running_totals / jnp.transpose(run_sum, (0, 2, 1))[..., None]
    log_total = run_max + jnp.log(run_sum)
    attended_low = attended.astype(jnp.bfloat16).reshape(total_rows, width)
    middle = residual + jnp.dot(
        attended_low, attention_output_weight, preferred_element_type=jnp.float32
    ).reshape(present_slots, local_len, width)
    normed_two, norm_two_back = jax.vjp(layer_norm, middle, feedforward_norm_gain)
    normed_two_low = normed_two.astype(jnp.bfloat16).reshape(total_rows, width)
    gate_pre = jnp.dot(normed_two_low, up_projection_weight, preferred_element_type=jnp.float32)
    activated, gelu_back = jax.vjp(partial(jax.nn.gelu, approximate=True), gate_pre)
    activated_low = activated.astype(jnp.bfloat16)
    completed_groups = middle + jnp.dot(
        activated_low, down_projection_weight, preferred_element_type=jnp.float32
    ).reshape(present_slots, local_len, width)
    output = (slot_alive_flags[..., None] * completed_groups).astype(jnp.bfloat16)
    final_gradient = slot_alive_flags[..., None] * cotangent.astype(jnp.float32)
    grad_down_low = final_gradient.reshape(total_rows, width).astype(jnp.bfloat16)
    down_grad = row_product(activated_low, grad_down_low)
    grad_gate = gelu_back(back_product(grad_down_low, down_projection_weight))[0].astype(
        jnp.bfloat16
    )
    up_grad = row_product(normed_two_low, grad_gate)
    grad_middle_norm, mlp_gain_grad = norm_two_back(
        back_product(grad_gate, up_projection_weight).reshape(present_slots, local_len, width)
    )
    grad_middle = final_gradient + grad_middle_norm
    grad_branch_low = grad_middle.reshape(total_rows, width).astype(jnp.bfloat16)
    out_grad = row_product(attended_low, grad_branch_low)
    grad_attended = (
        back_product(grad_branch_low, attention_output_weight)
        .astype(jnp.bfloat16)
        .reshape(present_slots, local_len, H, DH)
    )
    row_delta = jnp.transpose(
        jnp.sum(grad_attended.astype(jnp.float32) * attended, axis=-1), (0, 2, 1)
    )

    def key_terms(key_block, value_block, mask_block):
        attention_scores = masked_scores(queries, key_block, mask_block, scale_factor)
        probability = jnp.exp(attention_scores - log_total[..., None])
        grad_probs = jnp.einsum(
            "sqhd,skhd->shqk", grad_attended, value_block, preferred_element_type=jnp.float32
        )
        grad_scores = (probability * (grad_probs - row_delta[..., None])).astype(jnp.bfloat16)
        query_add = (
            jnp.einsum(
                "shqk,skhd->sqhd", grad_scores, key_block, preferred_element_type=jnp.float32
            )
            * scale_factor
        )
        key_add = (
            jnp.einsum("shqk,sqhd->skhd", grad_scores, queries, preferred_element_type=jnp.float32)
            * scale_factor
        )
        value_add = jnp.einsum(
            "shqk,sqhd->skhd",
            probability.astype(jnp.bfloat16),
            grad_attended,
            preferred_element_type=jnp.float32,
        )
        block_len = key_block.shape[1]
        return (
            query_add,
            key_add.reshape(present_slots, block_len, width),
            value_add.reshape(present_slots, block_len, width),
        )

    cycle_len = lax.axis_size("seq")
    query_zeros = jnp.zeros((present_slots, local_len, H, DH), jnp.float32)

    def visit(visit_index, loop_state):
        grad_queries, visiting, carried = loop_state
        query_add, key_add, value_add = key_terms(
            visiting[0].reshape(present_slots, local_len, H, DH),
            visiting[1].reshape(present_slots, local_len, H, DH),
            visiting[2],
        )
        carried = (carried[0] + key_add, carried[1] + value_add)
        visiting = from_behind((visiting[0], visiting[1], visiting[2]), "seq", 1)
        carried = (
            from_behind(carried[0].astype(jnp.bfloat16), "seq", 1).astype(jnp.float32),
            from_behind(carried[1].astype(jnp.bfloat16), "seq", 1).astype(jnp.float32),
        )
        return (grad_queries + query_add, tuple(visiting), tuple(carried))

    zeros_kv = jnp.zeros((present_slots, local_len, width), jnp.float32)
    grad_queries, visiting, carried = lax.fori_loop(
        0,
        cycle_len,
        visit,
        (query_zeros, (key_rows, value_rows, key_valid_mask), (zeros_kv, zeros_kv)),
    )
    grad_keys, grad_values = carried
    grad_packed = (
        jnp.concatenate(
            [grad_queries.reshape(present_slots, local_len, width), grad_keys, grad_values], axis=-1
        )
        .astype(jnp.bfloat16)
        .reshape(total_rows, 3 * width)
    )
    qkv_grad = row_product(normed_low, grad_packed)
    query_key_grad = qkv_grad[:, : 2 * width]
    value_grad = qkv_grad[:, 2 * width :]
    grad_start_norm, attn_gain_grad = norm_back(
        back_product(grad_packed, query_key_value_weight).reshape(present_slots, local_len, width)
    )
    grad_start = grad_middle + grad_start_norm
    inner_grad, outer_grad = time_back(jnp.sum(grad_start, axis=1))
    shares = (
        lax.psum_scatter(
            inner_grad.astype(jnp.bfloat16), "batch", scatter_dimension=1, tiled=True
        ).astype(jnp.float32),
        lax.psum_scatter(
            outer_grad.astype(jnp.bfloat16), "batch", scatter_dimension=1, tiled=True
        ).astype(jnp.float32),
        lax.psum_scatter(
            attn_gain_grad[None, :].astype(jnp.bfloat16), "batch", scatter_dimension=1, tiled=True
        ).astype(jnp.float32),
        lax.psum_scatter(
            query_key_grad.astype(jnp.bfloat16), "batch", scatter_dimension=1, tiled=True
        ).astype(jnp.float32),
        lax.psum_scatter(
            value_grad.astype(jnp.bfloat16), "batch", scatter_dimension=1, tiled=True
        ).astype(jnp.float32),
        lax.psum_scatter(
            out_grad.astype(jnp.bfloat16), "batch", scatter_dimension=1, tiled=True
        ).astype(jnp.float32),
        lax.psum_scatter(
            mlp_gain_grad[None, :].astype(jnp.bfloat16), "batch", scatter_dimension=1, tiled=True
        ).astype(jnp.float32),
        lax.psum_scatter(
            up_grad.astype(jnp.bfloat16), "batch", scatter_dimension=1, tiled=True
        ).astype(jnp.float32),
        lax.psum_scatter(
            down_grad.astype(jnp.bfloat16), "batch", scatter_dimension=1, tiled=True
        ).astype(jnp.float32),
    )
    summed = tuple(
        jax.tree.map(
            lambda part: part.astype(jnp.float32), lax.psum(shortened(tuple(shares)), "seq")
        )
    )
    return (
        output,
        grad_start,
        summed[0],
        summed[1],
        summed[2][0],
        summed[3],
        summed[4],
        summed[5],
        summed[6][0],
        summed[7],
        summed[8],
    )


BF = jnp.bfloat16
F32 = jnp.float32
MASKED = -1e9
GELU_A = 0.7978845608028654
GELU_B = 0.044715
VMEM_LIMIT = 62 * 2**20


def mm(left, right, left_dim, right_dim):
    return lax.dot_general(
        left, right, (((left_dim,), (right_dim,)), ((), ())), preferred_element_type=F32
    )


def attend_kernel(
    counts_ref, steps_ref, x_hbm, mask_hbm, cot_hbm, w1_ref, w2_ref, gain_ref, w_ref,
    o_ref, exact_ref, inv_ref, even_ref, odd_ref, live_ref, temb_ref, emb_ref, u_ref,
    q_hbm, kv_hbm, n1_hbm, xs_hbm, dm_hbm,
    xs, n1, q, kv, dm, mask, mask_far, bias, live, sems, send, receive,
    keys, query, v_even, v_odd, s_even, s_odd, m_even, m_odd,
):
    step = pl.program_id(0)
    last = pl.num_programs(0) - 1
    piece, width = xs.shape[0] // 4, xs.shape[1]
    length = 2 * piece
    lane = lax.broadcasted_iota(jnp.int32, (1, 128), 1)
    now = jnp.minimum(step, last - 1)
    before = jnp.maximum(step - 1, 0)
    me, seq = lax.axis_index("batch"), lax.axis_index("seq")
    blocks = [pl.ds(piece * i, piece) for i in range(4)]

    def to_partner(k, source, target):
        return pltpu.make_async_remote_copy(
            src_ref=source,
            dst_ref=target,
            send_sem=send.at[k],
            recv_sem=receive.at[k],
            device_id=(me, 1 - seq),
            device_id_type=pl.DeviceIdType.MESH,
        )

    x_one = to_partner(0, x_hbm.at[1 - seq], xs.at[blocks[1]])
    x_two = to_partner(1, x_hbm.at[2], xs.at[blocks[3]])
    cot_one = to_partner(2, cot_hbm.at[1 - seq], dm.at[blocks[1]])
    mask_there = to_partner(3, mask_hbm, mask_far)
    own = [
        pltpu.make_async_copy(x_hbm.at[seq], xs.at[blocks[0]], sems.at[0]),
        pltpu.make_async_copy(x_hbm.at[2], xs.at[blocks[2]], sems.at[1]),
        pltpu.make_async_copy(mask_hbm, mask, sems.at[2]),
        pltpu.make_async_copy(cot_hbm.at[seq], dm.at[blocks[0]], sems.at[3]),
        pltpu.make_async_copy(cot_hbm.at[2], dm.at[blocks[2]], sems.at[4]),
    ]
    keep_early = [
        pltpu.make_async_copy(q, q_hbm, sems.at[5]),
    ]
    keep_late = [
        pltpu.make_async_copy(kv, kv_hbm, sems.at[6]),
        pltpu.make_async_copy(n1, n1_hbm, sems.at[7]),
        pltpu.make_async_copy(xs, xs_hbm, sems.at[8]),
    ]
    keep_dm = pltpu.make_async_copy(dm, dm_hbm, sems.at[9])

    def project(i, with_queries):
        part = blocks[i]
        h = xs[part, :].astype(F32) + temb_ref[i // 2 : i // 2 + 1, :]
        centered = h - jnp.mean(h, axis=1, keepdims=True)
        variance = jnp.mean(centered * centered, axis=1, keepdims=True)
        normed = (centered * lax.rsqrt(variance + 1e-5) * gain_ref[...]).astype(BF)
        n1[part, :] = normed
        if with_queries:
            q[part, :] = (mm(normed, w_ref[:, :width], 1, 0) * 0.125).astype(BF)
        kv[part, :] = mm(normed, w_ref[:, width:], 1, 0).astype(BF)

    def lives(ref):
        rows = lax.broadcasted_iota(jnp.int32, (8, piece), 0)
        held = jnp.concatenate([ref[...], jnp.zeros((5, piece), jnp.int32)], axis=0)
        flags = jnp.where((held == 1) & (rows < counts_ref[0]), 1.0, 0.0)
        return flags.T

    def set_live(i, column):
        live[blocks[i], :] = jnp.broadcast_to(column, (piece, 128)).astype(BF)
        masked = jnp.where(lane == 0, MASKED, 0.0)
        bias[blocks[i], :] = jnp.where(column > 0.5, 0.0, masked).astype(BF)

    def mine(columns):
        return jnp.where(seq == 0, columns[:, 0:1], columns[:, 1:2])

    @pl.when(step == 0)
    def _():
        for copy in own:
            copy.start()
        greet_x()
        mask_there.start()
        x_one.start()
        row = lax.broadcasted_iota(jnp.int32, (8, 1), 0)
        times = jnp.where(
            row == 0, steps_ref[0], jnp.where(row == 1, steps_ref[1], steps_ref[2])
        ).astype(F32)
        half_width = TCH // 2
        column = lax.broadcasted_iota(jnp.int32, (1, TCH), 1)
        index = jnp.where(column < half_width, column, column - half_width).astype(F32)
        angles = times * jnp.exp(-math.log(10000.0) * index / half_width)
        emb = jnp.where(column < half_width, jnp.cos(angles), jnp.sin(angles))
        emb = jnp.where(row < 3, emb, 0.0)

        def exact_product(left, right):
            return lax.dot_general(
                left, right.astype(F32), (((1,), (0,)), ((), ())),
                precision=TOP_PRECISION, preferred_element_type=F32,
            )

        u = exact_product(emb, w1_ref[...])
        temb = exact_product(u / (1.0 + jnp.exp(-u)), w2_ref[...])
        emb_ref[...] = emb
        u_ref[...] = u
        temb_ref[0:1, :] = jnp.where(seq == 0, temb[0:1], temb[1:2])
        temb_ref[1:2, :] = temb[2:3]
        temb_ref[2:8, :] = jnp.zeros((6, width), F32)
        for copy in own[:3]:
            copy.wait()
        columns = lives(mask)
        set_live(0, mine(columns))
        set_live(2, columns[:, 2:3])
        project(0, True)
        project(2, True)
        for copy in own[3:]:
            copy.wait()
        dm[blocks[0], :] *= live[blocks[0], 0:1]
        dm[blocks[2], :] *= live[blocks[2], 0:1]
        mask_there.wait()
        columns = lives(mask_far)
        set_live(1, mine(columns))
        set_live(3, columns[:, 2:3])
        live_ref[...] = live[pl.ds(0, 3 * piece), :]
        x_one.wait()
        x_two.start()
        project(1, True)
        for copy in keep_early:
            copy.start()

    @pl.when(step == 8)
    def _():
        x_two.wait()
        cot_one.start()
        project(3, False)
        for copy in keep_late:
            copy.start()

    @pl.when(step == last)
    def _():
        cot_one.wait()
        dm[blocks[1], :] *= live[blocks[1], 0:1]
        keep_dm.start()

    query_rows = pl.ds(pl.multiple_of((now // 6) * piece, piece), piece)
    key_rows = pl.ds(pl.multiple_of((now // 12) * length, length), length)
    pair_lanes = pl.ds(pl.multiple_of((now % 6) * 128, 128), 128)
    value_lanes = pl.ds(pl.multiple_of(width + (now % 6) * 128, 128), 128)

    @pl.when(step % 6 == 0)
    def _():
        keys[:, 128:] = bias[key_rows, :]
        query[:, 128:] = jnp.where(
            lax.broadcasted_iota(jnp.int32, (piece, 128), 1) == 0, 1.0, 0.0
        ).astype(BF)
        v_even[64:, :] = jnp.ones((16, length), BF)
        v_odd[64:, :] = jnp.ones((16, length), BF)

    keys[:, :128] = kv[key_rows, pair_lanes]

    def half(head, made, made_max, used, used_max, values, at, out_ref):
        query[:, :128] = jnp.where((lane // 64) == head, q[query_rows, pair_lanes], jnp.zeros((), BF))
        top = used_max[0:1, :]
        scores = mm(keys[...], query[...], 1, 1)
        weight = jnp.exp(used[...] - top).astype(BF)
        made[...] = scores
        made_max[...] = jnp.broadcast_to(jnp.max(scores, axis=0, keepdims=True), made_max.shape)
        out_ref[0] = weight
        total = mm(values[...], weight, 1, 0)
        inverse = 1.0 / total[64:65]
        place = pl.ds(pl.multiple_of((at // 6) * piece, piece), piece)
        which = 2 * (at % 6) + 1 - head
        exact = total[:64] * inverse
        o_ref[which, :, place] = exact.astype(BF)
        exact_ref[which, :, place] = exact
        inv_ref[which, :, place] = jnp.broadcast_to(inverse, (8, piece))

    half(0, s_even, m_even, s_odd, m_odd, v_odd, before, odd_ref)
    turned = kv[key_rows, value_lanes].T
    v_even[:64, :] = turned[:64]
    v_odd[:64, :] = turned[64:]
    half(1, s_odd, m_odd, s_even, m_even, v_even, now, even_ref)

    @pl.when(step == last)
    def _():
        for copy in keep_early + keep_late + [keep_dm]:
            copy.wait()


def greet_x():
    partner = (lax.axis_index("batch"), 1 - lax.axis_index("seq"))
    barrier = pltpu.get_barrier_semaphore()
    pl.semaphore_signal(barrier, inc=1, device_id=partner, device_id_type=pl.DeviceIdType.MESH)
    pl.semaphore_wait(barrier, 1)


def attend(counts, timesteps, x, mask, cot, w1, w2, gain, w):
    _, piece, width = x.shape
    length = 2 * piece
    rows = 3 * piece
    steps = 18
    hidden = w1.shape[1]
    whole = pl.BlockSpec(memory_space=pltpu.VMEM)
    scalars = pl.BlockSpec(memory_space=pltpu.SMEM)
    anywhere = pl.BlockSpec(memory_space=pl.ANY)
    return pl.pallas_call(
        attend_kernel,
        grid=(steps + 1,),
        in_specs=[scalars] * 2 + [anywhere] * 3 + [whole] * 4,
        out_specs=[
            whole,
            whole,
            whole,
            pl.BlockSpec((1, length, piece), lambda t: (jnp.minimum(t, steps - 1), 0, 0)),
            pl.BlockSpec((1, length, piece), lambda t: (jnp.maximum(t - 1, 0), 0, 0)),
        ]
        + [whole] * 4
        + [anywhere] * 5,
        out_shape=[
            jax.ShapeDtypeStruct((H, DH, rows), BF),
            jax.ShapeDtypeStruct((H, DH, rows), F32),
            jax.ShapeDtypeStruct((H, 8, rows), F32),
            jax.ShapeDtypeStruct((steps, length, piece), BF),
            jax.ShapeDtypeStruct((steps, length, piece), BF),
            jax.ShapeDtypeStruct((rows, 128), BF),
            jax.ShapeDtypeStruct((8, width), F32),
            jax.ShapeDtypeStruct((8, TCH), F32),
            jax.ShapeDtypeStruct((8, hidden), F32),
            jax.ShapeDtypeStruct((rows, width), BF),
            jax.ShapeDtypeStruct((4 * piece, 2 * width), BF),
            jax.ShapeDtypeStruct((4 * piece, width), BF),
            jax.ShapeDtypeStruct((4 * piece, width), BF),
            jax.ShapeDtypeStruct((rows, width), BF),
        ],
        scratch_shapes=[
            pltpu.VMEM((4 * piece, width), BF),
            pltpu.VMEM((4 * piece, width), BF),
            pltpu.VMEM((rows, width), BF),
            pltpu.VMEM((4 * piece, 2 * width), BF),
            pltpu.VMEM((rows, width), BF),
            pltpu.VMEM((3, piece), jnp.int32),
            pltpu.VMEM((3, piece), jnp.int32),
            pltpu.VMEM((4 * piece, 128), BF),
            pltpu.VMEM((4 * piece, 128), BF),
            pltpu.SemaphoreType.DMA((10,)),
            pltpu.SemaphoreType.DMA((4,)),
            pltpu.SemaphoreType.DMA((4,)),
            pltpu.VMEM((length, 256), BF),
            pltpu.VMEM((piece, 256), BF),
            pltpu.VMEM((80, length), BF),
            pltpu.VMEM((80, length), BF),
            pltpu.VMEM((length, piece), F32),
            pltpu.VMEM((length, piece), F32),
            pltpu.VMEM((8, piece), F32),
            pltpu.VMEM((8, piece), F32),
        ],
        compiler_params=pltpu.CompilerParams(
            vmem_limit_bytes=VMEM_LIMIT, collective_id=4, has_side_effects=True
        ),
        cost_estimate=pl.CostEstimate(flops=20 * 10**9, bytes_accessed=60 * 10**6, transcendentals=19 * 10**6),
    )(counts, timesteps, x, mask, cot, w1, w2, gain, w)


def place_of(pair):
    return 4 * (pair & 1) + 2 * (pair >> 1 & 1) + (pair >> 2)


class Shares:
    def __init__(self, source, scratch, x_second):
        self.source = source
        self.x_second = x_second
        self.names = ["core", "rows", "y", "z", "join", "out"] if x_second else ["core", "y", "z", "x", "out"]
        self.acc, self.final, self.send, self.receive = scratch[0], scratch[1], scratch[-2], scratch[-1]
        boxes = [name for name in self.names if name not in ("join", "out")]
        self.inbox = dict(zip(boxes, scratch[2:-2]))
        me, far = lax.axis_index("batch"), lax.axis_index("seq")
        self.core, self.y, self.z0, self.z1 = [(me >> bit) & 1 for bit in range(4)]
        self.me, self.far = me, far
        self.half = self.acc.shape[2]
        rows = self.acc.shape[1]
        self.rows = slice(0, rows)
        if x_second:
            self.rows = pl.ds(pl.multiple_of(far * (rows // 2), 16), rows // 2)
            self.other_rows = pl.ds(pl.multiple_of((1 - far) * (rows // 2), 16), rows // 2)
        self.own = 4 * self.y + 2 * self.z0 + self.z1

    def partner(self, name):
        if name in ("x", "rows", "join"):
            return (self.me, 1 - self.far)
        return (self.me ^ {"core": 1, "y": 2, "out": 1}[name], self.far)

    def ends(self, name):
        acc, rows = self.acc, self.rows
        if name == "core":
            away = pl.multiple_of((1 - self.core) * self.half, 128)
            return self.source.at[:, :, pl.ds(away, self.half)], self.inbox[name]
        if name == "rows":
            return acc.at[:, self.other_rows], self.inbox[name]
        if name == "y":
            return acc.at[pl.ds(4 * (1 - self.y), 4), rows], self.inbox[name]
        if name == "x":
            return acc.at[self.own], self.inbox[name]
        if name == "join":
            return self.final.at[self.core, rows], self.final.at[self.core, rows]
        return self.final.at[self.core], self.final.at[self.core]

    def copies(self, stage):
        name = self.names[stage]
        if name != "z":
            here, there = self.ends(name)
            return [self.remote(stage, here, there, self.partner(name))]
        made = []
        for k in range(3):
            flip0, flip1 = (k + 1) & 1, (k + 1) >> 1
            z0 = 1 - self.z0 if flip0 else self.z0
            z1 = 1 - self.z1 if flip1 else self.z1
            here = self.acc.at[4 * self.y + 2 * z0 + z1, self.rows]
            other = (self.me ^ (4 * flip0 + 8 * flip1), self.far)
            made.append(self.remote(stage if k == 0 else 7 + k, here, self.inbox[name].at[k], other))
        return made

    def remote(self, which, here, there, other):
        return pltpu.make_async_remote_copy(
            src_ref=here,
            dst_ref=there,
            send_sem=self.send.at[which],
            recv_sem=self.receive.at[which],
            device_id=other,
            device_id_type=pl.DeviceIdType.MESH,
        )

    def start(self, stage):
        for copy in self.copies(stage):
            copy.start()

    def load(self):
        mine = pl.multiple_of(self.core * self.half, 128)
        return pltpu.make_async_copy(
            self.source.at[:, :, pl.ds(mine, self.half)], self.acc, self.send.at[7]
        )

    def begin(self):
        self.start(0)
        self.load().start()

    def add(self, name):
        acc, rows = self.acc, self.rows

        def total(one, other):
            return one + other

        if name in ("core", "rows", "y"):
            first, count = {"core": (0, 8), "rows": (0, 8), "y": (4 * self.y, 4)}[name]
            if name == "core":
                rows = slice(None)
            for k in range(count):
                acc[first + k, rows] = total(acc[first + k, rows], self.inbox[name][k])
        elif name == "z":
            parts = [acc[self.own, rows]] + [self.inbox[name][k] for k in range(3)]
            parts = [part.astype(F32) for part in parts]
            summed = ((parts[0] + parts[1]) + (parts[2] + parts[3])).astype(BF)
            if self.x_second:
                self.final[self.core, rows] = summed
            else:
                acc[self.own] = summed
        elif name == "x":
            self.final[self.core] = total(acc[self.own], self.inbox[name][...])

    def end(self, stage):
        if stage == 0:
            self.load().wait()
        for copy in self.copies(stage):
            copy.wait()
        self.add(self.names[stage])

    def go_on(self, stage):
        self.end(stage)
        if stage + 1 < len(self.names):
            self.start(stage + 1)

    def fetch(self):
        return pltpu.make_async_copy(self.source, self.acc, self.send.at[7])

    def resume(self, stage):
        self.fetch().wait()
        self.start(stage)


def share_scratch(rows, columns, x_second):
    half = columns // 2
    part = rows // 2 if x_second else rows
    shapes = [(8, rows, half), (2, rows, half), (8, rows, half)]
    shapes += [(8, part, half)] if x_second else []
    shapes += [(4, part, half), (3, part, half)]
    shapes += [] if x_second else [(rows, half)]
    return [pltpu.VMEM(shape, BF) for shape in shapes] + [
        pltpu.SemaphoreType.DMA((10,)),
        pltpu.SemaphoreType.DMA((10,)),
    ]


SCRATCH_COUNT = 8


def greet():
    me, far = lax.axis_index("batch"), lax.axis_index("seq")
    barrier = pltpu.get_barrier_semaphore()
    others = [(me ^ 1, far), (me ^ 2, far), (me ^ 4, far), (me ^ 8, far), (me ^ 12, far), (me, 1 - far)]
    for other in others:
        pl.semaphore_signal(barrier, inc=1, device_id=other, device_id_type=pl.DeviceIdType.MESH)
    pl.semaphore_wait(barrier, len(others))


def attend_back_kernel(
    plan, table, q_ref, k_ref, v_ref, do_ref, o_ref, inv_ref, even_ref, odd_ref, *rest
):
    count = len(plan)
    w_ref, out_hbm, *rest = rest
    sources, rest = rest[:count], rest[count:]
    width = w_ref.shape[0]
    (dq_ref, dk_ref, dv_ref, far_ref, output_hbm), rest = rest[:5], rest[5:]
    finals, rest = rest[:count], rest[count:]
    values, gradient, dk_sum, dv_sum, far_kv, far_send, far_got, out_got, far_sems, *rest = rest
    shares = []
    for i in range(count):
        own = rest[SCRATCH_COUNT * i : SCRATCH_COUNT * (i + 1)]
        shares.append(Shares(sources[i], own, plan[i]))
    step = pl.program_id(0)
    steps = pl.num_programs(0)
    pair, part = back_place(step)
    piece, length = q_ref.shape[0], k_ref.shape[0]
    lane = lax.broadcasted_iota(jnp.int32, (1, 128), 1)
    zero = jnp.zeros((), BF)
    far_copy = pltpu.make_async_remote_copy(
        src_ref=far_send,
        dst_ref=far_got,
        send_sem=far_sems.at[0],
        recv_sem=far_sems.at[1],
        device_id=(lax.axis_index("batch"), 1 - lax.axis_index("seq")),
        device_id_type=pl.DeviceIdType.MESH,
    )

    seq = lax.axis_index("seq")
    out_copy = pltpu.make_async_remote_copy(
        src_ref=out_hbm.at[pl.ds(piece, piece)],
        dst_ref=out_got,
        send_sem=far_sems.at[2],
        recv_sem=far_sems.at[3],
        device_id=(lax.axis_index("batch"), 1 - seq),
        device_id_type=pl.DeviceIdType.MESH,
    )
    returned = pltpu.make_async_copy(out_got, output_hbm, far_sems.at[4])

    @pl.when(step == 0)
    def _():
        for share in shares[:2]:
            share.fetch().start()
        greet()
        for share in shares[:2]:
            share.resume(2)
        for share in shares[2:]:
            share.begin()
        out_copy.start()
        values[:, 128:] = jnp.where(
            lax.broadcasted_iota(jnp.int32, (length, 128), 1) < 3, 1.0, 0.0
        ).astype(BF)
        gradient[...] = jnp.zeros_like(gradient)
        dk_sum[...] = jnp.zeros_like(dk_sum)
        dv_sum[...] = jnp.zeros_like(dv_sum)

    for when in sorted(table):
        if when < 18:

            @pl.when(step == when)
            def _(when=when):
                for i, stage in table[when]:
                    shares[i].go_on(stage)

    @pl.when(step == 11)
    def _():
        out_copy.wait()
        returned.start()

    @pl.when(step == 6)
    def _():
        far_send[...] = mm(far_kv[:, : 2 * width], w_ref[:, width:], 1, 1).astype(BF)
        far_copy.start()

    values[:, :128] = v_ref[...]
    inverse = jnp.concatenate(
        [jnp.broadcast_to(inv_ref[head, 0:1, :], (DH, piece)) for head in range(2)], axis=0
    )
    scaled = (do_ref[...].astype(F32) * inverse).astype(BF)
    product = scaled.astype(F32) * o_ref[...]
    for head in range(2):
        mine = slice(DH * head, DH * head + DH)
        place = slice(piece * head, piece * head + piece)
        delta = -jnp.sum(product[mine], axis=0, keepdims=True)
        high = delta.astype(BF).astype(F32)
        rest_of = delta - high
        middle = rest_of.astype(BF).astype(F32)
        gradient[mine, place] = scaled[mine]
        gradient[128:144, place] = jnp.concatenate(
            [high, middle, rest_of - middle, jnp.zeros((13, piece), F32)], axis=0
        ).astype(BF)
    dp = mm(values[...], gradient[...], 1, 0)
    turned_keys = k_ref[...].T
    natural = scaled.T
    weights = [even_ref[0], odd_ref[0]]
    ds = [
        (weights[head].astype(F32) * dp[:, piece * head : piece * head + piece]).astype(BF)
        for head in range(2)
    ]

    def apart(array):
        return jnp.concatenate(
            [jnp.where(lane < 64, array, zero), jnp.where(lane < 64, zero, array)], axis=0
        )

    dv = mm(jnp.concatenate(weights, axis=1), apart(natural), 1, 0)
    dk = mm(jnp.concatenate(ds, axis=1), apart(q_ref[...]), 1, 0)
    for head in range(2):
        mine = slice(DH * head, DH * head + DH)
        dq_ref[mine, :] = (mm(turned_keys[mine], ds[head], 1, 0) * 0.125).astype(BF)

    again = part == 1
    dk += jnp.where(again, dk_sum[...], 0.0)
    dv += jnp.where(again, dv_sum[...], 0.0)
    dk_sum[...] = dk
    dv_sum[...] = dv
    dk, dv = dk.astype(BF), dv.astype(BF)
    dk_ref[...] = dk
    dv_ref[...] = dv
    early = step < 6
    at = jnp.where(early, pair * 128, 2 * width)
    far_kv[:, pl.ds(pl.multiple_of(at, 128), 128)] = dk[piece:]
    at = jnp.where(early, width + pair * 128, 2 * width + 128)
    far_kv[:, pl.ds(pl.multiple_of(at, 128), 128)] = dv[piece:]

    @pl.when(step == steps - 1)
    def _():
        for when in sorted(table):
            if when >= 18:
                for i, stage in table[when]:
                    shares[i].go_on(stage)
        for i in range(count):
            finals[i][...] = shares[i].final[...]
        far_copy.wait()
        far_ref[...] = far_got[...]
        returned.wait()


def back_place(step):
    late = jnp.maximum(step - 6, 0)
    return jnp.where(step < 6, step, late // 2), jnp.where(step < 6, 2, late % 2)


def attend_back(q, kv, do, o, inv, even, odd, w, out, partials, plan, table):
    rows, width = q.shape
    length = 2 * rows // 3
    piece = rows // 3

    def spec(shape, index):
        return pl.BlockSpec(shape, lambda t: index(*back_place(t)))

    weight_spec = spec((1, length, piece), lambda p, j: (j * 6 + p, 0, 0))
    scratch = []
    sizes = [(a.shape[1], a.shape[2] * (2 if i < 2 else 1)) for i, a in enumerate(partials)]
    for size, x_second in zip(sizes, plan):
        scratch += share_scratch(*size, x_second)
    whole = pl.BlockSpec(memory_space=pltpu.VMEM)
    return pl.pallas_call(
        partial(attend_back_kernel, plan, table),
        grid=(18,),
        in_specs=[
            spec((piece, 128), lambda p, j: (j, p)),
            spec((length, 128), lambda p, j: (j // 2, p)),
            spec((length, 128), lambda p, j: (j // 2, 6 + p)),
            spec((128, piece), lambda p, j: (p, j)),
            spec((128, piece), lambda p, j: (p, j)),
            spec((2, 8, piece), lambda p, j: (p, 0, j)),
            weight_spec,
            weight_spec,
            whole,
        ]
        + [pl.BlockSpec(memory_space=pl.ANY)] * (1 + len(partials)),
        out_specs=[
            spec((128, piece), lambda p, j: (p, j)),
            spec((length, 128), lambda p, j: (j // 2, p)),
            spec((length, 128), lambda p, j: (j // 2, p)),
            whole,
            pl.BlockSpec(memory_space=pl.ANY),
        ]
        + [whole] * len(partials),
        out_shape=[
            jax.ShapeDtypeStruct((width, rows), BF),
            jax.ShapeDtypeStruct((2 * length, width), BF),
            jax.ShapeDtypeStruct((2 * length, width), BF),
            jax.ShapeDtypeStruct((piece, width), BF),
            jax.ShapeDtypeStruct((piece, width), BF),
        ]
        + [jax.ShapeDtypeStruct((2, a, b // 2), BF) for a, b in sizes],
        scratch_shapes=[
            pltpu.VMEM((length, 256), BF),
            pltpu.VMEM((256, 2 * piece), BF),
            pltpu.VMEM((length, 128), F32),
            pltpu.VMEM((length, 128), F32),
            pltpu.VMEM((piece, 2 * width + 256), BF),
            pltpu.VMEM((piece, width), BF),
            pltpu.VMEM((piece, width), BF),
            pltpu.VMEM((piece, width), BF),
            pltpu.SemaphoreType.DMA((5,)),
        ]
        + scratch,
        compiler_params=pltpu.CompilerParams(
            vmem_limit_bytes=VMEM_LIMIT, collective_id=1, has_side_effects=True
        ),
        cost_estimate=pl.CostEstimate(flops=30 * 10**9, bytes_accessed=60 * 10**6, transcendentals=0),
    )(q, kv, kv, do, o, inv, even, odd, w, out, *partials)


def finish_kernel(
    dq_hbm, dk_hbm, dv_hbm, n1_hbm, x_hbm, dh_hbm, w_hbm, far_ref, temb_ref, gain_ref, dgain2_ref,
    w2_ref, emb_ref, u_ref, *rest
):
    own_ref, far_out_ref, finals, rest = rest[0], rest[1], rest[2:7], rest[7:]
    dq, dk, dv, n1, x, dh, w, send, got, sems, far_sems = rest[:11]
    sources, rest = rest[11:16], rest[16:]
    shares = []
    for i in range(5):
        own = rest[SCRATCH_COUNT * i : SCRATCH_COUNT * (i + 1)]
        shares.append(Shares(sources[i], own, FINISH_PLAN[i]))
    half, width = far_ref.shape
    me, seq = lax.axis_index("batch"), lax.axis_index("seq")

    loads = {}

    def fetch(name, source, target):
        loads[name] = pltpu.make_async_copy(source, target, sems.at[len(loads)])
        loads[name].start()

    blocks = [slice(half * i, half * i + half) for i in range(4)]
    fetch("w", w_hbm, w)
    for b in (1, 0, 2):
        fetch(("dq", b), dq_hbm.at[:, blocks[b]], dq.at[:, blocks[b]])
        fetch(("dk", b), dk_hbm.at[blocks[b]], dk.at[blocks[b]])
        fetch(("dv", b), dv_hbm.at[blocks[b]], dv.at[blocks[b]])
        if b == 1:
            fetch("x", x_hbm.at[pl.ds(0, 3 * half)], x)
            fetch(("dh", 1), dh_hbm.at[blocks[1]], dh.at[blocks[1]])
    fetch(("dk", 3), dk_hbm.at[blocks[3]], dk.at[blocks[3]])
    fetch(("dv", 3), dv_hbm.at[blocks[3]], dv.at[blocks[3]])
    fetch("n1", n1_hbm, n1)
    fetch(("dh", 0), dh_hbm.at[blocks[0]], dh.at[blocks[0]])
    fetch(("dh", 2), dh_hbm.at[blocks[2]], dh.at[blocks[2]])
    back_copy = pltpu.make_async_remote_copy(
        src_ref=send,
        dst_ref=got,
        send_sem=far_sems.at[0],
        recv_sem=far_sems.at[1],
        device_id=(me, 1 - seq),
        device_id_type=pl.DeviceIdType.MESH,
    )
    greet()

    def norm_back(b, more):
        loads[("dh", b)].wait()
        part = blocks[b]
        dn = mm(dq[:, part], w[:, :width], 0, 1)
        dn += mm(dk[part, :], w[:, width : 2 * width], 1, 1)
        dn += mm(dv[part, :], w[:, 2 * width :], 1, 1)
        if more is not None:
            dn += more[...].astype(F32)
        h = x[part, :].astype(F32) + temb_ref[b // 2 : b // 2 + 1, :]
        centered = h - jnp.mean(h, axis=1, keepdims=True)
        r1 = lax.rsqrt(jnp.mean(centered * centered, axis=1, keepdims=True) + 1e-5)
        x1 = centered * r1
        e = dn * gain_ref[...]
        dh0 = dh[part, :] + r1 * (
            e - jnp.mean(e, axis=1, keepdims=True) - x1 * jnp.mean(e * x1, axis=1, keepdims=True)
        )
        return dh0, jnp.sum(dh0, axis=0, keepdims=True), jnp.sum(dn * x1, axis=0, keepdims=True)

    def weight_piece(f):
        columns = slice(256 * f, 256 * f + 256)
        q_part = mm(dq[...], n1[: 3 * half, columns], 1, 0).astype(BF)
        k_part = mm(dk[...], n1[:, columns], 0, 0).astype(BF)
        v_part = mm(dv[...], n1[:, columns], 0, 0).astype(BF)
        pair_rows = width // 4
        for k in range(8):
            source = q_part if k < 4 else k_part
            first = pair_rows * (k % 4)
            sources[f][place_of(k), :pair_rows, :] = source[first : first + pair_rows]
            first = width // 8 * k
            sources[f][place_of(k), pair_rows:, :] = v_part[first : first + width // 8]
        shares[f].begin()

    for name in loads:
        if name[0] != "dh":
            loads[name].wait()
    weight_piece(0)
    weight_piece(1)
    shares[0].go_on(0)
    weight_piece(2)
    shares[1].go_on(0)
    dh0, dtemb_a, dgain_a = norm_back(1, None)
    send[...] = dh0.astype(BF)
    back_copy.start()
    shares[2].go_on(0)
    dh0, dtemb_b, dgain_b = norm_back(0, None)
    own_ref[0] = dh0
    shares[0].go_on(1)
    dh0, dtemb_two, dgain_c = norm_back(2, far_ref)
    own_ref[1] = dh0

    dtemb_one = dtemb_a + dtemb_b
    first = (seq == 0).astype(F32)
    dtemb = jnp.concatenate(
        [first * dtemb_one, (1.0 - first) * dtemb_one, dtemb_two, jnp.zeros((5, width), F32)], axis=0
    )
    u = u_ref[...]
    sigmoid = 1.0 / (1.0 + jnp.exp(-u))
    outer = lax.dot_general(
        dtemb, u * sigmoid, (((0,), (0,)), ((), ())), precision=TOP_PRECISION, preferred_element_type=F32
    ).astype(BF)
    dsilu = lax.dot_general(
        dtemb, w2_ref[...].astype(F32), (((1,), (1,)), ((), ())), precision=TOP_PRECISION, preferred_element_type=F32
    )
    dpre = dsilu * (sigmoid * (1.0 + u * (1.0 - sigmoid)))
    inner = lax.dot_general(
        dpre, emb_ref[...], (((0,), (0,)), ((), ())), precision=TOP_PRECISION, preferred_element_type=F32
    ).astype(BF)
    dgain = dgain_a + dgain_b + dgain_c
    size, inner_size = width // 8, inner.shape[0] // 8
    sources[4][...] = jnp.zeros_like(sources[4])
    for k in range(8):
        sources[3][place_of(k)] = outer[size * k : size * k + size]
        sources[4][place_of(k), :, :128] = inner[inner_size * k : inner_size * k + inner_size]
        both = jnp.concatenate(
            [
                jnp.concatenate([g[:, size * k : size * k + size], jnp.zeros((1, 128 - size), F32)], axis=1)
                for g in (dgain, dgain2_ref[...])
            ]
            + [jnp.zeros((14, 128), F32)],
            axis=0,
        )
        sources[4][place_of(k), :16, 128:] = both.astype(BF)
    shares[3].begin()
    shares[4].begin()
    for i, stage in FINISH_ORDER:
        shares[i].go_on(stage)
    for i in range(5):
        finals[i][...] = shares[i].final[...]
    back_copy.wait()
    far_out_ref[...] = got[...]


FINISH_PLAN = [False, True, False, False, False]
FINISH_ORDER = [
    (1, 1), (3, 0), (4, 0), (0, 2), (2, 1), (1, 2), (2, 2), (3, 1), (4, 1), (0, 3), (1, 3), (3, 2),
    (4, 2), (2, 3), (0, 4), (1, 4), (3, 3), (4, 3), (2, 4), (1, 5), (3, 4), (4, 4),
]


def finish(dq, dk, dv, n1, x, dh1, w, far, temb, gain, dgain2, w2, emb, u):
    half, width = far.shape
    rows = 3 * half
    hidden = w2.shape[0]
    whole = pl.BlockSpec(memory_space=pltpu.VMEM)
    sizes = [(3 * width // 8, 256)] * 3 + [(width // 8, hidden), (hidden // 8, 256)]
    scratch = [pltpu.VMEM((8,) + size, BF) for size in sizes]
    for size, x_second in zip(sizes, FINISH_PLAN):
        scratch += share_scratch(*size, x_second)
    return pl.pallas_call(
        finish_kernel,
        in_specs=[pl.BlockSpec(memory_space=pl.ANY)] * 7 + [whole] * 7,
        out_specs=[whole] * 7,
        out_shape=[
            jax.ShapeDtypeStruct((2, half, width), F32),
            jax.ShapeDtypeStruct((half, width), BF),
        ]
        + [jax.ShapeDtypeStruct((2, a, b // 2), BF) for a, b in sizes],
        scratch_shapes=[
            pltpu.VMEM((width, rows), BF),
            pltpu.VMEM((4 * half, width), BF),
            pltpu.VMEM((4 * half, width), BF),
            pltpu.VMEM((4 * half, width), BF),
            pltpu.VMEM((rows, width), BF),
            pltpu.VMEM((rows, width), F32),
            pltpu.VMEM(w.shape, BF),
            pltpu.VMEM((half, width), BF),
            pltpu.VMEM((half, width), BF),
            pltpu.SemaphoreType.DMA((20,)),
            pltpu.SemaphoreType.DMA((2,)),
        ]
        + scratch,
        compiler_params=pltpu.CompilerParams(
            vmem_limit_bytes=VMEM_LIMIT, collective_id=2, has_side_effects=True
        ),
        cost_estimate=pl.CostEstimate(flops=15 * 10**9, bytes_accessed=60 * 10**6, transcendentals=0),
    )(dq, dk, dv, n1, x, dh1, w, far, temb, gain, dgain2, w2, emb, u)


def gelu_and_slope(g):
    square = g * g
    half_plus = 0.5 * jnp.tanh(g * (GELU_A + GELU_A * GELU_B * square)) + 0.5
    act = g * half_plus
    slope = half_plus + act * (2.0 - 2.0 * half_plus) * (GELU_A + 3.0 * GELU_A * GELU_B * square)
    return act, slope


FF_BEGIN = {6: (0, 1), 12: (2, 3)}
FF_PLAN = [False, True, False, True]
FF_TICKS = {
    8: [(0, 0), (1, 0)],
    12: [(0, 1), (1, 1)],
    14: [(1, 2), (2, 0), (3, 0)],
    15: [(0, 2)],
    17: [(0, 3), (1, 3)],
    18: [(0, 4), (1, 4)],
    20: [(1, 5)],
    21: [(2, 1), (3, 1)],
}


def feedforward_kernel(
    x_hbm, o_ref, dm_ref, live_ref, temb_ref, gain_ref, wo_ref, *rest
):
    wu_refs, wd_refs, rest = rest[:4], rest[4:8], rest[8:]
    out_hbm, dh1_hbm, do_ref, dwu_ref, dwd_ref, dwo_ref, dgain_ref, *rest = rest
    finals, rest = rest[:4], rest[4:]
    finals, handed = finals[:2], finals[2:]
    x, h1, n2, h2, dn2, sems, *rest = rest
    sources, rest = rest[:4], rest[4:]
    shares = []
    for i in range(4):
        own = rest[SCRATCH_COUNT * i : SCRATCH_COUNT * (i + 1)]
        shares.append(Shares(sources[i], own, FF_PLAN[i]))
    turn, side = pl.program_id(0), pl.program_id(1)
    chunk, chunks = 2 * turn + side, 6
    wu = jnp.concatenate([ref[...] for ref in wu_refs], axis=1)
    wd = jnp.concatenate([ref[...] for ref in wd_refs], axis=0)
    rows, width = x.shape
    block = rows // 2
    third = rows // 3
    blocks = [slice(block * i, block * i + block) for i in range(2)]
    thirds = [slice(third * i, third * i + third) for i in range(3)]
    size = width // 8

    def act_on(now):
        for i, stage in FF_TICKS.get(now, []):
            if i >= 2 and stage == 1:
                shares[i].end(stage)
            else:
                shares[i].go_on(stage)
        for i in FF_BEGIN.get(now, []):
            shares[i].begin()

    def tick(position):
        for now in sorted(set(FF_TICKS) | set(FF_BEGIN)):
            if now < 18 and now % 3 == position:
                pl.when(chunk == now // 3)(partial(act_on, now))

    load = pltpu.make_async_copy(x_hbm.at[pl.ds(0, rows)], x, sems.at[0])

    @pl.when(chunk == 0)
    def _():
        load.start()
        greet()
        load.wait()
        for i, part in enumerate(thirds):
            h0 = x[part, :].astype(F32) + temb_ref[i // 2 : i // 2 + 1, :]
            h = h0 + mm(o_ref[:, part], wo_ref[...], 0, 0)
            h1[part, :] = h
            centered = h - jnp.mean(h, axis=1, keepdims=True)
            variance = jnp.mean(centered * centered, axis=1, keepdims=True)
            n2[part, :] = (centered * lax.rsqrt(variance + 1e-5) * gain_ref[...]).astype(BF)
            h2[part, :] = h
            dn2[part, :] = jnp.zeros_like(h)

    def first(part):
        return mm(n2[part, :], wu, 1, 0), mm(dm_ref[part, :], wd, 1, 1)

    def second(pair):
        act, slope = gelu_and_slope(pair[0])
        return act.astype(BF), (pair[1] * slope).astype(BF)

    def third_step(part, pair):
        h2[part, :] += mm(pair[0], wd, 1, 0)
        dn2[part, :] += mm(pair[1], wu, 1, 1)

    tick(0)
    a = first(blocks[0])
    b = first(blocks[1])
    a = second(a)
    b = second(b)
    tick(1)
    third_step(blocks[0], a)
    third_step(blocks[1], b)
    tick(2)
    act = jnp.concatenate([a[0], b[0]], axis=0)
    dg = jnp.concatenate([a[1], b[1]], axis=0)
    dwd = mm(dm_ref[...], act, 0, 0).astype(BF)
    dwu = mm(dg, n2[...], 0, 0).astype(BF).reshape(4, 128, width)
    for c in range(3):
        up_to, down_to = (sources[2 * c], sources[2 * c + 1]) if c < 2 else (dwu_ref, dwd_ref)

        @pl.when(turn == c)
        def _(up_to=up_to, down_to=down_to):
            up_to[pl.ds(4 * side, 4)] = dwu
            for k in range(8):
                columns = pl.ds(pl.multiple_of(512 * side, 128), 512)
                down_to[place_of(k), :, columns] = dwd[size * k : size * k + size]

    @pl.when(chunk == chunks - 1)
    def _():
        act_on(18)
        dgain = jnp.zeros_like(dgain_ref)
        for i, part in enumerate(thirds):
            h = h1[part, :]
            live = live_ref[part, 0:1].astype(F32)
            x[part, :] = (live * h2[part, :]).astype(BF)
            centered = h - jnp.mean(h, axis=1, keepdims=True)
            variance = jnp.mean(centered * centered, axis=1, keepdims=True)
            r2 = lax.rsqrt(variance + 1e-5)
            x2 = centered * r2
            dn = dn2[part, :]
            dgain += jnp.sum(dn * x2, axis=0, keepdims=True)
            e = dn * gain_ref[...]
            dh1 = dm_ref[part, :].astype(F32) + r2 * (
                e
                - jnp.mean(e, axis=1, keepdims=True)
                - x2 * jnp.mean(e * x2, axis=1, keepdims=True)
            )
            h1[part, :] = dh1
            da = dh1.astype(BF)
            n2[part, :] = da
            do_ref[:, part] = mm(wo_ref[...], da, 1, 1).astype(BF)
            act_on(19 + i)
        for i in range(2):
            finals[i][...] = shares[i].final[...]
        stores = [
            pltpu.make_async_copy(x, out_hbm, sems.at[1]),
            pltpu.make_async_copy(h1, dh1_hbm, sems.at[2]),
            pltpu.make_async_copy(shares[2].acc, handed[0], sems.at[3]),
            pltpu.make_async_copy(shares[3].acc, handed[1], sems.at[4]),
        ]
        for store in stores:
            store.start()
        dgain_ref[...] = dgain
        dwo = mm(n2[...], o_ref[...], 0, 1).astype(BF)
        for k in range(8):
            dwo_ref[place_of(k)] = dwo[size * k : size * k + size]
        for store in stores:
            store.wait()


def feedforward(x, o, dm, live, temb, gain, wo, wu, wd):
    rows, width = dm.shape
    whole = pl.BlockSpec(memory_space=pltpu.VMEM)
    anywhere = pl.BlockSpec(memory_space=pl.ANY)

    def tile(c, h, i):
        return 3 * (4 * (i % 2) + 2 * (i // 2) + h) + c

    up_specs = [pl.BlockSpec((width, 128), lambda c, h, i=i: (0, tile(c, h, i))) for i in range(4)]
    down_specs = [pl.BlockSpec((128, width), lambda c, h, i=i: (tile(c, h, i), 0)) for i in range(4)]
    sizes = [(128, width), (width // 8, 1024)] * 2
    scratch = [pltpu.VMEM((8,) + size, BF) for size in sizes]
    for size, x_second in zip(sizes, FF_PLAN):
        scratch += share_scratch(*size, x_second)
    return pl.pallas_call(
        feedforward_kernel,
        grid=(3, 2),
        in_specs=[anywhere] + [whole] * 6 + up_specs + down_specs,
        out_specs=[anywhere] * 2 + [whole] * 7 + [anywhere] * 2,
        out_shape=[
            jax.ShapeDtypeStruct((rows, width), BF),
            jax.ShapeDtypeStruct((rows, width), F32),
            jax.ShapeDtypeStruct((width, rows), BF),
            jax.ShapeDtypeStruct((8, 128, width), BF),
            jax.ShapeDtypeStruct((8, width // 8, 1024), BF),
            jax.ShapeDtypeStruct((8, width // 8, width), BF),
            jax.ShapeDtypeStruct((1, width), F32),
        ]
        + [jax.ShapeDtypeStruct((2, a, b // 2), BF) for a, b in sizes[:2]]
        + [jax.ShapeDtypeStruct((8, a, b // 2), BF) for a, b in sizes[2:]],
        scratch_shapes=[
            pltpu.VMEM((rows, width), BF),
            pltpu.VMEM((rows, width), F32),
            pltpu.VMEM((rows, width), BF),
            pltpu.VMEM((rows, width), F32),
            pltpu.VMEM((rows, width), F32),
            pltpu.SemaphoreType.DMA((5,)),
        ]
        + scratch,
        compiler_params=pltpu.CompilerParams(
            vmem_limit_bytes=VMEM_LIMIT, collective_id=3, has_side_effects=True
        ),
        cost_estimate=pl.CostEstimate(flops=48 * 10**9, bytes_accessed=50 * 10**6, transcendentals=5 * 10**6),
    )(x, o, dm, live, temb, gain, wo, *[wu] * 4, *[wd] * 4)


def pair_plan(
    inputs,
    timesteps,
    counts,
    slot_token_mask,
    time_first_weight,
    time_second_weight,
    attention_norm_gain,
    query_key_value_weight,
    attention_output_weight,
    feedforward_norm_gain,
    up_projection_weight,
    down_projection_weight,
    cotangent,
):
    slots, half, width = inputs.shape
    batches = lax.axis_size("batch")
    (o, exact, inv, even, odd, live_wide, temb, emb, u, q, kv, n1, x, dm) = attend(
        counts,
        timesteps,
        inputs,
        slot_token_mask,
        cotangent,
        time_first_weight,
        time_second_weight,
        attention_norm_gain[None, :],
        query_key_value_weight,
    )
    o = o.reshape(width, 3 * half)
    out, dh1, do, dwu, dwd, dwo, dgain2, *early = feedforward(
        x,
        o,
        dm,
        live_wide,
        temb,
        feedforward_norm_gain[None, :],
        attention_output_weight,
        up_projection_weight,
        down_projection_weight,
    )
    dq, dk, dv, far, out_far, *sums = attend_back(
        q,
        kv,
        do,
        exact.reshape(width, 3 * half),
        inv,
        even,
        odd,
        query_key_value_weight,
        out,
        [*early[2:], dwu, dwd, dwo],
        BACK_PLAN,
        BACK_TABLE,
    )
    grad_own, grad_far, *last = finish(
        dq,
        dk,
        dv,
        n1,
        x,
        dh1,
        query_key_value_weight,
        far,
        temb,
        attention_norm_gain[None, :],
        dgain2,
        time_second_weight,
        emb,
        u,
    )
    up = [early[0], sums[0], sums[2]]
    down = [early[1], sums[1], sums[3]]
    output, grad_inputs, inner, outer, gain1, qk, v, out_sum, gain2, up, down = assemble(
        batches, out, out_far, grad_own, grad_far, up + down + [sums[4]] + last
    )
    return (
        output,
        grad_inputs,
        inner.T,
        outer.T,
        gain1[0],
        qk.T,
        v.T,
        out_sum.T,
        gain2[0],
        up.T,
        down.T,
    )


def assemble_kernel(seq_ref, out_ref, out_far_ref, grad_ref, grad_far_ref, *refs):
    ups, downs, (wo, *qkv), (outer, inner) = refs[0:3], refs[3:6], refs[6:10], refs[10:12]
    (output_to, grad_to, inner_to, outer_to, gain1_to, qk_to, v_to, out_to, gain2_to, up_to, down_to) = refs[12:]
    far = pl.program_id(0) == 1

    @pl.when(far)
    def _():
        output_to[0] = out_far_ref[...]
        grad_to[0] = grad_far_ref[...].astype(F32)

    @pl.when(jnp.logical_not(far))
    def _():
        output_to[0] = out_ref[...]
        grad_to[0] = grad_ref[0]

    core = lax.axis_index("batch") & 1

    def joined(ref):
        return jnp.concatenate([ref[0], ref[1]], axis=1)

    def own_half(array):
        size = array.shape[0] // 2
        return jnp.where(core == 0, array[:size], array[size:]).astype(F32)

    @pl.when(pl.program_id(0) == 0)
    def _():
        up_to[...] = own_half(jnp.concatenate([joined(ref) for ref in ups], axis=0))
        for c, ref in enumerate(downs):
            part = own_half(joined(ref))
            for k in range(8):
                first = 128 * place_of(k)
                down_to[:, 128 * (3 * k + c) : 128 * (3 * k + c + 1)] = part[:, first : first + 128]
        out_to[...] = own_half(joined(wo))
        whole = jnp.concatenate([joined(ref) for ref in qkv], axis=1)
        split = whole.shape[0] * 2 // 3
        qk_to[...] = own_half(whole[:split])
        v_to[...] = own_half(whole[split:])
        outer_to[...] = own_half(joined(outer))
        inner_to[...] = own_half(inner[0])
        size = gain1_to.shape[1]
        gains = inner[1, 0:16, :].astype(F32)
        for row, target in enumerate((gain1_to, gain2_to)):
            target[...] = jnp.where(
                core == 0, gains[row : row + 1, :size], gains[row : row + 1, size : 2 * size]
            )


def assemble(batches, out, out_far, grad_own, grad_far, parts):
    half, width = out_far.shape
    hidden = 4 * width
    size = width // batches
    time_hidden, channels = 2 * parts[10].shape[2], parts[11].shape[2]
    whole = pl.BlockSpec(memory_space=pltpu.VMEM)
    slot = pl.BlockSpec((1, half, width), lambda i, seq: (jnp.where(i == 1, 1 - seq[0], jnp.maximum(i, seq[0])), 0, 0))
    shapes = [
        (time_hidden // batches, channels),
        (size, time_hidden),
        (1, size),
        (2 * size, width),
        (size, width),
        (size, width),
        (1, size),
        (hidden // batches, width),
        (size, hidden),
    ]
    return pl.pallas_call(
        assemble_kernel,
        grid_spec=pltpu.PrefetchScalarGridSpec(
            num_scalar_prefetch=1,
            grid=(3,),
            in_specs=[
                pl.BlockSpec((half, width), lambda i, seq: (i // 2 * 2, 0)),
                whole,
                pl.BlockSpec((1, half, width), lambda i, seq: (i // 2, 0, 0)),
                whole,
            ]
            + [whole] * 12,
            out_specs=[slot] * 2 + [whole] * 9,
        ),
        out_shape=[
            jax.ShapeDtypeStruct((3, half, width), BF),
            jax.ShapeDtypeStruct((3, half, width), F32),
        ]
        + [jax.ShapeDtypeStruct(shape, F32) for shape in shapes],
        compiler_params=pltpu.CompilerParams(vmem_limit_bytes=VMEM_LIMIT),
    )(lax.axis_index("seq")[None], out, out_far, grad_own, grad_far, *parts)


BACK_PLAN = [False, True, False, False, False]
BACK_TABLE = {
    2: [(2, 0), (3, 0), (4, 0)],
    3: [(1, 2)],
    5: [(0, 2)],
    6: [(1, 3)],
    7: [(0, 3), (1, 4), (2, 1)],
    9: [(0, 4), (1, 5)],
    11: [(3, 1)],
    12: [(2, 2)],
    14: [(2, 3), (4, 1)],
    15: [(3, 2)],
    16: [(2, 4)],
    17: [(3, 3), (4, 2)],
    18: [(3, 4), (4, 3), (4, 4)],
}


def solution(mesh):
    on_device = pair_plan if mesh.shape["seq"] == 2 and mesh.shape["batch"] == 16 else ring_plan
    return jax.shard_map(
        on_device,
        mesh=mesh,
        in_specs=(
            P("batch", "seq", None),
            P("batch"),
            P("batch"),
            P("batch", "seq"),
            P(),
            P(),
            P(),
            P(),
            P(),
            P(),
            P(),
            P(),
            P("batch", "seq", None),
        ),
        out_specs=(
            P("batch", "seq", None),
            P("batch", "seq", None),
            P(None, "batch"),
            P(None, "batch"),
            P("batch"),
            P(None, "batch"),
            P(None, "batch"),
            P(None, "batch"),
            P("batch"),
            P(None, "batch"),
            P(None, "batch"),
        ),
        check_vma=False,
    )
```

```python
from functools import partial
import math

import jax
import jax.numpy as jnp
from jax import lax
from jax.experimental import pallas as pl
from jax.experimental.pallas import tpu as pltpu
from jax.sharding import PartitionSpec as P

H = 12
DH = 64
TCH = 128


TOP_PRECISION = lax.Precision.HIGHEST


def from_behind(array, axis, by):
    count = lax.axis_size(axis)
    return lax.ppermute(array, axis, [(i, (i + by) % count) for i in range(count)])


def shortened(array):

    def short(part):
        return part.astype(jnp.bfloat16) if part.dtype == jnp.float32 else part

    return jax.tree.map(short, array)


def sinusoid(steps):
    half_width = TCH // 2
    frequency = jnp.exp(
        -math.log(10000.0) * jnp.arange(half_width).astype(jnp.float32) / half_width
    )
    angles = steps.astype(jnp.float32)[:, None] * frequency[None, :]
    return jnp.concatenate([jnp.cos(angles), jnp.sin(angles)], axis=-1)


def layer_norm(hidden, gain):
    centered = hidden - jnp.mean(hidden, axis=-1, keepdims=True)
    variance = jnp.mean(centered * centered, axis=-1, keepdims=True)
    return centered * lax.rsqrt(variance + 1e-05) * gain


def time_mlp(time_embedding, time_first_weight, time_second_weight):
    pre_act = jnp.dot(time_embedding, time_first_weight, precision=TOP_PRECISION)
    return jnp.dot(jax.nn.silu(pre_act), time_second_weight, precision=TOP_PRECISION)


def row_product(left, right):
    return lax.dot_general(
        left, right, (((0,), (0,)), ((), ())), preferred_element_type=jnp.float32
    )


def back_product(left, right):
    return lax.dot_general(
        left, right, (((1,), (1,)), ((), ())), preferred_element_type=jnp.float32
    )


def masked_scores(queries, key_block, mask_block, scale_factor):
    attention_scores = (
        jnp.einsum("sqhd,skhd->shqk", queries, key_block, preferred_element_type=jnp.float32)
        * scale_factor
    )
    return jnp.where(mask_block[:, None, None, :] > 0.5, attention_scores, -1000000000.0)


def ring_plan(
    inputs,
    timesteps,
    counts,
    slot_token_mask,
    time_first_weight,
    time_second_weight,
    attention_norm_gain,
    query_key_value_weight,
    attention_output_weight,
    feedforward_norm_gain,
    up_projection_weight,
    down_projection_weight,
    cotangent,
):
    present_slots, local_len, width = inputs.shape
    total_rows = present_slots * local_len
    scale_factor = 1.0 / math.sqrt(DH)
    slot_alive_flags = (
        (jnp.arange(present_slots)[:, None] < counts[0]) & (slot_token_mask == 1)
    ).astype(jnp.float32)
    time_embedding = sinusoid(timesteps)
    time_vec, time_back = jax.vjp(
        partial(time_mlp, time_embedding),
        time_first_weight.astype(jnp.float32),
        time_second_weight.astype(jnp.float32),
    )
    residual = inputs.astype(jnp.float32) + time_vec[:, None, :]
    normed, norm_back = jax.vjp(layer_norm, residual, attention_norm_gain)
    normed_low = normed.astype(jnp.bfloat16).reshape(total_rows, width)
    packed = (
        jnp.dot(normed_low, query_key_value_weight, preferred_element_type=jnp.float32)
        .astype(jnp.bfloat16)
        .reshape(present_slots, local_len, 3 * width)
    )
    queries = packed[:, :, :width].reshape(present_slots, local_len, H, DH)
    key_rows = packed[:, :, width : 2 * width]
    value_rows = packed[:, :, 2 * width :]
    key_valid_mask = slot_alive_flags.astype(jnp.bfloat16)
    initial_state = (
        jnp.full((present_slots, H, local_len), -1e30, jnp.float32),
        jnp.zeros((present_slots, H, local_len), jnp.float32),
        jnp.zeros((present_slots, local_len, H, DH), jnp.float32),
    )
    key_piece = lax.all_gather(key_rows, "seq", axis=1, tiled=True)
    value_piece = lax.all_gather(value_rows, "seq", axis=1, tiled=True)
    mask_piece = lax.all_gather(key_valid_mask, "seq", axis=1, tiled=True)
    piece_len = key_piece.shape[1]
    block_len = min(piece_len, local_len)

    def one_block(position, inner_state):
        run_max, run_sum, running_totals = inner_state
        offset = position * block_len
        key_block = lax.dynamic_slice_in_dim(key_piece, offset, block_len, 1).reshape(
            present_slots, block_len, H, DH
        )
        value_block = lax.dynamic_slice_in_dim(value_piece, offset, block_len, 1).reshape(
            present_slots, block_len, H, DH
        )
        mask_block = lax.dynamic_slice_in_dim(mask_piece, offset, block_len, 1)
        attention_scores = masked_scores(queries, key_block, mask_block, scale_factor)
        new_max = jnp.maximum(run_max, jnp.max(attention_scores, axis=-1))
        exponent = jnp.exp(attention_scores - new_max[..., None])
        fading = jnp.exp(run_max - new_max)
        run_sum = run_sum * fading + jnp.sum(exponent, axis=-1)
        running_totals = running_totals * jnp.transpose(fading, (0, 2, 1))[..., None] + jnp.einsum(
            "shqk,skhd->sqhd",
            exponent.astype(jnp.bfloat16),
            value_block,
            preferred_element_type=jnp.float32,
        )
        return (new_max, run_sum, running_totals)

    run_max, run_sum, running_totals = lax.fori_loop(
        0, piece_len // block_len, one_block, initial_state
    )
    attended = running_totals / jnp.transpose(run_sum, (0, 2, 1))[..., None]
    log_total = run_max + jnp.log(run_sum)
    attended_low = attended.astype(jnp.bfloat16).reshape(total_rows, width)
    middle = residual + jnp.dot(
        attended_low, attention_output_weight, preferred_element_type=jnp.float32
    ).reshape(present_slots, local_len, width)
    normed_two, norm_two_back = jax.vjp(layer_norm, middle, feedforward_norm_gain)
    normed_two_low = normed_two.astype(jnp.bfloat16).reshape(total_rows, width)
    gate_pre = jnp.dot(normed_two_low, up_projection_weight, preferred_element_type=jnp.float32)
    activated, gelu_back = jax.vjp(partial(jax.nn.gelu, approximate=True), gate_pre)
    activated_low = activated.astype(jnp.bfloat16)
    completed_groups = middle + jnp.dot(
        activated_low, down_projection_weight, preferred_element_type=jnp.float32
    ).reshape(present_slots, local_len, width)
    output = (slot_alive_flags[..., None] * completed_groups).astype(jnp.bfloat16)
    final_gradient = slot_alive_flags[..., None] * cotangent.astype(jnp.float32)
    grad_down_low = final_gradient.reshape(total_rows, width).astype(jnp.bfloat16)
    down_grad = row_product(activated_low, grad_down_low)
    grad_gate = gelu_back(back_product(grad_down_low, down_projection_weight))[0].astype(
        jnp.bfloat16
    )
    up_grad = row_product(normed_two_low, grad_gate)
    grad_middle_norm, mlp_gain_grad = norm_two_back(
        back_product(grad_gate, up_projection_weight).reshape(present_slots, local_len, width)
    )
    grad_middle = final_gradient + grad_middle_norm
    grad_branch_low = grad_middle.reshape(total_rows, width).astype(jnp.bfloat16)
    out_grad = row_product(attended_low, grad_branch_low)
    grad_attended = (
        back_product(grad_branch_low, attention_output_weight)
        .astype(jnp.bfloat16)
        .reshape(present_slots, local_len, H, DH)
    )
    row_delta = jnp.transpose(
        jnp.sum(grad_attended.astype(jnp.float32) * attended, axis=-1), (0, 2, 1)
    )

    def key_terms(key_block, value_block, mask_block):
        attention_scores = masked_scores(queries, key_block, mask_block, scale_factor)
        probability = jnp.exp(attention_scores - log_total[..., None])
        grad_probs = jnp.einsum(
            "sqhd,skhd->shqk", grad_attended, value_block, preferred_element_type=jnp.float32
        )
        grad_scores = (probability * (grad_probs - row_delta[..., None])).astype(jnp.bfloat16)
        query_add = (
            jnp.einsum(
                "shqk,skhd->sqhd", grad_scores, key_block, preferred_element_type=jnp.float32
            )
            * scale_factor
        )
        key_add = (
            jnp.einsum("shqk,sqhd->skhd", grad_scores, queries, preferred_element_type=jnp.float32)
            * scale_factor
        )
        value_add = jnp.einsum(
            "shqk,sqhd->skhd",
            probability.astype(jnp.bfloat16),
            grad_attended,
            preferred_element_type=jnp.float32,
        )
        block_len = key_block.shape[1]
        return (
            query_add,
            key_add.reshape(present_slots, block_len, width),
            value_add.reshape(present_slots, block_len, width),
        )

    cycle_len = lax.axis_size("seq")
    query_zeros = jnp.zeros((present_slots, local_len, H, DH), jnp.float32)

    def visit(visit_index, loop_state):
        grad_queries, visiting, carried = loop_state
        query_add, key_add, value_add = key_terms(
            visiting[0].reshape(present_slots, local_len, H, DH),
            visiting[1].reshape(present_slots, local_len, H, DH),
            visiting[2],
        )
        carried = (carried[0] + key_add, carried[1] + value_add)
        visiting = from_behind((visiting[0], visiting[1], visiting[2]), "seq", 1)
        carried = (
            from_behind(carried[0].astype(jnp.bfloat16), "seq", 1).astype(jnp.float32),
            from_behind(carried[1].astype(jnp.bfloat16), "seq", 1).astype(jnp.float32),
        )
        return (grad_queries + query_add, tuple(visiting), tuple(carried))

    zeros_kv = jnp.zeros((present_slots, local_len, width), jnp.float32)
    grad_queries, visiting, carried = lax.fori_loop(
        0,
        cycle_len,
        visit,
        (query_zeros, (key_rows, value_rows, key_valid_mask), (zeros_kv, zeros_kv)),
    )
    grad_keys, grad_values = carried
    grad_packed = (
        jnp.concatenate(
            [grad_queries.reshape(present_slots, local_len, width), grad_keys, grad_values], axis=-1
        )
        .astype(jnp.bfloat16)
        .reshape(total_rows, 3 * width)
    )
    qkv_grad = row_product(normed_low, grad_packed)
    query_key_grad = qkv_grad[:, : 2 * width]
    value_grad = qkv_grad[:, 2 * width :]
    grad_start_norm, attn_gain_grad = norm_back(
        back_product(grad_packed, query_key_value_weight).reshape(present_slots, local_len, width)
    )
    grad_start = grad_middle + grad_start_norm
    inner_grad, outer_grad = time_back(jnp.sum(grad_start, axis=1))
    shares = (
        lax.psum_scatter(
            inner_grad.astype(jnp.bfloat16), "batch", scatter_dimension=1, tiled=True
        ).astype(jnp.float32),
        lax.psum_scatter(
            outer_grad.astype(jnp.bfloat16), "batch", scatter_dimension=1, tiled=True
        ).astype(jnp.float32),
        lax.psum_scatter(
            attn_gain_grad[None, :].astype(jnp.bfloat16), "batch", scatter_dimension=1, tiled=True
        ).astype(jnp.float32),
        lax.psum_scatter(
            query_key_grad.astype(jnp.bfloat16), "batch", scatter_dimension=1, tiled=True
        ).astype(jnp.float32),
        lax.psum_scatter(
            value_grad.astype(jnp.bfloat16), "batch", scatter_dimension=1, tiled=True
        ).astype(jnp.float32),
        lax.psum_scatter(
            out_grad.astype(jnp.bfloat16), "batch", scatter_dimension=1, tiled=True
        ).astype(jnp.float32),
        lax.psum_scatter(
            mlp_gain_grad[None, :].astype(jnp.bfloat16), "batch", scatter_dimension=1, tiled=True
        ).astype(jnp.float32),
        lax.psum_scatter(
            up_grad.astype(jnp.bfloat16), "batch", scatter_dimension=1, tiled=True
        ).astype(jnp.float32),
        lax.psum_scatter(
            down_grad.astype(jnp.bfloat16), "batch", scatter_dimension=1, tiled=True
        ).astype(jnp.float32),
    )
    summed = tuple(
        jax.tree.map(
            lambda part: part.astype(jnp.float32), lax.psum(shortened(tuple(shares)), "seq")
        )
    )
    return (
        output,
        grad_start,
        summed[0],
        summed[1],
        summed[2][0],
        summed[3],
        summed[4],
        summed[5],
        summed[6][0],
        summed[7],
        summed[8],
    )


BF = jnp.bfloat16
F32 = jnp.float32
MASKED = -1e9
GELU_A = 0.7978845608028654
GELU_B = 0.044715
VMEM_LIMIT = 62 * 2**20


def mm(left, right, left_dim, right_dim):
    return lax.dot_general(
        left, right, (((left_dim,), (right_dim,)), ((), ())), preferred_element_type=F32
    )


def attend_kernel(
    counts_ref, steps_ref, x_hbm, mask_hbm, cot_hbm, w1_ref, w2_ref, gain_ref, w_ref,
    o_ref, exact_ref, inv_ref, even_ref, odd_ref, live_ref, temb_ref, emb_ref, u_ref,
    q_hbm, kv_hbm, n1_hbm, xs_hbm, dm_hbm,
    xs, n1, q, kv, dm, mask, mask_far, bias, live, sems, send, receive,
    keys, query, v_even, v_odd, s_even, s_odd, m_even, m_odd,
):
    step = pl.program_id(0)
    last = pl.num_programs(0) - 1
    piece, width = xs.shape[0] // 4, xs.shape[1]
    length = 2 * piece
    lane = lax.broadcasted_iota(jnp.int32, (1, 128), 1)
    now = jnp.minimum(step, last - 1)
    before = jnp.maximum(step - 1, 0)
    me, seq = lax.axis_index("batch"), lax.axis_index("seq")
    blocks = [pl.ds(piece * i, piece) for i in range(4)]

    def to_partner(k, source, target):
        return pltpu.make_async_remote_copy(
            src_ref=source,
            dst_ref=target,
            send_sem=send.at[k],
            recv_sem=receive.at[k],
            device_id=(me, 1 - seq),
            device_id_type=pl.DeviceIdType.MESH,
        )

    x_one = to_partner(0, x_hbm.at[1 - seq], xs.at[blocks[1]])
    x_two = to_partner(1, x_hbm.at[2], xs.at[blocks[3]])
    cot_one = to_partner(2, cot_hbm.at[1 - seq], dm.at[blocks[1]])
    mask_there = to_partner(3, mask_hbm, mask_far)
    own = [
        pltpu.make_async_copy(x_hbm.at[seq], xs.at[blocks[0]], sems.at[0]),
        pltpu.make_async_copy(x_hbm.at[2], xs.at[blocks[2]], sems.at[1]),
        pltpu.make_async_copy(mask_hbm, mask, sems.at[2]),
        pltpu.make_async_copy(cot_hbm.at[seq], dm.at[blocks[0]], sems.at[3]),
        pltpu.make_async_copy(cot_hbm.at[2], dm.at[blocks[2]], sems.at[4]),
    ]
    keep_early = [
        pltpu.make_async_copy(q, q_hbm, sems.at[5]),
    ]
    keep_late = [
        pltpu.make_async_copy(kv, kv_hbm, sems.at[6]),
        pltpu.make_async_copy(n1, n1_hbm, sems.at[7]),
        pltpu.make_async_copy(xs, xs_hbm, sems.at[8]),
    ]
    keep_dm = pltpu.make_async_copy(dm, dm_hbm, sems.at[9])

    def project(i, with_queries):
        part = blocks[i]
        h = xs[part, :].astype(F32) + temb_ref[i // 2 : i // 2 + 1, :]
        centered = h - jnp.mean(h, axis=1, keepdims=True)
        variance = jnp.mean(centered * centered, axis=1, keepdims=True)
        normed = (centered * lax.rsqrt(variance + 1e-5) * gain_ref[...]).astype(BF)
        n1[part, :] = normed
        if with_queries:
            q[part, :] = (mm(normed, w_ref[:, :width], 1, 0) * 0.125).astype(BF)
        kv[part, :] = mm(normed, w_ref[:, width:], 1, 0).astype(BF)

    def lives(ref):
        rows = lax.broadcasted_iota(jnp.int32, (8, piece), 0)
        held = jnp.concatenate([ref[...], jnp.zeros((5, piece), jnp.int32)], axis=0)
        flags = jnp.where((held == 1) & (rows < counts_ref[0]), 1.0, 0.0)
        return flags.T

    def set_live(i, column):
        live[blocks[i], :] = jnp.broadcast_to(column, (piece, 128)).astype(BF)
        masked = jnp.where(lane == 0, MASKED, 0.0)
        bias[blocks[i], :] = jnp.where(column > 0.5, 0.0, masked).astype(BF)

    def mine(columns):
        return jnp.where(seq == 0, columns[:, 0:1], columns[:, 1:2])

    @pl.when(step == 0)
    def _():
        for copy in own:
            copy.start()
        greet_x()
        mask_there.start()
        x_one.start()
        row = lax.broadcasted_iota(jnp.int32, (8, 1), 0)
        times = jnp.where(
            row == 0, steps_ref[0], jnp.where(row == 1, steps_ref[1], steps_ref[2])
        ).astype(F32)
        half_width = TCH // 2
        column = lax.broadcasted_iota(jnp.int32, (1, TCH), 1)
        index = jnp.where(column < half_width, column, column - half_width).astype(F32)
        angles = times * jnp.exp(-math.log(10000.0) * index / half_width)
        emb = jnp.where(column < half_width, jnp.cos(angles), jnp.sin(angles))
        emb = jnp.where(row < 3, emb, 0.0)

        def exact_product(left, right):
            return lax.dot_general(
                left, right.astype(F32), (((1,), (0,)), ((), ())),
                precision=TOP_PRECISION, preferred_element_type=F32,
            )

        u = exact_product(emb, w1_ref[...])
        temb = exact_product(u / (1.0 + jnp.exp(-u)), w2_ref[...])
        emb_ref[...] = emb
        u_ref[...] = u
        temb_ref[0:1, :] = jnp.where(seq == 0, temb[0:1], temb[1:2])
        temb_ref[1:2, :] = temb[2:3]
        temb_ref[2:8, :] = jnp.zeros((6, width), F32)
        for copy in own[:3]:
            copy.wait()
        columns = lives(mask)
        set_live(0, mine(columns))
        set_live(2, columns[:, 2:3])
        project(0, True)
        project(2, True)
        for copy in own[3:]:
            copy.wait()
        dm[blocks[0], :] *= live[blocks[0], 0:1]
        dm[blocks[2], :] *= live[blocks[2], 0:1]
        mask_there.wait()
        columns = lives(mask_far)
        set_live(1, mine(columns))
        set_live(3, columns[:, 2:3])
        live_ref[...] = live[pl.ds(0, 3 * piece), :]
        x_one.wait()
        x_two.start()
        project(1, True)
        for copy in keep_early:
            copy.start()

    @pl.when(step == 8)
    def _():
        x_two.wait()
        cot_one.start()
        project(3, False)
        for copy in keep_late:
            copy.start()

    @pl.when(step == last)
    def _():
        cot_one.wait()
        dm[blocks[1], :] *= live[blocks[1], 0:1]
        keep_dm.start()

    query_rows = pl.ds(pl.multiple_of((now // 6) * piece, piece), piece)
    key_rows = pl.ds(pl.multiple_of((now // 12) * length, length), length)
    pair_lanes = pl.ds(pl.multiple_of((now % 6) * 128, 128), 128)
    value_lanes = pl.ds(pl.multiple_of(width + (now % 6) * 128, 128), 128)

    @pl.when(step % 6 == 0)
    def _():
        keys[:, 128:] = bias[key_rows, :]
        query[:, 128:] = jnp.where(
            lax.broadcasted_iota(jnp.int32, (piece, 128), 1) == 0, 1.0, 0.0
        ).astype(BF)
        v_even[64:, :] = jnp.ones((16, length), BF)
        v_odd[64:, :] = jnp.ones((16, length), BF)

    keys[:, :128] = kv[key_rows, pair_lanes]

    def half(head, made, made_max, used, used_max, values, at, out_ref):
        query[:, :128] = jnp.where((lane // 64) == head, q[query_rows, pair_lanes], jnp.zeros((), BF))
        top = used_max[0:1, :]
        scores = mm(keys[...], query[...], 1, 1)
        weight = jnp.exp(used[...] - top).astype(BF)
        made[...] = scores
        made_max[...] = jnp.broadcast_to(jnp.max(scores, axis=0, keepdims=True), made_max.shape)
        out_ref[0] = weight
        total = mm(values[...], weight, 1, 0)
        inverse = 1.0 / total[64:65]
        place = pl.ds(pl.multiple_of((at // 6) * piece, piece), piece)
        which = 2 * (at % 6) + 1 - head
        exact = total[:64] * inverse
        o_ref[which, :, place] = exact.astype(BF)
        exact_ref[which, :, place] = exact
        inv_ref[which, :, place] = jnp.broadcast_to(inverse, (8, piece))

    half(0, s_even, m_even, s_odd, m_odd, v_odd, before, odd_ref)
    turned = kv[key_rows, value_lanes].T
    v_even[:64, :] = turned[:64]
    v_odd[:64, :] = turned[64:]
    half(1, s_odd, m_odd, s_even, m_even, v_even, now, even_ref)

    @pl.when(step == last)
    def _():
        for copy in keep_early + keep_late + [keep_dm]:
            copy.wait()


def greet_x():
    partner = (lax.axis_index("batch"), 1 - lax.axis_index("seq"))
    barrier = pltpu.get_barrier_semaphore()
    pl.semaphore_signal(barrier, inc=1, device_id=partner, device_id_type=pl.DeviceIdType.MESH)
    pl.semaphore_wait(barrier, 1)


def attend(counts, timesteps, x, mask, cot, w1, w2, gain, w):
    _, piece, width = x.shape
    length = 2 * piece
    rows = 3 * piece
    steps = 18
    hidden = w1.shape[1]
    whole = pl.BlockSpec(memory_space=pltpu.VMEM)
    scalars = pl.BlockSpec(memory_space=pltpu.SMEM)
    anywhere = pl.BlockSpec(memory_space=pl.ANY)
    return pl.pallas_call(
        attend_kernel,
        grid=(steps + 1,),
        in_specs=[scalars] * 2 + [anywhere] * 3 + [whole] * 4,
        out_specs=[
            whole,
            whole,
            whole,
            pl.BlockSpec((1, length, piece), lambda t: (jnp.minimum(t, steps - 1), 0, 0)),
            pl.BlockSpec((1, length, piece), lambda t: (jnp.maximum(t - 1, 0), 0, 0)),
        ]
        + [whole] * 4
        + [anywhere] * 5,
        out_shape=[
            jax.ShapeDtypeStruct((H, DH, rows), BF),
            jax.ShapeDtypeStruct((H, DH, rows), F32),
            jax.ShapeDtypeStruct((H, 8, rows), F32),
            jax.ShapeDtypeStruct((steps, length, piece), BF),
            jax.ShapeDtypeStruct((steps, length, piece), BF),
            jax.ShapeDtypeStruct((rows, 128), BF),
            jax.ShapeDtypeStruct((8, width), F32),
            jax.ShapeDtypeStruct((8, TCH), F32),
            jax.ShapeDtypeStruct((8, hidden), F32),
            jax.ShapeDtypeStruct((rows, width), BF),
            jax.ShapeDtypeStruct((4 * piece, 2 * width), BF),
            jax.ShapeDtypeStruct((4 * piece, width), BF),
            jax.ShapeDtypeStruct((4 * piece, width), BF),
            jax.ShapeDtypeStruct((rows, width), BF),
        ],
        scratch_shapes=[
            pltpu.VMEM((4 * piece, width), BF),
            pltpu.VMEM((4 * piece, width), BF),
            pltpu.VMEM((rows, width), BF),
            pltpu.VMEM((4 * piece, 2 * width), BF),
            pltpu.VMEM((rows, width), BF),
            pltpu.VMEM((3, piece), jnp.int32),
            pltpu.VMEM((3, piece), jnp.int32),
            pltpu.VMEM((4 * piece, 128), BF),
            pltpu.VMEM((4 * piece, 128), BF),
            pltpu.SemaphoreType.DMA((10,)),
            pltpu.SemaphoreType.DMA((4,)),
            pltpu.SemaphoreType.DMA((4,)),
            pltpu.VMEM((length, 256), BF),
            pltpu.VMEM((piece, 256), BF),
            pltpu.VMEM((80, length), BF),
            pltpu.VMEM((80, length), BF),
            pltpu.VMEM((length, piece), F32),
            pltpu.VMEM((length, piece), F32),
            pltpu.VMEM((8, piece), F32),
            pltpu.VMEM((8, piece), F32),
        ],
        compiler_params=pltpu.CompilerParams(
            vmem_limit_bytes=VMEM_LIMIT, collective_id=4, has_side_effects=True
        ),
        cost_estimate=pl.CostEstimate(flops=20 * 10**9, bytes_accessed=60 * 10**6, transcendentals=19 * 10**6),
    )(counts, timesteps, x, mask, cot, w1, w2, gain, w)


def place_of(pair):
    return 4 * (pair & 1) + 2 * (pair >> 1 & 1) + (pair >> 2)


class Shares:
    def __init__(self, source, scratch, x_second):
        self.source = source
        self.x_second = x_second
        self.names = ["core", "rows", "y", "z", "join", "out"] if x_second else ["core", "y", "z", "x", "out"]
        self.acc, self.final, self.send, self.receive = scratch[0], scratch[1], scratch[-2], scratch[-1]
        boxes = [name for name in self.names if name not in ("join", "out")]
        self.inbox = dict(zip(boxes, scratch[2:-2]))
        me, far = lax.axis_index("batch"), lax.axis_index("seq")
        self.core, self.y, self.z0, self.z1 = [(me >> bit) & 1 for bit in range(4)]
        self.me, self.far = me, far
        self.half = self.acc.shape[2]
        rows = self.acc.shape[1]
        self.rows = slice(0, rows)
        if x_second:
            self.rows = pl.ds(pl.multiple_of(far * (rows // 2), 16), rows // 2)
            self.other_rows = pl.ds(pl.multiple_of((1 - far) * (rows // 2), 16), rows // 2)
        self.own = 4 * self.y + 2 * self.z0 + self.z1

    def partner(self, name):
        if name in ("x", "rows", "join"):
            return (self.me, 1 - self.far)
        return (self.me ^ {"core": 1, "y": 2, "out": 1}[name], self.far)

    def ends(self, name):
        acc, rows = self.acc, self.rows
        if name == "core":
            away = pl.multiple_of((1 - self.core) * self.half, 128)
            return self.source.at[:, :, pl.ds(away, self.half)], self.inbox[name]
        if name == "rows":
            return acc.at[:, self.other_rows], self.inbox[name]
        if name == "y":
            return acc.at[pl.ds(4 * (1 - self.y), 4), rows], self.inbox[name]
        if name == "x":
            return acc.at[self.own], self.inbox[name]
        if name == "join":
            return self.final.at[self.core, rows], self.final.at[self.core, rows]
        return self.final.at[self.core], self.final.at[self.core]

    def copies(self, stage):
        name = self.names[stage]
        if name != "z":
            here, there = self.ends(name)
            return [self.remote(stage, here, there, self.partner(name))]
        made = []
        for k in range(3):
            flip0, flip1 = (k + 1) & 1, (k + 1) >> 1
            z0 = 1 - self.z0 if flip0 else self.z0
            z1 = 1 - self.z1 if flip1 else self.z1
            here = self.acc.at[4 * self.y + 2 * z0 + z1, self.rows]
            other = (self.me ^ (4 * flip0 + 8 * flip1), self.far)
            made.append(self.remote(stage if k == 0 else 7 + k, here, self.inbox[name].at[k], other))
        return made

    def remote(self, which, here, there, other):
        return pltpu.make_async_remote_copy(
            src_ref=here,
            dst_ref=there,
            send_sem=self.send.at[which],
            recv_sem=self.receive.at[which],
            device_id=other,
            device_id_type=pl.DeviceIdType.MESH,
        )

    def start(self, stage):
        for copy in self.copies(stage):
            copy.start()

    def load(self):
        mine = pl.multiple_of(self.core * self.half, 128)
        return pltpu.make_async_copy(
            self.source.at[:, :, pl.ds(mine, self.half)], self.acc, self.send.at[7]
        )

    def begin(self):
        self.start(0)
        self.load().start()

    def add(self, name):
        acc, rows = self.acc, self.rows

        def total(one, other):
            return one + other

        if name in ("core", "rows", "y"):
            first, count = {"core": (0, 8), "rows": (0, 8), "y": (4 * self.y, 4)}[name]
            if name == "core":
                rows = slice(None)
            for k in range(count):
                acc[first + k, rows] = total(acc[first + k, rows], self.inbox[name][k])
        elif name == "z":
            parts = [acc[self.own, rows]] + [self.inbox[name][k] for k in range(3)]
            parts = [part.astype(F32) for part in parts]
            summed = ((parts[0] + parts[1]) + (parts[2] + parts[3])).astype(BF)
            if self.x_second:
                self.final[self.core, rows] = summed
            else:
                acc[self.own] = summed
        elif name == "x":
            self.final[self.core] = total(acc[self.own], self.inbox[name][...])

    def end(self, stage):
        if stage == 0:
            self.load().wait()
        for copy in self.copies(stage):
            copy.wait()
        self.add(self.names[stage])

    def go_on(self, stage):
        self.end(stage)
        if stage + 1 < len(self.names):
            self.start(stage + 1)

    def fetch(self):
        return pltpu.make_async_copy(self.source, self.acc, self.send.at[7])

    def resume(self, stage):
        self.fetch().wait()
        self.start(stage)


def share_scratch(rows, columns, x_second):
    half = columns // 2
    part = rows // 2 if x_second else rows
    shapes = [(8, rows, half), (2, rows, half), (8, rows, half)]
    shapes += [(8, part, half)] if x_second else []
    shapes += [(4, part, half), (3, part, half)]
    shapes += [] if x_second else [(rows, half)]
    return [pltpu.VMEM(shape, BF) for shape in shapes] + [
        pltpu.SemaphoreType.DMA((10,)),
        pltpu.SemaphoreType.DMA((10,)),
    ]


SCRATCH_COUNT = 8


def greet():
    me, far = lax.axis_index("batch"), lax.axis_index("seq")
    barrier = pltpu.get_barrier_semaphore()
    others = [(me ^ 1, far), (me ^ 2, far), (me ^ 4, far), (me ^ 8, far), (me ^ 12, far), (me, 1 - far)]
    for other in others:
        pl.semaphore_signal(barrier, inc=1, device_id=other, device_id_type=pl.DeviceIdType.MESH)
    pl.semaphore_wait(barrier, len(others))


def attend_back_kernel(
    plan, table, q_ref, k_ref, v_ref, do_ref, o_ref, inv_ref, even_ref, odd_ref, *rest
):
    count = len(plan)
    w_ref, out_hbm, *rest = rest
    sources, rest = rest[:count], rest[count:]
    width = w_ref.shape[0]
    (dq_ref, dk_ref, dv_ref, far_ref, output_hbm), rest = rest[:5], rest[5:]
    finals, rest = rest[:count], rest[count:]
    values, gradient, dk_sum, dv_sum, far_kv, far_send, far_got, out_got, far_sems, *rest = rest
    shares = []
    for i in range(count):
        own = rest[SCRATCH_COUNT * i : SCRATCH_COUNT * (i + 1)]
        shares.append(Shares(sources[i], own, plan[i]))
    step = pl.program_id(0)
    steps = pl.num_programs(0)
    pair, part = back_place(step)
    piece, length = q_ref.shape[0], k_ref.shape[0]
    lane = lax.broadcasted_iota(jnp.int32, (1, 128), 1)
    zero = jnp.zeros((), BF)
    far_copy = pltpu.make_async_remote_copy(
        src_ref=far_send,
        dst_ref=far_got,
        send_sem=far_sems.at[0],
        recv_sem=far_sems.at[1],
        device_id=(lax.axis_index("batch"), 1 - lax.axis_index("seq")),
        device_id_type=pl.DeviceIdType.MESH,
    )

    seq = lax.axis_index("seq")
    out_copy = pltpu.make_async_remote_copy(
        src_ref=out_hbm.at[pl.ds(piece, piece)],
        dst_ref=out_got,
        send_sem=far_sems.at[2],
        recv_sem=far_sems.at[3],
        device_id=(lax.axis_index("batch"), 1 - seq),
        device_id_type=pl.DeviceIdType.MESH,
    )
    returned = pltpu.make_async_copy(out_got, output_hbm, far_sems.at[4])

    @pl.when(step == 0)
    def _():
        for share in shares[:2]:
            share.fetch().start()
        greet()
        for share in shares[:2]:
            share.resume(2)
        for share in shares[2:]:
            share.begin()
        out_copy.start()
        values[:, 128:] = jnp.where(
            lax.broadcasted_iota(jnp.int32, (length, 128), 1) < 3, 1.0, 0.0
        ).astype(BF)
        gradient[...] = jnp.zeros_like(gradient)
        dk_sum[...] = jnp.zeros_like(dk_sum)
        dv_sum[...] = jnp.zeros_like(dv_sum)

    for when in sorted(table):
        if when < 18:

            @pl.when(step == when)
            def _(when=when):
                for i, stage in table[when]:
                    shares[i].go_on(stage)

    @pl.when(step == 11)
    def _():
        out_copy.wait()
        returned.start()

    @pl.when(step == 6)
    def _():
        far_send[...] = mm(far_kv[:, : 2 * width], w_ref[:, width:], 1, 1).astype(BF)
        far_copy.start()

    values[:, :128] = v_ref[...]
    inverse = jnp.concatenate(
        [jnp.broadcast_to(inv_ref[head, 0:1, :], (DH, piece)) for head in range(2)], axis=0
    )
    scaled = (do_ref[...].astype(F32) * inverse).astype(BF)
    product = scaled.astype(F32) * o_ref[...]
    for head in range(2):
        mine = slice(DH * head, DH * head + DH)
        place = slice(piece * head, piece * head + piece)
        delta = -jnp.sum(product[mine], axis=0, keepdims=True)
        high = delta.astype(BF).astype(F32)
        rest_of = delta - high
        middle = rest_of.astype(BF).astype(F32)
        gradient[mine, place] = scaled[mine]
        gradient[128:144, place] = jnp.concatenate(
            [high, middle, rest_of - middle, jnp.zeros((13, piece), F32)], axis=0
        ).astype(BF)
    dp = mm(values[...], gradient[...], 1, 0)
    turned_keys = k_ref[...].T
    natural = scaled.T
    weights = [even_ref[0], odd_ref[0]]
    ds = [
        (weights[head].astype(F32) * dp[:, piece * head : piece * head + piece]).astype(BF)
        for head in range(2)
    ]

    def apart(array):
        return jnp.concatenate(
            [jnp.where(lane < 64, array, zero), jnp.where(lane < 64, zero, array)], axis=0
        )

    dv = mm(jnp.concatenate(weights, axis=1), apart(natural), 1, 0)
    dk = mm(jnp.concatenate(ds, axis=1), apart(q_ref[...]), 1, 0)
    for head in range(2):
        mine = slice(DH * head, DH * head + DH)
        dq_ref[mine, :] = (mm(turned_keys[mine], ds[head], 1, 0) * 0.125).astype(BF)

    again = part == 1
    dk += jnp.where(again, dk_sum[...], 0.0)
    dv += jnp.where(again, dv_sum[...], 0.0)
    dk_sum[...] = dk
    dv_sum[...] = dv
    dk, dv = dk.astype(BF), dv.astype(BF)
    dk_ref[...] = dk
    dv_ref[...] = dv
    early = step < 6
    at = jnp.where(early, pair * 128, 2 * width)
    far_kv[:, pl.ds(pl.multiple_of(at, 128), 128)] = dk[piece:]
    at = jnp.where(early, width + pair * 128, 2 * width + 128)
    far_kv[:, pl.ds(pl.multiple_of(at, 128), 128)] = dv[piece:]

    @pl.when(step == steps - 1)
    def _():
        for when in sorted(table):
            if when >= 18:
                for i, stage in table[when]:
                    shares[i].go_on(stage)
        for i in range(count):
            finals[i][...] = shares[i].final[...]
        far_copy.wait()
        far_ref[...] = far_got[...]
        returned.wait()


def back_place(step):
    late = jnp.maximum(step - 6, 0)
    return jnp.where(step < 6, step, late // 2), jnp.where(step < 6, 2, late % 2)


def attend_back(q, kv, do, o, inv, even, odd, w, out, partials, plan, table):
    rows, width = q.shape
    length = 2 * rows // 3
    piece = rows // 3

    def spec(shape, index):
        return pl.BlockSpec(shape, lambda t: index(*back_place(t)))

    weight_spec = spec((1, length, piece), lambda p, j: (j * 6 + p, 0, 0))
    scratch = []
    sizes = [(a.shape[1], a.shape[2] * (2 if i < 2 else 1)) for i, a in enumerate(partials)]
    for size, x_second in zip(sizes, plan):
        scratch += share_scratch(*size, x_second)
    whole = pl.BlockSpec(memory_space=pltpu.VMEM)
    return pl.pallas_call(
        partial(attend_back_kernel, plan, table),
        grid=(18,),
        in_specs=[
            spec((piece, 128), lambda p, j: (j, p)),
            spec((length, 128), lambda p, j: (j // 2, p)),
            spec((length, 128), lambda p, j: (j // 2, 6 + p)),
            spec((128, piece), lambda p, j: (p, j)),
            spec((128, piece), lambda p, j: (p, j)),
            spec((2, 8, piece), lambda p, j: (p, 0, j)),
            weight_spec,
            weight_spec,
            whole,
        ]
        + [pl.BlockSpec(memory_space=pl.ANY)] * (1 + len(partials)),
        out_specs=[
            spec((128, piece), lambda p, j: (p, j)),
            spec((length, 128), lambda p, j: (j // 2, p)),
            spec((length, 128), lambda p, j: (j // 2, p)),
            whole,
            pl.BlockSpec(memory_space=pl.ANY),
        ]
        + [whole] * len(partials),
        out_shape=[
            jax.ShapeDtypeStruct((width, rows), BF),
            jax.ShapeDtypeStruct((2 * length, width), BF),
            jax.ShapeDtypeStruct((2 * length, width), BF),
            jax.ShapeDtypeStruct((piece, width), BF),
            jax.ShapeDtypeStruct((piece, width), BF),
        ]
        + [jax.ShapeDtypeStruct((2, a, b // 2), BF) for a, b in sizes],
        scratch_shapes=[
            pltpu.VMEM((length, 256), BF),
            pltpu.VMEM((256, 2 * piece), BF),
            pltpu.VMEM((length, 128), F32),
            pltpu.VMEM((length, 128), F32),
            pltpu.VMEM((piece, 2 * width + 256), BF),
            pltpu.VMEM((piece, width), BF),
            pltpu.VMEM((piece, width), BF),
            pltpu.VMEM((piece, width), BF),
            pltpu.SemaphoreType.DMA((5,)),
        ]
        + scratch,
        compiler_params=pltpu.CompilerParams(
            vmem_limit_bytes=VMEM_LIMIT, collective_id=1, has_side_effects=True
        ),
        cost_estimate=pl.CostEstimate(flops=30 * 10**9, bytes_accessed=60 * 10**6, transcendentals=0),
    )(q, kv, kv, do, o, inv, even, odd, w, out, *partials)


def finish_kernel(
    dq_hbm, dk_hbm, dv_hbm, n1_hbm, x_hbm, dh_hbm, w_hbm, far_ref, temb_ref, gain_ref, dgain2_ref,
    w2_ref, emb_ref, u_ref, *rest
):
    own_ref, far_out_ref, finals, rest = rest[0], rest[1], rest[2:7], rest[7:]
    dq, dk, dv, n1, x, dh, w, send, got, sems, far_sems = rest[:11]
    sources, rest = rest[11:16], rest[16:]
    shares = []
    for i in range(5):
        own = rest[SCRATCH_COUNT * i : SCRATCH_COUNT * (i + 1)]
        shares.append(Shares(sources[i], own, FINISH_PLAN[i]))
    half, width = far_ref.shape
    me, seq = lax.axis_index("batch"), lax.axis_index("seq")

    loads = {}

    def fetch(name, source, target):
        loads[name] = pltpu.make_async_copy(source, target, sems.at[len(loads)])
        loads[name].start()

    blocks = [slice(half * i, half * i + half) for i in range(4)]
    fetch("w", w_hbm, w)
    for b in (1, 0, 2):
        fetch(("dq", b), dq_hbm.at[:, blocks[b]], dq.at[:, blocks[b]])
        fetch(("dk", b), dk_hbm.at[blocks[b]], dk.at[blocks[b]])
        fetch(("dv", b), dv_hbm.at[blocks[b]], dv.at[blocks[b]])
        if b == 1:
            fetch("x", x_hbm.at[pl.ds(0, 3 * half)], x)
            fetch(("dh", 1), dh_hbm.at[blocks[1]], dh.at[blocks[1]])
    fetch(("dk", 3), dk_hbm.at[blocks[3]], dk.at[blocks[3]])
    fetch(("dv", 3), dv_hbm.at[blocks[3]], dv.at[blocks[3]])
    fetch("n1", n1_hbm, n1)
    fetch(("dh", 0), dh_hbm.at[blocks[0]], dh.at[blocks[0]])
    fetch(("dh", 2), dh_hbm.at[blocks[2]], dh.at[blocks[2]])
    back_copy = pltpu.make_async_remote_copy(
        src_ref=send,
        dst_ref=got,
        send_sem=far_sems.at[0],
        recv_sem=far_sems.at[1],
        device_id=(me, 1 - seq),
        device_id_type=pl.DeviceIdType.MESH,
    )
    greet()

    def norm_back(b, more):
        loads[("dh", b)].wait()
        part = blocks[b]
        dn = mm(dq[:, part], w[:, :width], 0, 1)
        dn += mm(dk[part, :], w[:, width : 2 * width], 1, 1)
        dn += mm(dv[part, :], w[:, 2 * width :], 1, 1)
        if more is not None:
            dn += more[...].astype(F32)
        h = x[part, :].astype(F32) + temb_ref[b // 2 : b // 2 + 1, :]
        centered = h - jnp.mean(h, axis=1, keepdims=True)
        r1 = lax.rsqrt(jnp.mean(centered * centered, axis=1, keepdims=True) + 1e-5)
        x1 = centered * r1
        e = dn * gain_ref[...]
        dh0 = dh[part, :] + r1 * (
            e - jnp.mean(e, axis=1, keepdims=True) - x1 * jnp.mean(e * x1, axis=1, keepdims=True)
        )
        return dh0, jnp.sum(dh0, axis=0, keepdims=True), jnp.sum(dn * x1, axis=0, keepdims=True)

    def weight_piece(f):
        columns = slice(256 * f, 256 * f + 256)
        q_part = mm(dq[...], n1[: 3 * half, columns], 1, 0).astype(BF)
        k_part = mm(dk[...], n1[:, columns], 0, 0).astype(BF)
        v_part = mm(dv[...], n1[:, columns], 0, 0).astype(BF)
        pair_rows = width // 4
        for k in range(8):
            source = q_part if k < 4 else k_part
            first = pair_rows * (k % 4)
            sources[f][place_of(k), :pair_rows, :] = source[first : first + pair_rows]
            first = width // 8 * k
            sources[f][place_of(k), pair_rows:, :] = v_part[first : first + width // 8]
        shares[f].begin()

    for name in loads:
        if name[0] != "dh":
            loads[name].wait()
    weight_piece(0)
    weight_piece(1)
    shares[0].go_on(0)
    weight_piece(2)
    shares[1].go_on(0)
    dh0, dtemb_a, dgain_a = norm_back(1, None)
    send[...] = dh0.astype(BF)
    back_copy.start()
    shares[2].go_on(0)
    dh0, dtemb_b, dgain_b = norm_back(0, None)
    own_ref[0] = dh0
    shares[0].go_on(1)
    dh0, dtemb_two, dgain_c = norm_back(2, far_ref)
    own_ref[1] = dh0

    dtemb_one = dtemb_a + dtemb_b
    first = (seq == 0).astype(F32)
    dtemb = jnp.concatenate(
        [first * dtemb_one, (1.0 - first) * dtemb_one, dtemb_two, jnp.zeros((5, width), F32)], axis=0
    )
    u = u_ref[...]
    sigmoid = 1.0 / (1.0 + jnp.exp(-u))
    outer = lax.dot_general(
        dtemb, u * sigmoid, (((0,), (0,)), ((), ())), precision=TOP_PRECISION, preferred_element_type=F32
    ).astype(BF)
    dsilu = lax.dot_general(
        dtemb, w2_ref[...].astype(F32), (((1,), (1,)), ((), ())), precision=TOP_PRECISION, preferred_element_type=F32
    )
    dpre = dsilu * (sigmoid * (1.0 + u * (1.0 - sigmoid)))
    inner = lax.dot_general(
        dpre, emb_ref[...], (((0,), (0,)), ((), ())), precision=TOP_PRECISION, preferred_element_type=F32
    ).astype(BF)
    dgain = dgain_a + dgain_b + dgain_c
    size, inner_size = width // 8, inner.shape[0] // 8
    sources[4][...] = jnp.zeros_like(sources[4])
    for k in range(8):
        sources[3][place_of(k)] = outer[size * k : size * k + size]
        sources[4][place_of(k), :, :128] = inner[inner_size * k : inner_size * k + inner_size]
        both = jnp.concatenate(
            [
                jnp.concatenate([g[:, size * k : size * k + size], jnp.zeros((1, 128 - size), F32)], axis=1)
                for g in (dgain, dgain2_ref[...])
            ]
            + [jnp.zeros((14, 128), F32)],
            axis=0,
        )
        sources[4][place_of(k), :16, 128:] = both.astype(BF)
    shares[3].begin()
    shares[4].begin()
    for i, stage in FINISH_ORDER:
        shares[i].go_on(stage)
    for i in range(5):
        finals[i][...] = shares[i].final[...]
    back_copy.wait()
    far_out_ref[...] = got[...]


FINISH_PLAN = [False, True, False, False, False]
FINISH_ORDER = [
    (1, 1), (3, 0), (4, 0), (0, 2), (2, 1), (1, 2), (2, 2), (3, 1), (4, 1), (0, 3), (1, 3), (3, 2),
    (4, 2), (2, 3), (0, 4), (1, 4), (3, 3), (4, 3), (2, 4), (1, 5), (3, 4), (4, 4),
]


def finish(dq, dk, dv, n1, x, dh1, w, far, temb, gain, dgain2, w2, emb, u):
    half, width = far.shape
    rows = 3 * half
    hidden = w2.shape[0]
    whole = pl.BlockSpec(memory_space=pltpu.VMEM)
    sizes = [(3 * width // 8, 256)] * 3 + [(width // 8, hidden), (hidden // 8, 256)]
    scratch = [pltpu.VMEM((8,) + size, BF) for size in sizes]
    for size, x_second in zip(sizes, FINISH_PLAN):
        scratch += share_scratch(*size, x_second)
    return pl.pallas_call(
        finish_kernel,
        in_specs=[pl.BlockSpec(memory_space=pl.ANY)] * 7 + [whole] * 7,
        out_specs=[whole] * 7,
        out_shape=[
            jax.ShapeDtypeStruct((2, half, width), F32),
            jax.ShapeDtypeStruct((half, width), BF),
        ]
        + [jax.ShapeDtypeStruct((2, a, b // 2), BF) for a, b in sizes],
        scratch_shapes=[
            pltpu.VMEM((width, rows), BF),
            pltpu.VMEM((4 * half, width), BF),
            pltpu.VMEM((4 * half, width), BF),
            pltpu.VMEM((4 * half, width), BF),
            pltpu.VMEM((rows, width), BF),
            pltpu.VMEM((rows, width), F32),
            pltpu.VMEM(w.shape, BF),
            pltpu.VMEM((half, width), BF),
            pltpu.VMEM((half, width), BF),
            pltpu.SemaphoreType.DMA((20,)),
            pltpu.SemaphoreType.DMA((2,)),
        ]
        + scratch,
        compiler_params=pltpu.CompilerParams(
            vmem_limit_bytes=VMEM_LIMIT, collective_id=2, has_side_effects=True
        ),
        cost_estimate=pl.CostEstimate(flops=15 * 10**9, bytes_accessed=60 * 10**6, transcendentals=0),
    )(dq, dk, dv, n1, x, dh1, w, far, temb, gain, dgain2, w2, emb, u)


def gelu_and_slope(g):
    square = g * g
    half_plus = 0.5 * jnp.tanh(g * (GELU_A + GELU_A * GELU_B * square)) + 0.5
    act = g * half_plus
    slope = half_plus + act * (2.0 - 2.0 * half_plus) * (GELU_A + 3.0 * GELU_A * GELU_B * square)
    return act, slope


FF_BEGIN = {6: (0, 1), 12: (2, 3)}
FF_PLAN = [False, True, False, True]
FF_TICKS = {
    9: [(0, 0), (1, 0)],
    12: [(0, 1), (1, 1)],
    15: [(0, 2), (1, 2), (2, 0), (3, 0)],
    18: [(0, 3), (1, 3)],
    20: [(0, 4), (1, 4)],
    21: [(1, 5), (2, 1), (3, 1)],
}


def feedforward_kernel(
    x_hbm, o_ref, dm_ref, live_ref, temb_ref, gain_ref, wo_ref, *rest
):
    wu_refs, wd_refs, rest = rest[:4], rest[4:8], rest[8:]
    out_hbm, dh1_hbm, do_ref, dwu_hbm, dwd_hbm, dwo_ref, dgain_ref, *rest = rest
    finals, rest = rest[:4], rest[4:]
    finals, handed = finals[:2], finals[2:]
    x, h1, n2, h2, dn2, sems, *rest = rest
    sources, rest = rest[:4], rest[4:]
    shares = []
    for i in range(4):
        own = rest[SCRATCH_COUNT * i : SCRATCH_COUNT * (i + 1)]
        shares.append(Shares(sources[i], own, FF_PLAN[i]))
    turn, side = pl.program_id(0), pl.program_id(1)
    chunk, chunks = 2 * turn + side, 6
    wu = jnp.concatenate([ref[...] for ref in wu_refs], axis=1)
    wd = jnp.concatenate([ref[...] for ref in wd_refs], axis=0)
    rows, width = x.shape
    block = rows // 2
    third = rows // 3
    blocks = [slice(block * i, block * i + block) for i in range(2)]
    thirds = [slice(third * i, third * i + third) for i in range(3)]
    size = width // 8

    def act_on(now):
        for i, stage in FF_TICKS.get(now, []):
            if i >= 2 and stage == 1:
                shares[i].end(stage)
            else:
                shares[i].go_on(stage)
        for i in FF_BEGIN.get(now, []):
            shares[i].begin()

    def tick():
        for now in sorted(set(FF_TICKS) | set(FF_BEGIN)):
            if now < 18:
                pl.when(chunk == now // 3)(partial(act_on, now))

    load = pltpu.make_async_copy(x_hbm.at[pl.ds(0, rows)], x, sems.at[0])

    @pl.when(chunk == 0)
    def _():
        load.start()
        greet()
        load.wait()
        for i, part in enumerate(thirds):
            h0 = x[part, :].astype(F32) + temb_ref[i // 2 : i // 2 + 1, :]
            h = h0 + mm(o_ref[:, part], wo_ref[...], 0, 0)
            h1[part, :] = h
            centered = h - jnp.mean(h, axis=1, keepdims=True)
            variance = jnp.mean(centered * centered, axis=1, keepdims=True)
            n2[part, :] = (centered * lax.rsqrt(variance + 1e-5) * gain_ref[...]).astype(BF)
            h2[part, :] = h
            dn2[part, :] = jnp.zeros_like(h)

    def first(part):
        return mm(n2[part, :], wu, 1, 0), mm(dm_ref[part, :], wd, 1, 1)

    def second(pair):
        act, slope = gelu_and_slope(pair[0])
        return act.astype(BF), (pair[1] * slope).astype(BF)

    def third_step(part, pair):
        h2[part, :] += mm(pair[0], wd, 1, 0)
        dn2[part, :] += mm(pair[1], wu, 1, 1)

    tick()
    a = first(blocks[0])
    b = first(blocks[1])
    a = second(a)
    b = second(b)
    third_step(blocks[0], a)
    third_step(blocks[1], b)
    act = jnp.concatenate([a[0], b[0]], axis=0)
    dg = jnp.concatenate([a[1], b[1]], axis=0)
    dwd = mm(dm_ref[...], act, 0, 0).astype(BF)
    dwu = mm(dg, n2[...], 0, 0).astype(BF).reshape(4, 128, width)
    for c in range(3):
        up_to, down_to = sources[2 * (c % 2)], sources[2 * (c % 2) + 1]

        @pl.when(turn == c)
        def _(up_to=up_to, down_to=down_to):
            up_to[pl.ds(4 * side, 4)] = dwu
            for k in range(8):
                columns = pl.ds(pl.multiple_of(512 * side, 128), 512)
                down_to[place_of(k), :, columns] = dwd[size * k : size * k + size]

    @pl.when(chunk == chunks - 1)
    def _():
        act_on(18)
        dgain = jnp.zeros_like(dgain_ref)
        for i, part in enumerate(thirds):
            h = h1[part, :]
            live = live_ref[part, 0:1].astype(F32)
            x[part, :] = (live * h2[part, :]).astype(BF)
            centered = h - jnp.mean(h, axis=1, keepdims=True)
            variance = jnp.mean(centered * centered, axis=1, keepdims=True)
            r2 = lax.rsqrt(variance + 1e-5)
            x2 = centered * r2
            dn = dn2[part, :]
            dgain += jnp.sum(dn * x2, axis=0, keepdims=True)
            e = dn * gain_ref[...]
            dh1 = dm_ref[part, :].astype(F32) + r2 * (
                e
                - jnp.mean(e, axis=1, keepdims=True)
                - x2 * jnp.mean(e * x2, axis=1, keepdims=True)
            )
            h1[part, :] = dh1
            da = dh1.astype(BF)
            n2[part, :] = da
            do_ref[:, part] = mm(wo_ref[...], da, 1, 1).astype(BF)
            act_on(19 + i)
        for i in range(2):
            finals[i][...] = shares[i].final[...]
        stores = [
            pltpu.make_async_copy(x, out_hbm, sems.at[1]),
            pltpu.make_async_copy(h1, dh1_hbm, sems.at[2]),
            pltpu.make_async_copy(shares[2].acc, handed[0], sems.at[3]),
            pltpu.make_async_copy(shares[3].acc, handed[1], sems.at[4]),
            pltpu.make_async_copy(sources[0], dwu_hbm, sems.at[5]),
            pltpu.make_async_copy(sources[1], dwd_hbm, sems.at[6]),
        ]
        for store in stores:
            store.start()
        dgain_ref[...] = dgain
        dwo = mm(n2[...], o_ref[...], 0, 1).astype(BF)
        for k in range(8):
            dwo_ref[place_of(k)] = dwo[size * k : size * k + size]
        for store in stores:
            store.wait()


def feedforward(x, o, dm, live, temb, gain, wo, wu, wd):
    rows, width = dm.shape
    whole = pl.BlockSpec(memory_space=pltpu.VMEM)
    anywhere = pl.BlockSpec(memory_space=pl.ANY)

    def tile(c, h, i):
        return 3 * (4 * (i % 2) + 2 * (i // 2) + h) + c

    up_specs = [pl.BlockSpec((width, 128), lambda c, h, i=i: (0, tile(c, h, i))) for i in range(4)]
    down_specs = [pl.BlockSpec((128, width), lambda c, h, i=i: (tile(c, h, i), 0)) for i in range(4)]
    sizes = [(128, width), (width // 8, 1024)] * 2
    scratch = [pltpu.VMEM((8,) + size, BF) for size in sizes]
    for size, x_second in zip(sizes, FF_PLAN):
        scratch += share_scratch(*size, x_second)
    return pl.pallas_call(
        feedforward_kernel,
        grid=(3, 2),
        in_specs=[anywhere] + [whole] * 6 + up_specs + down_specs,
        out_specs=[anywhere] * 2 + [whole] + [anywhere] * 2 + [whole] * 4 + [anywhere] * 2,
        out_shape=[
            jax.ShapeDtypeStruct((rows, width), BF),
            jax.ShapeDtypeStruct((rows, width), F32),
            jax.ShapeDtypeStruct((width, rows), BF),
            jax.ShapeDtypeStruct((8, 128, width), BF),
            jax.ShapeDtypeStruct((8, width // 8, 1024), BF),
            jax.ShapeDtypeStruct((8, width // 8, width), BF),
            jax.ShapeDtypeStruct((1, width), F32),
        ]
        + [jax.ShapeDtypeStruct((2, a, b // 2), BF) for a, b in sizes[:2]]
        + [jax.ShapeDtypeStruct((8, a, b // 2), BF) for a, b in sizes[2:]],
        scratch_shapes=[
            pltpu.VMEM((rows, width), BF),
            pltpu.VMEM((rows, width), F32),
            pltpu.VMEM((rows, width), BF),
            pltpu.VMEM((rows, width), F32),
            pltpu.VMEM((rows, width), F32),
            pltpu.SemaphoreType.DMA((7,)),
        ]
        + scratch,
        compiler_params=pltpu.CompilerParams(
            vmem_limit_bytes=VMEM_LIMIT, collective_id=3, has_side_effects=True
        ),
        cost_estimate=pl.CostEstimate(flops=48 * 10**9, bytes_accessed=50 * 10**6, transcendentals=5 * 10**6),
    )(x, o, dm, live, temb, gain, wo, *[wu] * 4, *[wd] * 4)


def pair_plan(
    inputs,
    timesteps,
    counts,
    slot_token_mask,
    time_first_weight,
    time_second_weight,
    attention_norm_gain,
    query_key_value_weight,
    attention_output_weight,
    feedforward_norm_gain,
    up_projection_weight,
    down_projection_weight,
    cotangent,
):
    slots, half, width = inputs.shape
    batches = lax.axis_size("batch")
    (o, exact, inv, even, odd, live_wide, temb, emb, u, q, kv, n1, x, dm) = attend(
        counts,
        timesteps,
        inputs,
        slot_token_mask,
        cotangent,
        time_first_weight,
        time_second_weight,
        attention_norm_gain[None, :],
        query_key_value_weight,
    )
    o = o.reshape(width, 3 * half)
    out, dh1, do, dwu, dwd, dwo, dgain2, *early = feedforward(
        x,
        o,
        dm,
        live_wide,
        temb,
        feedforward_norm_gain[None, :],
        attention_output_weight,
        up_projection_weight,
        down_projection_weight,
    )
    dq, dk, dv, far, out_far, *sums = attend_back(
        q,
        kv,
        do,
        exact.reshape(width, 3 * half),
        inv,
        even,
        odd,
        query_key_value_weight,
        out,
        [*early[2:], dwu, dwd, dwo],
        BACK_PLAN,
        BACK_TABLE,
    )
    grad_own, grad_far, *last = finish(
        dq,
        dk,
        dv,
        n1,
        x,
        dh1,
        query_key_value_weight,
        far,
        temb,
        attention_norm_gain[None, :],
        dgain2,
        time_second_weight,
        emb,
        u,
    )
    up = [early[0], sums[0], sums[2]]
    down = [early[1], sums[1], sums[3]]
    output, grad_inputs, inner, outer, gain1, qk, v, out_sum, gain2, up, down = assemble(
        batches, out, out_far, grad_own, grad_far, up + down + [sums[4]] + last
    )
    return (
        output,
        grad_inputs,
        inner.T,
        outer.T,
        gain1[0],
        qk.T,
        v.T,
        out_sum.T,
        gain2[0],
        up.T,
        down.T,
    )


def assemble_kernel(seq_ref, out_ref, out_far_ref, grad_ref, grad_far_ref, *refs):
    ups, downs, (wo, *qkv), (outer, inner) = refs[0:3], refs[3:6], refs[6:10], refs[10:12]
    (output_to, grad_to, inner_to, outer_to, gain1_to, qk_to, v_to, out_to, gain2_to, up_to, down_to) = refs[12:]
    far = pl.program_id(0) == 1

    @pl.when(far)
    def _():
        output_to[0] = out_far_ref[...]
        grad_to[0] = grad_far_ref[...].astype(F32)

    @pl.when(jnp.logical_not(far))
    def _():
        output_to[0] = out_ref[...]
        grad_to[0] = grad_ref[0]

    core = lax.axis_index("batch") & 1

    def joined(ref):
        return jnp.concatenate([ref[0], ref[1]], axis=1)

    def own_half(array):
        size = array.shape[0] // 2
        return jnp.where(core == 0, array[:size], array[size:]).astype(F32)

    @pl.when(pl.program_id(0) == 0)
    def _():
        up_to[...] = own_half(jnp.concatenate([joined(ref) for ref in ups], axis=0))
        for c, ref in enumerate(downs):
            part = own_half(joined(ref))
            for k in range(8):
                first = 128 * place_of(k)
                down_to[:, 128 * (3 * k + c) : 128 * (3 * k + c + 1)] = part[:, first : first + 128]
        out_to[...] = own_half(joined(wo))
        whole = jnp.concatenate([joined(ref) for ref in qkv], axis=1)
        split = whole.shape[0] * 2 // 3
        qk_to[...] = own_half(whole[:split])
        v_to[...] = own_half(whole[split:])
        outer_to[...] = own_half(joined(outer))
        inner_to[...] = own_half(inner[0])
        size = gain1_to.shape[1]
        gains = inner[1, 0:16, :].astype(F32)
        for row, target in enumerate((gain1_to, gain2_to)):
            target[...] = jnp.where(
                core == 0, gains[row : row + 1, :size], gains[row : row + 1, size : 2 * size]
            )


def assemble(batches, out, out_far, grad_own, grad_far, parts):
    half, width = out_far.shape
    hidden = 4 * width
    size = width // batches
    time_hidden, channels = 2 * parts[10].shape[2], parts[11].shape[2]
    whole = pl.BlockSpec(memory_space=pltpu.VMEM)
    slot = pl.BlockSpec((1, half, width), lambda i, seq: (jnp.where(i == 1, 1 - seq[0], jnp.maximum(i, seq[0])), 0, 0))
    shapes = [
        (time_hidden // batches, channels),
        (size, time_hidden),
        (1, size),
        (2 * size, width),
        (size, width),
        (size, width),
        (1, size),
        (hidden // batches, width),
        (size, hidden),
    ]
    return pl.pallas_call(
        assemble_kernel,
        grid_spec=pltpu.PrefetchScalarGridSpec(
            num_scalar_prefetch=1,
            grid=(3,),
            in_specs=[
                pl.BlockSpec((half, width), lambda i, seq: (i // 2 * 2, 0)),
                whole,
                pl.BlockSpec((1, half, width), lambda i, seq: (i // 2, 0, 0)),
                whole,
            ]
            + [whole] * 12,
            out_specs=[slot] * 2 + [whole] * 9,
        ),
        out_shape=[
            jax.ShapeDtypeStruct((3, half, width), BF),
            jax.ShapeDtypeStruct((3, half, width), F32),
        ]
        + [jax.ShapeDtypeStruct(shape, F32) for shape in shapes],
        compiler_params=pltpu.CompilerParams(vmem_limit_bytes=VMEM_LIMIT),
    )(lax.axis_index("seq")[None], out, out_far, grad_own, grad_far, *parts)


BACK_PLAN = [False, True, False, False, False]
BACK_TABLE = {
    2: [(2, 0), (3, 0), (4, 0)],
    3: [(1, 2)],
    5: [(0, 2)],
    6: [(1, 3)],
    7: [(0, 3), (1, 4), (2, 1)],
    9: [(0, 4), (1, 5)],
    11: [(3, 1)],
    12: [(2, 2)],
    14: [(2, 3), (4, 1)],
    15: [(3, 2)],
    16: [(2, 4)],
    17: [(3, 3), (4, 2)],
    18: [(3, 4), (4, 3), (4, 4)],
}


def solution(mesh):
    on_device = pair_plan if mesh.shape["seq"] == 2 and mesh.shape["batch"] == 16 else ring_plan
    return jax.shard_map(
        on_device,
        mesh=mesh,
        in_specs=(
            P("batch", "seq", None),
            P("batch"),
            P("batch"),
            P("batch", "seq"),
            P(),
            P(),
            P(),
            P(),
            P(),
            P(),
            P(),
            P(),
            P("batch", "seq", None),
        ),
        out_specs=(
            P("batch", "seq", None),
            P("batch", "seq", None),
            P(None, "batch"),
            P(None, "batch"),
            P("batch"),
            P(None, "batch"),
            P(None, "batch"),
            P(None, "batch"),
            P("batch"),
            P(None, "batch"),
            P(None, "batch"),
        ),
        check_vma=False,
    )
```

```python
from functools import partial
import math

import jax
import jax.numpy as jnp
from jax import lax
from jax.experimental import pallas as pl
from jax.experimental.pallas import tpu as pltpu
from jax.sharding import PartitionSpec as P

H = 12
DH = 64
TCH = 128


TOP_PRECISION = lax.Precision.HIGHEST


def from_behind(array, axis, by):
    count = lax.axis_size(axis)
    return lax.ppermute(array, axis, [(i, (i + by) % count) for i in range(count)])


def shortened(array):

    def short(part):
        return part.astype(jnp.bfloat16) if part.dtype == jnp.float32 else part

    return jax.tree.map(short, array)


def sinusoid(steps):
    half_width = TCH // 2
    frequency = jnp.exp(
        -math.log(10000.0) * jnp.arange(half_width).astype(jnp.float32) / half_width
    )
    angles = steps.astype(jnp.float32)[:, None] * frequency[None, :]
    return jnp.concatenate([jnp.cos(angles), jnp.sin(angles)], axis=-1)


def layer_norm(hidden, gain):
    centered = hidden - jnp.mean(hidden, axis=-1, keepdims=True)
    variance = jnp.mean(centered * centered, axis=-1, keepdims=True)
    return centered * lax.rsqrt(variance + 1e-05) * gain


def time_mlp(time_embedding, time_first_weight, time_second_weight):
    pre_act = jnp.dot(time_embedding, time_first_weight, precision=TOP_PRECISION)
    return jnp.dot(jax.nn.silu(pre_act), time_second_weight, precision=TOP_PRECISION)


def row_product(left, right):
    return lax.dot_general(
        left, right, (((0,), (0,)), ((), ())), preferred_element_type=jnp.float32
    )


def back_product(left, right):
    return lax.dot_general(
        left, right, (((1,), (1,)), ((), ())), preferred_element_type=jnp.float32
    )


def masked_scores(queries, key_block, mask_block, scale_factor):
    attention_scores = (
        jnp.einsum("sqhd,skhd->shqk", queries, key_block, preferred_element_type=jnp.float32)
        * scale_factor
    )
    return jnp.where(mask_block[:, None, None, :] > 0.5, attention_scores, -1000000000.0)


def ring_plan(
    inputs,
    timesteps,
    counts,
    slot_token_mask,
    time_first_weight,
    time_second_weight,
    attention_norm_gain,
    query_key_value_weight,
    attention_output_weight,
    feedforward_norm_gain,
    up_projection_weight,
    down_projection_weight,
    cotangent,
):
    present_slots, local_len, width = inputs.shape
    total_rows = present_slots * local_len
    scale_factor = 1.0 / math.sqrt(DH)
    slot_alive_flags = (
        (jnp.arange(present_slots)[:, None] < counts[0]) & (slot_token_mask == 1)
    ).astype(jnp.float32)
    time_embedding = sinusoid(timesteps)
    time_vec, time_back = jax.vjp(
        partial(time_mlp, time_embedding),
        time_first_weight.astype(jnp.float32),
        time_second_weight.astype(jnp.float32),
    )
    residual = inputs.astype(jnp.float32) + time_vec[:, None, :]
    normed, norm_back = jax.vjp(layer_norm, residual, attention_norm_gain)
    normed_low = normed.astype(jnp.bfloat16).reshape(total_rows, width)
    packed = (
        jnp.dot(normed_low, query_key_value_weight, preferred_element_type=jnp.float32)
        .astype(jnp.bfloat16)
        .reshape(present_slots, local_len, 3 * width)
    )
    queries = packed[:, :, :width].reshape(present_slots, local_len, H, DH)
    key_rows = packed[:, :, width : 2 * width]
    value_rows = packed[:, :, 2 * width :]
    key_valid_mask = slot_alive_flags.astype(jnp.bfloat16)
    initial_state = (
        jnp.full((present_slots, H, local_len), -1e30, jnp.float32),
        jnp.zeros((present_slots, H, local_len), jnp.float32),
        jnp.zeros((present_slots, local_len, H, DH), jnp.float32),
    )
    key_piece = lax.all_gather(key_rows, "seq", axis=1, tiled=True)
    value_piece = lax.all_gather(value_rows, "seq", axis=1, tiled=True)
    mask_piece = lax.all_gather(key_valid_mask, "seq", axis=1, tiled=True)
    piece_len = key_piece.shape[1]
    block_len = min(piece_len, local_len)

    def one_block(position, inner_state):
        run_max, run_sum, running_totals = inner_state
        offset = position * block_len
        key_block = lax.dynamic_slice_in_dim(key_piece, offset, block_len, 1).reshape(
            present_slots, block_len, H, DH
        )
        value_block = lax.dynamic_slice_in_dim(value_piece, offset, block_len, 1).reshape(
            present_slots, block_len, H, DH
        )
        mask_block = lax.dynamic_slice_in_dim(mask_piece, offset, block_len, 1)
        attention_scores = masked_scores(queries, key_block, mask_block, scale_factor)
        new_max = jnp.maximum(run_max, jnp.max(attention_scores, axis=-1))
        exponent = jnp.exp(attention_scores - new_max[..., None])
        fading = jnp.exp(run_max - new_max)
        run_sum = run_sum * fading + jnp.sum(exponent, axis=-1)
        running_totals = running_totals * jnp.transpose(fading, (0, 2, 1))[..., None] + jnp.einsum(
            "shqk,skhd->sqhd",
            exponent.astype(jnp.bfloat16),
            value_block,
            preferred_element_type=jnp.float32,
        )
        return (new_max, run_sum, running_totals)

    run_max, run_sum, running_totals = lax.fori_loop(
        0, piece_len // block_len, one_block, initial_state
    )
    attended = running_totals / jnp.transpose(run_sum, (0, 2, 1))[..., None]
    log_total = run_max + jnp.log(run_sum)
    attended_low = attended.astype(jnp.bfloat16).reshape(total_rows, width)
    middle = residual + jnp.dot(
        attended_low, attention_output_weight, preferred_element_type=jnp.float32
    ).reshape(present_slots, local_len, width)
    normed_two, norm_two_back = jax.vjp(layer_norm, middle, feedforward_norm_gain)
    normed_two_low = normed_two.astype(jnp.bfloat16).reshape(total_rows, width)
    gate_pre = jnp.dot(normed_two_low, up_projection_weight, preferred_element_type=jnp.float32)
    activated, gelu_back = jax.vjp(partial(jax.nn.gelu, approximate=True), gate_pre)
    activated_low = activated.astype(jnp.bfloat16)
    completed_groups = middle + jnp.dot(
        activated_low, down_projection_weight, preferred_element_type=jnp.float32
    ).reshape(present_slots, local_len, width)
    output = (slot_alive_flags[..., None] * completed_groups).astype(jnp.bfloat16)
    final_gradient = slot_alive_flags[..., None] * cotangent.astype(jnp.float32)
    grad_down_low = final_gradient.reshape(total_rows, width).astype(jnp.bfloat16)
    down_grad = row_product(activated_low, grad_down_low)
    grad_gate = gelu_back(back_product(grad_down_low, down_projection_weight))[0].astype(
        jnp.bfloat16
    )
    up_grad = row_product(normed_two_low, grad_gate)
    grad_middle_norm, mlp_gain_grad = norm_two_back(
        back_product(grad_gate, up_projection_weight).reshape(present_slots, local_len, width)
    )
    grad_middle = final_gradient + grad_middle_norm
    grad_branch_low = grad_middle.reshape(total_rows, width).astype(jnp.bfloat16)
    out_grad = row_product(attended_low, grad_branch_low)
    grad_attended = (
        back_product(grad_branch_low, attention_output_weight)
        .astype(jnp.bfloat16)
        .reshape(present_slots, local_len, H, DH)
    )
    row_delta = jnp.transpose(
        jnp.sum(grad_attended.astype(jnp.float32) * attended, axis=-1), (0, 2, 1)
    )

    def key_terms(key_block, value_block, mask_block):
        attention_scores = masked_scores(queries, key_block, mask_block, scale_factor)
        probability = jnp.exp(attention_scores - log_total[..., None])
        grad_probs = jnp.einsum(
            "sqhd,skhd->shqk", grad_attended, value_block, preferred_element_type=jnp.float32
        )
        grad_scores = (probability * (grad_probs - row_delta[..., None])).astype(jnp.bfloat16)
        query_add = (
            jnp.einsum(
                "shqk,skhd->sqhd", grad_scores, key_block, preferred_element_type=jnp.float32
            )
            * scale_factor
        )
        key_add = (
            jnp.einsum("shqk,sqhd->skhd", grad_scores, queries, preferred_element_type=jnp.float32)
            * scale_factor
        )
        value_add = jnp.einsum(
            "shqk,sqhd->skhd",
            probability.astype(jnp.bfloat16),
            grad_attended,
            preferred_element_type=jnp.float32,
        )
        block_len = key_block.shape[1]
        return (
            query_add,
            key_add.reshape(present_slots, block_len, width),
            value_add.reshape(present_slots, block_len, width),
        )

    cycle_len = lax.axis_size("seq")
    query_zeros = jnp.zeros((present_slots, local_len, H, DH), jnp.float32)

    def visit(visit_index, loop_state):
        grad_queries, visiting, carried = loop_state
        query_add, key_add, value_add = key_terms(
            visiting[0].reshape(present_slots, local_len, H, DH),
            visiting[1].reshape(present_slots, local_len, H, DH),
            visiting[2],
        )
        carried = (carried[0] + key_add, carried[1] + value_add)
        visiting = from_behind((visiting[0], visiting[1], visiting[2]), "seq", 1)
        carried = (
            from_behind(carried[0].astype(jnp.bfloat16), "seq", 1).astype(jnp.float32),
            from_behind(carried[1].astype(jnp.bfloat16), "seq", 1).astype(jnp.float32),
        )
        return (grad_queries + query_add, tuple(visiting), tuple(carried))

    zeros_kv = jnp.zeros((present_slots, local_len, width), jnp.float32)
    grad_queries, visiting, carried = lax.fori_loop(
        0,
        cycle_len,
        visit,
        (query_zeros, (key_rows, value_rows, key_valid_mask), (zeros_kv, zeros_kv)),
    )
    grad_keys, grad_values = carried
    grad_packed = (
        jnp.concatenate(
            [grad_queries.reshape(present_slots, local_len, width), grad_keys, grad_values], axis=-1
        )
        .astype(jnp.bfloat16)
        .reshape(total_rows, 3 * width)
    )
    qkv_grad = row_product(normed_low, grad_packed)
    query_key_grad = qkv_grad[:, : 2 * width]
    value_grad = qkv_grad[:, 2 * width :]
    grad_start_norm, attn_gain_grad = norm_back(
        back_product(grad_packed, query_key_value_weight).reshape(present_slots, local_len, width)
    )
    grad_start = grad_middle + grad_start_norm
    inner_grad, outer_grad = time_back(jnp.sum(grad_start, axis=1))
    shares = (
        lax.psum_scatter(
            inner_grad.astype(jnp.bfloat16), "batch", scatter_dimension=1, tiled=True
        ).astype(jnp.float32),
        lax.psum_scatter(
            outer_grad.astype(jnp.bfloat16), "batch", scatter_dimension=1, tiled=True
        ).astype(jnp.float32),
        lax.psum_scatter(
            attn_gain_grad[None, :].astype(jnp.bfloat16), "batch", scatter_dimension=1, tiled=True
        ).astype(jnp.float32),
        lax.psum_scatter(
            query_key_grad.astype(jnp.bfloat16), "batch", scatter_dimension=1, tiled=True
        ).astype(jnp.float32),
        lax.psum_scatter(
            value_grad.astype(jnp.bfloat16), "batch", scatter_dimension=1, tiled=True
        ).astype(jnp.float32),
        lax.psum_scatter(
            out_grad.astype(jnp.bfloat16), "batch", scatter_dimension=1, tiled=True
        ).astype(jnp.float32),
        lax.psum_scatter(
            mlp_gain_grad[None, :].astype(jnp.bfloat16), "batch", scatter_dimension=1, tiled=True
        ).astype(jnp.float32),
        lax.psum_scatter(
            up_grad.astype(jnp.bfloat16), "batch", scatter_dimension=1, tiled=True
        ).astype(jnp.float32),
        lax.psum_scatter(
            down_grad.astype(jnp.bfloat16), "batch", scatter_dimension=1, tiled=True
        ).astype(jnp.float32),
    )
    summed = tuple(
        jax.tree.map(
            lambda part: part.astype(jnp.float32), lax.psum(shortened(tuple(shares)), "seq")
        )
    )
    return (
        output,
        grad_start,
        summed[0],
        summed[1],
        summed[2][0],
        summed[3],
        summed[4],
        summed[5],
        summed[6][0],
        summed[7],
        summed[8],
    )


BF = jnp.bfloat16
F32 = jnp.float32
MASKED = -1e9
GELU_A = 0.7978845608028654
GELU_B = 0.044715
VMEM_LIMIT = 62 * 2**20


def mm(left, right, left_dim, right_dim):
    return lax.dot_general(
        left, right, (((left_dim,), (right_dim,)), ((), ())), preferred_element_type=F32
    )


def attend_kernel(
    counts_ref, steps_ref, x_hbm, mask_hbm, cot_hbm, w1_ref, w2_ref, gain_ref, w_ref,
    o_ref, exact_ref, inv_ref, even_ref, odd_ref, live_ref, temb_ref, emb_ref, u_ref,
    q_hbm, kv_hbm, n1_hbm, xs_hbm, dm_hbm,
    xs, n1, q, kv, dm, mask, mask_far, bias, live, sems, send, receive,
    keys, query, v_even, v_odd, s_even, s_odd, m_even, m_odd,
):
    step = pl.program_id(0)
    last = pl.num_programs(0) - 1
    piece, width = xs.shape[0] // 4, xs.shape[1]
    length = 2 * piece
    lane = lax.broadcasted_iota(jnp.int32, (1, 128), 1)
    now = jnp.minimum(step, last - 1)
    before = jnp.maximum(step - 1, 0)
    me, seq = lax.axis_index("batch"), lax.axis_index("seq")
    blocks = [pl.ds(piece * i, piece) for i in range(4)]

    def to_partner(k, source, target):
        return pltpu.make_async_remote_copy(
            src_ref=source,
            dst_ref=target,
            send_sem=send.at[k],
            recv_sem=receive.at[k],
            device_id=(me, 1 - seq),
            device_id_type=pl.DeviceIdType.MESH,
        )

    x_one = to_partner(0, x_hbm.at[1 - seq], xs.at[blocks[1]])
    x_two = to_partner(1, x_hbm.at[2], xs.at[blocks[3]])
    cot_one = to_partner(2, cot_hbm.at[1 - seq], dm.at[blocks[1]])
    mask_there = to_partner(3, mask_hbm, mask_far)
    own = [
        pltpu.make_async_copy(x_hbm.at[seq], xs.at[blocks[0]], sems.at[0]),
        pltpu.make_async_copy(x_hbm.at[2], xs.at[blocks[2]], sems.at[1]),
        pltpu.make_async_copy(mask_hbm, mask, sems.at[2]),
        pltpu.make_async_copy(cot_hbm.at[seq], dm.at[blocks[0]], sems.at[3]),
        pltpu.make_async_copy(cot_hbm.at[2], dm.at[blocks[2]], sems.at[4]),
    ]
    keep_early = [
        pltpu.make_async_copy(q, q_hbm, sems.at[5]),
    ]
    keep_late = [
        pltpu.make_async_copy(kv, kv_hbm, sems.at[6]),
        pltpu.make_async_copy(n1, n1_hbm, sems.at[7]),
        pltpu.make_async_copy(xs, xs_hbm, sems.at[8]),
    ]
    keep_dm = pltpu.make_async_copy(dm, dm_hbm, sems.at[9])

    def project(i, with_queries):
        part = blocks[i]
        h = xs[part, :].astype(F32) + temb_ref[i // 2 : i // 2 + 1, :]
        centered = h - jnp.mean(h, axis=1, keepdims=True)
        variance = jnp.mean(centered * centered, axis=1, keepdims=True)
        normed = (centered * lax.rsqrt(variance + 1e-5) * gain_ref[...]).astype(BF)
        n1[part, :] = normed
        if with_queries:
            q[part, :] = (mm(normed, w_ref[:, :width], 1, 0) * 0.125).astype(BF)
        kv[part, :] = mm(normed, w_ref[:, width:], 1, 0).astype(BF)

    def lives(ref):
        rows = lax.broadcasted_iota(jnp.int32, (8, piece), 0)
        held = jnp.concatenate([ref[...], jnp.zeros((5, piece), jnp.int32)], axis=0)
        flags = jnp.where((held == 1) & (rows < counts_ref[0]), 1.0, 0.0)
        return flags.T

    def set_live(i, column):
        live[blocks[i], :] = jnp.broadcast_to(column, (piece, 128)).astype(BF)
        masked = jnp.where(lane == 0, MASKED, 0.0)
        bias[blocks[i], :] = jnp.where(column > 0.5, 0.0, masked).astype(BF)

    def mine(columns):
        return jnp.where(seq == 0, columns[:, 0:1], columns[:, 1:2])

    @pl.when(step == 0)
    def _():
        for copy in own:
            copy.start()
        greet_x()
        mask_there.start()
        x_one.start()
        row = lax.broadcasted_iota(jnp.int32, (8, 1), 0)
        times = jnp.where(
            row == 0, steps_ref[0], jnp.where(row == 1, steps_ref[1], steps_ref[2])
        ).astype(F32)
        half_width = TCH // 2
        column = lax.broadcasted_iota(jnp.int32, (1, TCH), 1)
        index = jnp.where(column < half_width, column, column - half_width).astype(F32)
        angles = times * jnp.exp(-math.log(10000.0) * index / half_width)
        emb = jnp.where(column < half_width, jnp.cos(angles), jnp.sin(angles))
        emb = jnp.where(row < 3, emb, 0.0)

        def exact_product(left, right):
            return lax.dot_general(
                left, right.astype(F32), (((1,), (0,)), ((), ())),
                precision=TOP_PRECISION, preferred_element_type=F32,
            )

        u = exact_product(emb, w1_ref[...])
        temb = exact_product(u / (1.0 + jnp.exp(-u)), w2_ref[...])
        emb_ref[...] = emb
        u_ref[...] = u
        temb_ref[0:1, :] = jnp.where(seq == 0, temb[0:1], temb[1:2])
        temb_ref[1:2, :] = temb[2:3]
        temb_ref[2:8, :] = jnp.zeros((6, width), F32)
        for copy in own[:3]:
            copy.wait()
        columns = lives(mask)
        set_live(0, mine(columns))
        set_live(2, columns[:, 2:3])
        project(0, True)
        project(2, True)
        for copy in own[3:]:
            copy.wait()
        dm[blocks[0], :] *= live[blocks[0], 0:1]
        dm[blocks[2], :] *= live[blocks[2], 0:1]
        mask_there.wait()
        columns = lives(mask_far)
        set_live(1, mine(columns))
        set_live(3, columns[:, 2:3])
        live_ref[...] = live[pl.ds(0, 3 * piece), :]
        x_one.wait()
        x_two.start()
        project(1, True)
        for copy in keep_early:
            copy.start()

    @pl.when(step == 8)
    def _():
        x_two.wait()
        cot_one.start()
        project(3, False)
        for copy in keep_late:
            copy.start()

    @pl.when(step == last)
    def _():
        cot_one.wait()
        dm[blocks[1], :] *= live[blocks[1], 0:1]
        keep_dm.start()

    query_rows = pl.ds(pl.multiple_of((now // 6) * piece, piece), piece)
    key_rows = pl.ds(pl.multiple_of((now // 12) * length, length), length)
    pair_lanes = pl.ds(pl.multiple_of((now % 6) * 128, 128), 128)
    value_lanes = pl.ds(pl.multiple_of(width + (now % 6) * 128, 128), 128)

    @pl.when(step % 6 == 0)
    def _():
        keys[:, 128:] = bias[key_rows, :]
        query[:, 128:] = jnp.where(
            lax.broadcasted_iota(jnp.int32, (piece, 128), 1) == 0, 1.0, 0.0
        ).astype(BF)
        v_even[64:, :] = jnp.ones((16, length), BF)
        v_odd[64:, :] = jnp.ones((16, length), BF)

    keys[:, :128] = kv[key_rows, pair_lanes]

    def half(head, made, made_max, used, used_max, values, at, out_ref):
        query[:, :128] = jnp.where((lane // 64) == head, q[query_rows, pair_lanes], jnp.zeros((), BF))
        top = used_max[0:1, :]
        scores = mm(keys[...], query[...], 1, 1)
        weight = jnp.exp(used[...] - top).astype(BF)
        made[...] = scores
        made_max[...] = jnp.broadcast_to(jnp.max(scores, axis=0, keepdims=True), made_max.shape)
        out_ref[0] = weight
        total = mm(values[...], weight, 1, 0)
        inverse = 1.0 / total[64:65]
        place = pl.ds(pl.multiple_of((at // 6) * piece, piece), piece)
        which = 2 * (at % 6) + 1 - head
        exact = total[:64] * inverse
        o_ref[which, :, place] = exact.astype(BF)
        exact_ref[which, :, place] = exact
        inv_ref[which, :, place] = jnp.broadcast_to(inverse, (8, piece))

    half(0, s_even, m_even, s_odd, m_odd, v_odd, before, odd_ref)
    turned = kv[key_rows, value_lanes].T
    v_even[:64, :] = turned[:64]
    v_odd[:64, :] = turned[64:]
    half(1, s_odd, m_odd, s_even, m_even, v_even, now, even_ref)

    @pl.when(step == last)
    def _():
        for copy in keep_early + keep_late + [keep_dm]:
            copy.wait()


def greet_x():
    partner = (lax.axis_index("batch"), 1 - lax.axis_index("seq"))
    barrier = pltpu.get_barrier_semaphore()
    pl.semaphore_signal(barrier, inc=1, device_id=partner, device_id_type=pl.DeviceIdType.MESH)
    pl.semaphore_wait(barrier, 1)


def attend(counts, timesteps, x, mask, cot, w1, w2, gain, w):
    _, piece, width = x.shape
    length = 2 * piece
    rows = 3 * piece
    steps = 18
    hidden = w1.shape[1]
    whole = pl.BlockSpec(memory_space=pltpu.VMEM)
    scalars = pl.BlockSpec(memory_space=pltpu.SMEM)
    anywhere = pl.BlockSpec(memory_space=pl.ANY)
    return pl.pallas_call(
        attend_kernel,
        grid=(steps + 1,),
        in_specs=[scalars] * 2 + [anywhere] * 3 + [whole] * 4,
        out_specs=[
            whole,
            whole,
            whole,
            pl.BlockSpec((1, length, piece), lambda t: (jnp.minimum(t, steps - 1), 0, 0)),
            pl.BlockSpec((1, length, piece), lambda t: (jnp.maximum(t - 1, 0), 0, 0)),
        ]
        + [whole] * 4
        + [anywhere] * 5,
        out_shape=[
            jax.ShapeDtypeStruct((H, DH, rows), BF),
            jax.ShapeDtypeStruct((H, DH, rows), F32),
            jax.ShapeDtypeStruct((H, 8, rows), F32),
            jax.ShapeDtypeStruct((steps, length, piece), BF),
            jax.ShapeDtypeStruct((steps, length, piece), BF),
            jax.ShapeDtypeStruct((rows, 128), BF),
            jax.ShapeDtypeStruct((8, width), F32),
            jax.ShapeDtypeStruct((8, TCH), F32),
            jax.ShapeDtypeStruct((8, hidden), F32),
            jax.ShapeDtypeStruct((rows, width), BF),
            jax.ShapeDtypeStruct((4 * piece, 2 * width), BF),
            jax.ShapeDtypeStruct((4 * piece, width), BF),
            jax.ShapeDtypeStruct((4 * piece, width), BF),
            jax.ShapeDtypeStruct((rows, width), BF),
        ],
        scratch_shapes=[
            pltpu.VMEM((4 * piece, width), BF),
            pltpu.VMEM((4 * piece, width), BF),
            pltpu.VMEM((rows, width), BF),
            pltpu.VMEM((4 * piece, 2 * width), BF),
            pltpu.VMEM((rows, width), BF),
            pltpu.VMEM((3, piece), jnp.int32),
            pltpu.VMEM((3, piece), jnp.int32),
            pltpu.VMEM((4 * piece, 128), BF),
            pltpu.VMEM((4 * piece, 128), BF),
            pltpu.SemaphoreType.DMA((10,)),
            pltpu.SemaphoreType.DMA((4,)),
            pltpu.SemaphoreType.DMA((4,)),
            pltpu.VMEM((length, 256), BF),
            pltpu.VMEM((piece, 256), BF),
            pltpu.VMEM((80, length), BF),
            pltpu.VMEM((80, length), BF),
            pltpu.VMEM((length, piece), F32),
            pltpu.VMEM((length, piece), F32),
            pltpu.VMEM((8, piece), F32),
            pltpu.VMEM((8, piece), F32),
        ],
        compiler_params=pltpu.CompilerParams(
            vmem_limit_bytes=VMEM_LIMIT, collective_id=4, has_side_effects=True
        ),
        cost_estimate=pl.CostEstimate(flops=20 * 10**9, bytes_accessed=60 * 10**6, transcendentals=19 * 10**6),
    )(counts, timesteps, x, mask, cot, w1, w2, gain, w)


def place_of(pair):
    return 4 * (pair & 1) + 2 * (pair >> 1 & 1) + (pair >> 2)


class Shares:
    def __init__(self, source, scratch, x_second):
        self.source = source
        self.x_second = x_second
        self.names = ["core", "rows", "y", "z", "join", "out"] if x_second else ["core", "y", "z", "x", "out"]
        self.acc, self.final, self.send, self.receive = scratch[0], scratch[1], scratch[-2], scratch[-1]
        boxes = [name for name in self.names if name not in ("join", "out")]
        self.inbox = dict(zip(boxes, scratch[2:-2]))
        me, far = lax.axis_index("batch"), lax.axis_index("seq")
        self.core, self.y, self.z0, self.z1 = [(me >> bit) & 1 for bit in range(4)]
        self.me, self.far = me, far
        self.half = self.acc.shape[2]
        rows = self.acc.shape[1]
        self.rows = slice(0, rows)
        if x_second:
            self.rows = pl.ds(pl.multiple_of(far * (rows // 2), 16), rows // 2)
            self.other_rows = pl.ds(pl.multiple_of((1 - far) * (rows // 2), 16), rows // 2)
        self.own = 4 * self.y + 2 * self.z0 + self.z1

    def partner(self, name):
        if name in ("x", "rows", "join"):
            return (self.me, 1 - self.far)
        return (self.me ^ {"core": 1, "y": 2, "out": 1}[name], self.far)

    def ends(self, name):
        acc, rows = self.acc, self.rows
        if name == "core":
            away = pl.multiple_of((1 - self.core) * self.half, 128)
            return self.source.at[:, :, pl.ds(away, self.half)], self.inbox[name]
        if name == "rows":
            return acc.at[:, self.other_rows], self.inbox[name]
        if name == "y":
            return acc.at[pl.ds(4 * (1 - self.y), 4), rows], self.inbox[name]
        if name == "x":
            return acc.at[self.own], self.inbox[name]
        if name == "join":
            return self.final.at[self.core, rows], self.final.at[self.core, rows]
        return self.final.at[self.core], self.final.at[self.core]

    def copies(self, stage):
        name = self.names[stage]
        if name != "z":
            here, there = self.ends(name)
            return [self.remote(stage, here, there, self.partner(name))]
        made = []
        for k in range(3):
            flip0, flip1 = (k + 1) & 1, (k + 1) >> 1
            z0 = 1 - self.z0 if flip0 else self.z0
            z1 = 1 - self.z1 if flip1 else self.z1
            here = self.acc.at[4 * self.y + 2 * z0 + z1, self.rows]
            other = (self.me ^ (4 * flip0 + 8 * flip1), self.far)
            made.append(self.remote(stage if k == 0 else 7 + k, here, self.inbox[name].at[k], other))
        return made

    def remote(self, which, here, there, other):
        return pltpu.make_async_remote_copy(
            src_ref=here,
            dst_ref=there,
            send_sem=self.send.at[which],
            recv_sem=self.receive.at[which],
            device_id=other,
            device_id_type=pl.DeviceIdType.MESH,
        )

    def start(self, stage):
        for copy in self.copies(stage):
            copy.start()

    def load(self):
        mine = pl.multiple_of(self.core * self.half, 128)
        return pltpu.make_async_copy(
            self.source.at[:, :, pl.ds(mine, self.half)], self.acc, self.send.at[7]
        )

    def begin(self):
        self.start(0)
        self.load().start()

    def add(self, name):
        acc, rows = self.acc, self.rows

        def total(one, other):
            return one + other

        if name in ("core", "rows", "y"):
            first, count = {"core": (0, 8), "rows": (0, 8), "y": (4 * self.y, 4)}[name]
            if name == "core":
                rows = slice(None)
            for k in range(count):
                acc[first + k, rows] = total(acc[first + k, rows], self.inbox[name][k])
        elif name == "z":
            parts = [acc[self.own, rows]] + [self.inbox[name][k] for k in range(3)]
            parts = [part.astype(F32) for part in parts]
            summed = ((parts[0] + parts[1]) + (parts[2] + parts[3])).astype(BF)
            if self.x_second:
                self.final[self.core, rows] = summed
            else:
                acc[self.own] = summed
        elif name == "x":
            self.final[self.core] = total(acc[self.own], self.inbox[name][...])

    def end(self, stage):
        if stage == 0:
            self.load().wait()
        for copy in self.copies(stage):
            copy.wait()
        self.add(self.names[stage])

    def go_on(self, stage):
        self.end(stage)
        if stage + 1 < len(self.names):
            self.start(stage + 1)

    def fetch(self):
        return pltpu.make_async_copy(self.source, self.acc, self.send.at[7])

    def resume(self, stage):
        self.fetch().wait()
        self.start(stage)


def share_scratch(rows, columns, x_second):
    half = columns // 2
    part = rows // 2 if x_second else rows
    shapes = [(8, rows, half), (2, rows, half), (8, rows, half)]
    shapes += [(8, part, half)] if x_second else []
    shapes += [(4, part, half), (3, part, half)]
    shapes += [] if x_second else [(rows, half)]
    return [pltpu.VMEM(shape, BF) for shape in shapes] + [
        pltpu.SemaphoreType.DMA((10,)),
        pltpu.SemaphoreType.DMA((10,)),
    ]


SCRATCH_COUNT = 8


def greet():
    call()
    pl.semaphore_wait(pltpu.get_barrier_semaphore(), GREETED)


GREETED = 6


def call():
    me, far = lax.axis_index("batch"), lax.axis_index("seq")
    barrier = pltpu.get_barrier_semaphore()
    others = [(me ^ 1, far), (me ^ 2, far), (me ^ 4, far), (me ^ 8, far), (me ^ 12, far), (me, 1 - far)]
    for other in others:
        pl.semaphore_signal(barrier, inc=1, device_id=other, device_id_type=pl.DeviceIdType.MESH)


def attend_back_kernel(
    plan, table, q_ref, k_ref, v_ref, do_ref, o_ref, inv_ref, even_ref, odd_ref, *rest
):
    count = len(plan)
    w_hbm, out_hbm, *rest = rest
    sources, rest = rest[:count], rest[count:]
    width = w_hbm.shape[0]
    (dq_ref, dk_ref, dv_ref, far_ref, output_hbm), rest = rest[:5], rest[5:]
    finals, rest = rest[:count], rest[count:]
    values, gradient, dk_sum, dv_sum, far_kv, far_send, far_got, out_got, far_sems, w_kv, *rest = rest
    w_load = pltpu.make_async_copy(w_hbm.at[:, pl.ds(width, 2 * width)], w_kv, far_sems.at[5])
    shares = []
    for i in range(count):
        own = rest[SCRATCH_COUNT * i : SCRATCH_COUNT * (i + 1)]
        shares.append(Shares(sources[i], own, plan[i]))
    step = pl.program_id(0)
    steps = pl.num_programs(0)
    pair, part = back_place(step)
    piece, length = q_ref.shape[0], k_ref.shape[0]
    lane = lax.broadcasted_iota(jnp.int32, (1, 128), 1)
    zero = jnp.zeros((), BF)
    far_copy = pltpu.make_async_remote_copy(
        src_ref=far_send,
        dst_ref=far_got,
        send_sem=far_sems.at[0],
        recv_sem=far_sems.at[1],
        device_id=(lax.axis_index("batch"), 1 - lax.axis_index("seq")),
        device_id_type=pl.DeviceIdType.MESH,
    )

    seq = lax.axis_index("seq")
    out_copy = pltpu.make_async_remote_copy(
        src_ref=out_hbm.at[pl.ds(piece, piece)],
        dst_ref=out_got,
        send_sem=far_sems.at[2],
        recv_sem=far_sems.at[3],
        device_id=(lax.axis_index("batch"), 1 - seq),
        device_id_type=pl.DeviceIdType.MESH,
    )
    returned = pltpu.make_async_copy(out_got, output_hbm, far_sems.at[4])

    @pl.when(step == 0)
    def _():
        for share in shares[:2]:
            share.fetch().start()
        w_load.start()
        greet()
        for share in shares[:2]:
            share.resume(2)
        for share in shares[2:]:
            share.begin()
        out_copy.start()
        values[:, 128:] = jnp.where(
            lax.broadcasted_iota(jnp.int32, (length, 128), 1) < 3, 1.0, 0.0
        ).astype(BF)
        gradient[...] = jnp.zeros_like(gradient)
        dk_sum[...] = jnp.zeros_like(dk_sum)
        dv_sum[...] = jnp.zeros_like(dv_sum)

    for when in sorted(table):
        if when < 18:

            @pl.when(step == when)
            def _(when=when):
                for i, stage in table[when]:
                    shares[i].go_on(stage)

    @pl.when(step == 11)
    def _():
        out_copy.wait()
        returned.start()

    @pl.when(step == 6)
    def _():
        w_load.wait()
        far_send[...] = mm(far_kv[:, : 2 * width], w_kv[...], 1, 1).astype(BF)
        far_copy.start()

    values[:, :128] = v_ref[...]
    inverse = jnp.concatenate(
        [jnp.broadcast_to(inv_ref[head, 0:1, :], (DH, piece)) for head in range(2)], axis=0
    )
    scaled = (do_ref[...].astype(F32) * inverse).astype(BF)
    product = scaled.astype(F32) * o_ref[...]
    for head in range(2):
        mine = slice(DH * head, DH * head + DH)
        place = slice(piece * head, piece * head + piece)
        delta = -jnp.sum(product[mine], axis=0, keepdims=True)
        high = delta.astype(BF).astype(F32)
        rest_of = delta - high
        middle = rest_of.astype(BF).astype(F32)
        gradient[mine, place] = scaled[mine]
        gradient[128:144, place] = jnp.concatenate(
            [high, middle, rest_of - middle, jnp.zeros((13, piece), F32)], axis=0
        ).astype(BF)
    dp = mm(values[...], gradient[...], 1, 0)
    turned_keys = k_ref[...].T
    natural = scaled.T
    weights = [even_ref[0], odd_ref[0]]
    ds = [
        (weights[head].astype(F32) * dp[:, piece * head : piece * head + piece]).astype(BF)
        for head in range(2)
    ]

    def apart(array):
        return jnp.concatenate(
            [jnp.where(lane < 64, array, zero), jnp.where(lane < 64, zero, array)], axis=0
        )

    dv = mm(jnp.concatenate(weights, axis=1), apart(natural), 1, 0)
    dk = mm(jnp.concatenate(ds, axis=1), apart(q_ref[...]), 1, 0)
    for head in range(2):
        mine = slice(DH * head, DH * head + DH)
        dq_ref[mine, :] = (mm(turned_keys[mine], ds[head], 1, 0) * 0.125).astype(BF)

    again = part == 1
    dk += jnp.where(again, dk_sum[...], 0.0)
    dv += jnp.where(again, dv_sum[...], 0.0)
    dk_sum[...] = dk
    dv_sum[...] = dv
    dk, dv = dk.astype(BF), dv.astype(BF)
    dk_ref[...] = dk
    dv_ref[...] = dv
    early = step < 6
    at = jnp.where(early, pair * 128, 2 * width)
    far_kv[:, pl.ds(pl.multiple_of(at, 128), 128)] = dk[piece:]
    at = jnp.where(early, width + pair * 128, 2 * width + 128)
    far_kv[:, pl.ds(pl.multiple_of(at, 128), 128)] = dv[piece:]

    @pl.when(step == steps - 1)
    def _():
        for when in sorted(table):
            if when >= 18:
                for i, stage in table[when]:
                    shares[i].go_on(stage)
        for i in range(count):
            finals[i][...] = shares[i].final[...]
        far_copy.wait()
        far_ref[...] = far_got[...]
        returned.wait()


def back_place(step):
    late = jnp.maximum(step - 6, 0)
    return jnp.where(step < 6, step, late // 2), jnp.where(step < 6, 2, late % 2)


def attend_back(q, kv, do, o, inv, even, odd, w, out, partials, plan, table):
    rows, width = q.shape
    length = 2 * rows // 3
    piece = rows // 3

    def spec(shape, index):
        return pl.BlockSpec(shape, lambda t: index(*back_place(t)))

    weight_spec = spec((1, length, piece), lambda p, j: (j * 6 + p, 0, 0))
    scratch = []
    sizes = [(a.shape[1], a.shape[2] * (2 if i < 2 else 1)) for i, a in enumerate(partials)]
    for size, x_second in zip(sizes, plan):
        scratch += share_scratch(*size, x_second)
    whole = pl.BlockSpec(memory_space=pltpu.VMEM)
    return pl.pallas_call(
        partial(attend_back_kernel, plan, table),
        grid=(18,),
        in_specs=[
            spec((piece, 128), lambda p, j: (j, p)),
            spec((length, 128), lambda p, j: (j // 2, p)),
            spec((length, 128), lambda p, j: (j // 2, 6 + p)),
            spec((128, piece), lambda p, j: (p, j)),
            spec((128, piece), lambda p, j: (p, j)),
            spec((2, 8, piece), lambda p, j: (p, 0, j)),
            weight_spec,
            weight_spec,
        ]
        + [pl.BlockSpec(memory_space=pl.ANY)] * (2 + len(partials)),
        out_specs=[
            spec((128, piece), lambda p, j: (p, j)),
            spec((length, 128), lambda p, j: (j // 2, p)),
            spec((length, 128), lambda p, j: (j // 2, p)),
            whole,
            pl.BlockSpec(memory_space=pl.ANY),
        ]
        + [whole] * len(partials),
        out_shape=[
            jax.ShapeDtypeStruct((width, rows), BF),
            jax.ShapeDtypeStruct((2 * length, width), BF),
            jax.ShapeDtypeStruct((2 * length, width), BF),
            jax.ShapeDtypeStruct((piece, width), BF),
            jax.ShapeDtypeStruct((piece, width), BF),
        ]
        + [jax.ShapeDtypeStruct((2, a, b // 2), BF) for a, b in sizes],
        scratch_shapes=[
            pltpu.VMEM((length, 256), BF),
            pltpu.VMEM((256, 2 * piece), BF),
            pltpu.VMEM((length, 128), F32),
            pltpu.VMEM((length, 128), F32),
            pltpu.VMEM((piece, 2 * width + 256), BF),
            pltpu.VMEM((piece, width), BF),
            pltpu.VMEM((piece, width), BF),
            pltpu.VMEM((piece, width), BF),
            pltpu.SemaphoreType.DMA((6,)),
            pltpu.VMEM((width, 2 * width), BF),
        ]
        + scratch,
        compiler_params=pltpu.CompilerParams(
            vmem_limit_bytes=VMEM_LIMIT, collective_id=1, has_side_effects=True
        ),
        cost_estimate=pl.CostEstimate(flops=30 * 10**9, bytes_accessed=60 * 10**6, transcendentals=0),
    )(q, kv, kv, do, o, inv, even, odd, w, out, *partials)


def finish_kernel(
    dq_hbm, dk_hbm, dv_hbm, n1_hbm, x_hbm, dh_hbm, w_hbm, far_ref, temb_ref, gain_ref, dgain2_ref,
    w2_ref, emb_ref, u_ref, *rest
):
    own_ref, far_out_ref, finals, rest = rest[0], rest[1], rest[2:7], rest[7:]
    dq, dk, dv, n1, x, dh, w, send, got, sems, far_sems = rest[:11]
    sources, rest = rest[11:16], rest[16:]
    shares = []
    for i in range(5):
        own = rest[SCRATCH_COUNT * i : SCRATCH_COUNT * (i + 1)]
        shares.append(Shares(sources[i], own, FINISH_PLAN[i]))
    half, width = far_ref.shape
    me, seq = lax.axis_index("batch"), lax.axis_index("seq")

    loads = {}

    def fetch(name, source, target):
        loads[name] = pltpu.make_async_copy(source, target, sems.at[len(loads)])
        loads[name].start()

    blocks = [slice(half * i, half * i + half) for i in range(4)]
    fetch("w", w_hbm, w)
    for b in (1, 0, 2):
        fetch(("dq", b), dq_hbm.at[:, blocks[b]], dq.at[:, blocks[b]])
        fetch(("dk", b), dk_hbm.at[blocks[b]], dk.at[blocks[b]])
        fetch(("dv", b), dv_hbm.at[blocks[b]], dv.at[blocks[b]])
        if b == 1:
            fetch("x", x_hbm.at[pl.ds(0, 3 * half)], x)
            fetch(("dh", 1), dh_hbm.at[blocks[1]], dh.at[blocks[1]])
    fetch(("dk", 3), dk_hbm.at[blocks[3]], dk.at[blocks[3]])
    fetch(("dv", 3), dv_hbm.at[blocks[3]], dv.at[blocks[3]])
    fetch("n1", n1_hbm, n1)
    fetch(("dh", 0), dh_hbm.at[blocks[0]], dh.at[blocks[0]])
    fetch(("dh", 2), dh_hbm.at[blocks[2]], dh.at[blocks[2]])
    back_copy = pltpu.make_async_remote_copy(
        src_ref=send,
        dst_ref=got,
        send_sem=far_sems.at[0],
        recv_sem=far_sems.at[1],
        device_id=(me, 1 - seq),
        device_id_type=pl.DeviceIdType.MESH,
    )
    greet()

    def norm_back(b, more):
        loads[("dh", b)].wait()
        part = blocks[b]
        dn = mm(dq[:, part], w[:, :width], 0, 1)
        dn += mm(dk[part, :], w[:, width : 2 * width], 1, 1)
        dn += mm(dv[part, :], w[:, 2 * width :], 1, 1)
        if more is not None:
            dn += more[...].astype(F32)
        h = x[part, :].astype(F32) + temb_ref[b // 2 : b // 2 + 1, :]
        centered = h - jnp.mean(h, axis=1, keepdims=True)
        r1 = lax.rsqrt(jnp.mean(centered * centered, axis=1, keepdims=True) + 1e-5)
        x1 = centered * r1
        e = dn * gain_ref[...]
        dh0 = dh[part, :] + r1 * (
            e - jnp.mean(e, axis=1, keepdims=True) - x1 * jnp.mean(e * x1, axis=1, keepdims=True)
        )
        return dh0, jnp.sum(dh0, axis=0, keepdims=True), jnp.sum(dn * x1, axis=0, keepdims=True)

    def weight_piece(f):
        columns = slice(256 * f, 256 * f + 256)
        q_part = mm(dq[...], n1[: 3 * half, columns], 1, 0).astype(BF)
        k_part = mm(dk[...], n1[:, columns], 0, 0).astype(BF)
        v_part = mm(dv[...], n1[:, columns], 0, 0).astype(BF)
        pair_rows = width // 4
        for k in range(8):
            source = q_part if k < 4 else k_part
            first = pair_rows * (k % 4)
            sources[f][place_of(k), :pair_rows, :] = source[first : first + pair_rows]
            first = width // 8 * k
            sources[f][place_of(k), pair_rows:, :] = v_part[first : first + width // 8]
        shares[f].begin()

    for name in loads:
        if name[0] != "dh":
            loads[name].wait()
    weight_piece(0)
    weight_piece(1)
    shares[0].go_on(0)
    weight_piece(2)
    shares[1].go_on(0)
    dh0, dtemb_a, dgain_a = norm_back(1, None)
    send[...] = dh0.astype(BF)
    back_copy.start()
    shares[2].go_on(0)
    dh0, dtemb_b, dgain_b = norm_back(0, None)
    own_ref[0] = dh0
    shares[0].go_on(1)
    dh0, dtemb_two, dgain_c = norm_back(2, far_ref)
    own_ref[1] = dh0

    dtemb_one = dtemb_a + dtemb_b
    first = (seq == 0).astype(F32)
    dtemb = jnp.concatenate(
        [first * dtemb_one, (1.0 - first) * dtemb_one, dtemb_two, jnp.zeros((5, width), F32)], axis=0
    )
    u = u_ref[...]
    sigmoid = 1.0 / (1.0 + jnp.exp(-u))
    outer = lax.dot_general(
        dtemb, u * sigmoid, (((0,), (0,)), ((), ())), precision=TOP_PRECISION, preferred_element_type=F32
    ).astype(BF)
    dsilu = lax.dot_general(
        dtemb, w2_ref[...].astype(F32), (((1,), (1,)), ((), ())), precision=TOP_PRECISION, preferred_element_type=F32
    )
    dpre = dsilu * (sigmoid * (1.0 + u * (1.0 - sigmoid)))
    inner = lax.dot_general(
        dpre, emb_ref[...], (((0,), (0,)), ((), ())), precision=TOP_PRECISION, preferred_element_type=F32
    ).astype(BF)
    dgain = dgain_a + dgain_b + dgain_c
    size, inner_size = width // 8, inner.shape[0] // 8
    sources[4][...] = jnp.zeros_like(sources[4])
    for k in range(8):
        sources[3][place_of(k)] = outer[size * k : size * k + size]
        sources[4][place_of(k), :, :128] = inner[inner_size * k : inner_size * k + inner_size]
        both = jnp.concatenate(
            [
                jnp.concatenate([g[:, size * k : size * k + size], jnp.zeros((1, 128 - size), F32)], axis=1)
                for g in (dgain, dgain2_ref[...])
            ]
            + [jnp.zeros((14, 128), F32)],
            axis=0,
        )
        sources[4][place_of(k), :16, 128:] = both.astype(BF)
    shares[3].begin()
    shares[4].begin()
    for i, stage in FINISH_ORDER:
        shares[i].go_on(stage)
    for i in range(5):
        finals[i][...] = shares[i].final[...]
    back_copy.wait()
    far_out_ref[...] = got[...]


FINISH_PLAN = [False, True, False, False, False]
FINISH_ORDER = [
    (1, 1), (3, 0), (4, 0), (0, 2), (2, 1), (1, 2), (2, 2), (3, 1), (4, 1), (0, 3), (1, 3), (3, 2),
    (4, 2), (2, 3), (0, 4), (1, 4), (3, 3), (4, 3), (2, 4), (1, 5), (3, 4), (4, 4),
]


def finish(dq, dk, dv, n1, x, dh1, w, far, temb, gain, dgain2, w2, emb, u):
    half, width = far.shape
    rows = 3 * half
    hidden = w2.shape[0]
    whole = pl.BlockSpec(memory_space=pltpu.VMEM)
    sizes = [(3 * width // 8, 256)] * 3 + [(width // 8, hidden), (hidden // 8, 256)]
    scratch = [pltpu.VMEM((8,) + size, BF) for size in sizes]
    for size, x_second in zip(sizes, FINISH_PLAN):
        scratch += share_scratch(*size, x_second)
    return pl.pallas_call(
        finish_kernel,
        in_specs=[pl.BlockSpec(memory_space=pl.ANY)] * 7 + [whole] * 7,
        out_specs=[whole] * 7,
        out_shape=[
            jax.ShapeDtypeStruct((2, half, width), F32),
            jax.ShapeDtypeStruct((half, width), BF),
        ]
        + [jax.ShapeDtypeStruct((2, a, b // 2), BF) for a, b in sizes],
        scratch_shapes=[
            pltpu.VMEM((width, rows), BF),
            pltpu.VMEM((4 * half, width), BF),
            pltpu.VMEM((4 * half, width), BF),
            pltpu.VMEM((4 * half, width), BF),
            pltpu.VMEM((rows, width), BF),
            pltpu.VMEM((rows, width), F32),
            pltpu.VMEM(w.shape, BF),
            pltpu.VMEM((half, width), BF),
            pltpu.VMEM((half, width), BF),
            pltpu.SemaphoreType.DMA((20,)),
            pltpu.SemaphoreType.DMA((2,)),
        ]
        + scratch,
        compiler_params=pltpu.CompilerParams(
            vmem_limit_bytes=VMEM_LIMIT, collective_id=2, has_side_effects=True
        ),
        cost_estimate=pl.CostEstimate(flops=15 * 10**9, bytes_accessed=60 * 10**6, transcendentals=0),
    )(dq, dk, dv, n1, x, dh1, w, far, temb, gain, dgain2, w2, emb, u)


def gelu_and_slope(g):
    square = g * g
    half_plus = 0.5 * jnp.tanh(g * (GELU_A + GELU_A * GELU_B * square)) + 0.5
    act = g * half_plus
    slope = half_plus + act * (2.0 - 2.0 * half_plus) * (GELU_A + 3.0 * GELU_A * GELU_B * square)
    return act, slope


FF_BEGIN = {6: (0, 1), 12: (2, 3)}
FF_PLAN = [False, True, False, True]
FF_TICKS = {
    9: [(0, 0), (1, 0)],
    12: [(0, 1), (1, 1)],
    15: [(0, 2), (1, 2), (2, 0), (3, 0)],
    18: [(0, 3), (1, 3)],
    21: [(0, 4), (1, 4), (1, 5), (2, 1), (3, 1)],
}


def feedforward_kernel(
    x_hbm, o_ref, dm_ref, live_ref, temb_ref, gain_ref, wo_ref, *rest
):
    wu_refs, wd_refs, rest = rest[:4], rest[4:8], rest[8:]
    out_hbm, dh1_hbm, do_ref, dwu_hbm, dwd_hbm, dwo_ref, dgain_ref, *rest = rest
    finals, rest = rest[:4], rest[4:]
    finals, handed = finals[:2], finals[2:]
    x, h1, n2, h2, dn2, sems, *rest = rest
    sources, rest = rest[:4], rest[4:]
    shares = []
    for i in range(4):
        own = rest[SCRATCH_COUNT * i : SCRATCH_COUNT * (i + 1)]
        shares.append(Shares(sources[i], own, FF_PLAN[i]))
    turn, side = pl.program_id(0), pl.program_id(1)
    chunk, chunks = 2 * turn + side, 6
    wu = jnp.concatenate([ref[...] for ref in wu_refs], axis=1)
    wd = jnp.concatenate([ref[...] for ref in wd_refs], axis=0)
    rows, width = x.shape
    block = rows // 2
    third = rows // 3
    blocks = [slice(block * i, block * i + block) for i in range(2)]
    thirds = [slice(third * i, third * i + third) for i in range(3)]
    size = width // 8

    def act_on(now):
        for i, stage in FF_TICKS.get(now, []):
            if i >= 2 and stage == 1:
                shares[i].end(stage)
            else:
                shares[i].go_on(stage)
        for i in FF_BEGIN.get(now, []):
            shares[i].begin()

    def tick():
        for now in sorted(set(FF_TICKS) | set(FF_BEGIN)):
            if now < 18:
                pl.when(chunk == now // 3)(partial(act_on, now))

    load = pltpu.make_async_copy(x_hbm.at[pl.ds(0, rows)], x, sems.at[0])

    @pl.when(chunk == 0)
    def _():
        load.start()
        call()
        load.wait()
        for i, part in enumerate(thirds):
            h0 = x[part, :].astype(F32) + temb_ref[i // 2 : i // 2 + 1, :]
            h = h0 + mm(o_ref[:, part], wo_ref[...], 0, 0)
            h1[part, :] = h
            centered = h - jnp.mean(h, axis=1, keepdims=True)
            variance = jnp.mean(centered * centered, axis=1, keepdims=True)
            n2[part, :] = (centered * lax.rsqrt(variance + 1e-5) * gain_ref[...]).astype(BF)
            h2[part, :] = h
            dn2[part, :] = jnp.zeros_like(h)

    def first(part):
        return mm(n2[part, :], wu, 1, 0), mm(dm_ref[part, :], wd, 1, 1)

    def second(pair):
        act, slope = gelu_and_slope(pair[0])
        return act.astype(BF), (pair[1] * slope).astype(BF)

    def third_step(part, pair):
        h2[part, :] += mm(pair[0], wd, 1, 0)
        dn2[part, :] += mm(pair[1], wu, 1, 1)

    @pl.when(chunk == 2)
    def _():
        pl.semaphore_wait(pltpu.get_barrier_semaphore(), GREETED)

    tick()
    a = first(blocks[0])
    b = first(blocks[1])
    a = second(a)
    b = second(b)
    third_step(blocks[0], a)
    third_step(blocks[1], b)
    act = jnp.concatenate([a[0], b[0]], axis=0)
    dg = jnp.concatenate([a[1], b[1]], axis=0)
    dwd = mm(dm_ref[...], act, 0, 0).astype(BF)
    dwu = mm(dg, n2[...], 0, 0).astype(BF).reshape(4, 128, width)
    for c in range(3):
        up_to, down_to = sources[2 * (c % 2)], sources[2 * (c % 2) + 1]

        @pl.when(turn == c)
        def _(up_to=up_to, down_to=down_to):
            up_to[pl.ds(4 * side, 4)] = dwu
            for k in range(8):
                columns = pl.ds(pl.multiple_of(512 * side, 128), 512)
                down_to[place_of(k), :, columns] = dwd[size * k : size * k + size]

    @pl.when(chunk == chunks - 1)
    def _():
        act_on(18)
        dgain = jnp.zeros_like(dgain_ref)
        for i, part in enumerate(thirds):
            h = h1[part, :]
            live = live_ref[part, 0:1].astype(F32)
            x[part, :] = (live * h2[part, :]).astype(BF)
            centered = h - jnp.mean(h, axis=1, keepdims=True)
            variance = jnp.mean(centered * centered, axis=1, keepdims=True)
            r2 = lax.rsqrt(variance + 1e-5)
            x2 = centered * r2
            dn = dn2[part, :]
            dgain += jnp.sum(dn * x2, axis=0, keepdims=True)
            e = dn * gain_ref[...]
            dh1 = dm_ref[part, :].astype(F32) + r2 * (
                e
                - jnp.mean(e, axis=1, keepdims=True)
                - x2 * jnp.mean(e * x2, axis=1, keepdims=True)
            )
            h1[part, :] = dh1
            da = dh1.astype(BF)
            n2[part, :] = da
            do_ref[:, part] = mm(wo_ref[...], da, 1, 1).astype(BF)
            act_on(19 + i)
        for i in range(2):
            finals[i][...] = shares[i].final[...]
        stores = [
            pltpu.make_async_copy(x, out_hbm, sems.at[1]),
            pltpu.make_async_copy(h1, dh1_hbm, sems.at[2]),
            pltpu.make_async_copy(shares[2].acc, handed[0], sems.at[3]),
            pltpu.make_async_copy(shares[3].acc, handed[1], sems.at[4]),
            pltpu.make_async_copy(sources[0], dwu_hbm, sems.at[5]),
            pltpu.make_async_copy(sources[1], dwd_hbm, sems.at[6]),
        ]
        for store in stores:
            store.start()
        dgain_ref[...] = dgain
        dwo = mm(n2[...], o_ref[...], 0, 1).astype(BF)
        for k in range(8):
            dwo_ref[place_of(k)] = dwo[size * k : size * k + size]
        for store in stores:
            store.wait()


def feedforward(x, o, dm, live, temb, gain, wo, wu, wd):
    rows, width = dm.shape
    whole = pl.BlockSpec(memory_space=pltpu.VMEM)
    anywhere = pl.BlockSpec(memory_space=pl.ANY)

    def tile(c, h, i):
        return 3 * (4 * (i % 2) + 2 * (i // 2) + h) + c

    up_specs = [pl.BlockSpec((width, 128), lambda c, h, i=i: (0, tile(c, h, i))) for i in range(4)]
    down_specs = [pl.BlockSpec((128, width), lambda c, h, i=i: (tile(c, h, i), 0)) for i in range(4)]
    sizes = [(128, width), (width // 8, 1024)] * 2
    scratch = [pltpu.VMEM((8,) + size, BF) for size in sizes]
    for size, x_second in zip(sizes, FF_PLAN):
        scratch += share_scratch(*size, x_second)
    return pl.pallas_call(
        feedforward_kernel,
        grid=(3, 2),
        in_specs=[anywhere] + [whole] * 6 + up_specs + down_specs,
        out_specs=[anywhere] * 2 + [whole] + [anywhere] * 2 + [whole] * 4 + [anywhere] * 2,
        out_shape=[
            jax.ShapeDtypeStruct((rows, width), BF),
            jax.ShapeDtypeStruct((rows, width), F32),
            jax.ShapeDtypeStruct((width, rows), BF),
            jax.ShapeDtypeStruct((8, 128, width), BF),
            jax.ShapeDtypeStruct((8, width // 8, 1024), BF),
            jax.ShapeDtypeStruct((8, width // 8, width), BF),
            jax.ShapeDtypeStruct((1, width), F32),
        ]
        + [jax.ShapeDtypeStruct((2, a, b // 2), BF) for a, b in sizes[:2]]
        + [jax.ShapeDtypeStruct((8, a, b // 2), BF) for a, b in sizes[2:]],
        scratch_shapes=[
            pltpu.VMEM((rows, width), BF),
            pltpu.VMEM((rows, width), F32),
            pltpu.VMEM((rows, width), BF),
            pltpu.VMEM((rows, width), F32),
            pltpu.VMEM((rows, width), F32),
            pltpu.SemaphoreType.DMA((7,)),
        ]
        + scratch,
        compiler_params=pltpu.CompilerParams(
            vmem_limit_bytes=VMEM_LIMIT, collective_id=3, has_side_effects=True
        ),
        cost_estimate=pl.CostEstimate(flops=48 * 10**9, bytes_accessed=50 * 10**6, transcendentals=5 * 10**6),
    )(x, o, dm, live, temb, gain, wo, *[wu] * 4, *[wd] * 4)


def pair_plan(
    inputs,
    timesteps,
    counts,
    slot_token_mask,
    time_first_weight,
    time_second_weight,
    attention_norm_gain,
    query_key_value_weight,
    attention_output_weight,
    feedforward_norm_gain,
    up_projection_weight,
    down_projection_weight,
    cotangent,
):
    slots, half, width = inputs.shape
    batches = lax.axis_size("batch")
    (o, exact, inv, even, odd, live_wide, temb, emb, u, q, kv, n1, x, dm) = attend(
        counts,
        timesteps,
        inputs,
        slot_token_mask,
        cotangent,
        time_first_weight,
        time_second_weight,
        attention_norm_gain[None, :],
        query_key_value_weight,
    )
    o = o.reshape(width, 3 * half)
    out, dh1, do, dwu, dwd, dwo, dgain2, *early = feedforward(
        x,
        o,
        dm,
        live_wide,
        temb,
        feedforward_norm_gain[None, :],
        attention_output_weight,
        up_projection_weight,
        down_projection_weight,
    )
    dq, dk, dv, far, out_far, *sums = attend_back(
        q,
        kv,
        do,
        exact.reshape(width, 3 * half),
        inv,
        even,
        odd,
        query_key_value_weight,
        out,
        [*early[2:], dwu, dwd, dwo],
        BACK_PLAN,
        BACK_TABLE,
    )
    grad_own, grad_far, *last = finish(
        dq,
        dk,
        dv,
        n1,
        x,
        dh1,
        query_key_value_weight,
        far,
        temb,
        attention_norm_gain[None, :],
        dgain2,
        time_second_weight,
        emb,
        u,
    )
    up = [early[0], sums[0], sums[2]]
    down = [early[1], sums[1], sums[3]]
    output, grad_inputs, inner, outer, gain1, qk, v, out_sum, gain2, up, down = assemble(
        batches, out, out_far, grad_own, grad_far, up + down + [sums[4]] + last
    )
    return (
        output,
        grad_inputs,
        inner.T,
        outer.T,
        gain1[0],
        qk.T,
        v.T,
        out_sum.T,
        gain2[0],
        up.T,
        down.T,
    )


def assemble_kernel(seq_ref, out_ref, out_far_ref, grad_ref, grad_far_ref, *refs):
    ups, downs, (wo, *qkv), (outer, inner) = refs[0:3], refs[3:6], refs[6:10], refs[10:12]
    (output_to, grad_to, inner_to, outer_to, gain1_to, qk_to, v_to, out_to, gain2_to, up_to, down_to) = refs[12:]
    far = pl.program_id(0) == 1

    @pl.when(far)
    def _():
        output_to[0] = out_far_ref[...]
        grad_to[0] = grad_far_ref[...].astype(F32)

    @pl.when(jnp.logical_not(far))
    def _():
        output_to[0] = out_ref[...]
        grad_to[0] = grad_ref[0]

    core = lax.axis_index("batch") & 1

    def joined(ref):
        return jnp.concatenate([ref[0], ref[1]], axis=1)

    def own_half(array):
        size = array.shape[0] // 2
        return jnp.where(core == 0, array[:size], array[size:]).astype(F32)

    @pl.when(pl.program_id(0) == 0)
    def _():
        up_to[...] = own_half(jnp.concatenate([joined(ref) for ref in ups], axis=0))
        for c, ref in enumerate(downs):
            part = own_half(joined(ref))
            for k in range(8):
                first = 128 * place_of(k)
                down_to[:, 128 * (3 * k + c) : 128 * (3 * k + c + 1)] = part[:, first : first + 128]
        out_to[...] = own_half(joined(wo))
        whole = jnp.concatenate([joined(ref) for ref in qkv], axis=1)
        split = whole.shape[0] * 2 // 3
        qk_to[...] = own_half(whole[:split])
        v_to[...] = own_half(whole[split:])
        outer_to[...] = own_half(joined(outer))
        inner_to[...] = own_half(inner[0])
        size = gain1_to.shape[1]
        gains = inner[1, 0:16, :].astype(F32)
        for row, target in enumerate((gain1_to, gain2_to)):
            target[...] = jnp.where(
                core == 0, gains[row : row + 1, :size], gains[row : row + 1, size : 2 * size]
            )


def assemble(batches, out, out_far, grad_own, grad_far, parts):
    half, width = out_far.shape
    hidden = 4 * width
    size = width // batches
    time_hidden, channels = 2 * parts[10].shape[2], parts[11].shape[2]
    whole = pl.BlockSpec(memory_space=pltpu.VMEM)
    slot = pl.BlockSpec((1, half, width), lambda i, seq: (jnp.where(i == 1, 1 - seq[0], jnp.maximum(i, seq[0])), 0, 0))
    shapes = [
        (time_hidden // batches, channels),
        (size, time_hidden),
        (1, size),
        (2 * size, width),
        (size, width),
        (size, width),
        (1, size),
        (hidden // batches, width),
        (size, hidden),
    ]
    return pl.pallas_call(
        assemble_kernel,
        grid_spec=pltpu.PrefetchScalarGridSpec(
            num_scalar_prefetch=1,
            grid=(3,),
            in_specs=[
                pl.BlockSpec((half, width), lambda i, seq: (i // 2 * 2, 0)),
                whole,
                pl.BlockSpec((1, half, width), lambda i, seq: (i // 2, 0, 0)),
                whole,
            ]
            + [whole] * 12,
            out_specs=[slot] * 2 + [whole] * 9,
        ),
        out_shape=[
            jax.ShapeDtypeStruct((3, half, width), BF),
            jax.ShapeDtypeStruct((3, half, width), F32),
        ]
        + [jax.ShapeDtypeStruct(shape, F32) for shape in shapes],
        compiler_params=pltpu.CompilerParams(vmem_limit_bytes=VMEM_LIMIT),
    )(lax.axis_index("seq")[None], out, out_far, grad_own, grad_far, *parts)


BACK_PLAN = [False, True, False, False, False]
BACK_TABLE = {
    2: [(2, 0), (3, 0), (4, 0)],
    3: [(1, 2)],
    5: [(0, 2)],
    6: [(1, 3)],
    7: [(0, 3), (1, 4), (2, 1)],
    9: [(0, 4), (1, 5)],
    11: [(3, 1)],
    12: [(2, 2)],
    14: [(2, 3), (4, 1)],
    15: [(3, 2)],
    16: [(2, 4)],
    17: [(3, 3), (4, 2)],
    18: [(3, 4), (4, 3), (4, 4)],
}


def solution(mesh):
    on_device = pair_plan if mesh.shape["seq"] == 2 and mesh.shape["batch"] == 16 else ring_plan
    return jax.shard_map(
        on_device,
        mesh=mesh,
        in_specs=(
            P("batch", "seq", None),
            P("batch"),
            P("batch"),
            P("batch", "seq"),
            P(),
            P(),
            P(),
            P(),
            P(),
            P(),
            P(),
            P(),
            P("batch", "seq", None),
        ),
        out_specs=(
            P("batch", "seq", None),
            P("batch", "seq", None),
            P(None, "batch"),
            P(None, "batch"),
            P("batch"),
            P(None, "batch"),
            P(None, "batch"),
            P(None, "batch"),
            P("batch"),
            P(None, "batch"),
            P(None, "batch"),
        ),
        check_vma=False,
    )
```

```python
from functools import partial
import math

import jax
import jax.numpy as jnp
from jax import lax
from jax.experimental import pallas as pl
from jax.experimental.pallas import tpu as pltpu
from jax.sharding import PartitionSpec as P

H = 12
DH = 64
TCH = 128


TOP_PRECISION = lax.Precision.HIGHEST


def from_behind(array, axis, by):
    count = lax.axis_size(axis)
    return lax.ppermute(array, axis, [(i, (i + by) % count) for i in range(count)])


def shortened(array):

    def short(part):
        return part.astype(jnp.bfloat16) if part.dtype == jnp.float32 else part

    return jax.tree.map(short, array)


def sinusoid(steps):
    half_width = TCH // 2
    frequency = jnp.exp(
        -math.log(10000.0) * jnp.arange(half_width).astype(jnp.float32) / half_width
    )
    angles = steps.astype(jnp.float32)[:, None] * frequency[None, :]
    return jnp.concatenate([jnp.cos(angles), jnp.sin(angles)], axis=-1)


def layer_norm(hidden, gain):
    centered = hidden - jnp.mean(hidden, axis=-1, keepdims=True)
    variance = jnp.mean(centered * centered, axis=-1, keepdims=True)
    return centered * lax.rsqrt(variance + 1e-05) * gain


def time_mlp(time_embedding, time_first_weight, time_second_weight):
    pre_act = jnp.dot(time_embedding, time_first_weight, precision=TOP_PRECISION)
    return jnp.dot(jax.nn.silu(pre_act), time_second_weight, precision=TOP_PRECISION)


def row_product(left, right):
    return lax.dot_general(
        left, right, (((0,), (0,)), ((), ())), preferred_element_type=jnp.float32
    )


def back_product(left, right):
    return lax.dot_general(
        left, right, (((1,), (1,)), ((), ())), preferred_element_type=jnp.float32
    )


def masked_scores(queries, key_block, mask_block, scale_factor):
    attention_scores = (
        jnp.einsum("sqhd,skhd->shqk", queries, key_block, preferred_element_type=jnp.float32)
        * scale_factor
    )
    return jnp.where(mask_block[:, None, None, :] > 0.5, attention_scores, -1000000000.0)


def ring_plan(
    inputs,
    timesteps,
    counts,
    slot_token_mask,
    time_first_weight,
    time_second_weight,
    attention_norm_gain,
    query_key_value_weight,
    attention_output_weight,
    feedforward_norm_gain,
    up_projection_weight,
    down_projection_weight,
    cotangent,
):
    present_slots, local_len, width = inputs.shape
    total_rows = present_slots * local_len
    scale_factor = 1.0 / math.sqrt(DH)
    slot_alive_flags = (
        (jnp.arange(present_slots)[:, None] < counts[0]) & (slot_token_mask == 1)
    ).astype(jnp.float32)
    time_embedding = sinusoid(timesteps)
    time_vec, time_back = jax.vjp(
        partial(time_mlp, time_embedding),
        time_first_weight.astype(jnp.float32),
        time_second_weight.astype(jnp.float32),
    )
    residual = inputs.astype(jnp.float32) + time_vec[:, None, :]
    normed, norm_back = jax.vjp(layer_norm, residual, attention_norm_gain)
    normed_low = normed.astype(jnp.bfloat16).reshape(total_rows, width)
    packed = (
        jnp.dot(normed_low, query_key_value_weight, preferred_element_type=jnp.float32)
        .astype(jnp.bfloat16)
        .reshape(present_slots, local_len, 3 * width)
    )
    queries = packed[:, :, :width].reshape(present_slots, local_len, H, DH)
    key_rows = packed[:, :, width : 2 * width]
    value_rows = packed[:, :, 2 * width :]
    key_valid_mask = slot_alive_flags.astype(jnp.bfloat16)
    initial_state = (
        jnp.full((present_slots, H, local_len), -1e30, jnp.float32),
        jnp.zeros((present_slots, H, local_len), jnp.float32),
        jnp.zeros((present_slots, local_len, H, DH), jnp.float32),
    )
    key_piece = lax.all_gather(key_rows, "seq", axis=1, tiled=True)
    value_piece = lax.all_gather(value_rows, "seq", axis=1, tiled=True)
    mask_piece = lax.all_gather(key_valid_mask, "seq", axis=1, tiled=True)
    piece_len = key_piece.shape[1]
    block_len = min(piece_len, local_len)

    def one_block(position, inner_state):
        run_max, run_sum, running_totals = inner_state
        offset = position * block_len
        key_block = lax.dynamic_slice_in_dim(key_piece, offset, block_len, 1).reshape(
            present_slots, block_len, H, DH
        )
        value_block = lax.dynamic_slice_in_dim(value_piece, offset, block_len, 1).reshape(
            present_slots, block_len, H, DH
        )
        mask_block = lax.dynamic_slice_in_dim(mask_piece, offset, block_len, 1)
        attention_scores = masked_scores(queries, key_block, mask_block, scale_factor)
        new_max = jnp.maximum(run_max, jnp.max(attention_scores, axis=-1))
        exponent = jnp.exp(attention_scores - new_max[..., None])
        fading = jnp.exp(run_max - new_max)
        run_sum = run_sum * fading + jnp.sum(exponent, axis=-1)
        running_totals = running_totals * jnp.transpose(fading, (0, 2, 1))[..., None] + jnp.einsum(
            "shqk,skhd->sqhd",
            exponent.astype(jnp.bfloat16),
            value_block,
            preferred_element_type=jnp.float32,
        )
        return (new_max, run_sum, running_totals)

    run_max, run_sum, running_totals = lax.fori_loop(
        0, piece_len // block_len, one_block, initial_state
    )
    attended = running_totals / jnp.transpose(run_sum, (0, 2, 1))[..., None]
    log_total = run_max + jnp.log(run_sum)
    attended_low = attended.astype(jnp.bfloat16).reshape(total_rows, width)
    middle = residual + jnp.dot(
        attended_low, attention_output_weight, preferred_element_type=jnp.float32
    ).reshape(present_slots, local_len, width)
    normed_two, norm_two_back = jax.vjp(layer_norm, middle, feedforward_norm_gain)
    normed_two_low = normed_two.astype(jnp.bfloat16).reshape(total_rows, width)
    gate_pre = jnp.dot(normed_two_low, up_projection_weight, preferred_element_type=jnp.float32)
    activated, gelu_back = jax.vjp(partial(jax.nn.gelu, approximate=True), gate_pre)
    activated_low = activated.astype(jnp.bfloat16)
    completed_groups = middle + jnp.dot(
        activated_low, down_projection_weight, preferred_element_type=jnp.float32
    ).reshape(present_slots, local_len, width)
    output = (slot_alive_flags[..., None] * completed_groups).astype(jnp.bfloat16)
    final_gradient = slot_alive_flags[..., None] * cotangent.astype(jnp.float32)
    grad_down_low = final_gradient.reshape(total_rows, width).astype(jnp.bfloat16)
    down_grad = row_product(activated_low, grad_down_low)
    grad_gate = gelu_back(back_product(grad_down_low, down_projection_weight))[0].astype(
        jnp.bfloat16
    )
    up_grad = row_product(normed_two_low, grad_gate)
    grad_middle_norm, mlp_gain_grad = norm_two_back(
        back_product(grad_gate, up_projection_weight).reshape(present_slots, local_len, width)
    )
    grad_middle = final_gradient + grad_middle_norm
    grad_branch_low = grad_middle.reshape(total_rows, width).astype(jnp.bfloat16)
    out_grad = row_product(attended_low, grad_branch_low)
    grad_attended = (
        back_product(grad_branch_low, attention_output_weight)
        .astype(jnp.bfloat16)
        .reshape(present_slots, local_len, H, DH)
    )
    row_delta = jnp.transpose(
        jnp.sum(grad_attended.astype(jnp.float32) * attended, axis=-1), (0, 2, 1)
    )

    def key_terms(key_block, value_block, mask_block):
        attention_scores = masked_scores(queries, key_block, mask_block, scale_factor)
        probability = jnp.exp(attention_scores - log_total[..., None])
        grad_probs = jnp.einsum(
            "sqhd,skhd->shqk", grad_attended, value_block, preferred_element_type=jnp.float32
        )
        grad_scores = (probability * (grad_probs - row_delta[..., None])).astype(jnp.bfloat16)
        query_add = (
            jnp.einsum(
                "shqk,skhd->sqhd", grad_scores, key_block, preferred_element_type=jnp.float32
            )
            * scale_factor
        )
        key_add = (
            jnp.einsum("shqk,sqhd->skhd", grad_scores, queries, preferred_element_type=jnp.float32)
            * scale_factor
        )
        value_add = jnp.einsum(
            "shqk,sqhd->skhd",
            probability.astype(jnp.bfloat16),
            grad_attended,
            preferred_element_type=jnp.float32,
        )
        block_len = key_block.shape[1]
        return (
            query_add,
            key_add.reshape(present_slots, block_len, width),
            value_add.reshape(present_slots, block_len, width),
        )

    cycle_len = lax.axis_size("seq")
    query_zeros = jnp.zeros((present_slots, local_len, H, DH), jnp.float32)

    def visit(visit_index, loop_state):
        grad_queries, visiting, carried = loop_state
        query_add, key_add, value_add = key_terms(
            visiting[0].reshape(present_slots, local_len, H, DH),
            visiting[1].reshape(present_slots, local_len, H, DH),
            visiting[2],
        )
        carried = (carried[0] + key_add, carried[1] + value_add)
        visiting = from_behind((visiting[0], visiting[1], visiting[2]), "seq", 1)
        carried = (
            from_behind(carried[0].astype(jnp.bfloat16), "seq", 1).astype(jnp.float32),
            from_behind(carried[1].astype(jnp.bfloat16), "seq", 1).astype(jnp.float32),
        )
        return (grad_queries + query_add, tuple(visiting), tuple(carried))

    zeros_kv = jnp.zeros((present_slots, local_len, width), jnp.float32)
    grad_queries, visiting, carried = lax.fori_loop(
        0,
        cycle_len,
        visit,
        (query_zeros, (key_rows, value_rows, key_valid_mask), (zeros_kv, zeros_kv)),
    )
    grad_keys, grad_values = carried
    grad_packed = (
        jnp.concatenate(
            [grad_queries.reshape(present_slots, local_len, width), grad_keys, grad_values], axis=-1
        )
        .astype(jnp.bfloat16)
        .reshape(total_rows, 3 * width)
    )
    qkv_grad = row_product(normed_low, grad_packed)
    query_key_grad = qkv_grad[:, : 2 * width]
    value_grad = qkv_grad[:, 2 * width :]
    grad_start_norm, attn_gain_grad = norm_back(
        back_product(grad_packed, query_key_value_weight).reshape(present_slots, local_len, width)
    )
    grad_start = grad_middle + grad_start_norm
    inner_grad, outer_grad = time_back(jnp.sum(grad_start, axis=1))
    shares = (
        lax.psum_scatter(
            inner_grad.astype(jnp.bfloat16), "batch", scatter_dimension=1, tiled=True
        ).astype(jnp.float32),
        lax.psum_scatter(
            outer_grad.astype(jnp.bfloat16), "batch", scatter_dimension=1, tiled=True
        ).astype(jnp.float32),
        lax.psum_scatter(
            attn_gain_grad[None, :].astype(jnp.bfloat16), "batch", scatter_dimension=1, tiled=True
        ).astype(jnp.float32),
        lax.psum_scatter(
            query_key_grad.astype(jnp.bfloat16), "batch", scatter_dimension=1, tiled=True
        ).astype(jnp.float32),
        lax.psum_scatter(
            value_grad.astype(jnp.bfloat16), "batch", scatter_dimension=1, tiled=True
        ).astype(jnp.float32),
        lax.psum_scatter(
            out_grad.astype(jnp.bfloat16), "batch", scatter_dimension=1, tiled=True
        ).astype(jnp.float32),
        lax.psum_scatter(
            mlp_gain_grad[None, :].astype(jnp.bfloat16), "batch", scatter_dimension=1, tiled=True
        ).astype(jnp.float32),
        lax.psum_scatter(
            up_grad.astype(jnp.bfloat16), "batch", scatter_dimension=1, tiled=True
        ).astype(jnp.float32),
        lax.psum_scatter(
            down_grad.astype(jnp.bfloat16), "batch", scatter_dimension=1, tiled=True
        ).astype(jnp.float32),
    )
    summed = tuple(
        jax.tree.map(
            lambda part: part.astype(jnp.float32), lax.psum(shortened(tuple(shares)), "seq")
        )
    )
    return (
        output,
        grad_start,
        summed[0],
        summed[1],
        summed[2][0],
        summed[3],
        summed[4],
        summed[5],
        summed[6][0],
        summed[7],
        summed[8],
    )


BF = jnp.bfloat16
F32 = jnp.float32
MASKED = -1e9
GELU_A = 0.7978845608028654
GELU_B = 0.044715
VMEM_LIMIT = 62 * 2**20


def mm(left, right, left_dim, right_dim):
    return lax.dot_general(
        left, right, (((left_dim,), (right_dim,)), ((), ())), preferred_element_type=F32
    )


def attend_kernel(
    counts_ref, steps_ref, x_hbm, mask_hbm, cot_hbm, w1_ref, w2_ref, gain_ref, w_ref,
    o_ref, exact_ref, inv_ref, even_ref, odd_ref, live_ref, temb_ref, emb_ref, u_ref,
    q_hbm, kv_hbm, n1_hbm, xs_hbm, dm_hbm,
    xs, n1, q, kv, dm, mask, mask_far, bias, live, sems, send, receive,
    keys, query, v_even, v_odd, s_even, s_odd, m_even, m_odd,
):
    step = pl.program_id(0)
    last = pl.num_programs(0) - 1
    piece, width = xs.shape[0] // 4, xs.shape[1]
    length = 2 * piece
    lane = lax.broadcasted_iota(jnp.int32, (1, 128), 1)
    now = jnp.minimum(step, last - 1)
    before = jnp.maximum(step - 1, 0)
    me, seq = lax.axis_index("batch"), lax.axis_index("seq")
    blocks = [pl.ds(piece * i, piece) for i in range(4)]

    def to_partner(k, source, target):
        return pltpu.make_async_remote_copy(
            src_ref=source,
            dst_ref=target,
            send_sem=send.at[k],
            recv_sem=receive.at[k],
            device_id=(me, 1 - seq),
            device_id_type=pl.DeviceIdType.MESH,
        )

    x_one = to_partner(0, x_hbm.at[1 - seq], xs.at[blocks[1]])
    x_two = to_partner(1, x_hbm.at[2], xs.at[blocks[3]])
    cot_one = to_partner(2, cot_hbm.at[1 - seq], dm.at[blocks[1]])
    mask_there = to_partner(3, mask_hbm, mask_far)
    own = [
        pltpu.make_async_copy(x_hbm.at[seq], xs.at[blocks[0]], sems.at[0]),
        pltpu.make_async_copy(x_hbm.at[2], xs.at[blocks[2]], sems.at[1]),
        pltpu.make_async_copy(mask_hbm, mask, sems.at[2]),
        pltpu.make_async_copy(cot_hbm.at[seq], dm.at[blocks[0]], sems.at[3]),
        pltpu.make_async_copy(cot_hbm.at[2], dm.at[blocks[2]], sems.at[4]),
    ]
    keep_early = [
        pltpu.make_async_copy(q, q_hbm, sems.at[5]),
    ]
    keep_late = [
        pltpu.make_async_copy(kv, kv_hbm, sems.at[6]),
        pltpu.make_async_copy(n1, n1_hbm, sems.at[7]),
        pltpu.make_async_copy(xs, xs_hbm, sems.at[8]),
    ]
    keep_dm = pltpu.make_async_copy(dm, dm_hbm, sems.at[9])

    def project(i, with_queries):
        part = blocks[i]
        h = xs[part, :].astype(F32) + temb_ref[i // 2 : i // 2 + 1, :]
        centered = h - jnp.mean(h, axis=1, keepdims=True)
        variance = jnp.mean(centered * centered, axis=1, keepdims=True)
        normed = (centered * lax.rsqrt(variance + 1e-5) * gain_ref[...]).astype(BF)
        n1[part, :] = normed
        if with_queries:
            q[part, :] = (mm(normed, w_ref[:, :width], 1, 0) * 0.125).astype(BF)
        kv[part, :] = mm(normed, w_ref[:, width:], 1, 0).astype(BF)

    def lives(ref):
        rows = lax.broadcasted_iota(jnp.int32, (8, piece), 0)
        held = jnp.concatenate([ref[...], jnp.zeros((5, piece), jnp.int32)], axis=0)
        flags = jnp.where((held == 1) & (rows < counts_ref[0]), 1.0, 0.0)
        return flags.T

    def set_live(i, column):
        live[blocks[i], :] = jnp.broadcast_to(column, (piece, 128)).astype(BF)
        masked = jnp.where(lane == 0, MASKED, 0.0)
        bias[blocks[i], :] = jnp.where(column > 0.5, 0.0, masked).astype(BF)

    def mine(columns):
        return jnp.where(seq == 0, columns[:, 0:1], columns[:, 1:2])

    @pl.when(step == 0)
    def _():
        for copy in own:
            copy.start()
        greet_x()
        mask_there.start()
        x_one.start()
        row = lax.broadcasted_iota(jnp.int32, (8, 1), 0)
        times = jnp.where(
            row == 0, steps_ref[0], jnp.where(row == 1, steps_ref[1], steps_ref[2])
        ).astype(F32)
        half_width = TCH // 2
        column = lax.broadcasted_iota(jnp.int32, (1, TCH), 1)
        index = jnp.where(column < half_width, column, column - half_width).astype(F32)
        angles = times * jnp.exp(-math.log(10000.0) * index / half_width)
        emb = jnp.where(column < half_width, jnp.cos(angles), jnp.sin(angles))
        emb = jnp.where(row < 3, emb, 0.0)

        def exact_product(left, right):
            return lax.dot_general(
                left, right.astype(F32), (((1,), (0,)), ((), ())),
                precision=TOP_PRECISION, preferred_element_type=F32,
            )

        u = exact_product(emb, w1_ref[...])
        temb = exact_product(u / (1.0 + jnp.exp(-u)), w2_ref[...])
        emb_ref[...] = emb
        u_ref[...] = u
        temb_ref[0:1, :] = jnp.where(seq == 0, temb[0:1], temb[1:2])
        temb_ref[1:2, :] = temb[2:3]
        temb_ref[2:8, :] = jnp.zeros((6, width), F32)
        for copy in own[:3]:
            copy.wait()
        columns = lives(mask)
        set_live(0, mine(columns))
        set_live(2, columns[:, 2:3])
        project(0, True)
        project(2, True)
        for copy in own[3:]:
            copy.wait()
        dm[blocks[0], :] *= live[blocks[0], 0:1]
        dm[blocks[2], :] *= live[blocks[2], 0:1]
        mask_there.wait()
        columns = lives(mask_far)
        set_live(1, mine(columns))
        set_live(3, columns[:, 2:3])
        live_ref[...] = live[pl.ds(0, 3 * piece), :]
        x_one.wait()
        x_two.start()
        project(1, True)
        for copy in keep_early:
            copy.start()

    @pl.when(step == 8)
    def _():
        x_two.wait()
        cot_one.start()
        project(3, False)
        for copy in keep_late:
            copy.start()

    @pl.when(step == last)
    def _():
        cot_one.wait()
        dm[blocks[1], :] *= live[blocks[1], 0:1]
        keep_dm.start()

    query_rows = pl.ds(pl.multiple_of((now // 6) * piece, piece), piece)
    key_rows = pl.ds(pl.multiple_of((now // 12) * length, length), length)
    pair_lanes = pl.ds(pl.multiple_of((now % 6) * 128, 128), 128)
    value_lanes = pl.ds(pl.multiple_of(width + (now % 6) * 128, 128), 128)

    @pl.when(step % 6 == 0)
    def _():
        keys[:, 128:] = bias[key_rows, :]
        query[:, 128:] = jnp.where(
            lax.broadcasted_iota(jnp.int32, (piece, 128), 1) == 0, 1.0, 0.0
        ).astype(BF)
        v_even[64:, :] = jnp.ones((16, length), BF)
        v_odd[64:, :] = jnp.ones((16, length), BF)

    keys[:, :128] = kv[key_rows, pair_lanes]

    def half(head, made, made_max, used, used_max, values, at, out_ref):
        query[:, :128] = jnp.where((lane // 64) == head, q[query_rows, pair_lanes], jnp.zeros((), BF))
        top = used_max[0:1, :]
        scores = mm(keys[...], query[...], 1, 1)
        weight = jnp.exp(used[...] - top).astype(BF)
        made[...] = scores
        made_max[...] = jnp.broadcast_to(jnp.max(scores, axis=0, keepdims=True), made_max.shape)
        out_ref[0] = weight
        total = mm(values[...], weight, 1, 0)
        inverse = 1.0 / total[64:65]
        place = pl.ds(pl.multiple_of((at // 6) * piece, piece), piece)
        which = 2 * (at % 6) + 1 - head
        exact = total[:64] * inverse
        o_ref[which, :, place] = exact.astype(BF)
        exact_ref[which, :, place] = exact
        inv_ref[which, :, place] = jnp.broadcast_to(inverse, (8, piece))

    half(0, s_even, m_even, s_odd, m_odd, v_odd, before, odd_ref)
    turned = kv[key_rows, value_lanes].T
    v_even[:64, :] = turned[:64]
    v_odd[:64, :] = turned[64:]
    half(1, s_odd, m_odd, s_even, m_even, v_even, now, even_ref)

    @pl.when(step == last)
    def _():
        for copy in keep_early + keep_late + [keep_dm]:
            copy.wait()


def greet_x():
    partner = (lax.axis_index("batch"), 1 - lax.axis_index("seq"))
    barrier = pltpu.get_barrier_semaphore()
    pl.semaphore_signal(barrier, inc=1, device_id=partner, device_id_type=pl.DeviceIdType.MESH)
    pl.semaphore_wait(barrier, 1)


def attend(counts, timesteps, x, mask, cot, w1, w2, gain, w):
    _, piece, width = x.shape
    length = 2 * piece
    rows = 3 * piece
    steps = 18
    hidden = w1.shape[1]
    whole = pl.BlockSpec(memory_space=pltpu.VMEM)
    scalars = pl.BlockSpec(memory_space=pltpu.SMEM)
    anywhere = pl.BlockSpec(memory_space=pl.ANY)
    return pl.pallas_call(
        attend_kernel,
        grid=(steps + 1,),
        in_specs=[scalars] * 2 + [anywhere] * 3 + [whole] * 4,
        out_specs=[
            whole,
            whole,
            whole,
            pl.BlockSpec((1, length, piece), lambda t: (jnp.minimum(t, steps - 1), 0, 0)),
            pl.BlockSpec((1, length, piece), lambda t: (jnp.maximum(t - 1, 0), 0, 0)),
        ]
        + [whole] * 4
        + [anywhere] * 5,
        out_shape=[
            jax.ShapeDtypeStruct((H, DH, rows), BF),
            jax.ShapeDtypeStruct((H, DH, rows), F32),
            jax.ShapeDtypeStruct((H, 8, rows), F32),
            jax.ShapeDtypeStruct((steps, length, piece), BF),
            jax.ShapeDtypeStruct((steps, length, piece), BF),
            jax.ShapeDtypeStruct((rows, 128), BF),
            jax.ShapeDtypeStruct((8, width), F32),
            jax.ShapeDtypeStruct((8, TCH), F32),
            jax.ShapeDtypeStruct((8, hidden), F32),
            jax.ShapeDtypeStruct((rows, width), BF),
            jax.ShapeDtypeStruct((4 * piece, 2 * width), BF),
            jax.ShapeDtypeStruct((4 * piece, width), BF),
            jax.ShapeDtypeStruct((4 * piece, width), BF),
            jax.ShapeDtypeStruct((rows, width), BF),
        ],
        scratch_shapes=[
            pltpu.VMEM((4 * piece, width), BF),
            pltpu.VMEM((4 * piece, width), BF),
            pltpu.VMEM((rows, width), BF),
            pltpu.VMEM((4 * piece, 2 * width), BF),
            pltpu.VMEM((rows, width), BF),
            pltpu.VMEM((3, piece), jnp.int32),
            pltpu.VMEM((3, piece), jnp.int32),
            pltpu.VMEM((4 * piece, 128), BF),
            pltpu.VMEM((4 * piece, 128), BF),
            pltpu.SemaphoreType.DMA((10,)),
            pltpu.SemaphoreType.DMA((4,)),
            pltpu.SemaphoreType.DMA((4,)),
            pltpu.VMEM((length, 256), BF),
            pltpu.VMEM((piece, 256), BF),
            pltpu.VMEM((80, length), BF),
            pltpu.VMEM((80, length), BF),
            pltpu.VMEM((length, piece), F32),
            pltpu.VMEM((length, piece), F32),
            pltpu.VMEM((8, piece), F32),
            pltpu.VMEM((8, piece), F32),
        ],
        compiler_params=pltpu.CompilerParams(
            vmem_limit_bytes=VMEM_LIMIT, collective_id=4, has_side_effects=True
        ),
        cost_estimate=pl.CostEstimate(flops=20 * 10**9, bytes_accessed=60 * 10**6, transcendentals=19 * 10**6),
    )(counts, timesteps, x, mask, cot, w1, w2, gain, w)


def place_of(pair):
    return 4 * (pair & 1) + 2 * (pair >> 1 & 1) + (pair >> 2)


class Shares:
    def __init__(self, source, scratch, x_second):
        self.source = source
        self.x_second = x_second
        self.names = ["core", "rows", "y", "z", "join", "out"] if x_second else ["core", "y", "z", "x", "out"]
        self.acc, self.final, self.send, self.receive = scratch[0], scratch[1], scratch[-2], scratch[-1]
        boxes = [name for name in self.names if name not in ("join", "out")]
        self.inbox = dict(zip(boxes, scratch[2:-2]))
        me, far = lax.axis_index("batch"), lax.axis_index("seq")
        self.core, self.y, self.z0, self.z1 = [(me >> bit) & 1 for bit in range(4)]
        self.me, self.far = me, far
        self.half = self.acc.shape[2]
        rows = self.acc.shape[1]
        self.rows = slice(0, rows)
        if x_second:
            self.rows = pl.ds(pl.multiple_of(far * (rows // 2), 16), rows // 2)
            self.other_rows = pl.ds(pl.multiple_of((1 - far) * (rows // 2), 16), rows // 2)
        self.own = 4 * self.y + 2 * self.z0 + self.z1

    def partner(self, name):
        if name in ("x", "rows", "join"):
            return (self.me, 1 - self.far)
        return (self.me ^ {"core": 1, "y": 2, "out": 1}[name], self.far)

    def ends(self, name):
        acc, rows = self.acc, self.rows
        if name == "core":
            away = pl.multiple_of((1 - self.core) * self.half, 128)
            return self.source.at[:, :, pl.ds(away, self.half)], self.inbox[name]
        if name == "rows":
            return acc.at[:, self.other_rows], self.inbox[name]
        if name == "y":
            return acc.at[pl.ds(4 * (1 - self.y), 4), rows], self.inbox[name]
        if name == "x":
            return acc.at[self.own], self.inbox[name]
        if name == "join":
            return self.final.at[self.core, rows], self.final.at[self.core, rows]
        return self.final.at[self.core], self.final.at[self.core]

    def copies(self, stage):
        name = self.names[stage]
        if name != "z":
            here, there = self.ends(name)
            return [self.remote(stage, here, there, self.partner(name))]
        made = []
        for k in range(3):
            flip0, flip1 = (k + 1) & 1, (k + 1) >> 1
            z0 = 1 - self.z0 if flip0 else self.z0
            z1 = 1 - self.z1 if flip1 else self.z1
            here = self.acc.at[4 * self.y + 2 * z0 + z1, self.rows]
            other = (self.me ^ (4 * flip0 + 8 * flip1), self.far)
            made.append(self.remote(stage if k == 0 else 7 + k, here, self.inbox[name].at[k], other))
        return made

    def remote(self, which, here, there, other):
        return pltpu.make_async_remote_copy(
            src_ref=here,
            dst_ref=there,
            send_sem=self.send.at[which],
            recv_sem=self.receive.at[which],
            device_id=other,
            device_id_type=pl.DeviceIdType.MESH,
        )

    def start(self, stage):
        for copy in self.copies(stage):
            copy.start()

    def load(self):
        mine = pl.multiple_of(self.core * self.half, 128)
        return pltpu.make_async_copy(
            self.source.at[:, :, pl.ds(mine, self.half)], self.acc, self.send.at[7]
        )

    def begin(self):
        self.start(0)
        self.load().start()

    def add(self, name):
        acc, rows = self.acc, self.rows

        def total(one, other):
            return one + other

        if name in ("core", "rows", "y"):
            first, count = {"core": (0, 8), "rows": (0, 8), "y": (4 * self.y, 4)}[name]
            if name == "core":
                rows = slice(None)
            for k in range(count):
                acc[first + k, rows] = total(acc[first + k, rows], self.inbox[name][k])
        elif name == "z":
            parts = [acc[self.own, rows]] + [self.inbox[name][k] for k in range(3)]
            parts = [part.astype(F32) for part in parts]
            summed = ((parts[0] + parts[1]) + (parts[2] + parts[3])).astype(BF)
            if self.x_second:
                self.final[self.core, rows] = summed
            else:
                acc[self.own] = summed
        elif name == "x":
            self.final[self.core] = total(acc[self.own], self.inbox[name][...])

    def end(self, stage):
        if stage == 0:
            self.load().wait()
        for copy in self.copies(stage):
            copy.wait()
        self.add(self.names[stage])

    def go_on(self, stage):
        self.end(stage)
        if stage + 1 < len(self.names):
            self.start(stage + 1)

    def fetch(self):
        return pltpu.make_async_copy(self.source, self.acc, self.send.at[7])

    def resume(self, stage):
        self.fetch().wait()
        self.start(stage)


def share_scratch(rows, columns, x_second):
    half = columns // 2
    part = rows // 2 if x_second else rows
    shapes = [(8, rows, half), (2, rows, half), (8, rows, half)]
    shapes += [(8, part, half)] if x_second else []
    shapes += [(4, part, half), (3, part, half)]
    shapes += [] if x_second else [(rows, half)]
    return [pltpu.VMEM(shape, BF) for shape in shapes] + [
        pltpu.SemaphoreType.DMA((10,)),
        pltpu.SemaphoreType.DMA((10,)),
    ]


SCRATCH_COUNT = 8


def greet():
    call()
    pl.semaphore_wait(pltpu.get_barrier_semaphore(), GREETED)


GREETED = 6


def call():
    me, far = lax.axis_index("batch"), lax.axis_index("seq")
    barrier = pltpu.get_barrier_semaphore()
    others = [(me ^ 1, far), (me ^ 2, far), (me ^ 4, far), (me ^ 8, far), (me ^ 12, far), (me, 1 - far)]
    for other in others:
        pl.semaphore_signal(barrier, inc=1, device_id=other, device_id_type=pl.DeviceIdType.MESH)


def attend_back_kernel(
    plan, table, q_ref, k_ref, v_ref, do_ref, o_ref, inv_ref, even_ref, odd_ref, *rest
):
    count = len(plan)
    w_hbm, out_hbm, *rest = rest
    sources, rest = rest[:count], rest[count:]
    width = w_hbm.shape[0]
    (dq_ref, dk_ref, dv_ref, far_ref, output_hbm), rest = rest[:5], rest[5:]
    finals, rest = rest[:count], rest[count:]
    values, gradient, dk_sum, dv_sum, far_kv, far_send, far_got, out_got, far_sems, w_kv, *rest = rest
    w_load = pltpu.make_async_copy(w_hbm.at[:, pl.ds(width, 2 * width)], w_kv, far_sems.at[5])
    shares = []
    for i in range(count):
        own = rest[SCRATCH_COUNT * i : SCRATCH_COUNT * (i + 1)]
        shares.append(Shares(sources[i], own, plan[i]))
    step = pl.program_id(0)
    steps = pl.num_programs(0)
    pair, part = back_place(step)
    piece, length = q_ref.shape[0], k_ref.shape[0]
    lane = lax.broadcasted_iota(jnp.int32, (1, 128), 1)
    zero = jnp.zeros((), BF)
    far_copy = pltpu.make_async_remote_copy(
        src_ref=far_send,
        dst_ref=far_got,
        send_sem=far_sems.at[0],
        recv_sem=far_sems.at[1],
        device_id=(lax.axis_index("batch"), 1 - lax.axis_index("seq")),
        device_id_type=pl.DeviceIdType.MESH,
    )

    seq = lax.axis_index("seq")
    out_copy = pltpu.make_async_remote_copy(
        src_ref=out_hbm.at[pl.ds(piece, piece)],
        dst_ref=out_got,
        send_sem=far_sems.at[2],
        recv_sem=far_sems.at[3],
        device_id=(lax.axis_index("batch"), 1 - seq),
        device_id_type=pl.DeviceIdType.MESH,
    )
    returned = pltpu.make_async_copy(out_got, output_hbm, far_sems.at[4])

    @pl.when(step == 0)
    def _():
        for share in shares[:2]:
            share.fetch().start()
        w_load.start()
        greet()
        for share in shares[:2]:
            share.resume(2)
        for share in shares[2:]:
            share.begin()
        out_copy.start()
        values[:, 128:] = jnp.where(
            lax.broadcasted_iota(jnp.int32, (length, 128), 1) < 3, 1.0, 0.0
        ).astype(BF)
        gradient[...] = jnp.zeros_like(gradient)
        dk_sum[...] = jnp.zeros_like(dk_sum)
        dv_sum[...] = jnp.zeros_like(dv_sum)

    for when in sorted(table):
        if when < 18:

            @pl.when(step == when)
            def _(when=when):
                for i, stage in table[when]:
                    shares[i].go_on(stage)

    @pl.when(step == 11)
    def _():
        out_copy.wait()
        returned.start()

    @pl.when(step == 6)
    def _():
        w_load.wait()
        far_send[...] = mm(far_kv[:, : 2 * width], w_kv[...], 1, 1).astype(BF)
        far_copy.start()

    values[:, :128] = v_ref[...]
    inverse = jnp.concatenate(
        [jnp.broadcast_to(inv_ref[head, 0:1, :], (DH, piece)) for head in range(2)], axis=0
    )
    scaled = (do_ref[...].astype(F32) * inverse).astype(BF)
    product = scaled.astype(F32) * o_ref[...]
    for head in range(2):
        mine = slice(DH * head, DH * head + DH)
        place = slice(piece * head, piece * head + piece)
        delta = -jnp.sum(product[mine], axis=0, keepdims=True)
        high = delta.astype(BF).astype(F32)
        rest_of = delta - high
        middle = rest_of.astype(BF).astype(F32)
        gradient[mine, place] = scaled[mine]
        gradient[128:144, place] = jnp.concatenate(
            [high, middle, rest_of - middle, jnp.zeros((13, piece), F32)], axis=0
        ).astype(BF)
    dp = mm(values[...], gradient[...], 1, 0)
    turned_keys = k_ref[...].T
    natural = scaled.T
    weights = [even_ref[0], odd_ref[0]]
    ds = [
        (weights[head].astype(F32) * dp[:, piece * head : piece * head + piece]).astype(BF)
        for head in range(2)
    ]

    def apart(array):
        return jnp.concatenate(
            [jnp.where(lane < 64, array, zero), jnp.where(lane < 64, zero, array)], axis=0
        )

    dv = mm(jnp.concatenate(weights, axis=1), apart(natural), 1, 0)
    dk = mm(jnp.concatenate(ds, axis=1), apart(q_ref[...]), 1, 0)
    for head in range(2):
        mine = slice(DH * head, DH * head + DH)
        dq_ref[mine, :] = (mm(turned_keys[mine], ds[head], 1, 0) * 0.125).astype(BF)

    again = part == 1
    dk += jnp.where(again, dk_sum[...], 0.0)
    dv += jnp.where(again, dv_sum[...], 0.0)
    dk_sum[...] = dk
    dv_sum[...] = dv
    dk, dv = dk.astype(BF), dv.astype(BF)
    dk_ref[...] = dk
    dv_ref[...] = dv
    early = step < 6
    at = jnp.where(early, pair * 128, 2 * width)
    far_kv[:, pl.ds(pl.multiple_of(at, 128), 128)] = dk[piece:]
    at = jnp.where(early, width + pair * 128, 2 * width + 128)
    far_kv[:, pl.ds(pl.multiple_of(at, 128), 128)] = dv[piece:]

    @pl.when(step == steps - 1)
    def _():
        for when in sorted(table):
            if when >= 18:
                for i, stage in table[when]:
                    shares[i].go_on(stage)
        for i in range(count):
            finals[i][...] = shares[i].final[...]
        far_copy.wait()
        far_ref[...] = far_got[...]
        returned.wait()


def back_place(step):
    late = jnp.maximum(step - 6, 0)
    return jnp.where(step < 6, step, late // 2), jnp.where(step < 6, 2, late % 2)


def attend_back(q, kv, do, o, inv, even, odd, w, out, partials, plan, table):
    rows, width = q.shape
    length = 2 * rows // 3
    piece = rows // 3

    def spec(shape, index):
        return pl.BlockSpec(shape, lambda t: index(*back_place(t)))

    weight_spec = spec((1, length, piece), lambda p, j: (j * 6 + p, 0, 0))
    scratch = []
    sizes = [(a.shape[1], a.shape[2] * (2 if i < 2 else 1)) for i, a in enumerate(partials)]
    for size, x_second in zip(sizes, plan):
        scratch += share_scratch(*size, x_second)
    whole = pl.BlockSpec(memory_space=pltpu.VMEM)
    return pl.pallas_call(
        partial(attend_back_kernel, plan, table),
        grid=(18,),
        in_specs=[
            spec((piece, 128), lambda p, j: (j, p)),
            spec((length, 128), lambda p, j: (j // 2, p)),
            spec((length, 128), lambda p, j: (j // 2, 6 + p)),
            spec((128, piece), lambda p, j: (p, j)),
            spec((128, piece), lambda p, j: (p, j)),
            spec((2, 8, piece), lambda p, j: (p, 0, j)),
            weight_spec,
            weight_spec,
        ]
        + [pl.BlockSpec(memory_space=pl.ANY)] * (2 + len(partials)),
        out_specs=[
            spec((128, piece), lambda p, j: (p, j)),
            spec((length, 128), lambda p, j: (j // 2, p)),
            spec((length, 128), lambda p, j: (j // 2, p)),
            whole,
            pl.BlockSpec(memory_space=pl.ANY),
        ]
        + [whole] * len(partials),
        out_shape=[
            jax.ShapeDtypeStruct((width, rows), BF),
            jax.ShapeDtypeStruct((2 * length, width), BF),
            jax.ShapeDtypeStruct((2 * length, width), BF),
            jax.ShapeDtypeStruct((piece, width), BF),
            jax.ShapeDtypeStruct((piece, width), BF),
        ]
        + [jax.ShapeDtypeStruct((2, a, b // 2), BF) for a, b in sizes],
        scratch_shapes=[
            pltpu.VMEM((length, 256), BF),
            pltpu.VMEM((256, 2 * piece), BF),
            pltpu.VMEM((length, 128), F32),
            pltpu.VMEM((length, 128), F32),
            pltpu.VMEM((piece, 2 * width + 256), BF),
            pltpu.VMEM((piece, width), BF),
            pltpu.VMEM((piece, width), BF),
            pltpu.VMEM((piece, width), BF),
            pltpu.SemaphoreType.DMA((6,)),
            pltpu.VMEM((width, 2 * width), BF),
        ]
        + scratch,
        compiler_params=pltpu.CompilerParams(
            vmem_limit_bytes=VMEM_LIMIT, collective_id=1, has_side_effects=True
        ),
        cost_estimate=pl.CostEstimate(flops=30 * 10**9, bytes_accessed=60 * 10**6, transcendentals=0),
    )(q, kv, kv, do, o, inv, even, odd, w, out, *partials)


def finish_kernel(
    dq_hbm, dk_hbm, dv_hbm, n1_hbm, x_hbm, dh_hbm, w_hbm, far_ref, temb_ref, gain_ref, dgain2_ref,
    w2_ref, emb_ref, u_ref, *rest
):
    own_ref, far_out_ref, finals, rest = rest[0], rest[1], rest[2:7], rest[7:]
    dq, dk, dv, n1, x, dh, w, send, got, sems, far_sems = rest[:11]
    sources, rest = rest[11:16], rest[16:]
    shares = []
    for i in range(5):
        own = rest[SCRATCH_COUNT * i : SCRATCH_COUNT * (i + 1)]
        shares.append(Shares(sources[i], own, FINISH_PLAN[i]))
    half, width = far_ref.shape
    me, seq = lax.axis_index("batch"), lax.axis_index("seq")

    loads = {}

    def fetch(name, source, target):
        loads[name] = pltpu.make_async_copy(source, target, sems.at[len(loads)])
        loads[name].start()

    blocks = [slice(half * i, half * i + half) for i in range(4)]
    fetch("w", w_hbm, w)
    for b in (1, 0, 2):
        fetch(("dq", b), dq_hbm.at[:, blocks[b]], dq.at[:, blocks[b]])
        fetch(("dk", b), dk_hbm.at[blocks[b]], dk.at[blocks[b]])
        fetch(("dv", b), dv_hbm.at[blocks[b]], dv.at[blocks[b]])
        if b == 1:
            fetch("x", x_hbm.at[pl.ds(0, 3 * half)], x)
            fetch(("dh", 1), dh_hbm.at[blocks[1]], dh.at[blocks[1]])
    fetch(("dk", 3), dk_hbm.at[blocks[3]], dk.at[blocks[3]])
    fetch(("dv", 3), dv_hbm.at[blocks[3]], dv.at[blocks[3]])
    fetch("n1", n1_hbm, n1)
    fetch(("dh", 0), dh_hbm.at[blocks[0]], dh.at[blocks[0]])
    fetch(("dh", 2), dh_hbm.at[blocks[2]], dh.at[blocks[2]])
    back_copy = pltpu.make_async_remote_copy(
        src_ref=send,
        dst_ref=got,
        send_sem=far_sems.at[0],
        recv_sem=far_sems.at[1],
        device_id=(me, 1 - seq),
        device_id_type=pl.DeviceIdType.MESH,
    )
    greet()

    def norm_back(b, more):
        loads[("dh", b)].wait()
        part = blocks[b]
        dn = mm(dq[:, part], w[:, :width], 0, 1)
        dn += mm(dk[part, :], w[:, width : 2 * width], 1, 1)
        dn += mm(dv[part, :], w[:, 2 * width :], 1, 1)
        if more is not None:
            dn += more[...].astype(F32)
        h = x[part, :].astype(F32) + temb_ref[b // 2 : b // 2 + 1, :]
        centered = h - jnp.mean(h, axis=1, keepdims=True)
        r1 = lax.rsqrt(jnp.mean(centered * centered, axis=1, keepdims=True) + 1e-5)
        x1 = centered * r1
        e = dn * gain_ref[...]
        dh0 = dh[part, :] + r1 * (
            e - jnp.mean(e, axis=1, keepdims=True) - x1 * jnp.mean(e * x1, axis=1, keepdims=True)
        )
        return dh0, jnp.sum(dh0, axis=0, keepdims=True), jnp.sum(dn * x1, axis=0, keepdims=True)

    def weight_piece(f):
        columns = slice(256 * f, 256 * f + 256)
        q_part = mm(dq[...], n1[: 3 * half, columns], 1, 0).astype(BF)
        k_part = mm(dk[...], n1[:, columns], 0, 0).astype(BF)
        v_part = mm(dv[...], n1[:, columns], 0, 0).astype(BF)
        pair_rows = width // 4
        for k in range(8):
            source = q_part if k < 4 else k_part
            first = pair_rows * (k % 4)
            sources[f][place_of(k), :pair_rows, :] = source[first : first + pair_rows]
            first = width // 8 * k
            sources[f][place_of(k), pair_rows:, :] = v_part[first : first + width // 8]
        shares[f].begin()

    first_loads = ("w", "x", ("dq", 1), ("dk", 1), ("dv", 1))
    for name in first_loads:
        loads[name].wait()
    dh0, dtemb_a, dgain_a = norm_back(1, None)
    send[...] = dh0.astype(BF)
    back_copy.start()
    for name in loads:
        if name[0] != "dh" and name not in first_loads:
            loads[name].wait()
    weight_piece(0)
    weight_piece(1)
    shares[0].go_on(0)
    weight_piece(2)
    shares[1].go_on(0)
    shares[2].go_on(0)
    dh0, dtemb_b, dgain_b = norm_back(0, None)
    own_ref[0] = dh0
    shares[0].go_on(1)
    dh0, dtemb_two, dgain_c = norm_back(2, far_ref)
    own_ref[1] = dh0

    dtemb_one = dtemb_a + dtemb_b
    first = (seq == 0).astype(F32)
    dtemb = jnp.concatenate(
        [first * dtemb_one, (1.0 - first) * dtemb_one, dtemb_two, jnp.zeros((5, width), F32)], axis=0
    )
    u = u_ref[...]
    sigmoid = 1.0 / (1.0 + jnp.exp(-u))
    outer = lax.dot_general(
        dtemb, u * sigmoid, (((0,), (0,)), ((), ())), precision=TOP_PRECISION, preferred_element_type=F32
    ).astype(BF)
    dsilu = lax.dot_general(
        dtemb, w2_ref[...].astype(F32), (((1,), (1,)), ((), ())), precision=TOP_PRECISION, preferred_element_type=F32
    )
    dpre = dsilu * (sigmoid * (1.0 + u * (1.0 - sigmoid)))
    inner = lax.dot_general(
        dpre, emb_ref[...], (((0,), (0,)), ((), ())), precision=TOP_PRECISION, preferred_element_type=F32
    ).astype(BF)
    dgain = dgain_a + dgain_b + dgain_c
    size, inner_size = width // 8, inner.shape[0] // 8
    sources[4][...] = jnp.zeros_like(sources[4])
    for k in range(8):
        sources[3][place_of(k)] = outer[size * k : size * k + size]
        sources[4][place_of(k), :, :128] = inner[inner_size * k : inner_size * k + inner_size]
        both = jnp.concatenate(
            [
                jnp.concatenate([g[:, size * k : size * k + size], jnp.zeros((1, 128 - size), F32)], axis=1)
                for g in (dgain, dgain2_ref[...])
            ]
            + [jnp.zeros((14, 128), F32)],
            axis=0,
        )
        sources[4][place_of(k), :16, 128:] = both.astype(BF)
    shares[3].begin()
    shares[4].begin()
    for i, stage in FINISH_ORDER:
        shares[i].go_on(stage)
    for i in range(5):
        finals[i][...] = shares[i].final[...]
    back_copy.wait()
    far_out_ref[...] = got[...]


FINISH_PLAN = [False, True, False, False, False]
FINISH_ORDER = [
    (1, 1), (3, 0), (4, 0), (0, 2), (2, 1), (1, 2), (2, 2), (3, 1), (4, 1), (0, 3), (1, 3), (3, 2),
    (4, 2), (2, 3), (0, 4), (1, 4), (3, 3), (4, 3), (2, 4), (1, 5), (3, 4), (4, 4),
]


def finish(dq, dk, dv, n1, x, dh1, w, far, temb, gain, dgain2, w2, emb, u):
    half, width = far.shape
    rows = 3 * half
    hidden = w2.shape[0]
    whole = pl.BlockSpec(memory_space=pltpu.VMEM)
    sizes = [(3 * width // 8, 256)] * 3 + [(width // 8, hidden), (hidden // 8, 256)]
    scratch = [pltpu.VMEM((8,) + size, BF) for size in sizes]
    for size, x_second in zip(sizes, FINISH_PLAN):
        scratch += share_scratch(*size, x_second)
    return pl.pallas_call(
        finish_kernel,
        in_specs=[pl.BlockSpec(memory_space=pl.ANY)] * 7 + [whole] * 7,
        out_specs=[whole] * 7,
        out_shape=[
            jax.ShapeDtypeStruct((2, half, width), F32),
            jax.ShapeDtypeStruct((half, width), BF),
        ]
        + [jax.ShapeDtypeStruct((2, a, b // 2), BF) for a, b in sizes],
        scratch_shapes=[
            pltpu.VMEM((width, rows), BF),
            pltpu.VMEM((4 * half, width), BF),
            pltpu.VMEM((4 * half, width), BF),
            pltpu.VMEM((4 * half, width), BF),
            pltpu.VMEM((rows, width), BF),
            pltpu.VMEM((rows, width), F32),
            pltpu.VMEM(w.shape, BF),
            pltpu.VMEM((half, width), BF),
            pltpu.VMEM((half, width), BF),
            pltpu.SemaphoreType.DMA((20,)),
            pltpu.SemaphoreType.DMA((2,)),
        ]
        + scratch,
        compiler_params=pltpu.CompilerParams(
            vmem_limit_bytes=VMEM_LIMIT, collective_id=2, has_side_effects=True
        ),
        cost_estimate=pl.CostEstimate(flops=15 * 10**9, bytes_accessed=60 * 10**6, transcendentals=0),
    )(dq, dk, dv, n1, x, dh1, w, far, temb, gain, dgain2, w2, emb, u)


def gelu_and_slope(g):
    square = g * g
    half_plus = 0.5 * jnp.tanh(g * (GELU_A + GELU_A * GELU_B * square)) + 0.5
    act = g * half_plus
    slope = half_plus + act * (2.0 - 2.0 * half_plus) * (GELU_A + 3.0 * GELU_A * GELU_B * square)
    return act, slope


FF_BEGIN = {6: (0, 1), 12: (2, 3)}
FF_PLAN = [False, True, False, True]
FF_TICKS = {
    9: [(0, 0), (1, 0)],
    12: [(0, 1), (1, 1)],
    15: [(0, 2), (1, 2), (2, 0), (3, 0)],
    18: [(0, 3), (1, 3)],
    21: [(0, 4), (1, 4), (1, 5), (2, 1), (3, 1)],
}


def feedforward_kernel(
    x_hbm, o_ref, dm_ref, live_ref, temb_ref, gain_ref, wo_ref, *rest
):
    wu_refs, wd_refs, rest = rest[:4], rest[4:8], rest[8:]
    out_hbm, dh1_hbm, do_ref, dwu_hbm, dwd_hbm, dwo_ref, dgain_ref, *rest = rest
    finals, rest = rest[:4], rest[4:]
    finals, handed = finals[:2], finals[2:]
    x, h1, n2, h2, dn2, sems, *rest = rest
    up_sources, down_sources, *rest = rest
    sources = [ref.at[c] for c in range(2) for ref in (up_sources, down_sources)]
    shares = []
    for i in range(4):
        own = rest[SCRATCH_COUNT * i : SCRATCH_COUNT * (i + 1)]
        shares.append(Shares(sources[i], own, FF_PLAN[i]))
    turn, side = pl.program_id(0), pl.program_id(1)
    chunk, chunks = 2 * turn + side, 6
    wu = jnp.concatenate([ref[...] for ref in wu_refs], axis=1)
    wd = jnp.concatenate([ref[...] for ref in wd_refs], axis=0)
    rows, width = x.shape
    block = rows // 2
    third = rows // 3
    blocks = [slice(block * i, block * i + block) for i in range(2)]
    thirds = [slice(third * i, third * i + third) for i in range(3)]
    size = width // 8

    def act_on(now):
        for i, stage in FF_TICKS.get(now, []):
            if i >= 2 and stage == 1:
                shares[i].end(stage)
            else:
                shares[i].go_on(stage)
        for i in FF_BEGIN.get(now, []):
            shares[i].begin()

    def tick():
        for now in sorted(set(FF_TICKS) | set(FF_BEGIN)):
            if now < 18:
                pl.when(chunk == now // 3)(partial(act_on, now))

    load = pltpu.make_async_copy(x_hbm.at[pl.ds(0, rows)], x, sems.at[0])

    @pl.when(chunk == 0)
    def _():
        load.start()
        call()
        load.wait()
        for i, part in enumerate(thirds):
            h0 = x[part, :].astype(F32) + temb_ref[i // 2 : i // 2 + 1, :]
            h = h0 + mm(o_ref[:, part], wo_ref[...], 0, 0)
            h1[part, :] = h
            centered = h - jnp.mean(h, axis=1, keepdims=True)
            variance = jnp.mean(centered * centered, axis=1, keepdims=True)
            n2[part, :] = (centered * lax.rsqrt(variance + 1e-5) * gain_ref[...]).astype(BF)
            h2[part, :] = h
            dn2[part, :] = jnp.zeros_like(h)

    def first(part):
        return mm(n2[part, :], wu, 1, 0), mm(dm_ref[part, :], wd, 1, 1)

    def second(pair):
        act, slope = gelu_and_slope(pair[0])
        return act.astype(BF), (pair[1] * slope).astype(BF)

    def third_step(part, pair):
        h2[part, :] += mm(pair[0], wd, 1, 0)
        dn2[part, :] += mm(pair[1], wu, 1, 1)

    @pl.when(chunk == 2)
    def _():
        pl.semaphore_wait(pltpu.get_barrier_semaphore(), GREETED)

    tick()
    a = first(blocks[0])
    b = first(blocks[1])
    a = second(a)
    b = second(b)
    third_step(blocks[0], a)
    third_step(blocks[1], b)
    act = jnp.concatenate([a[0], b[0]], axis=0)
    dg = jnp.concatenate([a[1], b[1]], axis=0)
    dwd = mm(dm_ref[...], act, 0, 0).astype(BF)
    dwu = mm(dg, n2[...], 0, 0).astype(BF).reshape(4, 128, width)
    up_sources[turn % 2, pl.ds(4 * side, 4)] = dwu
    columns = pl.ds(pl.multiple_of(512 * side, 128), 512)
    for k in range(8):
        down_sources[turn % 2, place_of(k), :, columns] = dwd[size * k : size * k + size]

    @pl.when(chunk == chunks - 1)
    def _():
        act_on(18)
        dgain = jnp.zeros_like(dgain_ref)
        for i, part in enumerate(thirds):
            h = h1[part, :]
            live = live_ref[part, 0:1].astype(F32)
            x[part, :] = (live * h2[part, :]).astype(BF)
            centered = h - jnp.mean(h, axis=1, keepdims=True)
            variance = jnp.mean(centered * centered, axis=1, keepdims=True)
            r2 = lax.rsqrt(variance + 1e-5)
            x2 = centered * r2
            dn = dn2[part, :]
            dgain += jnp.sum(dn * x2, axis=0, keepdims=True)
            e = dn * gain_ref[...]
            dh1 = dm_ref[part, :].astype(F32) + r2 * (
                e
                - jnp.mean(e, axis=1, keepdims=True)
                - x2 * jnp.mean(e * x2, axis=1, keepdims=True)
            )
            h1[part, :] = dh1
            da = dh1.astype(BF)
            n2[part, :] = da
            do_ref[:, part] = mm(wo_ref[...], da, 1, 1).astype(BF)
            act_on(19 + i)
        for i in range(2):
            finals[i][...] = shares[i].final[...]
        stores = [
            pltpu.make_async_copy(x, out_hbm, sems.at[1]),
            pltpu.make_async_copy(h1, dh1_hbm, sems.at[2]),
            pltpu.make_async_copy(shares[2].acc, handed[0], sems.at[3]),
            pltpu.make_async_copy(shares[3].acc, handed[1], sems.at[4]),
            pltpu.make_async_copy(sources[0], dwu_hbm, sems.at[5]),
            pltpu.make_async_copy(sources[1], dwd_hbm, sems.at[6]),
        ]
        for store in stores:
            store.start()
        dgain_ref[...] = dgain
        dwo = mm(n2[...], o_ref[...], 0, 1).astype(BF)
        for k in range(8):
            dwo_ref[place_of(k)] = dwo[size * k : size * k + size]
        for store in stores:
            store.wait()


def feedforward(x, o, dm, live, temb, gain, wo, wu, wd):
    rows, width = dm.shape
    whole = pl.BlockSpec(memory_space=pltpu.VMEM)
    anywhere = pl.BlockSpec(memory_space=pl.ANY)

    def tile(c, h, i):
        return 3 * (4 * (i % 2) + 2 * (i // 2) + h) + c

    up_specs = [pl.BlockSpec((width, 128), lambda c, h, i=i: (0, tile(c, h, i))) for i in range(4)]
    down_specs = [pl.BlockSpec((128, width), lambda c, h, i=i: (tile(c, h, i), 0)) for i in range(4)]
    sizes = [(128, width), (width // 8, 1024)] * 2
    scratch = [pltpu.VMEM((2, 8) + size, BF) for size in sizes[:2]]
    for size, x_second in zip(sizes, FF_PLAN):
        scratch += share_scratch(*size, x_second)
    return pl.pallas_call(
        feedforward_kernel,
        grid=(3, 2),
        in_specs=[anywhere] + [whole] * 6 + up_specs + down_specs,
        out_specs=[anywhere] * 2 + [whole] + [anywhere] * 2 + [whole] * 4 + [anywhere] * 2,
        out_shape=[
            jax.ShapeDtypeStruct((rows, width), BF),
            jax.ShapeDtypeStruct((rows, width), F32),
            jax.ShapeDtypeStruct((width, rows), BF),
            jax.ShapeDtypeStruct((8, 128, width), BF),
            jax.ShapeDtypeStruct((8, width // 8, 1024), BF),
            jax.ShapeDtypeStruct((8, width // 8, width), BF),
            jax.ShapeDtypeStruct((1, width), F32),
        ]
        + [jax.ShapeDtypeStruct((2, a, b // 2), BF) for a, b in sizes[:2]]
        + [jax.ShapeDtypeStruct((8, a, b // 2), BF) for a, b in sizes[2:]],
        scratch_shapes=[
            pltpu.VMEM((rows, width), BF),
            pltpu.VMEM((rows, width), F32),
            pltpu.VMEM((rows, width), BF),
            pltpu.VMEM((rows, width), F32),
            pltpu.VMEM((rows, width), F32),
            pltpu.SemaphoreType.DMA((7,)),
        ]
        + scratch,
        compiler_params=pltpu.CompilerParams(
            vmem_limit_bytes=VMEM_LIMIT, collective_id=3, has_side_effects=True
        ),
        cost_estimate=pl.CostEstimate(flops=48 * 10**9, bytes_accessed=50 * 10**6, transcendentals=5 * 10**6),
    )(x, o, dm, live, temb, gain, wo, *[wu] * 4, *[wd] * 4)


def pair_plan(
    inputs,
    timesteps,
    counts,
    slot_token_mask,
    time_first_weight,
    time_second_weight,
    attention_norm_gain,
    query_key_value_weight,
    attention_output_weight,
    feedforward_norm_gain,
    up_projection_weight,
    down_projection_weight,
    cotangent,
):
    slots, half, width = inputs.shape
    batches = lax.axis_size("batch")
    (o, exact, inv, even, odd, live_wide, temb, emb, u, q, kv, n1, x, dm) = attend(
        counts,
        timesteps,
        inputs,
        slot_token_mask,
        cotangent,
        time_first_weight,
        time_second_weight,
        attention_norm_gain[None, :],
        query_key_value_weight,
    )
    o = o.reshape(width, 3 * half)
    out, dh1, do, dwu, dwd, dwo, dgain2, *early = feedforward(
        x,
        o,
        dm,
        live_wide,
        temb,
        feedforward_norm_gain[None, :],
        attention_output_weight,
        up_projection_weight,
        down_projection_weight,
    )
    dq, dk, dv, far, out_far, *sums = attend_back(
        q,
        kv,
        do,
        exact.reshape(width, 3 * half),
        inv,
        even,
        odd,
        query_key_value_weight,
        out,
        [*early[2:], dwu, dwd, dwo],
        BACK_PLAN,
        BACK_TABLE,
    )
    grad_own, grad_far, *last = finish(
        dq,
        dk,
        dv,
        n1,
        x,
        dh1,
        query_key_value_weight,
        far,
        temb,
        attention_norm_gain[None, :],
        dgain2,
        time_second_weight,
        emb,
        u,
    )
    up = [early[0], sums[0], sums[2]]
    down = [early[1], sums[1], sums[3]]
    output, grad_inputs, inner, outer, gain1, qk, v, out_sum, gain2, up, down = assemble(
        batches, out, out_far, grad_own, grad_far, up + down + [sums[4]] + last
    )
    return (
        output,
        grad_inputs,
        inner.T,
        outer.T,
        gain1[0],
        qk.T,
        v.T,
        out_sum.T,
        gain2[0],
        up.T,
        down.T,
    )


def assemble_kernel(seq_ref, out_ref, out_far_ref, grad_ref, grad_far_ref, *refs):
    ups, downs, (wo, *qkv), (outer, inner) = refs[0:3], refs[3:6], refs[6:10], refs[10:12]
    (output_to, grad_to, inner_to, outer_to, gain1_to, qk_to, v_to, out_to, gain2_to, up_to, down_to) = refs[12:]
    far = pl.program_id(0) == 1

    @pl.when(far)
    def _():
        output_to[0] = out_far_ref[...]
        grad_to[0] = grad_far_ref[...].astype(F32)

    @pl.when(jnp.logical_not(far))
    def _():
        output_to[0] = out_ref[...]
        grad_to[0] = grad_ref[0]

    core = lax.axis_index("batch") & 1

    def joined(ref):
        return jnp.concatenate([ref[0], ref[1]], axis=1)

    def own_half(array):
        size = array.shape[0] // 2
        return jnp.where(core == 0, array[:size], array[size:]).astype(F32)

    @pl.when(pl.program_id(0) == 0)
    def _():
        up_to[...] = own_half(jnp.concatenate([joined(ref) for ref in ups], axis=0))
        for c, ref in enumerate(downs):
            part = own_half(joined(ref))
            for k in range(8):
                first = 128 * place_of(k)
                down_to[:, 128 * (3 * k + c) : 128 * (3 * k + c + 1)] = part[:, first : first + 128]
        out_to[...] = own_half(joined(wo))
        whole = jnp.concatenate([joined(ref) for ref in qkv], axis=1)
        split = whole.shape[0] * 2 // 3
        qk_to[...] = own_half(whole[:split])
        v_to[...] = own_half(whole[split:])
        outer_to[...] = own_half(joined(outer))
        inner_to[...] = own_half(inner[0])
        size = gain1_to.shape[1]
        gains = inner[1, 0:16, :].astype(F32)
        for row, target in enumerate((gain1_to, gain2_to)):
            target[...] = jnp.where(
                core == 0, gains[row : row + 1, :size], gains[row : row + 1, size : 2 * size]
            )


def assemble(batches, out, out_far, grad_own, grad_far, parts):
    half, width = out_far.shape
    hidden = 4 * width
    size = width // batches
    time_hidden, channels = 2 * parts[10].shape[2], parts[11].shape[2]
    whole = pl.BlockSpec(memory_space=pltpu.VMEM)
    slot = pl.BlockSpec((1, half, width), lambda i, seq: (jnp.where(i == 1, 1 - seq[0], jnp.maximum(i, seq[0])), 0, 0))
    shapes = [
        (time_hidden // batches, channels),
        (size, time_hidden),
        (1, size),
        (2 * size, width),
        (size, width),
        (size, width),
        (1, size),
        (hidden // batches, width),
        (size, hidden),
    ]
    return pl.pallas_call(
        assemble_kernel,
        grid_spec=pltpu.PrefetchScalarGridSpec(
            num_scalar_prefetch=1,
            grid=(3,),
            in_specs=[
                pl.BlockSpec((half, width), lambda i, seq: (i // 2 * 2, 0)),
                whole,
                pl.BlockSpec((1, half, width), lambda i, seq: (i // 2, 0, 0)),
                whole,
            ]
            + [whole] * 12,
            out_specs=[slot] * 2 + [whole] * 9,
        ),
        out_shape=[
            jax.ShapeDtypeStruct((3, half, width), BF),
            jax.ShapeDtypeStruct((3, half, width), F32),
        ]
        + [jax.ShapeDtypeStruct(shape, F32) for shape in shapes],
        compiler_params=pltpu.CompilerParams(vmem_limit_bytes=VMEM_LIMIT),
    )(lax.axis_index("seq")[None], out, out_far, grad_own, grad_far, *parts)


BACK_PLAN = [False, True, False, False, False]
BACK_TABLE = {
    2: [(2, 0), (3, 0), (4, 0)],
    3: [(1, 2)],
    5: [(0, 2)],
    6: [(1, 3)],
    7: [(0, 3), (1, 4), (2, 1)],
    9: [(0, 4), (1, 5)],
    11: [(3, 1)],
    12: [(2, 2)],
    14: [(2, 3), (4, 1)],
    15: [(3, 2)],
    16: [(2, 4)],
    17: [(3, 3), (4, 2)],
    18: [(3, 4), (4, 3), (4, 4)],
}


def solution(mesh):
    on_device = pair_plan if mesh.shape["seq"] == 2 and mesh.shape["batch"] == 16 else ring_plan
    return jax.shard_map(
        on_device,
        mesh=mesh,
        in_specs=(
            P("batch", "seq", None),
            P("batch"),
            P("batch"),
            P("batch", "seq"),
            P(),
            P(),
            P(),
            P(),
            P(),
            P(),
            P(),
            P(),
            P("batch", "seq", None),
        ),
        out_specs=(
            P("batch", "seq", None),
            P("batch", "seq", None),
            P(None, "batch"),
            P(None, "batch"),
            P("batch"),
            P(None, "batch"),
            P(None, "batch"),
            P(None, "batch"),
            P("batch"),
            P(None, "batch"),
            P(None, "batch"),
        ),
        check_vma=False,
    )
```
